32 devices in a mesh: dp: 8 (over y, x, core), phase: 4 (over z).
Axes of the slice: x: 2, y: 2, z: 4, core: 2. Of those that a mesh axis runs over, the one named last changes fastest.
Arguments:
- expression: bfloat16 [16, 192, 2048], P('dp', 'phase'), may hold values from -6 to 6
- targets: bfloat16 [16, 192, 2048], P('dp', 'phase'), may hold values from -6 to 6
- noise: bfloat16 [16, 192, 512], P('dp', 'phase'), may hold values from -5 to 5
- gene_masks: int32 [16, 2048], P('dp'), may hold values 0 or 1
- segment_ids: int32 [16, 192], P('dp'), may hold values from 0 to 2, as said below
- w_gene: bfloat16 [2048, 1024], replicated, may hold values from -0.125 to 0.125
- emb_gain: float32 [1024], replicated, may hold values from 0.1 to 1.9
- emb_shift: float32 [1024], replicated, may hold values from -1.75 to 1.75
- attn_gain: float32 [1024], replicated, may hold values from 0.1 to 1.9
- attn_shift: float32 [1024], replicated, may hold values from -1.75 to 1.75
- w_qkv: bfloat16 [1024, 3072], replicated, may hold values from -0.1875 to 0.1875
- b_qkv: float32 [3072], replicated, may hold values from -1.75 to 1.75
- w_out: bfloat16 [1024, 1024], replicated, may hold values from -1.5 to 1.5
- b_out: float32 [1024], replicated, may hold values from -1.75 to 1.75
- ffn_gain: float32 [1024], replicated, may hold values from 0.1 to 1.9
- ffn_shift: float32 [1024], replicated, may hold values from -1.75 to 1.75
- w_up: bfloat16 [1024, 4096], replicated, may hold values from -0.1875 to 0.1875
- b_up: float32 [4096], replicated, may hold values from -1.75 to 1.75
- w_down: bfloat16 [4096, 1024], replicated, may hold values from -0.09375 to 0.09375
- b_down: float32 [1024], replicated, may hold values from -1.75 to 1.75
- bot_gain: float32 [1024], replicated, may hold values from 0.1 to 1.9
- bot_shift: float32 [1024], replicated, may hold values from -1.75 to 1.75
- w_enc: bfloat16 [1024, 1024], replicated, may hold values from -0.09375 to 0.09375
- b_enc: float32 [1024], replicated, may hold values from -1.75 to 1.75
- comp_mean: float32 [16, 512], replicated, may hold values from -3 to 3
- comp_logvar: float32 [16, 512], replicated, may hold values from -0.5 to 0.5
- w_lat: bfloat16 [512, 1024], replicated, may hold values from -0.25 to 0.25
- b_lat: float32 [1024], replicated, may hold values from -1.75 to 1.75
- dec_gain: float32 [1024], replicated, may hold values from 0.1 to 1.9
- dec_shift: float32 [1024], replicated, may hold values from -1.75 to 1.75
- w_dec: bfloat16 [1024, 2048], replicated, may hold values from -0.1875 to 0.1875
- b_dec: float32 [2048], replicated, may hold values from -1.75 to 1.75
Outputs:
- input_grad: float32 [16, 192, 2048], P('dp', 'phase')
- w_gene_grad: float32 [2048, 1024], P('dp')
- emb_gain_grad: float32 [1024], P('dp')
- emb_shift_grad: float32 [1024], P('dp')
- attn_gain_grad: float32 [1024], P('dp')
- attn_shift_grad: float32 [1024], P('dp')
- w_qkv_grad: float32 [1024, 3072], P('dp')
- b_query_grad: float32 [1024], P('dp')
- b_value_grad: float32 [1024], P('dp')
- w_out_grad: float32 [1024, 1024], P('dp')
- b_out_grad: float32 [1024], P('dp')
- ffn_gain_grad: float32 [1024], P('dp')
- ffn_shift_grad: float32 [1024], P('dp')
- w_up_grad: float32 [1024, 4096], P('dp')
- b_up_grad: float32 [4096], P('dp')
- w_down_grad: float32 [4096, 1024], P('dp')
- b_down_grad: float32 [1024], P('dp')
- bot_gain_grad: float32 [1024], P('dp')
- bot_shift_grad: float32 [1024], P('dp')
- w_enc_grad: float32 [1024, 1024], P('dp')
- b_enc_grad: float32 [1024], P('dp')
- comp_mean_grad: float32 [16, 512], P(None, 'dp')
- comp_logvar_grad: float32 [16, 512], P(None, 'dp')
- w_lat_grad: float32 [512, 1024], P('dp')
- b_lat_grad: float32 [1024], P('dp')
- dec_gain_grad: float32 [1024], P('dp')
- dec_shift_grad: float32 [1024], P('dp')
- w_dec_grad: float32 [1024, 2048], P('dp')
- b_dec_grad: float32 [2048], P('dp')
The draws below stay inside these ranges and needn't reach their ends.
Inputs may be any that keep to these rules, and one draw needn't show every extreme that they name: `segment_ids`: each sequence holds three runs of positions numbered 0, 1, 2 in order; the first and the last run each hold 1 to 24 positions.
All inputs are finite; a program needn't handle non-finite values. No bound on the sum of `gene_masks` on one device may be relied on, other than what follows from the above.
Results may differ from the reference program's by a relative error of at most 0.015.
Values may be sent and summed in bfloat16 or wider, within the bound.
A program may use at most 320 MiB of HBM per device.

```python
import math
import jax
import jax.numpy as jnp
from jax import lax

D = 1024
FF = 4096
HEADS = 16
LATENT = 512
COMPONENTS = 16
GENES = 2048
LEN = 192
SEQS = 16


def draw_segment_ids(key, part):
    key = jax.random.fold_in(key, 11)
    first_key, last_key = jax.random.split(key)
    first_cut = jax.random.randint(first_key, (SEQS, 1), 1, LEN // 8 + 1)
    last_cut = LEN - jax.random.randint(last_key, (SEQS, 1), 1, LEN // 8 + 1)
    position = jnp.arange(LEN, dtype=jnp.int32)[None, :]
    return (position >= first_cut).astype(jnp.int32) + (position >= last_cut).astype(jnp.int32)


def touch_ends(array, key, smallest, high):
    longest = array.shape.index(max(array.shape))
    spots = []
    for shift in (0, 1):
        where = [jax.random.randint(jax.random.fold_in(key, axis), (), 0, length) for axis, length in enumerate(array.shape)]
        where[longest] = (where[longest] + shift) % array.shape[longest]
        spots.append(tuple(where))
    return array.at[spots[0]].set(smallest).at[spots[1]].set(high)


def steps_of(stream_key, extent, cuts, least, high):
    factor_of = 1.0
    for dim, shards_of in cuts:
        draws = jax.random.uniform(jax.random.fold_in(jax.random.fold_in(stream_key, 6), dim), (shards_of,), jnp.float32, least / len(cuts), high / len(cuts))
        factor_of = factor_of * jnp.repeat(jnp.exp(draws), extent[dim] // shards_of).reshape((-1,) + (1,) * (len(extent) - 1 - dim))
    return factor_of


def bell_draw(own_key, shape, scale, most, shards=(), kind=jnp.bfloat16):
    array = scale * jax.random.normal(own_key, shape, jnp.float32)
    if shards:
        array = array * steps_of(own_key, shape, shards, -0.22, 0.18)
    return jnp.clip(array, -most, most).astype(kind)


def setup_inputs(seed: int = 0) -> dict:
    keys = jax.random.split(jax.random.key(seed), 33)
    return {
        "expression": bell_draw(keys[0], (SEQS, LEN, GENES), 1.0, 6.0, ((0, 8), (1, 4))),
        "targets": bell_draw(keys[1], (SEQS, LEN, GENES), 1.0, 6.0, ((0, 8), (1, 4))),
        "noise": bell_draw(keys[2], (SEQS, LEN, LATENT), 1.0, 5.0, ((0, 8), (1, 4))),
        "gene_masks": touch_ends((jax.random.randint(keys[3], (SEQS, GENES), 0, 2) < 1).astype(jnp.int32), jax.random.fold_in(keys[3], 1), 0, 1),
        "segment_ids": draw_segment_ids(jax.random.fold_in(keys[32], 71), 0),
        "w_gene": bell_draw(keys[5], (GENES, D), GENES ** -0.5, 0.125),
        "emb_gain": jnp.clip(1.0 + 0.18 * jax.random.normal(keys[6], (D,), jnp.float32), 0.1, 1.9),
        "emb_shift": bell_draw(keys[7], (D,), 0.3, 1.75, (), jnp.float32),
        "attn_gain": jnp.clip(1.0 + 0.18 * jax.random.normal(keys[8], (D,), jnp.float32), 0.1, 1.9),
        "attn_shift": bell_draw(keys[9], (D,), 0.3, 1.75, (), jnp.float32),
        "w_qkv": bell_draw(keys[10], (D, 3 * D), D ** -0.5, 0.1875),
        "b_qkv": bell_draw(keys[11], (3 * D,), 0.3, 1.75, (), jnp.float32),
        "w_out": bell_draw(keys[12], (D, D), (D // 64) ** -0.5, 1.5),
        "b_out": bell_draw(keys[13], (D,), 0.3, 1.75, (), jnp.float32),
        "ffn_gain": jnp.clip(1.0 + 0.18 * jax.random.normal(keys[14], (D,), jnp.float32), 0.1, 1.9),
        "ffn_shift": bell_draw(keys[15], (D,), 0.3, 1.75, (), jnp.float32),
        "w_up": bell_draw(keys[16], (D, FF), D ** -0.5, 0.1875),
        "b_up": bell_draw(keys[17], (FF,), 0.3, 1.75, (), jnp.float32),
        "w_down": bell_draw(keys[18], (FF, D), FF ** -0.5, 0.09375),
        "b_down": bell_draw(keys[19], (D,), 0.3, 1.75, (), jnp.float32),
        "bot_gain": jnp.clip(1.0 + 0.18 * jax.random.normal(keys[20], (D,), jnp.float32), 0.1, 1.9),
        "bot_shift": bell_draw(keys[21], (D,), 0.3, 1.75, (), jnp.float32),
        "w_enc": bell_draw(keys[22], (D, 2 * LATENT), (4 * D) ** -0.5, 0.09375),
        "b_enc": bell_draw(keys[23], (2 * LATENT,), 0.3, 1.75, (), jnp.float32),
        "comp_mean": bell_draw(keys[24], (COMPONENTS, LATENT), 0.5, 3.0, (), jnp.float32),
        "comp_logvar": jnp.clip(jax.random.uniform(keys[25], (COMPONENTS, LATENT), jnp.float32, -0.5, 0.5), -0.5, 0.5),
        "w_lat": bell_draw(keys[26], (LATENT, D), LATENT ** -0.5, 0.25),
        "b_lat": bell_draw(keys[27], (D,), 0.3, 1.75, (), jnp.float32),
        "dec_gain": jnp.clip(1.0 + 0.18 * jax.random.normal(keys[28], (D,), jnp.float32), 0.1, 1.9),
        "dec_shift": bell_draw(keys[29], (D,), 0.3, 1.75, (), jnp.float32),
        "w_dec": bell_draw(keys[30], (D, GENES), D ** -0.5, 0.1875),
        "b_dec": bell_draw(keys[31], (GENES,), 0.3, 1.75, (), jnp.float32),
    }


@jax.custom_vjp
def low(v):
    return lax.optimization_barrier(v.astype(jnp.bfloat16)).astype(jnp.float32)

@jax.custom_vjp
def low_back(v):
    return v

def low_keep(v):
    return (low(v), None)

def low_pass(kept, grad):
    return (grad,)

def back_keep(v):
    return (v, None)

def back_low(kept, grad):
    return (low(grad),)
low.defvjp(low_keep, low_pass)
low_back.defvjp(back_keep, back_low)
norm_eps = 1e-05
mask_fill = -1000000000.0

def matmul(left, right):
    return jnp.dot(left, right, precision=lax.Precision.HIGHEST, preferred_element_type=jnp.float32)

def layer_norm(values, gain, shift):
    center = lax.optimization_barrier(jnp.mean(values, axis=-1, keepdims=True))
    centered = values - center
    spread = lax.optimization_barrier(jnp.mean(centered * centered, axis=-1, keepdims=True))
    return centered * lax.rsqrt(spread + norm_eps) * gain + shift

def positions(length, width):
    place_index = jnp.arange(length, dtype=jnp.float32)[:, None]
    frequency = jnp.exp(jnp.arange(width // 2, dtype=jnp.float32) * (-2.0 * math.log(10000.0) / width))
    angles = place_index * frequency[None, :]
    return jnp.stack([jnp.sin(angles), jnp.cos(angles)], axis=-1).reshape(length, width)

def split_heads(matrix):
    return matrix.reshape(matrix.shape[0], HEADS, matrix.shape[1] // HEADS)

def sample_and_kl(moments, noise_rows, comp_mean, comp_logvar):
    latent_width = moments.shape[1] // 2
    latent_mean = moments[:, :latent_width]
    logvar = moments[:, latent_width:]
    latent = latent_mean + jnp.exp(0.5 * logvar) * noise_rows
    inverse = jnp.exp(-comp_logvar)
    offsets = latent[:, None, :] - comp_mean[None]
    quadratic = lax.optimization_barrier(jnp.sum(offsets * offsets * inverse[None], axis=-1)) + lax.optimization_barrier(jnp.sum(comp_logvar, axis=-1))[None]
    scaled = -0.5 * quadratic
    highest = lax.optimization_barrier(jnp.max(scaled, axis=-1, keepdims=True))
    prior = jnp.log(lax.optimization_barrier(jnp.sum(jnp.exp(scaled - highest), axis=-1))) + highest[:, 0]
    divergence = jnp.sum(-0.5 * lax.optimization_barrier(jnp.sum(logvar, axis=-1)) - prior)
    return (latent, divergence)

def layer_block(stream, segments, weights):
    attn_gain, attn_shift, w_qkv, b_qkv, w_out, b_out, ffn_gain, ffn_shift, w_up, b_up, w_down, b_down = weights
    normed_attn = low(layer_norm(stream, attn_gain, attn_shift))
    projected = low(low_back(matmul(normed_attn, w_qkv) + b_qkv))
    query_heads = split_heads(projected[:, :D])
    key_heads = split_heads(projected[:, D:2 * D])
    value_heads = split_heads(projected[:, 2 * D:])
    scores = jnp.einsum('qhd,khd->hqk', query_heads, key_heads, precision=lax.Precision.HIGHEST)
    scores = low_back(scores * (D // HEADS) ** (-0.5))
    same_doc = segments[:, None] == segments[None, :]
    scores = jnp.where(same_doc[None], scores, mask_fill)
    shifted = jnp.exp(scores - lax.optimization_barrier(jnp.max(scores, axis=-1, keepdims=True)))
    probability = low(shifted / lax.optimization_barrier(jnp.sum(shifted, axis=-1, keepdims=True)))
    attended = jnp.einsum('hqk,khd->qhd', probability, value_heads, precision=lax.Precision.HIGHEST)
    attended = low(low_back(attended.reshape(stream.shape[0], D)))
    mixed_rows = stream + low_back(matmul(attended, w_out) + b_out)
    normed_ffn = low(layer_norm(mixed_rows, ffn_gain, ffn_shift))
    before = low_back(matmul(normed_ffn, w_up) + b_up)
    activated = low(jax.nn.gelu(before, approximate=False))
    return mixed_rows + low_back(matmul(activated, w_down) + b_down)

def sequence_loss(pieces, params):
    expr_rows, target_rows, noise_rows, segments, gene_mask = pieces
    w_gene, emb_gain, emb_shift = params[0:3]
    bot_gain, bot_shift, w_enc, b_enc, comp_mean, comp_logvar, w_lat, b_lat = params[15:23]
    dec_gain, dec_shift, w_dec, b_dec = params[23:27]
    mask_full = gene_mask.astype(jnp.float32)
    masked = low(expr_rows * (1.0 - mask_full)[None, :])
    embedded = low_back(matmul(masked, w_gene) + positions(LEN, D))
    stream = low(low_back(layer_norm(embedded, emb_gain, emb_shift)))
    stream = layer_block(stream, segments, params[3:15])
    stream = low(low_back(stream))
    normed_bot = low(layer_norm(stream, bot_gain, bot_shift))
    moments = low_back(matmul(normed_bot, w_enc) + b_enc)
    latent, divergence = sample_and_kl(moments, noise_rows, comp_mean, comp_logvar)
    lat_pre = low_back(matmul(low(latent), w_lat) + b_lat)
    stream = low(low_back(jax.nn.gelu(lat_pre, approximate=False)))
    normed_dec = low(layer_norm(stream, dec_gain, dec_shift))
    predicted = low_back(matmul(normed_dec, w_dec) + b_dec)
    residual = predicted - target_rows
    recon = 0.5 * jnp.sum(mask_full[None, :] * residual * residual)
    return recon + divergence

def reference(expression, targets, noise, gene_masks, segment_ids, w_gene, emb_gain, emb_shift, attn_gain, attn_shift, w_qkv, b_qkv, w_out, b_out, ffn_gain, ffn_shift, w_up, b_up, w_down, b_down, bot_gain, bot_shift, w_enc, b_enc, comp_mean, comp_logvar, w_lat, b_lat, dec_gain, dec_shift, w_dec, b_dec):
    params = tuple((param.astype(jnp.float32) for param in (w_gene, emb_gain, emb_shift, attn_gain, attn_shift, w_qkv, b_qkv, w_out, b_out, ffn_gain, ffn_shift, w_up, b_up, w_down, b_down, bot_gain, bot_shift, w_enc, b_enc, comp_mean, comp_logvar, w_lat, b_lat, dec_gain, dec_shift, w_dec, b_dec)))
    target_full = targets.astype(jnp.float32)
    noise_full = noise.astype(jnp.float32)

    def network(inputs, weights):

        def one_sequence(pieces):
            return sequence_loss(pieces, weights)
        losses = lax.map(jax.checkpoint(one_sequence), (inputs, target_full, noise_full, segment_ids, gene_masks))
        return jnp.sum(losses)
    total_loss, pullback = jax.vjp(network, expression.astype(jnp.float32), params)
    input_grad, grads = pullback(jnp.ones((), total_loss.dtype))
    bias_grad = grads[6]
    return (input_grad, grads[0], grads[1], grads[2], grads[3], grads[4], grads[5], bias_grad[:D], bias_grad[2 * D:], grads[7], grads[8], grads[9], grads[10], grads[11], grads[12], grads[13], grads[14], grads[15], grads[16], grads[17], grads[18], grads[19], grads[20], grads[21], grads[22], grads[23], grads[24], grads[25], grads[26])
```

```python
import functools
import math

import jax
import jax.numpy as jnp
from jax import lax
from jax.experimental import pallas as pl
from jax.experimental.pallas import tpu as pltpu
from jax.sharding import PartitionSpec as P

HEADS = 16
GROUP = 8
PIECE = 128
WIDE = 1024

norm_eps = 1e-05
mask_fill = -1000000000.0
MESH = pl.DeviceIdType.MESH


def layer_norm(values, gain, shift):
    center = jnp.mean(values, axis=-1, keepdims=True)
    centered = values - center
    spread = jnp.mean(centered * centered, axis=-1, keepdims=True)
    return centered * lax.rsqrt(spread + norm_eps) * gain + shift


def gelu_exact(values):
    return jax.nn.gelu(values, approximate=False)


def mm(left, right):
    return jnp.dot(left, right, preferred_element_type=jnp.float32)


def contract_last(left, right):
    return lax.dot_general(
        left, right, (((1,), (1,)), ((), ())), preferred_element_type=jnp.float32
    )


def column_sums(values):
    return jnp.sum(values, axis=0, dtype=jnp.float32)


def positions(start, length, width):
    place_index = (start + jnp.arange(length)).astype(jnp.float32)[:, None]
    frequency = jnp.exp(
        jnp.arange(width // 2, dtype=jnp.float32) * (-2.0 * math.log(10000.0) / width)
    )
    angles = place_index * frequency[None, :]
    return jnp.stack([jnp.sin(angles), jnp.cos(angles)], axis=-1).reshape(length, width)


def sample_and_kl(moments, noise_rows, comp_mean, comp_logvar):
    latent_width = moments.shape[1] // 2
    latent_mean = moments[:, :latent_width]
    logvar = moments[:, latent_width:]
    latent = latent_mean + jnp.exp(0.5 * logvar) * noise_rows
    inverse = jnp.exp(-comp_logvar)
    offsets = latent[:, None, :] - comp_mean[None]
    quadratic = (
        jnp.sum(offsets * offsets * inverse[None], axis=-1) + jnp.sum(comp_logvar, axis=-1)[None]
    )
    scaled = -0.5 * quadratic
    highest = jnp.max(scaled, axis=-1, keepdims=True)
    prior = jnp.log(jnp.sum(jnp.exp(scaled - highest), axis=-1)) + highest[:, 0]
    divergence = jnp.sum(-0.5 * jnp.sum(logvar, axis=-1) - prior)
    return (latent, divergence)


def grad_plan(layers):
    a_off, b_off, items, row = {}, {}, [], 0
    a_at, b_at = 0, 0
    for name, share, blocks in layers:
        a_off[name], b_off[name] = a_at, b_at
        for block in range(blocks):
            for start in range(0, share, PIECE):
                rows = min(PIECE, share - start)
                items.append((b_at + block, a_at + start, row, rows))
                row += rows
        a_at += -(-share // PIECE) * PIECE
        b_at += blocks
    return a_off, b_off, items, row, a_at, b_at


def grad_kernel(
    plan,
    a_groups,
    a_ref,
    b_ref,
    v_ref,
    out_ref,
    a_all,
    b_all,
    v_all,
    mine,
    sent,
    got,
    crossed,
    total,
    local_sem,
    a_send,
    a_recv,
    v_send,
    v_recv,
    b_send,
    b_recv,
    c_send,
    c_recv,
    o_sem,
):
    items, rows_all, _, blocks = plan[2:6]
    d = lax.axis_index("dp")
    z = lax.axis_index("phase")
    base = (d // GROUP) * GROUP
    r = d % GROUP
    core, cx, cy = r % 2, (r // 2) % 2, r // 4
    rc, rx, ry = r + 1 - 2 * core, r + 2 - 4 * cx, r + 4 - 8 * cy
    rxc, ryc = rx + 1 - 2 * core, ry + 1 - 2 * core
    rd = rx + 4 - 8 * cy
    rdc = rd + 1 - 2 * core
    middle = (z % 3) != 0
    inward = z + 1 - 2 * (z // 2)
    outward = z - 1 + 2 * (z // 2)
    half = WIDE // 2

    barrier = pltpu.get_barrier_semaphore()
    for step in range(1, GROUP):
        pl.semaphore_signal(
            barrier, inc=1, device_id=(base + (r + step) % GROUP, z), device_id_type=MESH
        )
    pl.semaphore_signal(barrier, inc=1, device_id=(d, inward), device_id_type=MESH)

    @pl.when(middle)
    def _():
        pl.semaphore_signal(barrier, inc=1, device_id=(d, outward), device_id_type=MESH)
        pl.semaphore_wait(barrier, GROUP + 1)

    @pl.when(jnp.logical_not(middle))
    def _():
        pl.semaphore_wait(barrier, GROUP)

    def remote(src, dst, send, recv, to):
        return pltpu.make_async_remote_copy(
            src_ref=src,
            dst_ref=dst,
            send_sem=send,
            recv_sem=recv,
            device_id=to,
            device_id_type=MESH,
        )

    def a_copy(group, step, slot):
        start, size = a_groups[group]
        to = (r + step) % GROUP
        return remote(
            a_ref.at[to, :, pl.ds(start, size)],
            a_all.at[slot, :, pl.ds(start, size)],
            a_send.at[group, step],
            a_recv.at[group, step],
            (base + to, z),
        )

    def v_copy(step, slot):
        to = (r + step) % GROUP
        return remote(
            v_ref.at[to], v_all.at[slot], v_send.at[step], v_recv.at[step], (base + to, z)
        )

    def b_copy(kind, block, source):
        col, width = block * WIDE, WIDE
        if kind in (5, 7):
            width = half
        if kind in (6, 8):
            col, width = col + half, half
        to = (rx, ry, rc, rc, rc, ry, rx, rc, rc)[kind]
        view = b_all.at[source, :, pl.ds(col, width)]
        src = b_ref.at[:, pl.ds(col, width)] if kind < 3 else view
        return remote(
            src, view, b_send.at[block, kind], b_recv.at[block, kind], (base + to, z)
        )

    comes = (rx, ry, rc, rxc, ryc, rd, rd, rdc, rdc)
    goes = (r, r, r, rx, ry, rx, ry, rd, rd)

    def b_start(kind, block):
        b_copy(kind, block, goes[kind]).start()

    def b_arrive(kind, block):
        b_copy(kind, block, comes[kind]).wait_recv()

    def own_start(block):
        for kind in (0, 1, 2):
            b_start(kind, block)

    def a_start(group):
        for step in range(1, GROUP):
            a_copy(group, step, r).start()

    def a_arrive(group):
        for step in range(1, GROUP):
            a_copy(group, step, (r + GROUP - step) % GROUP).wait_recv()

    group_of = {}
    for block, a_at, _, _ in items:
        for index, (start, size) in enumerate(a_groups):
            if start <= a_at < start + size:
                group_of[block] = index

    def piece(ref, row, rows):
        return ref.at[pl.ds(row, rows), :]

    chunks = [(row, rows) for _, _, row, rows in items] + [(rows_all - 16, 16)]

    def chain(index, src, dst, leg, to):
        row, rows = chunks[index]
        return remote(
            piece(src, row, rows),
            piece(dst, row, rows),
            c_send.at[index, leg],
            c_recv.at[index, leg],
            (d, to),
        )

    def out_copy(index, src):
        row, rows = chunks[index]
        return pltpu.make_async_copy(piece(src, row, rows), piece(out_ref, row, rows), o_sem.at[index])

    def push(index, value):
        row, rows = chunks[index]

        @pl.when(middle)
        def _():
            mine[row : row + rows, :] = value

        @pl.when(jnp.logical_not(middle))
        def _():
            sent[row : row + rows, :] = value.astype(jnp.bfloat16)
            chain(index, sent, got, 0, inward).start()

    def join(index):
        row, rows = chunks[index]

        @pl.when(middle)
        def _():
            chain(index, sent, got, 0, inward).wait_recv()
            part = mine[row : row + rows, :] + got[row : row + rows, :].astype(jnp.float32)
            sent[row : row + rows, :] = part.astype(jnp.bfloat16)
            chain(index, sent, crossed, 1, inward).start()

    def finish(index):
        row, rows = chunks[index]

        @pl.when(middle)
        def _():
            chain(index, sent, crossed, 1, inward).wait_recv()
            both = sent[row : row + rows, :].astype(jnp.float32) + crossed[
                row : row + rows, :
            ].astype(jnp.float32)
            total[row : row + rows, :] = both.astype(jnp.bfloat16)
            chain(index, total, got, 0, outward).start()
            out_copy(index, total).start()

    def land(index):
        @pl.when(jnp.logical_not(middle))
        def _():
            chain(index, total, got, 0, inward).wait_recv()
            out_copy(index, got).start()

    local = [
        pltpu.make_async_copy(b_ref, b_all.at[r], local_sem.at[0]),
        pltpu.make_async_copy(a_ref.at[r], a_all.at[r], local_sem.at[1]),
        pltpu.make_async_copy(v_ref.at[r], v_all.at[r], local_sem.at[2]),
    ]
    ahead = 2
    a_start(0)
    own_start(0)
    for copy in local:
        copy.start()
    for block in range(1, ahead):
        own_start(block)
    for copy in local:
        copy.wait()

    of_block = [
        [index for index, item in enumerate(items) if item[0] == block] for block in range(blocks)
    ]
    of_block.append([len(items)])
    arrived = set()
    for tick in range(blocks + 6):
        if tick + ahead < blocks:
            own_start(tick + ahead)
        if tick + 1 < len(a_groups):
            a_start(tick + 1)
        if tick == 1:
            for step in range(1, GROUP):
                v_copy(step, r).start()
        if tick < blocks:
            b_arrive(0, tick)
            b_start(5, tick)
            b_start(3, tick)
            b_arrive(1, tick)
            b_start(6, tick)
            b_start(4, tick)
        block = tick - 1
        if 0 <= block < blocks:
            b_arrive(5, block)
            b_start(7, block)
            b_arrive(6, block)
            b_start(8, block)
        block = tick - 2
        if 0 <= block < blocks:
            for kind in (2, 3, 4, 7, 8):
                b_arrive(kind, block)
            if group_of[block] not in arrived:
                arrived.add(group_of[block])
                a_arrive(group_of[block])
            for index in of_block[block]:
                _, a_at, row, rows = items[index]
                left = a_all[:, :, a_at : a_at + PIECE].reshape(-1, PIECE)
                right = b_all[:, :, block * WIDE : (block + 1) * WIDE].reshape(-1, WIDE)
                value = lax.dot_general(
                    left, right, (((0,), (0,)), ((), ())), preferred_element_type=jnp.float32
                )
                push(index, value[:rows])
        if block == blocks:
            for step in range(1, GROUP):
                v_copy(step, (r + GROUP - step) % GROUP).wait_recv()
            push(len(items), jnp.sum(v_all[...], axis=0))
        block = tick - 3
        if 0 <= block <= blocks:
            for index in of_block[block]:
                join(index)
        block = tick - 4
        if 0 <= block <= blocks:
            for index in of_block[block]:
                finish(index)
        block = tick - 6
        if 0 <= block <= blocks:
            for index in of_block[block]:
                land(index)

    for index in of_block[blocks]:
        land(index)
    for block in range(blocks):
        for kind in range(9):
            b_copy(kind, block, goes[kind]).wait_send()
    for step in range(1, GROUP):
        v_copy(step, r).wait_send()
        for group in range(len(a_groups)):
            a_copy(group, step, r).wait_send()
    for index in range(len(chunks)):
        chain(index, sent, got, 0, inward).wait_send()
        out_copy(index, got).wait()

        @pl.when(middle)
        def _():
            chain(index, sent, crossed, 1, inward).wait_send()


def summed_grads(layers, a_parts, b_parts, vectors):
    plan = grad_plan(layers)
    _, _, items, rows_all, a_cols, b_blocks = plan
    rows_all += 16
    plan = plan[:3] + (rows_all, a_cols, b_blocks)
    tokens = b_parts.shape[0]
    shares = {name: share for name, share, _ in layers}
    first = shares[layers[0][0]]
    second = first + shares[layers[1][0]]
    a_groups = ((0, first), (first, second - first), (second, a_cols - second))
    half_type, full_type = jnp.bfloat16, jnp.float32
    dma = pltpu.SemaphoreType.DMA
    chunks = len(items) + 1
    return pl.pallas_call(
        functools.partial(grad_kernel, plan, a_groups),
        out_shape=jax.ShapeDtypeStruct((rows_all, WIDE), half_type),
        in_specs=[pl.BlockSpec(memory_space=pl.ANY)] * 3,
        out_specs=pl.BlockSpec(memory_space=pl.ANY),
        scratch_shapes=[
            pltpu.VMEM((GROUP, tokens, a_cols), half_type),
            pltpu.VMEM((GROUP, tokens, b_blocks * WIDE), half_type),
            pltpu.VMEM((GROUP, 16, WIDE), full_type),
            pltpu.VMEM((rows_all, WIDE), full_type),
            pltpu.VMEM((rows_all, WIDE), half_type),
            pltpu.VMEM((rows_all, WIDE), half_type),
            pltpu.VMEM((rows_all, WIDE), half_type),
            pltpu.VMEM((rows_all, WIDE), half_type),
            dma((3,)),
            dma((len(a_groups), GROUP)),
            dma((len(a_groups), GROUP)),
            dma((GROUP,)),
            dma((GROUP,)),
            dma((b_blocks, 9)),
            dma((b_blocks, 9)),
            dma((chunks, 2)),
            dma((chunks, 2)),
            dma((chunks,)),
        ],
        compiler_params=pltpu.CompilerParams(
            collective_id=0, has_side_effects=True, vmem_limit_bytes=60 * 1024 * 1024
        ),
    )(a_parts, b_parts, vectors)


def body(
    expression,
    targets,
    noise,
    gene_masks,
    segment_ids,
    w_gene,
    emb_gain,
    emb_shift,
    attn_gain,
    attn_shift,
    w_qkv,
    b_qkv,
    w_out,
    b_out,
    ffn_gain,
    ffn_shift,
    w_up,
    b_up,
    w_down,
    b_down,
    bot_gain,
    bot_shift,
    w_enc,
    b_enc,
    comp_mean,
    comp_logvar,
    w_lat,
    b_lat,
    dec_gain,
    dec_shift,
    w_dec,
    b_dec,
):
    low, full = jnp.bfloat16, jnp.float32
    phase = lax.axis_index("phase")
    seqs, rows, genes = expression.shape
    width = w_gene.shape[1]
    head = width // HEADS
    tokens = seqs * rows

    def flat(values):
        return values.reshape(tokens, values.shape[-1])

    def spread(values):
        return jnp.repeat(values, rows, axis=0)

    keep = spread(1 - gene_masks)
    masked = flat(expression) * keep.astype(low)
    table = positions(phase * rows, rows, width)
    embedded = mm(masked, w_gene) + jnp.tile(table, (seqs, 1))
    x1, emb_back = jax.vjp(layer_norm, embedded, emb_gain, emb_shift)
    x1 = x1.astype(low).astype(full)
    h1, attn_back = jax.vjp(layer_norm, x1, attn_gain, attn_shift)
    h1 = h1.astype(low)
    projected = (mm(h1, w_qkv) + b_qkv).astype(low).reshape(seqs, rows, 3, HEADS, head)
    query = projected[:, :, 0]
    both = lax.all_gather(projected[:, :, 1:], "phase", axis=1, tiled=True)
    key, value = both[:, :, 0], both[:, :, 1]
    scale = head**-0.5
    scores = jnp.einsum("sqhd,skhd->shqk", query, key, preferred_element_type=full) * scale
    own_ids = lax.dynamic_slice_in_dim(segment_ids, phase * rows, rows, axis=1)
    same = own_ids[:, :, None] == segment_ids[:, None, :]
    scores = jnp.where(same[:, None], scores, mask_fill)
    shifted = jnp.exp(scores - jnp.max(scores, axis=-1, keepdims=True))
    prob = shifted / jnp.sum(shifted, axis=-1, keepdims=True)
    prob_low = prob.astype(low)
    attended = (
        jnp.einsum("shqk,skhd->sqhd", prob_low, value, preferred_element_type=full)
        .reshape(tokens, width)
        .astype(low)
    )
    mixed = x1 + (mm(attended, w_out) + b_out)
    h2, ffn_back = jax.vjp(layer_norm, mixed, ffn_gain, ffn_shift)
    h2 = h2.astype(low)
    before = mm(h2, w_up) + b_up
    activated, up_back = jax.vjp(gelu_exact, before)
    activated = activated.astype(low)
    x2 = (mixed + (mm(activated, w_down) + b_down)).astype(low).astype(full)
    h3, bot_back = jax.vjp(layer_norm, x2, bot_gain, bot_shift)
    h3 = h3.astype(low)
    moments = mm(h3, w_enc) + b_enc
    noise_full = flat(noise).astype(full)
    (latent, _), sample_back = jax.vjp(
        lambda m, a, b: sample_and_kl(m, noise_full, a, b), moments, comp_mean, comp_logvar
    )
    latent_low = latent.astype(low)
    lat_pre = mm(latent_low, w_lat) + b_lat
    x3, lat_back = jax.vjp(gelu_exact, lat_pre)
    x3 = x3.astype(low).astype(full)
    h4, dec_back = jax.vjp(layer_norm, x3, dec_gain, dec_shift)
    h4 = h4.astype(low)
    predicted = mm(h4, w_dec) + b_dec

    d_pred = (spread(gene_masks).astype(full) * (predicted - flat(targets).astype(full))).astype(low)
    d_x3, dec_gain_grad, dec_shift_grad = dec_back(contract_last(d_pred, w_dec))
    d_lat = lat_back(d_x3.astype(low).astype(full))[0].astype(low)
    d_moments, mean_grad, logvar_grad = sample_back(
        (contract_last(d_lat, w_lat), jnp.ones((), full))
    )
    d_moments = d_moments.astype(low)
    g, bot_gain_grad, bot_shift_grad = bot_back(contract_last(d_moments, w_enc))
    g = g.astype(low)
    d_before = up_back(contract_last(g, w_down))[0].astype(low)
    d_norm2, ffn_gain_grad, ffn_shift_grad = ffn_back(contract_last(d_before, w_up))
    d_mixed = g.astype(full) + d_norm2
    da = d_mixed.astype(low)
    d_att = contract_last(da, w_out).astype(low).reshape(seqs, rows, HEADS, head)
    d_value = jnp.einsum("shqk,sqhd->skhd", prob_low, d_att, preferred_element_type=full)
    d_prob = jnp.einsum("sqhd,skhd->shqk", d_att, value, preferred_element_type=full)
    d_score = prob * (d_prob - jnp.sum(prob * d_prob, axis=-1, keepdims=True))
    d_score = d_score.astype(low)
    d_query = jnp.einsum("shqk,skhd->sqhd", d_score, key, preferred_element_type=full) * scale
    d_key = jnp.einsum("shqk,sqhd->skhd", d_score, query, preferred_element_type=full) * scale
    d_both = lax.psum_scatter(
        jnp.stack([d_key, d_value], axis=2), "phase", scatter_dimension=1, tiled=True
    )
    d_projected = (
        jnp.concatenate([d_query[:, :, None], d_both], axis=2)
        .reshape(tokens, 3 * width)
        .astype(low)
    )
    d_norm1, attn_gain_grad, attn_shift_grad = attn_back(contract_last(d_projected, w_qkv))
    d_x1 = (d_mixed + d_norm1).astype(low).astype(full)
    d_embedded, emb_gain_grad, emb_shift_grad = emb_back(d_x1)
    d_embedded = d_embedded.astype(low)
    input_grad = contract_last(d_embedded, w_gene) * keep.astype(full)
    input_grad = input_grad.reshape(seqs, rows, genes)

    groups = lax.axis_size("dp") // GROUP
    lefts = {
        "down": activated,
        "gene": masked,
        "up": h2,
        "qkv": h1,
        "dec": h4,
        "enc": h3,
        "out": attended,
        "lat": latent_low,
    }
    rights = {
        "down": g,
        "gene": d_embedded,
        "up": d_before,
        "qkv": d_projected,
        "dec": d_pred,
        "enc": d_moments,
        "out": da,
        "lat": d_lat,
    }
    layers = [
        (name, lefts[name].shape[1] // GROUP, rights[name].shape[1] // WIDE) for name in lefts
    ]

    def by_owner(values, axis):
        shape = values.shape
        cut = shape[:axis] + (groups, GROUP, shape[axis] // (groups * GROUP)) + shape[axis + 1 :]
        moved = jnp.moveaxis(values.reshape(cut), axis + 1, 0)
        return moved, moved.shape

    def left_share(values):
        moved, shape = by_owner(values, 1)
        moved = moved.reshape(GROUP, tokens, -1)
        short = -moved.shape[2] % PIECE
        return jnp.pad(moved, ((0, 0), (0, 0), (0, short))) if short else moved

    a_parts = jnp.concatenate([left_share(lefts[name]) for name, _, _ in layers], axis=2)
    b_parts = jnp.concatenate([rights[name] for name, _, _ in layers], axis=1)
    d_projected_sums = column_sums(d_projected)
    vectors = {
        "emb_gain": emb_gain_grad,
        "emb_shift": emb_shift_grad,
        "attn_gain": attn_gain_grad,
        "attn_shift": attn_shift_grad,
        "b_query": d_projected_sums[:width],
        "b_value": d_projected_sums[2 * width :],
        "b_out": column_sums(da),
        "ffn_gain": ffn_gain_grad,
        "ffn_shift": ffn_shift_grad,
        "b_up": column_sums(d_before),
        "b_down": column_sums(g),
        "bot_gain": bot_gain_grad,
        "bot_shift": bot_shift_grad,
        "b_enc": column_sums(d_moments),
        "comp_mean": mean_grad,
        "comp_logvar": logvar_grad,
        "b_lat": column_sums(d_lat),
        "dec_gain": dec_gain_grad,
        "dec_shift": dec_shift_grad,
        "b_dec": column_sums(d_pred),
    }
    shares, places, at = [], {}, 0
    for name, values in vectors.items():
        cut = by_owner(values, values.ndim - 1)[0]
        if values.ndim == 2:
            cut = jnp.moveaxis(cut, 2, 1)
        places[name] = (at, cut.shape[2:])
        cut = cut.reshape(GROUP, groups, -1)
        at += cut.shape[2]
        shares.append(cut)
    packed = jnp.concatenate(shares, axis=2).reshape(GROUP, groups * at)
    packed = jnp.pad(packed, ((0, 0), (0, 16 * WIDE - groups * at))).reshape(GROUP, 16, WIDE)

    summed = summed_grads(layers, a_parts, b_parts, packed)

    def over_groups(values):
        if groups == 1:
            return values
        size = values.shape[0] // groups
        whole = lax.psum(
            values, "dp", axis_index_groups=[
                [other * GROUP + rank for other in range(groups)] for rank in range(GROUP)
            ],
        )
        return lax.dynamic_slice_in_dim(whole, lax.axis_index("dp") // GROUP * size, size, axis=0)

    grads, row = {}, 0
    for name, share, blocks in layers:
        parts = [
            summed[row + block * share : row + (block + 1) * share].astype(full)
            for block in range(blocks)
        ]
        row += blocks * share
        grads[name] = over_groups(parts[0] if blocks == 1 else jnp.concatenate(parts, axis=1))
    tail = summed[row : row + 16].astype(full).reshape(-1)[: groups * at].reshape(groups, at)
    tail = over_groups(tail)[0]
    for name, (start, shape) in places.items():
        grads[name] = tail[start : start + math.prod(shape)].reshape(shape)
    return (
        input_grad,
        grads["gene"],
        grads["emb_gain"],
        grads["emb_shift"],
        grads["attn_gain"],
        grads["attn_shift"],
        grads["qkv"],
        grads["b_query"],
        grads["b_value"],
        grads["out"],
        grads["b_out"],
        grads["ffn_gain"],
        grads["ffn_shift"],
        grads["up"],
        grads["b_up"],
        grads["down"],
        grads["b_down"],
        grads["bot_gain"],
        grads["bot_shift"],
        grads["enc"],
        grads["b_enc"],
        grads["comp_mean"],
        grads["comp_logvar"],
        grads["lat"],
        grads["b_lat"],
        grads["dec_gain"],
        grads["dec_shift"],
        grads["dec"],
        grads["b_dec"],
    )


def solution(mesh):
    rows = P("dp", "phase", None)
    return jax.shard_map(
        body,
        mesh=mesh,
        in_specs=(rows, rows, rows, P("dp", None), P("dp", None)) + (P(),) * 27,
        out_specs=(
            rows,
            P("dp", None),
            P("dp"),
            P("dp"),
            P("dp"),
            P("dp"),
            P("dp", None),
            P("dp"),
            P("dp"),
            P("dp", None),
            P("dp"),
            P("dp"),
            P("dp"),
            P("dp", None),
            P("dp"),
            P("dp", None),
            P("dp"),
            P("dp"),
            P("dp"),
            P("dp", None),
            P("dp"),
            P(None, "dp"),
            P(None, "dp"),
            P("dp", None),
            P("dp"),
            P("dp"),
            P("dp"),
            P("dp", None),
            P("dp"),
        ),
        check_vma=False,
    )
```

```python
import functools
import math

import jax
import jax.numpy as jnp
from jax import lax
from jax.experimental import pallas as pl
from jax.experimental.pallas import tpu as pltpu
from jax.sharding import PartitionSpec as P

HEADS = 16
GROUP = 8
PIECE = 128
WIDE = 1024

norm_eps = 1e-05
mask_fill = -1000000000.0
MESH = pl.DeviceIdType.MESH

(
    DOWN,
    GENE,
    UP,
    QKV,
    DEC,
    ENC,
    OUT,
    LAT,
    EMB_GAIN,
    EMB_SHIFT,
    ATTN_GAIN,
    ATTN_SHIFT,
    B_QKV,
    B_QUERY,
    B_VALUE,
    B_OUT,
    FFN_GAIN,
    FFN_SHIFT,
    B_UP,
    B_DOWN,
    BOT_GAIN,
    BOT_SHIFT,
    B_ENC,
    COMP_MEAN,
    COMP_LOGVAR,
    B_LAT,
    DEC_GAIN,
    DEC_SHIFT,
    B_DEC,
) = range(29)


def grad_plan(layers):
    a_off, b_off, items, row = {}, {}, [], 0
    a_at, b_at = 0, 0
    for name, share, blocks in layers:
        a_off[name], b_off[name] = a_at, b_at
        for block in range(blocks):
            for start in range(0, share, PIECE):
                rows = min(PIECE, share - start)
                items.append((b_at + block, a_at + start, row, rows))
                row += rows
        a_at += -(-share // PIECE) * PIECE
        b_at += blocks
    return a_off, b_off, items, row, a_at, b_at


def grad_kernel(
    plan,
    a_groups,
    a_ref,
    b_ref,
    v_ref,
    out_ref,
    tail_ref,
    a_all,
    b_all,
    v_all,
    mine,
    sent,
    got,
    crossed,
    total,
    v_mine,
    v_sent,
    v_got,
    v_crossed,
    v_total,
    local_sem,
    a_send,
    a_recv,
    v_send,
    v_recv,
    b_send,
    b_recv,
    c_send,
    c_recv,
    o_sem,
):
    items, rows_all, _, blocks = plan[2:6]
    d = lax.axis_index("dp")
    z = lax.axis_index("phase")
    base = (d // GROUP) * GROUP
    r = d % GROUP
    core, cx, cy = r % 2, (r // 2) % 2, r // 4
    rc, rx, ry = r + 1 - 2 * core, r + 2 - 4 * cx, r + 4 - 8 * cy
    rxc, ryc = rx + 1 - 2 * core, ry + 1 - 2 * core
    rd = rx + 4 - 8 * cy
    rdc = rd + 1 - 2 * core
    middle = (z % 3) != 0
    inward = z + 1 - 2 * (z // 2)
    outward = z - 1 + 2 * (z // 2)
    half = WIDE // 2

    barrier = pltpu.get_barrier_semaphore()
    for step in range(1, GROUP):
        pl.semaphore_signal(
            barrier, inc=1, device_id=(base + (r + step) % GROUP, z), device_id_type=MESH
        )
    pl.semaphore_signal(barrier, inc=1, device_id=(d, inward), device_id_type=MESH)

    @pl.when(middle)
    def _():
        pl.semaphore_signal(barrier, inc=1, device_id=(d, outward), device_id_type=MESH)
        pl.semaphore_wait(barrier, GROUP + 1)

    @pl.when(jnp.logical_not(middle))
    def _():
        pl.semaphore_wait(barrier, GROUP)

    def remote(src, dst, send, recv, to):
        return pltpu.make_async_remote_copy(
            src_ref=src,
            dst_ref=dst,
            send_sem=send,
            recv_sem=recv,
            device_id=to,
            device_id_type=MESH,
        )

    def a_copy(group, step, slot):
        start, size = a_groups[group]
        to = (r + step) % GROUP
        return remote(
            a_ref.at[to, :, pl.ds(start, size)],
            a_all.at[slot, :, pl.ds(start, size)],
            a_send.at[group, step],
            a_recv.at[group, step],
            (base + to, z),
        )

    def v_copy(step, slot):
        to = (r + step) % GROUP
        return remote(
            v_ref.at[to], v_all.at[slot], v_send.at[step], v_recv.at[step], (base + to, z)
        )

    def b_copy(kind, block, source):
        col, width = block * WIDE, WIDE
        if kind in (5, 7):
            width = half
        if kind in (6, 8):
            col, width = col + half, half
        to = (rx, ry, rc, rc, rc, ry, rx, rc, rc)[kind]
        view = b_all.at[source, :, pl.ds(col, width)]
        src = b_ref.at[:, pl.ds(col, width)] if kind < 3 else view
        return remote(
            src, view, b_send.at[block, kind], b_recv.at[block, kind], (base + to, z)
        )

    comes = (rx, ry, rc, rxc, ryc, rd, rd, rdc, rdc)
    goes = (r, r, r, rx, ry, rx, ry, rd, rd)

    def b_start(kind, block):
        b_copy(kind, block, goes[kind]).start()

    def b_arrive(kind, block):
        b_copy(kind, block, comes[kind]).wait_recv()

    def own_start(block):
        for kind in (0, 1, 2):
            b_start(kind, block)

    def a_start(group):
        for step in range(1, GROUP):
            a_copy(group, step, r).start()

    def a_arrive(group):
        for step in range(1, GROUP):
            a_copy(group, step, (r + GROUP - step) % GROUP).wait_recv()

    group_of = {}
    for block, a_at, _, _ in items:
        for index, (start, size) in enumerate(a_groups):
            if start <= a_at < start + size:
                group_of[block] = index

    def piece(ref, row, rows):
        return ref.at[pl.ds(row, rows), :]

    chunks = [(row, rows) for _, _, row, rows in items]
    vectors = len(items)
    legs = {"s": sent, "g": got, "c": crossed, "t": total}
    v_legs = {"s": v_sent, "g": v_got, "c": v_crossed, "t": v_total}

    def leg_of(name, index):
        if index == vectors:
            return v_legs[name]
        return piece(legs[name], *chunks[index])

    def chain(index, src, dst, leg, to):
        return remote(
            leg_of(src, index),
            leg_of(dst, index),
            c_send.at[index, leg],
            c_recv.at[index, leg],
            (d, to),
        )

    def out_copy(index, src):
        to = tail_ref if index == vectors else piece(out_ref, *chunks[index])
        return pltpu.make_async_copy(leg_of(src, index), to, o_sem.at[index])

    def push(index, value):
        @pl.when(middle)
        def _():
            if index == vectors:
                v_mine[...] = value
            else:
                row, rows = chunks[index]
                mine[row : row + rows, :] = value

        @pl.when(jnp.logical_not(middle))
        def _():
            ref = leg_of("s", index)
            ref[...] = value.astype(ref.dtype)
            chain(index, "s", "g", 0, inward).start()

    def join(index):
        @pl.when(middle)
        def _():
            chain(index, "s", "g", 0, inward).wait_recv()
            ref = leg_of("s", index)
            if index == vectors:
                own = v_mine[...]
            else:
                row, rows = chunks[index]
                own = mine[row : row + rows, :]
            ref[...] = (own + leg_of("g", index)[...].astype(jnp.float32)).astype(ref.dtype)
            chain(index, "s", "c", 1, inward).start()

    def finish(index):
        @pl.when(middle)
        def _():
            chain(index, "s", "c", 1, inward).wait_recv()
            ref = leg_of("t", index)
            both = leg_of("s", index)[...].astype(jnp.float32) + leg_of("c", index)[
                ...
            ].astype(jnp.float32)
            ref[...] = both.astype(ref.dtype)
            chain(index, "t", "g", 0, outward).start()
            out_copy(index, "t").start()

    def land(index):
        @pl.when(jnp.logical_not(middle))
        def _():
            chain(index, "t", "g", 0, inward).wait_recv()
            out_copy(index, "g").start()

    local = [
        pltpu.make_async_copy(b_ref, b_all.at[r], local_sem.at[0]),
        pltpu.make_async_copy(a_ref.at[r], a_all.at[r], local_sem.at[1]),
        pltpu.make_async_copy(v_ref.at[r], v_all.at[r], local_sem.at[2]),
    ]
    ahead = 2
    a_start(0)
    own_start(0)
    for copy in local:
        copy.start()
    for block in range(1, ahead):
        own_start(block)
    for copy in local:
        copy.wait()

    of_block = [
        [index for index, item in enumerate(items) if item[0] == block] for block in range(blocks)
    ]
    of_block.append([len(items)])
    arrived = set()
    for tick in range(blocks + 6):
        if tick + ahead < blocks:
            own_start(tick + ahead)
        if tick + 1 < len(a_groups):
            a_start(tick + 1)
        if tick == 1:
            for step in range(1, GROUP):
                v_copy(step, r).start()
        if tick < blocks:
            b_arrive(0, tick)
            b_start(5, tick)
            b_start(3, tick)
            b_arrive(1, tick)
            b_start(6, tick)
            b_start(4, tick)
        block = tick - 1
        if 0 <= block < blocks:
            b_arrive(5, block)
            b_start(7, block)
            b_arrive(6, block)
            b_start(8, block)
        block = tick - 2
        if 0 <= block < blocks:
            for kind in (2, 3, 4, 7, 8):
                b_arrive(kind, block)
            if group_of[block] not in arrived:
                arrived.add(group_of[block])
                a_arrive(group_of[block])
            for index in of_block[block]:
                _, a_at, row, rows = items[index]
                left = a_all[:, :, a_at : a_at + PIECE].reshape(-1, PIECE)
                right = b_all[:, :, block * WIDE : (block + 1) * WIDE].reshape(-1, WIDE)
                value = lax.dot_general(
                    left, right, (((0,), (0,)), ((), ())), preferred_element_type=jnp.float32
                )
                if rows < PIECE:
                    value = jnp.where(r % 2 == 1, value[rows : 2 * rows], value[:rows])
                push(index, value)
        if block == blocks:
            for step in range(1, GROUP):
                v_copy(step, (r + GROUP - step) % GROUP).wait_recv()
            push(len(items), jnp.sum(v_all[...], axis=0))
        block = tick - 3
        if 0 <= block <= blocks:
            for index in of_block[block]:
                join(index)
        block = tick - 4
        if 0 <= block <= blocks:
            for index in of_block[block]:
                finish(index)
        block = tick - 6
        if 0 <= block <= blocks:
            for index in of_block[block]:
                land(index)

    for index in of_block[blocks]:
        land(index)
    for block in range(blocks):
        for kind in range(9):
            b_copy(kind, block, goes[kind]).wait_send()
    for step in range(1, GROUP):
        v_copy(step, r).wait_send()
        for group in range(len(a_groups)):
            a_copy(group, step, r).wait_send()
    for index in range(len(chunks) + 1):
        chain(index, "s", "g", 0, inward).wait_send()
        out_copy(index, "g").wait()

        @pl.when(middle)
        def _():
            chain(index, "s", "c", 1, inward).wait_send()


def summed_grads(layers, a_parts, b_parts, vectors):
    plan = grad_plan(layers)
    _, _, items, rows_all, a_cols, b_blocks = plan
    tokens = b_parts.shape[0]
    shares = {name: share for name, share, _ in layers}
    first = shares[layers[0][0]]
    second = first + shares[layers[1][0]]
    a_groups = ((0, first), (first, second - first), (second, a_cols - second))
    half_type, full_type = jnp.bfloat16, jnp.float32
    dma = pltpu.SemaphoreType.DMA
    chunks = len(items) + 1
    return pl.pallas_call(
        functools.partial(grad_kernel, plan, a_groups),
        out_shape=(
            jax.ShapeDtypeStruct((rows_all, WIDE), half_type),
            jax.ShapeDtypeStruct(vectors.shape[1:], full_type),
        ),
        in_specs=[pl.BlockSpec(memory_space=pl.ANY)] * 3,
        out_specs=(pl.BlockSpec(memory_space=pl.ANY),) * 2,
        scratch_shapes=[
            pltpu.VMEM((GROUP, tokens, a_cols), half_type),
            pltpu.VMEM((GROUP, tokens, b_blocks * WIDE), half_type),
            pltpu.VMEM(vectors.shape, full_type),
            pltpu.VMEM((rows_all, WIDE), full_type),
            pltpu.VMEM((rows_all, WIDE), half_type),
            pltpu.VMEM((rows_all, WIDE), half_type),
            pltpu.VMEM((rows_all, WIDE), half_type),
            pltpu.VMEM((rows_all, WIDE), half_type),
            pltpu.VMEM(vectors.shape[1:], full_type),
            pltpu.VMEM(vectors.shape[1:], full_type),
            pltpu.VMEM(vectors.shape[1:], full_type),
            pltpu.VMEM(vectors.shape[1:], full_type),
            pltpu.VMEM(vectors.shape[1:], full_type),
            dma((3,)),
            dma((len(a_groups), GROUP)),
            dma((len(a_groups), GROUP)),
            dma((GROUP,)),
            dma((GROUP,)),
            dma((b_blocks, 9)),
            dma((b_blocks, 9)),
            dma((chunks, 2)),
            dma((chunks, 2)),
            dma((chunks,)),
        ],
        compiler_params=pltpu.CompilerParams(
            collective_id=0, has_side_effects=True, vmem_limit_bytes=60 * 1024 * 1024
        ),
    )(a_parts, b_parts, vectors)


SLOTS = 6


def positions(start, length, width):
    place_index = (start + jnp.arange(length)).astype(jnp.float32)[:, None]
    frequency = jnp.exp(
        jnp.arange(width // 2, dtype=jnp.float32) * (-2.0 * math.log(10000.0) / width)
    )
    angles = place_index * frequency[None, :]
    return jnp.stack([jnp.sin(angles), jnp.cos(angles)], axis=-1).reshape(length, width)


def mm(left, right):
    return jnp.dot(left, right, preferred_element_type=jnp.float32)


def mm_last(left, right):
    return lax.dot_general(
        left, right, (((1,), (1,)), ((), ())), preferred_element_type=jnp.float32
    )


def mm_first(left, right):
    return lax.dot_general(
        left, right, (((0,), (0,)), ((), ())), preferred_element_type=jnp.float32
    )


def normed(values):
    center = jnp.mean(values, axis=-1, keepdims=True)
    centered = values - center
    spread = jnp.mean(centered * centered, axis=-1, keepdims=True)
    scale = lax.rsqrt(spread + norm_eps)
    return centered * scale, scale


def normed_back(grad, hat, scale, gain):
    pulled = grad * gain
    mean = jnp.mean(pulled, axis=-1, keepdims=True)
    along = jnp.mean(pulled * hat, axis=-1, keepdims=True)
    return scale * (pulled - mean - hat * along)


def column_sums(values):
    return jnp.sum(values.astype(jnp.float32), axis=0, keepdims=True)


def gelu_and_slope(values):
    bell = 0.5 * (1.0 + lax.erf(values * (0.5**0.5)))
    slope = bell + values * jnp.exp(-0.5 * values * values) * (2.0 * math.pi) ** -0.5
    return values * bell, slope


VECTORS = (
    (EMB_GAIN, 1),
    (EMB_SHIFT, 1),
    (ATTN_GAIN, 1),
    (ATTN_SHIFT, 1),
    (B_QKV, 3),
    (B_OUT, 1),
    (FFN_GAIN, 1),
    (FFN_SHIFT, 1),
    (B_UP, 4),
    (B_DOWN, 1),
    (BOT_GAIN, 1),
    (BOT_SHIFT, 1),
    (B_ENC, 1),
    (B_LAT, 1),
    (DEC_GAIN, 1),
    (DEC_SHIFT, 1),
    (B_DEC, 2),
)
VECTOR_AT = {name: sum(n for _, n in VECTORS[:i]) for i, (name, _) in enumerate(VECTORS)}
SUMS = (
    (COMP_MEAN, 16),
    (COMP_LOGVAR, 16),
    (EMB_GAIN, 1),
    (EMB_SHIFT, 1),
    (ATTN_GAIN, 1),
    (ATTN_SHIFT, 1),
    (B_QUERY, 1),
    (B_VALUE, 1),
    (B_OUT, 1),
    (FFN_GAIN, 1),
    (FFN_SHIFT, 1),
    (B_UP, 4),
    (B_DOWN, 1),
    (BOT_GAIN, 1),
    (BOT_SHIFT, 1),
    (B_ENC, 1),
    (B_LAT, 1),
    (DEC_GAIN, 1),
    (DEC_SHIFT, 1),
    (B_DEC, 2),
)
SUM_AT = {name: sum(n for _, n in SUMS[:i]) for i, (name, _) in enumerate(SUMS)}
SUM_ROWS = 64


def rows_kernel(
    layers,
    expr_ref,
    target_ref,
    noise_ref,
    masks_ref,
    table_ref,
    vec_ref,
    mean_ref,
    logvar_ref,
    w_gene,
    w_qkv,
    w_out,
    w_up,
    w_down,
    w_enc,
    w_lat,
    w_dec,
    input_ref,
    a_out,
    b_out,
    v_out,
    ring,
    masks_all,
    target_in,
    noise_in,
    x1_out,
    x1_in,
    kv_all,
    query_own,
    probs,
    dkv_part,
    dkv_in,
    dx_out,
    dx_in,
    hats,
    scales,
    slopes,
    mixed_grad,
    ring_sem,
    hand_send,
    hand_recv,
    hand_local,
    pair_send,
    pair_recv,
    pair_local,
):
    low, full = jnp.bfloat16, jnp.float32
    d = lax.axis_index("dp")
    z = lax.axis_index("phase")
    core = d % 2
    partner = d + 1 - 2 * core
    owner = d - core + z // 2
    a_off, b_off = grad_plan(layers)[:2]
    shares = {name: share for name, share, _ in layers}
    seqs, rows, genes = expr_ref.shape
    tokens = seqs * rows
    width = table_ref.shape[1]
    hidden = w_up.shape[1]
    wide = WIDE

    barrier = pltpu.get_barrier_semaphore()
    pl.semaphore_signal(barrier, inc=1, device_id=(partner, z), device_id_type=MESH)
    own = core == z // 2
    for i in range(2):
        @pl.when(jnp.logical_not(own & (z % 2 == i)))
        def _():
            pl.semaphore_signal(
                barrier, inc=1, device_id=(owner, 2 * core + i), device_id_type=MESH
            )

    stream = []
    for j in range(genes // wide):
        stream.append(w_gene.at[pl.ds(j * wide, wide), :])
    for j in range(3):
        stream.append(w_qkv.at[:, pl.ds(j * wide, wide)])
    stream.append(w_out)
    for j in range(hidden // wide):
        stream.append(w_up.at[:, pl.ds(j * wide, wide)])
        stream.append(w_down.at[pl.ds(j * wide, wide), :])
    stream.append(w_enc)
    stream.append(w_lat)
    for j in range(genes // wide):
        stream.append(w_dec.at[:, pl.ds(j * wide, wide)])
    for j in range(hidden // wide):
        stream.append(w_down.at[pl.ds(j * wide, wide), :])
        stream.append(w_up.at[:, pl.ds(j * wide, wide)])
    stream.append(w_out)
    for j in range(3):
        stream.append(w_qkv.at[:, pl.ds(j * wide, wide)])
    for j in range(genes // wide):
        stream.append(w_gene.at[pl.ds(j * wide, wide), :])

    def load(k):
        depth = stream[k].shape[0]
        return pltpu.make_async_copy(
            stream[k], ring.at[k % SLOTS, pl.ds(0, depth), :], ring_sem.at[k % SLOTS]
        )

    def fetch(k):
        if k < len(stream):
            load(k).start()

    place = [0]

    def take():
        k = place[0]
        place[0] += 1
        load(k).wait()
        return k

    def block(k):
        return ring[k % SLOTS, : stream[k].shape[0], :]

    for k in range(SLOTS):
        fetch(k)

    @pl.when(own)
    def _():
        pl.semaphore_wait(barrier, 2)

    @pl.when(jnp.logical_not(own))
    def _():
        pl.semaphore_wait(barrier, 3)

    def hand(which, src, dst, i):
        return pltpu.make_async_remote_copy(
            src_ref=src.at[i],
            dst_ref=dst.at[z % 2],
            send_sem=hand_send.at[which, i],
            recv_sem=hand_recv.at[which, z % 2],
            device_id=(owner, 2 * core + i),
            device_id_type=MESH,
        )

    def hand_here(which, src, dst, i):
        return pltpu.make_async_copy(src.at[i], dst.at[i], hand_local.at[which])

    def hand_start(which, src, dst):
        for i in range(2):
            here = own & (z % 2 == i)

            @pl.when(here)
            def _():
                hand_here(which, src, dst, i).start()

            @pl.when(jnp.logical_not(here))
            def _():
                hand(which, src, dst, i).start()

    def hand_arrive(which, src, dst):
        for i in range(2):
            here = own & (z % 2 == i)

            @pl.when(here)
            def _():
                hand_here(which, src, dst, i).wait()

            @pl.when(jnp.logical_not(here))
            def _():
                pltpu.make_async_remote_copy(
                    src_ref=src.at[i],
                    dst_ref=dst.at[i],
                    send_sem=hand_send.at[which, i],
                    recv_sem=hand_recv.at[which, i],
                    device_id=(owner, 2 * core + i),
                    device_id_type=MESH,
                ).wait_recv()

    def hand_sent(which, src, dst):
        for i in range(2):
            @pl.when(jnp.logical_not(own & (z % 2 == i)))
            def _():
                hand(which, src, dst, i).wait_send()

    def pair(which, src, dst):
        return pltpu.make_async_remote_copy(
            src_ref=src,
            dst_ref=dst,
            send_sem=pair_send.at[which],
            recv_sem=pair_recv.at[which],
            device_id=(partner, z),
            device_id_type=MESH,
        )

    pair(0, masks_ref, masks_all.at[core]).start()
    own_masks = pltpu.make_async_copy(masks_ref, masks_all.at[core], pair_local)
    own_masks.start()

    def vec(name, j=0):
        at = VECTOR_AT[name] + j
        return vec_ref[at : at + 1, :]

    def put_a(name, values):
        off, share = a_off[name], shares[name]
        step = max(share, PIECE)
        for o in range(GROUP):
            start = o * share // step * step
            a_out[o, :, off : off + step] = values[:, start : start + step]

    def put_b(name, j, values):
        at = (b_off[name] + j) * wide
        b_out[:, at : at + wide] = values

    def put_sum(name, values, j=0):
        each = SUM_LANES[name]
        for o in range(values.shape[1] // 128):
            at = j * wide + o * 128
            to, row = at // (128 * each), SUM_AT[name] + at // 128 % each
            v_out[to, row : row + 1, :] = values[:, o * 128 : o * 128 + 128]

    def normalize(index, values, gain, shift):
        hat, scale = normed(values)
        hats[index] = hat
        scales[index] = jnp.broadcast_to(scale, scales.shape[1:])
        return hat * vec(gain) + vec(shift)

    def normalize_back(index, grad, gain, gain_name, shift_name):
        hat, scale = hats[index], scales[index, :, :1]
        put_sum(gain_name, jnp.sum(grad * hat, axis=0, keepdims=True))
        put_sum(shift_name, jnp.sum(grad, axis=0, keepdims=True))
        return normed_back(grad, hat, scale, vec(gain))

    keep = 1.0 - masks_ref[:seqs, :genes]
    keep = jnp.concatenate(
        [jnp.broadcast_to(keep[s : s + 1], (rows, genes)) for s in range(seqs)], axis=0
    )
    masked = (expr_ref[...].reshape(tokens, genes).astype(full) * keep).astype(low)
    put_a(GENE, masked)
    embedded = jnp.concatenate([table_ref[...]] * seqs, axis=0)
    for j in range(genes // wide):
        k = take()
        embedded += mm(masked[:, j * wide : (j + 1) * wide], block(k))
        fetch(k + SLOTS)
    x1_out[...] = (
        normalize(0, embedded, EMB_GAIN, EMB_SHIFT).astype(low).reshape(seqs, rows, width)
    )
    hand_start(0, x1_out, x1_in)
    hand_start(1, noise_ref, noise_in)
    hand_start(2, target_ref, target_in)
    own_masks.wait()
    pair(0, masks_ref, masks_all.at[1 - core]).wait_recv()
    odd = z % 2 == 1
    both_masks = masks_all[pl.ds(z // 2, 1)][0]
    mask_row = jnp.where(odd, both_masks[1:2], both_masks[0:1])
    gene_row = mask_row[:, :genes]
    length = 2 * tokens
    segments = mask_row[:, genes : genes + length]
    place_q = lax.broadcasted_iota(jnp.int32, (tokens, length), 0) + core * tokens
    place_k = lax.broadcasted_iota(jnp.int32, (tokens, length), 1)
    own_segments = jnp.sum(
        jnp.where(place_q == place_k, segments, 0.0), axis=-1, keepdims=True
    )
    same = own_segments == segments
    same = jnp.concatenate([same.astype(full)] * 2, axis=0) > 0.5

    hand_arrive(0, x1_out, x1_in)
    x1 = x1_in[...].reshape(tokens, width).astype(full)
    h1 = normalize(1, x1, ATTN_GAIN, ATTN_SHIFT).astype(low)
    put_a(QKV, h1)
    head = width // HEADS
    scale = head**-0.5
    k_query = take()
    query_own[...] = (mm(h1, block(k_query)) + vec(B_QKV, 0)).astype(low)
    fetch(k_query + SLOTS)
    for j in (1, 2):
        k = take()
        kv_all[core, :, (j - 1) * wide : j * wide] = (
            mm(h1, block(k)) + vec(B_QKV, j)
        ).astype(low)
        fetch(k + SLOTS)
    pair(1, kv_all.at[core], kv_all.at[core]).start()
    pair(1, kv_all.at[core], kv_all.at[1 - core]).wait_recv()

    lanes = lax.broadcasted_iota(jnp.int32, (tokens, 2 * head), 1)
    first = lanes < head
    pairs = HEADS // 2

    def two(values):
        none = jnp.zeros_like(values)
        return jnp.concatenate([jnp.where(first, values, none), jnp.where(first, none, values)], axis=0)

    def one(values):
        return jnp.where(first, values[:tokens], values[tokens:])

    def columns(p):
        return pl.ds(pl.multiple_of(p * 2 * head, 2 * head), 2 * head)

    def keys_of(p):
        return kv_all[:, :, columns(p)].reshape(length, 2 * head)

    def values_of(p):
        at = pl.ds(pl.multiple_of(width + p * 2 * head, 2 * head), 2 * head)
        return kv_all[:, :, at].reshape(length, 2 * head)

    def attend(p, carry):
        scores = mm_last(two(query_own[:, columns(p)]), keys_of(p)) * scale
        scores = jnp.where(same, scores, mask_fill)
        shifted = jnp.exp(scores - jnp.max(scores, axis=-1, keepdims=True))
        prob = shifted / jnp.sum(shifted, axis=-1, keepdims=True)
        probs[p] = prob
        att = one(mm(prob.astype(low), values_of(p))).astype(low)
        a_out[p, :, a_off[OUT] : a_off[OUT] + 2 * head] = att
        return carry

    lax.fori_loop(0, pairs, attend, 0)
    attended = jnp.concatenate(
        [a_out[o, :, a_off[OUT] : a_off[OUT] + 2 * head] for o in range(pairs)], axis=1
    )
    k = take()
    mixed = x1 + (mm(attended, block(k)) + vec(B_OUT))
    fetch(k + SLOTS)
    h2 = normalize(2, mixed, FFN_GAIN, FFN_SHIFT).astype(low)
    put_a(UP, h2)
    x2 = mixed + vec(B_DOWN)
    per_owner = shares[DOWN]
    for j in range(hidden // wide):
        k = take()
        before = mm(h2, block(k)) + vec(B_UP, j)
        fetch(k + SLOTS)
        active, slope = gelu_and_slope(before)
        slopes[:, j * wide : (j + 1) * wide] = slope
        active = active.astype(low)
        for o in range(wide // per_owner):
            a_out[
                j * (wide // per_owner) + o, :, a_off[DOWN] : a_off[DOWN] + per_owner
            ] = active[:, o * per_owner : (o + 1) * per_owner]
        k = take()
        x2 += mm(active, block(k))
        fetch(k + SLOTS)
    x2 = x2.astype(low).astype(full)
    h3 = normalize(3, x2, BOT_GAIN, BOT_SHIFT).astype(low)
    put_a(ENC, h3)
    k_enc = take()
    moments = mm(h3, block(k_enc)) + vec(B_ENC)
    latents = width // 2
    logvar = moments[:, latents:]
    hand_arrive(1, noise_ref, noise_in)
    swing = jnp.exp(0.5 * logvar) * noise_in[...].reshape(tokens, latents).astype(full)
    latent = moments[:, :latents] + swing
    latent_low = latent.astype(low)
    put_a(LAT, latent_low)
    k_lat = take()
    lat_active, lat_slope = gelu_and_slope(mm(latent_low, block(k_lat)) + vec(B_LAT))
    x3 = lat_active.astype(low).astype(full)
    h4 = normalize(4, x3, DEC_GAIN, DEC_SHIFT).astype(low)
    put_a(DEC, h4)
    hand_arrive(2, target_ref, target_in)

    grad = jnp.zeros((tokens, width), full)
    for j in range(genes // wide):
        k = take()
        at = slice(j * wide, (j + 1) * wide)
        predicted = mm(h4, block(k)) + vec(B_DEC, j)
        wanted = target_in[:, :, at].reshape(tokens, wide).astype(full)
        d_pred = (gene_row[:, at] * (predicted - wanted)).astype(low)
        put_b(DEC, j, d_pred)
        put_sum(B_DEC, column_sums(d_pred), j)
        grad += mm_last(d_pred, block(k))
    d_x3 = normalize_back(4, grad, DEC_GAIN, DEC_GAIN, DEC_SHIFT).astype(low).astype(full)
    d_lat = (lat_slope * d_x3).astype(low)
    put_b(LAT, 0, d_lat)
    put_sum(B_LAT, column_sums(d_lat))
    d_latent = mm_last(d_lat, block(k_lat))

    inverse = jnp.exp(-logvar_ref[...])
    volume = jnp.sum(logvar_ref[...], axis=-1, keepdims=True)
    count = mean_ref.shape[0]
    scaled = []
    for c in range(count):
        offset = latent - mean_ref[c : c + 1, :]
        quad = jnp.sum(offset * offset * inverse[c : c + 1], axis=-1, keepdims=True)
        scaled.append(-0.5 * (quad + volume[c : c + 1]))
    highest = functools.reduce(jnp.maximum, scaled)
    shares_c = [jnp.exp(s - highest) for s in scaled]
    whole = functools.reduce(jnp.add, shares_c)
    for c in range(count):
        part = shares_c[c] / whole
        offset = latent - mean_ref[c : c + 1, :]
        pull = offset * inverse[c : c + 1]
        weighted = part * pull
        d_latent += weighted
        mean_grad = -jnp.sum(weighted, axis=0, keepdims=True)
        logvar_grad = 0.5 * jnp.sum(part - weighted * offset, axis=0, keepdims=True)
        for o in range(GROUP):
            at = slice(o // 2 * 128, o // 2 * 128 + 128)
            row = SUM_AT[COMP_MEAN] + c
            v_out[o, row : row + 1, :] = mean_grad[:, at]
            row = SUM_AT[COMP_LOGVAR] + c
            v_out[o, row : row + 1, :] = logvar_grad[:, at]
    d_moments = jnp.concatenate([d_latent, 0.5 * d_latent * swing - 0.5], axis=1).astype(low)
    put_b(ENC, 0, d_moments)
    put_sum(B_ENC, column_sums(d_moments))
    grad = mm_last(d_moments, block(k_enc))
    for k in range(k_enc, k_enc + 2 + genes // wide):
        fetch(k + SLOTS)
    g = normalize_back(3, grad, BOT_GAIN, BOT_GAIN, BOT_SHIFT).astype(low)
    put_b(DOWN, 0, g)
    put_sum(B_DOWN, column_sums(g))
    grad = jnp.zeros((tokens, width), full)
    for j in range(hidden // wide):
        k = take()
        d_active = mm_last(g, block(k))
        fetch(k + SLOTS)
        d_before = (slopes[:, j * wide : (j + 1) * wide] * d_active).astype(low)
        put_b(UP, j, d_before)
        put_sum(B_UP, column_sums(d_before), j)
        k = take()
        grad += mm_last(d_before, block(k))
        fetch(k + SLOTS)
    d_mixed = g.astype(full) + normalize_back(2, grad, FFN_GAIN, FFN_GAIN, FFN_SHIFT)
    mixed_grad[...] = d_mixed
    da = d_mixed.astype(low)
    put_b(OUT, 0, da)
    put_sum(B_OUT, column_sums(da))
    k = take()
    x1_in[...] = mm_last(da, block(k)).astype(low).reshape(seqs, rows, width)
    fetch(k + SLOTS)
    q_at = b_off[QKV] * wide

    def attend_back(p, carry):
        query = two(query_own[:, columns(p)])
        d_att = two(x1_in[:, :, columns(p)].reshape(tokens, 2 * head))
        prob = probs[p]
        keys = keys_of(p)
        d_value = mm_first(prob.astype(low), d_att)
        d_prob = mm_last(d_att, values_of(p))
        d_score = prob * (d_prob - jnp.sum(prob * d_prob, axis=-1, keepdims=True))
        d_score = d_score.astype(low)
        d_query = one(mm(d_score, keys)) * scale
        d_key = mm_first(d_score, query) * scale
        b_out[:, pl.ds(pl.multiple_of(q_at + p * 2 * head, 2 * head), 2 * head)] = d_query.astype(
            low
        )
        dkv_part[:, :, columns(p)] = d_key.reshape(2, tokens, 2 * head)
        at = pl.ds(pl.multiple_of(width + p * 2 * head, 2 * head), 2 * head)
        dkv_part[:, :, at] = d_value.reshape(2, tokens, 2 * head)
        return carry

    lax.fori_loop(0, pairs, attend_back, 0)
    pair(2, dkv_part.at[1 - core], dkv_in).start()
    d_query = b_out[:, q_at : q_at + wide]
    put_sum(B_QUERY, column_sums(d_query))
    k = take()
    grad = mm_last(d_query, block(k))
    fetch(k + SLOTS)
    pair(2, dkv_part.at[1 - core], dkv_in).wait_recv()
    for j in (1, 2):
        at = slice((j - 1) * wide, j * wide)
        d_part = (dkv_part[core, :, at] + dkv_in[:, at]).astype(low)
        put_b(QKV, j, d_part)
        if j == 2:
            put_sum(B_VALUE, column_sums(d_part))
        k = take()
        grad += mm_last(d_part, block(k))
        fetch(k + SLOTS)
    d_x1 = mixed_grad[...] + normalize_back(1, grad, ATTN_GAIN, ATTN_GAIN, ATTN_SHIFT)
    dx_out[...] = d_x1.astype(low).reshape(seqs, rows, width)
    hand_start(3, dx_out, dx_in)
    hand_arrive(3, dx_out, dx_in)
    d_x1 = dx_in[...].reshape(tokens, width).astype(full)
    d_embedded = normalize_back(0, d_x1, EMB_GAIN, EMB_GAIN, EMB_SHIFT).astype(low)
    put_b(GENE, 0, d_embedded)
    for j in range(genes // wide):
        k = take()
        at = slice(j * wide, (j + 1) * wide)
        input_ref[:, at] = mm_last(d_embedded, block(k)) * jnp.concatenate(
            [
                jnp.broadcast_to(1.0 - masks_ref[s : s + 1, at], (rows, wide))
                for s in range(seqs)
            ],
            axis=0,
        )
    hand_sent(0, x1_out, x1_in)
    hand_sent(1, noise_ref, noise_in)
    hand_sent(2, target_ref, target_in)
    hand_sent(3, dx_out, dx_in)
    pair(0, masks_ref, masks_all.at[core]).wait_send()
    pair(1, kv_all.at[core], kv_all.at[core]).wait_send()
    pair(2, dkv_part.at[1 - core], dkv_in).wait_send()


SUM_LANES = dict(SUMS)


def through_rows(layers, expression, targets, noise, masks, table, vectors, tables, weights):
    low, full = jnp.bfloat16, jnp.float32
    seqs, rows, genes = expression.shape
    width = table.shape[1]
    latents = noise.shape[2]
    tokens = seqs * rows
    hidden = weights[3].shape[1]
    _, _, _, _, a_cols, b_blocks = grad_plan(layers)
    vmem = pl.BlockSpec(memory_space=pltpu.VMEM)
    anywhere = pl.BlockSpec(memory_space=pl.ANY)
    dma = pltpu.SemaphoreType.DMA
    return pl.pallas_call(
        functools.partial(rows_kernel, layers),
        out_shape=(
            jax.ShapeDtypeStruct((tokens, genes), full),
            jax.ShapeDtypeStruct((GROUP, tokens, a_cols), low),
            jax.ShapeDtypeStruct((tokens, b_blocks * WIDE), low),
            jax.ShapeDtypeStruct((GROUP, SUM_ROWS, 128), full),
        ),
        in_specs=[vmem, anywhere, anywhere] + [vmem] * 5 + [anywhere] * 8,
        out_specs=(vmem,) * 4,
        scratch_shapes=[
            pltpu.VMEM((SLOTS, WIDE, WIDE), low),
            pltpu.VMEM((2,) + masks.shape, full),
            pltpu.VMEM((2, rows, genes), low),
            pltpu.VMEM((2, rows, latents), low),
            pltpu.VMEM((2, rows, width), low),
            pltpu.VMEM((2, rows, width), low),
            pltpu.VMEM((2, tokens, 2 * width), low),
            pltpu.VMEM((tokens, width), low),
            pltpu.VMEM((HEADS // 2, 2 * tokens, 2 * tokens), full),
            pltpu.VMEM((2, tokens, 2 * width), full),
            pltpu.VMEM((tokens, 2 * width), full),
            pltpu.VMEM((2, rows, width), low),
            pltpu.VMEM((2, rows, width), low),
            pltpu.VMEM((5, tokens, width), full),
            pltpu.VMEM((5, tokens, 128), full),
            pltpu.VMEM((tokens, hidden), full),
            pltpu.VMEM((tokens, width), full),
            dma((SLOTS,)),
            dma((4, 2)),
            dma((4, 2)),
            dma((4,)),
            dma((3,)),
            dma((3,)),
            dma,
        ],
        compiler_params=pltpu.CompilerParams(
            collective_id=1, has_side_effects=True, vmem_limit_bytes=60 * 1024 * 1024
        ),
    )(expression, targets, noise, masks, table, vectors, *tables, *weights)


def body(
    expression,
    targets,
    noise,
    gene_masks,
    segment_ids,
    w_gene,
    emb_gain,
    emb_shift,
    attn_gain,
    attn_shift,
    w_qkv,
    b_qkv,
    w_out,
    b_out,
    ffn_gain,
    ffn_shift,
    w_up,
    b_up,
    w_down,
    b_down,
    bot_gain,
    bot_shift,
    w_enc,
    b_enc,
    comp_mean,
    comp_logvar,
    w_lat,
    b_lat,
    dec_gain,
    dec_shift,
    w_dec,
    b_dec,
):
    full = jnp.float32
    phase = lax.axis_index("phase")
    seqs, rows, genes = expression.shape
    width = w_gene.shape[1]
    length = segment_ids.shape[1]
    table = positions(phase * rows, rows, width)
    masks = jnp.concatenate([gene_masks, segment_ids], axis=1).astype(full)
    masks = jnp.pad(masks, ((0, 8 - seqs), (0, -length % 128)))
    given = {
        EMB_GAIN: emb_gain,
        EMB_SHIFT: emb_shift,
        ATTN_GAIN: attn_gain,
        ATTN_SHIFT: attn_shift,
        B_QKV: b_qkv,
        B_OUT: b_out,
        FFN_GAIN: ffn_gain,
        FFN_SHIFT: ffn_shift,
        B_UP: b_up,
        B_DOWN: b_down,
        BOT_GAIN: bot_gain,
        BOT_SHIFT: bot_shift,
        B_ENC: b_enc,
        B_LAT: b_lat,
        DEC_GAIN: dec_gain,
        DEC_SHIFT: dec_shift,
        B_DEC: b_dec,
    }
    vectors = jnp.concatenate([given[name] for name, _ in VECTORS]).reshape(-1, width)
    vectors = jnp.pad(vectors, ((0, -vectors.shape[0] % 8), (0, 0)))
    sizes = {
        DOWN: w_down.shape,
        GENE: w_gene.shape,
        UP: w_up.shape,
        QKV: w_qkv.shape,
        DEC: w_dec.shape,
        ENC: w_enc.shape,
        OUT: w_out.shape,
        LAT: w_lat.shape,
    }
    layers = [(name, tall // GROUP, across // WIDE) for name, (tall, across) in sizes.items()]
    input_grad, a_parts, b_parts, sums = through_rows(
        layers,
        expression,
        targets,
        noise,
        masks,
        table,
        vectors,
        (comp_mean, comp_logvar),
        (w_gene, w_qkv, w_out, w_up, w_down, w_enc, w_lat, w_dec),
    )
    summed, tail = summed_grads(layers, a_parts, b_parts, sums)

    groups = lax.axis_size("dp") // GROUP
    d = lax.axis_index("dp")

    def shared_out(values, axis):
        if groups == 1:
            return values
        across = [[g * GROUP + r for g in range(groups)] for r in range(GROUP)]
        within = [[g * GROUP + r for r in range(GROUP)] for g in range(groups)]
        values = lax.psum(values, "dp", axis_index_groups=across)
        values = lax.all_gather(values, "dp", axis=axis, tiled=True, axis_index_groups=within)
        size = values.shape[axis] // (groups * GROUP)
        return lax.dynamic_slice_in_dim(values, d * size, size, axis=axis)

    grads, row = {}, 0
    for name, share, blocks in layers:
        parts = [
            summed[row + block * share : row + (block + 1) * share].astype(full)
            for block in range(blocks)
        ]
        row += blocks * share
        grads[name] = shared_out(parts[0] if blocks == 1 else jnp.concatenate(parts, axis=1), 0)
    for name, count in SUMS:
        values = tail[SUM_AT[name] : SUM_AT[name] + count]
        if name in (COMP_MEAN, COMP_LOGVAR):
            values = lax.dynamic_slice_in_dim(values, d % 2 * 64, 64, axis=1)
            grads[name] = shared_out(values, 1)
        else:
            grads[name] = shared_out(values.reshape(-1), 0)
    return (
        input_grad.reshape(seqs, rows, genes),
        grads[GENE],
        grads[EMB_GAIN],
        grads[EMB_SHIFT],
        grads[ATTN_GAIN],
        grads[ATTN_SHIFT],
        grads[QKV],
        grads[B_QUERY],
        grads[B_VALUE],
        grads[OUT],
        grads[B_OUT],
        grads[FFN_GAIN],
        grads[FFN_SHIFT],
        grads[UP],
        grads[B_UP],
        grads[DOWN],
        grads[B_DOWN],
        grads[BOT_GAIN],
        grads[BOT_SHIFT],
        grads[ENC],
        grads[B_ENC],
        grads[COMP_MEAN],
        grads[COMP_LOGVAR],
        grads[LAT],
        grads[B_LAT],
        grads[DEC_GAIN],
        grads[DEC_SHIFT],
        grads[DEC],
        grads[B_DEC],
    )


def solution(mesh):
    rows = P("dp", "phase", None)
    return jax.shard_map(
        body,
        mesh=mesh,
        in_specs=(rows, rows, rows, P("dp", None), P("dp", None)) + (P(),) * 27,
        out_specs=(
            rows,
            P("dp", None),
            P("dp"),
            P("dp"),
            P("dp"),
            P("dp"),
            P("dp", None),
            P("dp"),
            P("dp"),
            P("dp", None),
            P("dp"),
            P("dp"),
            P("dp"),
            P("dp", None),
            P("dp"),
            P("dp", None),
            P("dp"),
            P("dp"),
            P("dp"),
            P("dp", None),
            P("dp"),
            P(None, "dp"),
            P(None, "dp"),
            P("dp", None),
            P("dp"),
            P("dp"),
            P("dp"),
            P("dp", None),
            P("dp"),
        ),
        check_vma=False,
    )
```

```python
import functools
import math

import jax
import jax.numpy as jnp
import numpy as np
from jax import lax
from jax.experimental import pallas as pl
from jax.experimental.pallas import tpu as pltpu
from jax.sharding import PartitionSpec as P

HEADS = 16
GROUP = 8
PIECE = 128
WIDE = 1024
HALF = 512
SLOTS = 4

norm_eps = 1e-05
mask_fill = -1000000000.0
MESH = pl.DeviceIdType.MESH

(
    DOWN,
    GENE,
    UP,
    QKV,
    DEC,
    ENC,
    OUT,
    LAT,
    EMB_GAIN,
    EMB_SHIFT,
    ATTN_GAIN,
    ATTN_SHIFT,
    B_QKV,
    B_QUERY,
    B_VALUE,
    B_OUT,
    FFN_GAIN,
    FFN_SHIFT,
    B_UP,
    B_DOWN,
    BOT_GAIN,
    BOT_SHIFT,
    B_ENC,
    COMP_MEAN,
    COMP_LOGVAR,
    B_LAT,
    DEC_GAIN,
    DEC_SHIFT,
    B_DEC,
) = range(29)


LAYERS = (DEC, DOWN, LAT, ENC, UP, OUT, QKV, GENE)
VECTORS = (
    EMB_GAIN,
    EMB_SHIFT,
    ATTN_GAIN,
    ATTN_SHIFT,
    B_QKV,
    B_OUT,
    FFN_GAIN,
    FFN_SHIFT,
    B_UP,
    B_DOWN,
    BOT_GAIN,
    BOT_SHIFT,
    B_ENC,
    B_LAT,
    DEC_GAIN,
    DEC_SHIFT,
    B_DEC,
)
SUMS = (
    (COMP_MEAN, 16),
    (COMP_LOGVAR, 16),
    (EMB_GAIN, 1),
    (EMB_SHIFT, 1),
    (ATTN_GAIN, 1),
    (ATTN_SHIFT, 1),
    (B_QUERY, 1),
    (B_VALUE, 1),
    (B_OUT, 1),
    (FFN_GAIN, 1),
    (FFN_SHIFT, 1),
    (B_UP, 4),
    (B_DOWN, 1),
    (BOT_GAIN, 1),
    (BOT_SHIFT, 1),
    (B_ENC, 1),
    (B_LAT, 1),
    (DEC_GAIN, 1),
    (DEC_SHIFT, 1),
    (B_DEC, 2),
)
SUM_AT = {name: sum(n for _, n in SUMS[:i]) for i, (name, _) in enumerate(SUMS)}
SUM_ROWS = 64


def mm(left, right):
    return jnp.dot(left, right, preferred_element_type=jnp.float32)


def mm_last(left, right):
    return lax.dot_general(
        left, right, (((1,), (1,)), ((), ())), preferred_element_type=jnp.float32
    )


def mm_first(left, right):
    return lax.dot_general(
        left, right, (((0,), (0,)), ((), ())), preferred_element_type=jnp.float32
    )


def normed(values):
    center = jnp.mean(values, axis=-1, keepdims=True)
    centered = values - center
    spread = jnp.mean(centered * centered, axis=-1, keepdims=True)
    scale = lax.rsqrt(spread + norm_eps)
    return centered * scale, scale


def normed_back(grad, hat, scale, gain):
    pulled = grad * gain
    mean = jnp.mean(pulled, axis=-1, keepdims=True)
    along = jnp.mean(pulled * hat, axis=-1, keepdims=True)
    return scale * (pulled - mean - hat * along)


def column_sums(values):
    return jnp.sum(values.astype(jnp.float32), axis=0, keepdims=True)


def gelu_and_slope(values):
    bell = 0.5 * (1.0 + lax.erf(values * (0.5**0.5)))
    slope = bell + values * jnp.exp(-0.5 * values * values) * (2.0 * math.pi) ** -0.5
    return values * bell, slope


def grad_plan(layers):
    a_off, b_off, items = {}, {}, []
    a_at, b_at, row = 0, 0, 0
    for name, share, blocks in layers:
        a_off[name], b_off[name] = a_at, b_at
        for block in range(blocks):
            for start in range(0, share, PIECE):
                rows = min(PIECE, share - start)
                for half in range(WIDE // HALF):
                    items.append((name, block, start, rows, half, row))
                row += rows
        a_at += -(-share // PIECE) * PIECE
        b_at += blocks
    return a_off, b_off, items, row, a_at, b_at


ORDER = (
    0, 1, 2, 3, 4, 5, 6, 7, 8, 9, 100, 10, 11, 12, 13, 200, 101, 102,
    14, 15, 16, 17, 300, 18, 400, 500, 19, 501, 201, 103, 20, 202, 104, 600, 301, 601,
    401, 502, 503, 21, 203, 105, 302, 700, 701, 602, 402, 204, 106, 800, 603, 303, 403, 504,
    702, 505, 205, 107, 506, 507, 508, 22, 304, 703, 509, 604, 404, 510, 605, 511, 206, 108,
    606, 305, 512, 414, 704, 513, 536, 607, 405, 514, 207, 109, 515, 705, 608, 516, 306, 706,
    517, 801, 802, 803, 804, 609, 406, 707, 610, 208, 110, 307, 518, 708, 519, 805, 806, 807,
    611, 407, 520, 612, 636, 709, 521, 808, 613, 209, 111, 710, 809, 614, 308, 711, 408, 522,
    615, 523, 810, 712, 736, 210, 112, 713, 811, 616, 309, 714, 409, 524, 617, 525, 812, 813,
    211, 113, 715, 814, 836, 618, 310, 716, 619, 410, 526, 717, 527, 815, 816, 620, 212, 311,
    718, 621, 411, 528, 719, 529, 817, 818, 622, 213, 720, 819, 623, 312, 313, 721, 412, 530,
    624, 413, 531, 820, 722, 532, 533, 625, 723, 534, 535, 821, 822, 626, 724, 823, 627, 725,
    824, 628, 726, 825, 629, 727, 826, 630, 728, 827, 631, 729, 828, 632, 730, 829, 633, 731,
    830, 634, 732, 831, 635, 733, 832, 734, 833, 735, 834, 835,
)


def everything(layers, n_vec, *refs):
    low, full = jnp.bfloat16, jnp.float32
    refs = list(refs)

    def pop(count):
        taken = refs[:count]
        del refs[:count]
        return taken

    expr_ref, gene_masks_ref, segments_ref, mean_ref, logvar_ref = pop(5)
    vec_refs = dict(zip(VECTORS, pop(n_vec)))
    table_ref, target_ref, noise_ref = pop(3)
    w_gene, w_qkv, w_out, w_up, w_down, w_enc, w_lat, w_dec = pop(8)
    (input_ref,) = pop(1)
    out_refs = dict(zip([name for name, _, _ in layers], pop(len(layers))))
    (tail_ref,) = pop(1)
    ring, masks_own, masks_all, table, target_in, noise_in, x1_out, x1_in = pop(8)
    kv_all, query_own, probs, dkv_part, dkv_in, dx_out, dx_in = pop(7)
    hats, scales, slopes, mixed_grad, input_grad = pop(5)
    a_src, a_all, b_all, v_src, v_all, near, far, v_near, v_far = pop(9)
    ring_sem, hand_send, hand_recv, hand_local, pair_send, pair_recv = pop(6)
    one_sem, a_send, a_recv, a_local, v_send, v_recv, b_send, b_recv, c_send, c_recv, o_sem = pop(11)

    d = lax.axis_index("dp")
    z = lax.axis_index("phase")
    base = (d // GROUP) * GROUP
    r = d % GROUP
    core, cx, cy = r % 2, (r // 2) % 2, r // 4
    partner = d + 1 - 2 * core
    owner = d - core + z // 2
    own = core == z // 2
    rc, rx, ry = r + 1 - 2 * core, r + 2 - 4 * cx, r + 4 - 8 * cy
    rxc, ryc = rx + 1 - 2 * core, ry + 1 - 2 * core
    rd = rx + 4 - 8 * cy
    rdc = rd + 1 - 2 * core
    middle = (z % 3) != 0
    inward = z + 1 - 2 * (z // 2)
    outward = z - 1 + 2 * (z // 2)
    a_off, b_off, items, _, _, blocks = grad_plan(layers)
    shares = {name: share for name, share, _ in layers}
    index_of = {name: index for index, (name, _, _) in enumerate(layers)}
    seqs, rows, genes = expr_ref.shape
    tokens = seqs * rows
    width = table.shape[1]
    hidden = w_up.shape[1]
    length = segments_ref.shape[1]
    wide = WIDE

    barrier = pltpu.get_barrier_semaphore()

    def greet(to):
        pl.semaphore_signal(barrier, inc=1, device_id=to, device_id_type=MESH)

    for step in range(1, GROUP):
        greet((base + (r + step) % GROUP, z))
    greet((d, inward))

    @pl.when(middle)
    def _():
        greet((d, outward))

    for i in range(2):

        @pl.when(jnp.logical_not(own & (z % 2 == i)))
        def _():
            greet((owner, 2 * core + i))

    def barrier_wait():
        pl.semaphore_wait(barrier, GROUP + 1 + (z % 3 + 1) // 2 + (core + z // 2) % 2)

    def remote(src, dst, send, recv, to):
        return pltpu.make_async_remote_copy(
            src_ref=src,
            dst_ref=dst,
            send_sem=send,
            recv_sem=recv,
            device_id=to,
            device_id_type=MESH,
        )

    def columns_of(name):
        return pl.ds(a_off[name], -(-shares[name] // PIECE) * PIECE)

    def a_copy(name, step, slot):
        at, index, to = columns_of(name), index_of[name], (r + step) % GROUP
        return remote(
            a_src.at[to, :, at],
            a_all.at[slot, :, at],
            a_send.at[index, step],
            a_recv.at[index, step],
            (base + to, z),
        )

    def a_own(name):
        at = columns_of(name)
        return pltpu.make_async_copy(
            a_src.at[r, :, at], a_all.at[r, :, at], a_local.at[index_of[name]]
        )

    def send_a(name):
        for step in range(1, GROUP):
            a_copy(name, step, r).start()
        a_own(name).start()

    def arrive_a(name):
        a_own(name).wait()
        for step in range(1, GROUP):
            a_copy(name, step, (r + GROUP - step) % GROUP).wait_recv()

    def v_copy(step, slot):
        to = (r + step) % GROUP
        return remote(
            v_src.at[to], v_all.at[slot], v_send.at[step], v_recv.at[step], (base + to, z)
        )

    own_sums = pltpu.make_async_copy(v_src.at[r], v_all.at[r], one_sem.at[0])

    comes = (rx, ry, rc, rxc, ryc, rd, rd, rdc, rdc)
    goes = (r, r, r, rx, ry, rx, ry, rd, rd)

    def b_copy(kind, block, source):
        col, size = block * WIDE, WIDE
        if kind in (5, 7):
            size = HALF
        if kind in (6, 8):
            col, size = col + HALF, HALF
        to = (rx, ry, rc, rc, rc, ry, rx, rc, rc)[kind]
        view = b_all.at[source, :, pl.ds(col, size)]
        return remote(view, view, b_send.at[block, kind], b_recv.at[block, kind], (base + to, z))

    def b_start(kind, block):
        b_copy(kind, block, goes[kind]).start()

    def b_arrive(kind, block):
        b_copy(kind, block, comes[kind]).wait_recv()

    vectors = len(items)

    def place_of(ref, v_ref, index):
        if index == vectors:
            return v_ref
        _, _, _, count, half, row = items[index]
        return ref.at[pl.ds(row, count), pl.ds(half * HALF, HALF)]

    def to_middle(index, to):
        ref = place_of(near, v_near, index)
        return remote(ref, ref, c_send.at[index, 0], c_recv.at[index, 0], (d, to))

    def across(index):
        src, dst = place_of(near, v_near, index), place_of(far, v_far, index)
        return remote(src, dst, c_send.at[index, 1], c_recv.at[index, 1], (d, inward))

    def to_end(index, to):
        ref = place_of(far, v_far, index)
        return remote(ref, ref, c_send.at[index, 0], c_recv.at[index, 0], (d, to))

    def result(index, ref, v_ref):
        src = place_of(ref, v_ref, index)
        if index == vectors:
            return pltpu.make_async_copy(src, tail_ref, o_sem.at[index])
        name, block, start, count, half, _ = items[index]
        to = out_refs[name].at[pl.ds(start, count), pl.ds(block * WIDE + half * HALF, HALF)]
        return pltpu.make_async_copy(src, to, o_sem.at[index])

    def product(index):
        if index == vectors:
            return jnp.sum(v_all[...], axis=0)
        name, block, start, count, half, _ = items[index]
        a_at = a_off[name] + start
        b_at = (b_off[name] + block) * WIDE + half * HALF
        left = a_all[:, :, a_at : a_at + PIECE].reshape(-1, PIECE)
        right = b_all[:, :, b_at : b_at + HALF].reshape(-1, HALF)
        value = mm_first(left, right)
        if count < PIECE:
            value = jnp.where(r % 2 == 1, value[count : 2 * count], value[:count])
        return value

    def end_push(index):
        @pl.when(jnp.logical_not(middle))
        def _():
            ref = place_of(near, v_near, index)
            ref[...] = product(index).astype(ref.dtype)
            to_middle(index, inward).start()

    def middle_join(index):
        @pl.when(middle)
        def _():
            value = product(index)
            to_middle(index, inward).wait_recv()
            ref = place_of(near, v_near, index)
            ref[...] = (value + ref[...].astype(full)).astype(ref.dtype)
            across(index).start()

    def middle_total(index):
        @pl.when(middle)
        def _():
            across(index).wait_recv()
            mine, theirs = place_of(near, v_near, index), place_of(far, v_far, index)
            both = mine[...].astype(full) + theirs[...].astype(full)
            theirs[...] = both.astype(theirs.dtype)
            to_end(index, outward).start()
            result(index, far, v_far).start()

    def end_land(index):
        @pl.when(jnp.logical_not(middle))
        def _():
            to_end(index, inward).wait_recv()
            result(index, far, v_far).start()

    block_layer = [name for name, _, count in layers for _ in range(count)]
    arrived = set()

    def get(block):
        if block == blocks:
            own_sums.wait()
            for step in range(1, GROUP):
                v_copy(step, (r + GROUP - step) % GROUP).wait_recv()
            return
        for kind in (2, 3, 4, 7, 8):
            b_arrive(kind, block)
        name = block_layer[block]
        if name not in arrived:
            arrived.add(name)
            arrive_a(name)

    table_copy = pltpu.make_async_copy(
        table_ref.at[pl.ds(z * rows, rows), :], table, one_sem.at[1]
    )
    input_copy = pltpu.make_async_copy(input_grad, input_ref, one_sem.at[2])
    pair_local = one_sem.at[3]
    table_copy.start()

    def rows_work():
        stream = []
        for j in range(genes // wide):
            stream.append(w_gene.at[pl.ds(j * wide, wide), :])
        for j in range(3):
            stream.append(w_qkv.at[:, pl.ds(j * wide, wide)])
        stream.append(w_out)
        for j in range(hidden // wide):
            stream.append(w_up.at[:, pl.ds(j * wide, wide)])
            stream.append(w_down.at[pl.ds(j * wide, wide), :])
        stream.append(w_enc)
        stream.append(w_lat)
        for j in range(genes // wide):
            stream.append(w_dec.at[:, pl.ds(j * wide, wide)])
        stream.append(w_lat)
        stream.append(w_enc)
        for j in range(hidden // wide):
            stream.append(w_down.at[pl.ds(j * wide, wide), :])
            stream.append(w_up.at[:, pl.ds(j * wide, wide)])
        stream.append(w_out)
        for j in range(3):
            stream.append(w_qkv.at[:, pl.ds(j * wide, wide)])
        for j in range(genes // wide):
            stream.append(w_gene.at[pl.ds(j * wide, wide), :])

        def load(k):
            depth = stream[k].shape[0]
            return pltpu.make_async_copy(
                stream[k], ring.at[k % SLOTS, pl.ds(0, depth), :], ring_sem.at[k % SLOTS]
            )

        def fetch(k):
            if k < len(stream):
                load(k).start()

        place = [0]

        def take():
            k = place[0]
            place[0] += 1
            load(k).wait()
            return k

        def block(k):
            return ring[k % SLOTS, : stream[k].shape[0], :]

        for k in range(SLOTS):
            fetch(k)

        barrier_wait()

        def hand(which, src, dst, i):
            return pltpu.make_async_remote_copy(
                src_ref=src.at[i],
                dst_ref=dst.at[z % 2],
                send_sem=hand_send.at[which, i],
                recv_sem=hand_recv.at[which, z % 2],
                device_id=(owner, 2 * core + i),
                device_id_type=MESH,
            )

        def hand_here(which, src, dst, i):
            return pltpu.make_async_copy(src.at[i], dst.at[i], hand_local.at[which])

        def hand_start(which, src, dst):
            for i in range(2):
                here = own & (z % 2 == i)

                @pl.when(here)
                def _():
                    hand_here(which, src, dst, i).start()

                @pl.when(jnp.logical_not(here))
                def _():
                    hand(which, src, dst, i).start()

        def hand_arrive(which, src, dst):
            for i in range(2):
                here = own & (z % 2 == i)

                @pl.when(here)
                def _():
                    hand_here(which, src, dst, i).wait()

                @pl.when(jnp.logical_not(here))
                def _():
                    pltpu.make_async_remote_copy(
                        src_ref=src.at[i],
                        dst_ref=dst.at[i],
                        send_sem=hand_send.at[which, i],
                        recv_sem=hand_recv.at[which, i],
                        device_id=(owner, 2 * core + i),
                        device_id_type=MESH,
                    ).wait_recv()

        def hand_sent(which, src, dst):
            for i in range(2):
                @pl.when(jnp.logical_not(own & (z % 2 == i)))
                def _():
                    hand(which, src, dst, i).wait_send()

        def pair(which, src, dst):
            return pltpu.make_async_remote_copy(
                src_ref=src,
                dst_ref=dst,
                send_sem=pair_send.at[which],
                recv_sem=pair_recv.at[which],
                device_id=(partner, z),
                device_id_type=MESH,
            )

        masks_own[:seqs, :genes] = gene_masks_ref[...].astype(full)
        masks_own[:seqs, genes : genes + length] = segments_ref[...].astype(full)
        pair(0, masks_own, masks_all.at[core]).start()
        own_masks = pltpu.make_async_copy(masks_own, masks_all.at[core], pair_local)
        own_masks.start()

        def vec(name, j=0):
            return vec_refs[name][:, j * wide : (j + 1) * wide]

        def put_a(name, values):
            off, share = a_off[name], shares[name]
            step = max(share, PIECE)
            for o in range(GROUP):
                start = o * share // step * step
                a_src[o, :, off : off + step] = values[:, start : start + step]

        def put_b(name, j, values):
            at = (b_off[name] + j) * wide
            b_all[r, :, at : at + wide] = values

        def put_sum(name, values, j=0):
            each = SUM_LANES[name]
            for o in range(values.shape[1] // 128):
                at = j * wide + o * 128
                to, row = at // (128 * each), SUM_AT[name] + at // 128 % each
                v_src[to, row : row + 1, :] = values[:, o * 128 : o * 128 + 128]

        def normalize(index, values, gain, shift):
            hat, scale = normed(values)
            hats[index] = hat
            scales[index] = jnp.broadcast_to(scale, scales.shape[1:])
            return hat * vec(gain) + vec(shift)

        def normalize_back(index, grad, gain, gain_name, shift_name):
            hat, scale = hats[index], scales[index, :, :1]
            put_sum(gain_name, jnp.sum(grad * hat, axis=0, keepdims=True))
            put_sum(shift_name, jnp.sum(grad, axis=0, keepdims=True))
            return normed_back(grad, hat, scale, vec(gain))

        keep = 1.0 - masks_own[:seqs, :genes]
        keep = jnp.concatenate(
            [jnp.broadcast_to(keep[s : s + 1], (rows, genes)) for s in range(seqs)], axis=0
        )
        masked = (expr_ref[...].reshape(tokens, genes).astype(full) * keep).astype(low)
        put_a(GENE, masked)
        send_a(GENE)
        table_copy.wait()
        embedded = jnp.concatenate([table[...]] * seqs, axis=0)
        for j in range(genes // wide):
            k = take()
            embedded += mm(masked[:, j * wide : (j + 1) * wide], block(k))
            fetch(k + SLOTS)
        x1_out[...] = (
            normalize(0, embedded, EMB_GAIN, EMB_SHIFT).astype(low).reshape(seqs, rows, width)
        )
        hand_start(0, x1_out, x1_in)
        hand_start(1, noise_ref, noise_in)
        hand_start(2, target_ref, target_in)
        yield
        own_masks.wait()
        pair(0, masks_own, masks_all.at[1 - core]).wait_recv()
        odd = z % 2 == 1
        both_masks = masks_all[pl.ds(z // 2, 1)][0]
        mask_row = jnp.where(odd, both_masks[1:2], both_masks[0:1])
        gene_row = mask_row[:, :genes]
        segments = mask_row[:, genes : genes + length]
        place_q = lax.broadcasted_iota(jnp.int32, (tokens, length), 0) + core * tokens
        place_k = lax.broadcasted_iota(jnp.int32, (tokens, length), 1)
        own_segments = jnp.sum(
            jnp.where(place_q == place_k, segments, 0.0), axis=-1, keepdims=True
        )
        same = own_segments == segments
        same = jnp.concatenate([same.astype(full)] * 2, axis=0) > 0.5

        hand_arrive(0, x1_out, x1_in)
        x1 = x1_in[...].reshape(tokens, width).astype(full)
        h1 = normalize(1, x1, ATTN_GAIN, ATTN_SHIFT).astype(low)
        put_a(QKV, h1)
        send_a(QKV)
        head = width // HEADS
        scale = head**-0.5
        k_query = take()
        query_own[...] = (mm(h1, block(k_query)) + vec(B_QKV, 0)).astype(low)
        fetch(k_query + SLOTS)
        for j in (1, 2):
            k = take()
            kv_all[core, :, (j - 1) * wide : j * wide] = (
                mm(h1, block(k)) + vec(B_QKV, j)
            ).astype(low)
            fetch(k + SLOTS)
        pair(1, kv_all.at[core], kv_all.at[core]).start()
        yield
        pair(1, kv_all.at[core], kv_all.at[1 - core]).wait_recv()

        lanes = lax.broadcasted_iota(jnp.int32, (tokens, 2 * head), 1)
        first = lanes < head
        pairs = HEADS // 2

        def two(values):
            none = jnp.zeros_like(values)
            return jnp.concatenate([jnp.where(first, values, none), jnp.where(first, none, values)], axis=0)

        def one(values):
            return jnp.where(first, values[:tokens], values[tokens:])

        def columns(p):
            return pl.ds(pl.multiple_of(p * 2 * head, 2 * head), 2 * head)

        def keys_of(p):
            return kv_all[:, :, columns(p)].reshape(length, 2 * head)

        def values_of(p):
            at = pl.ds(pl.multiple_of(width + p * 2 * head, 2 * head), 2 * head)
            return kv_all[:, :, at].reshape(length, 2 * head)

        def attend(p, carry):
            scores = mm_last(two(query_own[:, columns(p)]), keys_of(p)) * scale
            scores = jnp.where(same, scores, mask_fill)
            shifted = jnp.exp(scores - jnp.max(scores, axis=-1, keepdims=True))
            prob = shifted / jnp.sum(shifted, axis=-1, keepdims=True)
            probs[p] = prob
            att = one(mm(prob.astype(low), values_of(p))).astype(low)
            a_src[p, :, a_off[OUT] : a_off[OUT] + 2 * head] = att
            return carry

        lax.fori_loop(0, pairs, attend, 0)
        send_a(OUT)
        yield
        attended = jnp.concatenate(
            [a_src[o, :, a_off[OUT] : a_off[OUT] + 2 * head] for o in range(pairs)], axis=1
        )
        k = take()
        mixed = x1 + (mm(attended, block(k)) + vec(B_OUT))
        fetch(k + SLOTS)
        h2 = normalize(2, mixed, FFN_GAIN, FFN_SHIFT).astype(low)
        put_a(UP, h2)
        send_a(UP)
        yield
        x2 = mixed + vec(B_DOWN)
        per_owner = shares[DOWN]
        for j in range(hidden // wide):
            k = take()
            before = mm(h2, block(k)) + vec(B_UP, j)
            fetch(k + SLOTS)
            active, slope = gelu_and_slope(before)
            slopes[:, j * wide : (j + 1) * wide] = slope
            active = active.astype(low)
            for o in range(wide // per_owner):
                a_src[
                    j * (wide // per_owner) + o, :, a_off[DOWN] : a_off[DOWN] + per_owner
                ] = active[:, o * per_owner : (o + 1) * per_owner]
            k = take()
            x2 += mm(active, block(k))
            fetch(k + SLOTS)
            if j == hidden // wide - 1:
                send_a(DOWN)
            yield
        x2 = x2.astype(low).astype(full)
        h3 = normalize(3, x2, BOT_GAIN, BOT_SHIFT).astype(low)
        put_a(ENC, h3)
        k_enc = take()
        moments = mm(h3, block(k_enc)) + vec(B_ENC)
        latents = width // 2
        logvar = moments[:, latents:]
        hand_arrive(1, noise_ref, noise_in)
        swing = jnp.exp(0.5 * logvar) * noise_in[...].reshape(tokens, latents).astype(full)
        latent = moments[:, :latents] + swing
        latent_low = latent.astype(low)
        put_a(LAT, latent_low)
        fetch(k_enc + SLOTS)
        k_lat = take()
        lat_active, lat_slope = gelu_and_slope(mm(latent_low, block(k_lat)) + vec(B_LAT))
        fetch(k_lat + SLOTS)
        x3 = lat_active.astype(low).astype(full)
        h4 = normalize(4, x3, DEC_GAIN, DEC_SHIFT).astype(low)
        put_a(DEC, h4)
        send_a(DEC)
        yield
        hand_arrive(2, target_ref, target_in)

        grad = jnp.zeros((tokens, width), full)
        for j in range(genes // wide):
            k = take()
            at = slice(j * wide, (j + 1) * wide)
            predicted = mm(h4, block(k)) + vec(B_DEC, j)
            wanted = target_in[:, :, at].reshape(tokens, wide).astype(full)
            d_pred = (gene_row[:, at] * (predicted - wanted)).astype(low)
            put_b(DEC, j, d_pred)
            put_sum(B_DEC, column_sums(d_pred), j)
            grad += mm_last(d_pred, block(k))
            fetch(k + SLOTS)
            yield
        d_x3 = normalize_back(4, grad, DEC_GAIN, DEC_GAIN, DEC_SHIFT).astype(low).astype(full)
        d_lat = (lat_slope * d_x3).astype(low)
        put_b(LAT, 0, d_lat)
        put_sum(B_LAT, column_sums(d_lat))
        k = take()
        d_latent = mm_last(d_lat, block(k))
        fetch(k + SLOTS)
        send_a(ENC)
        send_a(LAT)
        yield

        inverse = jnp.exp(-logvar_ref[...])
        volume = jnp.sum(logvar_ref[...], axis=-1, keepdims=True)
        count = mean_ref.shape[0]
        scaled = []
        for c in range(count):
            offset = latent - mean_ref[c : c + 1, :]
            quad = jnp.sum(offset * offset * inverse[c : c + 1], axis=-1, keepdims=True)
            scaled.append(-0.5 * (quad + volume[c : c + 1]))
        highest = functools.reduce(jnp.maximum, scaled)
        shares_c = [jnp.exp(s - highest) for s in scaled]
        whole = functools.reduce(jnp.add, shares_c)
        for c in range(count):
            part = shares_c[c] / whole
            offset = latent - mean_ref[c : c + 1, :]
            pull = offset * inverse[c : c + 1]
            weighted = part * pull
            d_latent += weighted
            mean_grad = -jnp.sum(weighted, axis=0, keepdims=True)
            logvar_grad = 0.5 * jnp.sum(part - weighted * offset, axis=0, keepdims=True)
            for o in range(GROUP):
                at = slice(o // 2 * 128, o // 2 * 128 + 128)
                row = SUM_AT[COMP_MEAN] + c
                v_src[o, row : row + 1, :] = mean_grad[:, at]
                row = SUM_AT[COMP_LOGVAR] + c
                v_src[o, row : row + 1, :] = logvar_grad[:, at]
        d_moments = jnp.concatenate([d_latent, 0.5 * d_latent * swing - 0.5], axis=1).astype(low)
        put_b(ENC, 0, d_moments)
        put_sum(B_ENC, column_sums(d_moments))
        yield
        k = take()
        grad = mm_last(d_moments, block(k))
        fetch(k + SLOTS)
        g = normalize_back(3, grad, BOT_GAIN, BOT_GAIN, BOT_SHIFT).astype(low)
        put_b(DOWN, 0, g)
        put_sum(B_DOWN, column_sums(g))
        yield
        grad = jnp.zeros((tokens, width), full)
        for j in range(hidden // wide):
            k = take()
            d_active = mm_last(g, block(k))
            fetch(k + SLOTS)
            d_before = (slopes[:, j * wide : (j + 1) * wide] * d_active).astype(low)
            put_b(UP, j, d_before)
            put_sum(B_UP, column_sums(d_before), j)
            k = take()
            grad += mm_last(d_before, block(k))
            fetch(k + SLOTS)
            yield
        d_mixed = g.astype(full) + normalize_back(2, grad, FFN_GAIN, FFN_GAIN, FFN_SHIFT)
        mixed_grad[...] = d_mixed
        da = d_mixed.astype(low)
        put_b(OUT, 0, da)
        put_sum(B_OUT, column_sums(da))
        k = take()
        x1_in[...] = mm_last(da, block(k)).astype(low).reshape(seqs, rows, width)
        fetch(k + SLOTS)
        yield
        q_at = b_off[QKV] * wide

        def attend_back(p, carry):
            query = two(query_own[:, columns(p)])
            d_att = two(x1_in[:, :, columns(p)].reshape(tokens, 2 * head))
            prob = probs[p]
            keys = keys_of(p)
            d_value = mm_first(prob.astype(low), d_att)
            d_prob = mm_last(d_att, values_of(p))
            d_score = prob * (d_prob - jnp.sum(prob * d_prob, axis=-1, keepdims=True))
            d_score = d_score.astype(low)
            d_query = one(mm(d_score, keys)) * scale
            d_key = mm_first(d_score, query) * scale
            to = pl.ds(pl.multiple_of(q_at + p * 2 * head, 2 * head), 2 * head)
            b_all[r, :, to] = d_query.astype(low)
            dkv_part[:, :, columns(p)] = d_key.reshape(2, tokens, 2 * head)
            at = pl.ds(pl.multiple_of(width + p * 2 * head, 2 * head), 2 * head)
            dkv_part[:, :, at] = d_value.reshape(2, tokens, 2 * head)
            return carry

        lax.fori_loop(0, pairs // 2, attend_back, 0)
        yield
        lax.fori_loop(pairs // 2, pairs, attend_back, 0)
        pair(2, dkv_part.at[1 - core], dkv_in).start()
        yield
        d_query = b_all[r, :, q_at : q_at + wide]
        put_sum(B_QUERY, column_sums(d_query))
        k = take()
        grad = mm_last(d_query, block(k))
        fetch(k + SLOTS)
        pair(2, dkv_part.at[1 - core], dkv_in).wait_recv()
        for j in (1, 2):
            at = slice((j - 1) * wide, j * wide)
            d_part = (dkv_part[core, :, at] + dkv_in[:, at]).astype(low)
            put_b(QKV, j, d_part)
            if j == 2:
                put_sum(B_VALUE, column_sums(d_part))
            k = take()
            grad += mm_last(d_part, block(k))
            fetch(k + SLOTS)
        d_x1 = mixed_grad[...] + normalize_back(1, grad, ATTN_GAIN, ATTN_GAIN, ATTN_SHIFT)
        dx_out[...] = d_x1.astype(low).reshape(seqs, rows, width)
        hand_start(3, dx_out, dx_in)
        yield
        hand_arrive(3, dx_out, dx_in)
        d_x1 = dx_in[...].reshape(tokens, width).astype(full)
        d_embedded = normalize_back(0, d_x1, EMB_GAIN, EMB_GAIN, EMB_SHIFT).astype(low)
        put_b(GENE, 0, d_embedded)
        for j in range(genes // wide):
            k = take()
            at = slice(j * wide, (j + 1) * wide)
            input_grad[:, at] = mm_last(d_embedded, block(k)) * jnp.concatenate(
                [
                    jnp.broadcast_to(1.0 - masks_own[s : s + 1, at], (rows, wide))
                    for s in range(seqs)
                ],
                axis=0,
            )
        input_copy.start()
        for step in range(1, GROUP):
            v_copy(step, r).start()
        own_sums.start()
        yield
        input_copy.wait()
        hand_sent(0, x1_out, x1_in)
        hand_sent(1, noise_ref, noise_in)
        hand_sent(2, target_ref, target_in)
        hand_sent(3, dx_out, dx_in)
        pair(0, masks_own, masks_all.at[core]).wait_send()
        pair(1, kv_all.at[core], kv_all.at[core]).wait_send()
        pair(2, dkv_part.at[1 - core], dkv_in).wait_send()


    work = rows_work()
    for code in ORDER:
        kind, index = code // 100, code % 100
        if kind == 0:
            next(work)
        elif kind == 1:
            for way in (0, 1, 2):
                b_start(way, index)
        elif kind == 2:
            b_arrive(0, index)
            b_start(5, index)
            b_start(3, index)
            b_arrive(1, index)
            b_start(6, index)
            b_start(4, index)
        elif kind == 3:
            b_arrive(5, index)
            b_start(7, index)
            b_arrive(6, index)
            b_start(8, index)
        else:
            (get, end_push, middle_join, middle_total, end_land)[kind - 4](index)
    next(work, None)
    for block in range(blocks):
        for kind in range(9):
            b_copy(kind, block, goes[kind]).wait_send()
    for step in range(1, GROUP):
        v_copy(step, r).wait_send()
        for name, _, _ in layers:
            a_copy(name, step, r).wait_send()
    for index in range(len(items) + 1):
        to_middle(index, inward).wait_send()
        result(index, far, v_far).wait()

        @pl.when(middle)
        def _():
            across(index).wait_send()


SUM_LANES = dict(SUMS)


def finish(layers, core_of, *refs):
    refs = list(refs)
    count = len(layers)
    low_refs, refs = refs[:count], refs[count:]
    input_ref, tail_ref = refs[:2]
    refs = refs[2:]
    full_refs, refs = refs[:count], refs[count:]
    input_out = refs[0]
    sum_refs = dict(zip([name for name, _ in SUMS], refs[1 : 1 + len(SUMS)]))
    refs = refs[1 + len(SUMS) :]
    low_bufs, full_bufs, (in_sem, out_sem, move_sem) = refs[:count], refs[count : 2 * count], refs[2 * count :]
    move = pltpu.make_async_copy(input_ref, input_out, move_sem)
    ins = [
        pltpu.make_async_copy(src, dst, in_sem.at[i])
        for i, (src, dst) in enumerate(zip(low_refs, low_bufs))
    ]
    outs = [
        pltpu.make_async_copy(src, dst, out_sem.at[i])
        for i, (src, dst) in enumerate(zip(full_bufs, full_refs))
    ]
    for copy in ins:
        copy.start()
    move.start()
    odd = lax.axis_index("dp") % 2 == 1
    for name, rows in SUMS:
        at = SUM_AT[name]
        if name in (COMP_MEAN, COMP_LOGVAR):
            both = tail_ref[at : at + rows, :]
            sum_refs[name][...] = jnp.where(odd, both[:, 64:], both[:, :64])
        else:
            for row in range(rows):
                sum_refs[name][:, row * 128 : row * 128 + 128] = tail_ref[at + row : at + row + 1, :]
    for i in range(count):
        ins[i].wait()
        full_bufs[i][...] = low_bufs[i][...].astype(jnp.float32)
        outs[i].start()
    for copy in outs:
        copy.wait()
    move.wait()


def positions(length, width):
    frequency = np.exp(np.arange(width // 2, dtype=np.float32) * np.float32(-2.0 * math.log(10000.0) / width))
    angles = np.arange(length, dtype=np.float32)[:, None] * frequency[None, :]
    return np.stack([np.sin(angles), np.cos(angles)], axis=-1).reshape(length, width)


def body(expression, targets, noise, gene_masks, segment_ids, w_gene, emb_gain, emb_shift, attn_gain, attn_shift, w_qkv, b_qkv, w_out, b_out, ffn_gain, ffn_shift, w_up, b_up, w_down, b_down, bot_gain, bot_shift, w_enc, b_enc, comp_mean, comp_logvar, w_lat, b_lat, dec_gain, dec_shift, w_dec, b_dec):
    low, full = jnp.bfloat16, jnp.float32
    seqs, rows, genes = expression.shape
    width = w_gene.shape[1]
    hidden = w_up.shape[1]
    latents = noise.shape[2]
    length = segment_ids.shape[1]
    tokens = seqs * rows
    given = {
        EMB_GAIN: emb_gain,
        EMB_SHIFT: emb_shift,
        ATTN_GAIN: attn_gain,
        ATTN_SHIFT: attn_shift,
        B_QKV: b_qkv,
        B_OUT: b_out,
        FFN_GAIN: ffn_gain,
        FFN_SHIFT: ffn_shift,
        B_UP: b_up,
        B_DOWN: b_down,
        BOT_GAIN: bot_gain,
        BOT_SHIFT: bot_shift,
        B_ENC: b_enc,
        B_LAT: b_lat,
        DEC_GAIN: dec_gain,
        DEC_SHIFT: dec_shift,
        B_DEC: b_dec,
    }
    weights = {
        GENE: w_gene,
        QKV: w_qkv,
        OUT: w_out,
        UP: w_up,
        DOWN: w_down,
        ENC: w_enc,
        LAT: w_lat,
        DEC: w_dec,
    }
    layers = [
        (name, weights[name].shape[0] // GROUP, weights[name].shape[1] // WIDE) for name in LAYERS
    ]
    _, _, items, rows_all, a_cols, b_blocks = grad_plan(layers)
    vmem = pl.BlockSpec(memory_space=pltpu.VMEM)
    anywhere = pl.BlockSpec(memory_space=pl.ANY)
    dma = pltpu.SemaphoreType.DMA
    mask_lanes = genes + length + -length % 128
    share_shapes = [(share, count * WIDE) for _, share, count in layers]
    chunks = len(items) + 1
    results = pl.pallas_call(
        functools.partial(everything, layers, len(VECTORS)),
        out_shape=(jax.ShapeDtypeStruct((tokens, genes), full),)
        + tuple(jax.ShapeDtypeStruct(shape, low) for shape in share_shapes)
        + (jax.ShapeDtypeStruct((SUM_ROWS, 128), full),),
        in_specs=[vmem] * (5 + len(VECTORS)) + [anywhere] * 11,
        out_specs=(anywhere,) * (2 + len(layers)),
        scratch_shapes=[
            pltpu.VMEM((SLOTS, WIDE, WIDE), low),
            pltpu.VMEM((8, mask_lanes), full),
            pltpu.VMEM((2, 8, mask_lanes), full),
            pltpu.VMEM((rows, width), full),
            pltpu.VMEM((2, rows, genes), low),
            pltpu.VMEM((2, rows, latents), low),
            pltpu.VMEM((2, rows, width), low),
            pltpu.VMEM((2, rows, width), low),
            pltpu.VMEM((2, tokens, 2 * width), low),
            pltpu.VMEM((tokens, width), low),
            pltpu.VMEM((HEADS // 2, 2 * tokens, 2 * tokens), full),
            pltpu.VMEM((2, tokens, 2 * width), full),
            pltpu.VMEM((tokens, 2 * width), full),
            pltpu.VMEM((2, rows, width), low),
            pltpu.VMEM((2, rows, width), low),
            pltpu.VMEM((5, tokens, width), full),
            pltpu.VMEM((5, tokens, 128), full),
            pltpu.VMEM((tokens, hidden), full),
            pltpu.VMEM((tokens, width), full),
            pltpu.VMEM((tokens, genes), full),
            pltpu.VMEM((GROUP, tokens, a_cols), low),
            pltpu.VMEM((GROUP, tokens, a_cols), low),
            pltpu.VMEM((GROUP, tokens, b_blocks * WIDE), low),
            pltpu.VMEM((GROUP, SUM_ROWS, 128), full),
            pltpu.VMEM((GROUP, SUM_ROWS, 128), full),
            pltpu.VMEM((rows_all, WIDE), low),
            pltpu.VMEM((rows_all, WIDE), low),
            pltpu.VMEM((SUM_ROWS, 128), full),
            pltpu.VMEM((SUM_ROWS, 128), full),
            dma((SLOTS,)),
            dma((4, 2)),
            dma((4, 2)),
            dma((4,)),
            dma((3,)),
            dma((3,)),
            dma((4,)),
            dma((len(layers), GROUP)),
            dma((len(layers), GROUP)),
            dma((len(layers),)),
            dma((GROUP,)),
            dma((GROUP,)),
            dma((b_blocks, 9)),
            dma((b_blocks, 9)),
            dma((chunks, 2)),
            dma((chunks, 2)),
            dma((chunks,)),
        ],
        compiler_params=pltpu.CompilerParams(
            collective_id=0, has_side_effects=True, vmem_limit_bytes=63 * 1024 * 1024
        ),
    )(
        expression,
        gene_masks,
        segment_ids,
        comp_mean,
        comp_logvar,
        *[given[name].reshape(1, -1) for name in VECTORS],
        positions(length, width),
        targets,
        noise,
        *weights.values(),
    )
    input_grad, sums, tail = results[0], results[1:-1], results[-1]

    def sum_shape(name, count):
        return (count, 64) if name in (COMP_MEAN, COMP_LOGVAR) else (1, count * 128)

    finished = pl.pallas_call(
        functools.partial(finish, layers, None),
        out_shape=tuple(jax.ShapeDtypeStruct(shape, full) for shape in share_shapes)
        + (jax.ShapeDtypeStruct((tokens, genes), full),)
        + tuple(jax.ShapeDtypeStruct(sum_shape(name, count), full) for name, count in SUMS),
        in_specs=[anywhere] * (len(layers) + 1) + [vmem],
        out_specs=(anywhere,) * (len(layers) + 1) + (vmem,) * len(SUMS),
        scratch_shapes=[pltpu.VMEM(shape, low) for shape in share_shapes]
        + [pltpu.VMEM(shape, full) for shape in share_shapes]
        + [dma((len(layers),)), dma((len(layers),)), dma],
        compiler_params=pltpu.CompilerParams(vmem_limit_bytes=32 * 1024 * 1024),
    )(*sums, input_grad, tail)

    groups = lax.axis_size("dp") // GROUP
    d = lax.axis_index("dp")

    def shared_out(values, axis):
        if groups == 1:
            return values
        across = [[g * GROUP + r for g in range(groups)] for r in range(GROUP)]
        within = [[g * GROUP + r for r in range(GROUP)] for g in range(groups)]
        values = lax.psum(values, "dp", axis_index_groups=across)
        values = lax.all_gather(values, "dp", axis=axis, tiled=True, axis_index_groups=within)
        size = values.shape[axis] // (groups * GROUP)
        return lax.dynamic_slice_in_dim(values, d * size, size, axis=axis)

    grads = {}
    for name, values in zip(LAYERS, finished):
        grads[name] = shared_out(values, 0)
    for (name, _), values in zip(SUMS, finished[len(layers) + 1 :]):
        if name in (COMP_MEAN, COMP_LOGVAR):
            grads[name] = shared_out(values, 1)
        else:
            grads[name] = shared_out(values.reshape(-1), 0)
    return (
        finished[len(layers)].reshape(seqs, rows, genes),
        grads[GENE],
        grads[EMB_GAIN],
        grads[EMB_SHIFT],
        grads[ATTN_GAIN],
        grads[ATTN_SHIFT],
        grads[QKV],
        grads[B_QUERY],
        grads[B_VALUE],
        grads[OUT],
        grads[B_OUT],
        grads[FFN_GAIN],
        grads[FFN_SHIFT],
        grads[UP],
        grads[B_UP],
        grads[DOWN],
        grads[B_DOWN],
        grads[BOT_GAIN],
        grads[BOT_SHIFT],
        grads[ENC],
        grads[B_ENC],
        grads[COMP_MEAN],
        grads[COMP_LOGVAR],
        grads[LAT],
        grads[B_LAT],
        grads[DEC_GAIN],
        grads[DEC_SHIFT],
        grads[DEC],
        grads[B_DEC],
    )


def solution(mesh):
    rows = P("dp", "phase", None)
    return jax.shard_map(
        body,
        mesh=mesh,
        in_specs=(rows, rows, rows, P("dp", None), P("dp", None)) + (P(),) * 27,
        out_specs=(
            rows,
            P("dp", None),
            P("dp"),
            P("dp"),
            P("dp"),
            P("dp"),
            P("dp", None),
            P("dp"),
            P("dp"),
            P("dp", None),
            P("dp"),
            P("dp"),
            P("dp"),
            P("dp", None),
            P("dp"),
            P("dp", None),
            P("dp"),
            P("dp"),
            P("dp"),
            P("dp", None),
            P("dp"),
            P(None, "dp"),
            P(None, "dp"),
            P("dp", None),
            P("dp"),
            P("dp"),
            P("dp"),
            P("dp", None),
            P("dp"),
        ),
        check_vma=False,
    )
```

```python
import functools
import math

import jax
import jax.numpy as jnp
import numpy as np
from jax import lax
from jax.experimental import pallas as pl
from jax.experimental.pallas import tpu as pltpu
from jax.sharding import PartitionSpec as P

HEADS = 16
GROUP = 8
PIECE = 128
WIDE = 1024
HALF = 512
SLOTS = 4

norm_eps = 1e-05
mask_fill = -1000000000.0
MESH = pl.DeviceIdType.MESH

(
    DOWN,
    GENE,
    UP,
    QKV,
    DEC,
    ENC,
    OUT,
    LAT,
    EMB_GAIN,
    EMB_SHIFT,
    ATTN_GAIN,
    ATTN_SHIFT,
    B_QKV,
    B_QUERY,
    B_VALUE,
    B_OUT,
    FFN_GAIN,
    FFN_SHIFT,
    B_UP,
    B_DOWN,
    BOT_GAIN,
    BOT_SHIFT,
    B_ENC,
    COMP_MEAN,
    COMP_LOGVAR,
    B_LAT,
    DEC_GAIN,
    DEC_SHIFT,
    B_DEC,
) = range(29)


LAYERS = (DEC, DOWN, LAT, ENC, UP, OUT, QKV, GENE)
VECTORS = (
    EMB_GAIN,
    EMB_SHIFT,
    ATTN_GAIN,
    ATTN_SHIFT,
    B_QKV,
    B_OUT,
    FFN_GAIN,
    FFN_SHIFT,
    B_UP,
    B_DOWN,
    BOT_GAIN,
    BOT_SHIFT,
    B_ENC,
    B_LAT,
    DEC_GAIN,
    DEC_SHIFT,
    B_DEC,
)
SUMS = (
    (COMP_MEAN, 16),
    (COMP_LOGVAR, 16),
    (EMB_GAIN, 1),
    (EMB_SHIFT, 1),
    (ATTN_GAIN, 1),
    (ATTN_SHIFT, 1),
    (B_QUERY, 1),
    (B_VALUE, 1),
    (B_OUT, 1),
    (FFN_GAIN, 1),
    (FFN_SHIFT, 1),
    (B_UP, 4),
    (B_DOWN, 1),
    (BOT_GAIN, 1),
    (BOT_SHIFT, 1),
    (B_ENC, 1),
    (B_LAT, 1),
    (DEC_GAIN, 1),
    (DEC_SHIFT, 1),
    (B_DEC, 2),
)
SUM_AT = {name: sum(n for _, n in SUMS[:i]) for i, (name, _) in enumerate(SUMS)}
SUM_ROWS = 64


def mm(left, right):
    return jnp.dot(left, right, preferred_element_type=jnp.float32)


def mm_last(left, right):
    return lax.dot_general(
        left, right, (((1,), (1,)), ((), ())), preferred_element_type=jnp.float32
    )


def mm_first(left, right):
    return lax.dot_general(
        left, right, (((0,), (0,)), ((), ())), preferred_element_type=jnp.float32
    )


def normed(values):
    center = jnp.mean(values, axis=-1, keepdims=True)
    centered = values - center
    spread = jnp.mean(centered * centered, axis=-1, keepdims=True)
    scale = lax.rsqrt(spread + norm_eps)
    return centered * scale, scale


def normed_back(grad, hat, scale, gain):
    pulled = grad * gain
    mean = jnp.mean(pulled, axis=-1, keepdims=True)
    along = jnp.mean(pulled * hat, axis=-1, keepdims=True)
    return scale * (pulled - mean - hat * along)


def column_sums(values):
    return jnp.sum(values.astype(jnp.float32), axis=0, keepdims=True)


def gelu_and_slope(values):
    bell = 0.5 * (1.0 + lax.erf(values * (0.5**0.5)))
    slope = bell + values * jnp.exp(-0.5 * values * values) * (2.0 * math.pi) ** -0.5
    return values * bell, slope


def grad_plan(layers):
    a_off, b_off, items = {}, {}, []
    a_at, b_at, row = 0, 0, 0
    for name, share, blocks in layers:
        a_off[name], b_off[name] = a_at, b_at
        for block in range(blocks):
            for start in range(0, share, PIECE):
                rows = min(PIECE, share - start)
                for half in range(WIDE // HALF):
                    items.append((name, block, start, rows, half, row))
                row += rows
        a_at += -(-share // PIECE) * PIECE
        b_at += blocks
    return a_off, b_off, items, row, a_at, b_at


ORDER = (
    0, 1, 2, 3, 4, 5, 6, 7, 8, 9, 100, 10, 11, 12, 13, 14, 15, 16,
    17, 18, 19, 200, 102, 904, 905, 20, 21, 300, 400, 500, 501, 22, 202, 101, 103, 600,
    601, 302, 402, 504, 700, 505, 506, 507, 23, 508, 201, 104, 701, 509, 604, 510, 203, 105,
    511, 800, 605, 301, 414, 704, 801, 606, 401, 502, 536, 705, 503, 607, 204, 804, 106, 303,
    706, 608, 403, 512, 513, 805, 707, 609, 205, 806, 107, 708, 807, 610, 304, 404, 514, 709,
    515, 611, 808, 206, 108, 710, 602, 636, 809, 305, 405, 711, 516, 603, 517, 810, 612, 207,
    109, 702, 613, 811, 306, 703, 614, 406, 518, 712, 736, 519, 802, 713, 803, 615, 208, 110,
    307, 812, 714, 616, 407, 520, 521, 813, 836, 715, 617, 209, 814, 111, 716, 618, 308, 815,
    408, 522, 717, 523, 619, 816, 210, 112, 718, 620, 817, 309, 409, 719, 524, 621, 525, 818,
    211, 113, 720, 622, 819, 310, 721, 623, 410, 526, 527, 820, 722, 624, 821, 212, 311, 723,
    625, 411, 528, 529, 822, 724, 626, 823, 213, 725, 627, 824, 312, 313, 412, 530, 726, 531,
    628, 413, 825, 532, 727, 533, 629, 534, 535, 826, 728, 630, 827, 729, 631, 828, 730, 632,
    829, 731, 633, 830, 732, 634, 831, 733, 635, 832, 734, 833, 735, 834, 835,
)


def everything(layers, n_vec, *refs):
    low, full = jnp.bfloat16, jnp.float32
    refs = list(refs)

    def pop(count):
        taken = refs[:count]
        del refs[:count]
        return taken

    expr_ref, gene_masks_ref, segments_ref, mean_ref, logvar_ref = pop(5)
    vec_refs = dict(zip(VECTORS, pop(n_vec)))
    table_ref, target_ref, noise_ref = pop(3)
    w_gene, w_qkv, w_out, w_up, w_down, w_enc, w_lat, w_dec = pop(8)
    (input_ref,) = pop(1)
    out_refs = dict(zip([name for name, _, _ in layers], pop(len(layers))))
    (tail_ref,) = pop(1)
    ring, masks_own, masks_all, table, target_in, noise_in, x1_out, x1_in = pop(8)
    kv_all, query_own, probs, dkv_part, dkv_in, dx_out, dx_in = pop(7)
    hats, scales, slopes, mixed_grad, input_grad = pop(5)
    a_src, a_all, b_all, v_src, v_all, near, far, v_near, v_far = pop(9)
    ring_sem, hand_send, hand_recv, hand_local, pair_send, pair_recv = pop(6)
    one_sem, a_send, a_recv, a_local, v_send, v_recv, b_send, b_recv, c_send, c_recv, o_sem = pop(11)

    d = lax.axis_index("dp")
    z = lax.axis_index("phase")
    base = (d // GROUP) * GROUP
    r = d % GROUP
    core, cx, cy = r % 2, (r // 2) % 2, r // 4
    partner = d + 1 - 2 * core
    owner = d - core + z // 2
    own = core == z // 2
    rc, rx, ry = r + 1 - 2 * core, r + 2 - 4 * cx, r + 4 - 8 * cy
    rxc, ryc = rx + 1 - 2 * core, ry + 1 - 2 * core
    rd = rx + 4 - 8 * cy
    rdc = rd + 1 - 2 * core
    middle = (z % 3) != 0
    inward = z + 1 - 2 * (z // 2)
    outward = z - 1 + 2 * (z // 2)
    a_off, b_off, items, _, _, blocks = grad_plan(layers)
    shares = {name: share for name, share, _ in layers}
    index_of = {name: index for index, (name, _, _) in enumerate(layers)}
    seqs, rows, genes = expr_ref.shape
    tokens = seqs * rows
    width = table.shape[1]
    hidden = w_up.shape[1]
    length = segments_ref.shape[1]
    wide = WIDE

    barrier = pltpu.get_barrier_semaphore()

    def greet(to):
        pl.semaphore_signal(barrier, inc=1, device_id=to, device_id_type=MESH)

    for step in range(1, GROUP):
        greet((base + (r + step) % GROUP, z))
    greet((d, inward))

    @pl.when(middle)
    def _():
        greet((d, outward))

    for i in range(2):

        @pl.when(jnp.logical_not(own & (z % 2 == i)))
        def _():
            greet((owner, 2 * core + i))

    def barrier_wait():
        pl.semaphore_wait(barrier, GROUP + 1 + (z % 3 + 1) // 2 + (core + z // 2) % 2)

    def remote(src, dst, send, recv, to):
        return pltpu.make_async_remote_copy(
            src_ref=src,
            dst_ref=dst,
            send_sem=send,
            recv_sem=recv,
            device_id=to,
            device_id_type=MESH,
        )

    def columns_of(name):
        return pl.ds(a_off[name], -(-shares[name] // PIECE) * PIECE)

    def a_copy(name, step, slot):
        at, index, to = columns_of(name), index_of[name], (r + step) % GROUP
        return remote(
            a_src.at[to, :, at],
            a_all.at[slot, :, at],
            a_send.at[index, step],
            a_recv.at[index, step],
            (base + to, z),
        )

    def a_own(name):
        at = columns_of(name)
        return pltpu.make_async_copy(
            a_src.at[r, :, at], a_all.at[r, :, at], a_local.at[index_of[name]]
        )

    def send_a(name):
        for step in range(1, GROUP):
            a_copy(name, step, r).start()
        a_own(name).start()

    def send_a_to(name, to):
        step = (to - r + GROUP) % GROUP

        @pl.when(r == to)
        def _():
            a_own(name).start()

        @pl.when(r != to)
        def _():
            a_copy(name, step, r).start()

    def send_late(index):
        send_a(layers[index][0])

    def arrive_a(name):
        a_own(name).wait()
        for step in range(1, GROUP):
            a_copy(name, step, (r + GROUP - step) % GROUP).wait_recv()

    def v_copy(step, slot):
        to = (r + step) % GROUP
        return remote(
            v_src.at[to], v_all.at[slot], v_send.at[step], v_recv.at[step], (base + to, z)
        )

    own_sums = pltpu.make_async_copy(v_src.at[r], v_all.at[r], one_sem.at[0])

    comes = (rx, ry, rc, rxc, ryc, rd, rd, rdc, rdc)
    goes = (r, r, r, rx, ry, rx, ry, rd, rd)

    def b_copy(kind, block, source):
        col, size = block * WIDE, WIDE
        if kind in (5, 7):
            size = HALF
        if kind in (6, 8):
            col, size = col + HALF, HALF
        to = (rx, ry, rc, rc, rc, ry, rx, rc, rc)[kind]
        view = b_all.at[source, :, pl.ds(col, size)]
        return remote(view, view, b_send.at[block, kind], b_recv.at[block, kind], (base + to, z))

    def b_start(kind, block):
        b_copy(kind, block, goes[kind]).start()

    def b_arrive(kind, block):
        b_copy(kind, block, comes[kind]).wait_recv()

    vectors = len(items)

    def place_of(ref, v_ref, index):
        if index == vectors:
            return v_ref
        _, _, _, count, half, row = items[index]
        return ref.at[pl.ds(row, count), pl.ds(half * HALF, HALF)]

    def to_middle(index, to):
        ref = place_of(near, v_near, index)
        return remote(ref, ref, c_send.at[index, 0], c_recv.at[index, 0], (d, to))

    def across(index):
        src, dst = place_of(near, v_near, index), place_of(far, v_far, index)
        return remote(src, dst, c_send.at[index, 1], c_recv.at[index, 1], (d, inward))

    def to_end(index, to):
        ref = place_of(far, v_far, index)
        return remote(ref, ref, c_send.at[index, 0], c_recv.at[index, 0], (d, to))

    def result(index, ref, v_ref):
        src = place_of(ref, v_ref, index)
        if index == vectors:
            return pltpu.make_async_copy(src, tail_ref, o_sem.at[index])
        name, block, start, count, half, _ = items[index]
        to = out_refs[name].at[pl.ds(start, count), pl.ds(block * WIDE + half * HALF, HALF)]
        return pltpu.make_async_copy(src, to, o_sem.at[index])

    def product(index):
        if index == vectors:
            return jnp.sum(v_all[...], axis=0)
        name, block, start, count, half, _ = items[index]
        a_at = a_off[name] + start
        b_at = (b_off[name] + block) * WIDE + half * HALF
        left = a_all[:, :, a_at : a_at + PIECE].reshape(-1, PIECE)
        right = b_all[:, :, b_at : b_at + HALF].reshape(-1, HALF)
        value = mm_first(left, right)
        if count < PIECE:
            value = jnp.where(r % 2 == 1, value[count : 2 * count], value[:count])
        return value

    def end_push(index):
        @pl.when(jnp.logical_not(middle))
        def _():
            ref = place_of(near, v_near, index)
            ref[...] = product(index).astype(ref.dtype)
            to_middle(index, inward).start()

    def middle_join(index):
        @pl.when(middle)
        def _():
            value = product(index)
            to_middle(index, inward).wait_recv()
            ref = place_of(near, v_near, index)
            ref[...] = (value + ref[...].astype(full)).astype(ref.dtype)
            across(index).start()

    def middle_total(index):
        @pl.when(middle)
        def _():
            across(index).wait_recv()
            mine, theirs = place_of(near, v_near, index), place_of(far, v_far, index)
            both = mine[...].astype(full) + theirs[...].astype(full)
            theirs[...] = both.astype(theirs.dtype)
            to_end(index, outward).start()
            result(index, far, v_far).start()

    def end_land(index):
        @pl.when(jnp.logical_not(middle))
        def _():
            to_end(index, inward).wait_recv()
            result(index, far, v_far).start()

    block_layer = [name for name, _, count in layers for _ in range(count)]
    arrived = set()

    def get(block):
        if block == blocks:
            own_sums.wait()
            for step in range(1, GROUP):
                v_copy(step, (r + GROUP - step) % GROUP).wait_recv()
            return
        for kind in (2, 3, 4, 7, 8):
            b_arrive(kind, block)
        name = block_layer[block]
        if name not in arrived:
            arrived.add(name)
            arrive_a(name)

    table_copy = pltpu.make_async_copy(
        table_ref.at[pl.ds(z * rows, rows), :], table, one_sem.at[1]
    )
    input_copy = pltpu.make_async_copy(input_grad, input_ref, one_sem.at[2])
    pair_local = one_sem.at[3]
    table_copy.start()

    def rows_work():
        stream = []
        for j in range(genes // wide):
            stream.append(w_gene.at[pl.ds(j * wide, wide), :])
        for j in range(3):
            stream.append(w_qkv.at[:, pl.ds(j * wide, wide)])
        stream.append(w_out)
        for j in range(hidden // wide):
            stream.append(w_up.at[:, pl.ds(j * wide, wide)])
            stream.append(w_down.at[pl.ds(j * wide, wide), :])
        stream.append(w_enc)
        stream.append(w_lat)
        for j in range(genes // wide):
            stream.append(w_dec.at[:, pl.ds(j * wide, wide)])
        stream.append(w_lat)
        stream.append(w_enc)
        for j in range(hidden // wide):
            stream.append(w_down.at[pl.ds(j * wide, wide), :])
            stream.append(w_up.at[:, pl.ds(j * wide, wide)])
        stream.append(w_out)
        for j in range(3):
            stream.append(w_qkv.at[:, pl.ds(j * wide, wide)])
        for j in range(genes // wide):
            stream.append(w_gene.at[pl.ds(j * wide, wide), :])

        def load(k):
            depth = stream[k].shape[0]
            return pltpu.make_async_copy(
                stream[k], ring.at[k % SLOTS, pl.ds(0, depth), :], ring_sem.at[k % SLOTS]
            )

        def fetch(k):
            if k < len(stream):
                load(k).start()

        place = [0]

        def take():
            k = place[0]
            place[0] += 1
            load(k).wait()
            return k

        def block(k):
            return ring[k % SLOTS, : stream[k].shape[0], :]

        for k in range(SLOTS):
            fetch(k)

        barrier_wait()

        def hand(which, src, dst, i):
            return pltpu.make_async_remote_copy(
                src_ref=src.at[i],
                dst_ref=dst.at[z % 2],
                send_sem=hand_send.at[which, i],
                recv_sem=hand_recv.at[which, z % 2],
                device_id=(owner, 2 * core + i),
                device_id_type=MESH,
            )

        def hand_here(which, src, dst, i):
            return pltpu.make_async_copy(src.at[i], dst.at[i], hand_local.at[which])

        def hand_start(which, src, dst):
            for i in range(2):
                here = own & (z % 2 == i)

                @pl.when(here)
                def _():
                    hand_here(which, src, dst, i).start()

                @pl.when(jnp.logical_not(here))
                def _():
                    hand(which, src, dst, i).start()

        def hand_arrive(which, src, dst):
            for i in range(2):
                here = own & (z % 2 == i)

                @pl.when(here)
                def _():
                    hand_here(which, src, dst, i).wait()

                @pl.when(jnp.logical_not(here))
                def _():
                    pltpu.make_async_remote_copy(
                        src_ref=src.at[i],
                        dst_ref=dst.at[i],
                        send_sem=hand_send.at[which, i],
                        recv_sem=hand_recv.at[which, i],
                        device_id=(owner, 2 * core + i),
                        device_id_type=MESH,
                    ).wait_recv()

        def hand_sent(which, src, dst):
            for i in range(2):
                @pl.when(jnp.logical_not(own & (z % 2 == i)))
                def _():
                    hand(which, src, dst, i).wait_send()

        def pair(which, src, dst):
            return pltpu.make_async_remote_copy(
                src_ref=src,
                dst_ref=dst,
                send_sem=pair_send.at[which],
                recv_sem=pair_recv.at[which],
                device_id=(partner, z),
                device_id_type=MESH,
            )

        masks_own[:seqs, :genes] = gene_masks_ref[...].astype(full)
        masks_own[:seqs, genes : genes + length] = segments_ref[...].astype(full)
        pair(0, masks_own, masks_all.at[core]).start()
        own_masks = pltpu.make_async_copy(masks_own, masks_all.at[core], pair_local)
        own_masks.start()

        def vec(name, j=0):
            return vec_refs[name][:, j * wide : (j + 1) * wide]

        def put_a(name, values):
            off, share = a_off[name], shares[name]
            step = max(share, PIECE)
            for o in range(GROUP):
                start = o * share // step * step
                a_src[o, :, off : off + step] = values[:, start : start + step]

        def put_b(name, j, values):
            at = (b_off[name] + j) * wide
            b_all[r, :, at : at + wide] = values

        def put_sum(name, values, j=0):
            each = SUM_LANES[name]
            for o in range(values.shape[1] // 128):
                at = j * wide + o * 128
                to, row = at // (128 * each), SUM_AT[name] + at // 128 % each
                v_src[to, row : row + 1, :] = values[:, o * 128 : o * 128 + 128]

        def normalize(index, values, gain, shift):
            hat, scale = normed(values)
            hats[index] = hat
            scales[index] = jnp.broadcast_to(scale, scales.shape[1:])
            return hat * vec(gain) + vec(shift)

        def normalize_back(index, grad, gain, gain_name, shift_name):
            hat, scale = hats[index], scales[index, :, :1]
            put_sum(gain_name, jnp.sum(grad * hat, axis=0, keepdims=True))
            put_sum(shift_name, jnp.sum(grad, axis=0, keepdims=True))
            return normed_back(grad, hat, scale, vec(gain))

        keep = 1.0 - masks_own[:seqs, :genes]
        keep = jnp.concatenate(
            [jnp.broadcast_to(keep[s : s + 1], (rows, genes)) for s in range(seqs)], axis=0
        )
        masked = (expr_ref[...].reshape(tokens, genes).astype(full) * keep).astype(low)
        put_a(GENE, masked)
        send_a(GENE)
        table_copy.wait()
        embedded = jnp.concatenate([table[...]] * seqs, axis=0)
        for j in range(genes // wide):
            k = take()
            embedded += mm(masked[:, j * wide : (j + 1) * wide], block(k))
            fetch(k + SLOTS)
        x1_out[...] = (
            normalize(0, embedded, EMB_GAIN, EMB_SHIFT).astype(low).reshape(seqs, rows, width)
        )
        hand_start(0, x1_out, x1_in)
        hand_start(1, noise_ref, noise_in)
        hand_start(2, target_ref, target_in)
        yield
        own_masks.wait()
        pair(0, masks_own, masks_all.at[1 - core]).wait_recv()
        odd = z % 2 == 1
        both_masks = masks_all[pl.ds(z // 2, 1)][0]
        mask_row = jnp.where(odd, both_masks[1:2], both_masks[0:1])
        gene_row = mask_row[:, :genes]
        segments = mask_row[:, genes : genes + length]
        place_q = lax.broadcasted_iota(jnp.int32, (tokens, length), 0) + core * tokens
        place_k = lax.broadcasted_iota(jnp.int32, (tokens, length), 1)
        own_segments = jnp.sum(
            jnp.where(place_q == place_k, segments, 0.0), axis=-1, keepdims=True
        )
        same = own_segments == segments
        same = jnp.concatenate([same.astype(full)] * 2, axis=0) > 0.5

        hand_arrive(0, x1_out, x1_in)
        x1 = x1_in[...].reshape(tokens, width).astype(full)
        h1 = normalize(1, x1, ATTN_GAIN, ATTN_SHIFT).astype(low)
        put_a(QKV, h1)
        send_a(QKV)
        head = width // HEADS
        scale = head**-0.5
        k_query = take()
        query_own[...] = (mm(h1, block(k_query)) + vec(B_QKV, 0)).astype(low)
        fetch(k_query + SLOTS)
        for j in (1, 2):
            k = take()
            kv_all[core, :, (j - 1) * wide : j * wide] = (
                mm(h1, block(k)) + vec(B_QKV, j)
            ).astype(low)
            fetch(k + SLOTS)
        pair(1, kv_all.at[core], kv_all.at[core]).start()
        yield
        pair(1, kv_all.at[core], kv_all.at[1 - core]).wait_recv()

        lanes = lax.broadcasted_iota(jnp.int32, (tokens, 2 * head), 1)
        first = lanes < head
        pairs = HEADS // 2

        def two(values):
            none = jnp.zeros_like(values)
            return jnp.concatenate([jnp.where(first, values, none), jnp.where(first, none, values)], axis=0)

        def one(values):
            return jnp.where(first, values[:tokens], values[tokens:])

        def columns(p):
            return pl.ds(pl.multiple_of(p * 2 * head, 2 * head), 2 * head)

        def keys_of(p):
            return kv_all[:, :, columns(p)].reshape(length, 2 * head)

        def values_of(p):
            at = pl.ds(pl.multiple_of(width + p * 2 * head, 2 * head), 2 * head)
            return kv_all[:, :, at].reshape(length, 2 * head)

        def attend(p, carry):
            scores = mm_last(two(query_own[:, columns(p)]), keys_of(p)) * scale
            scores = jnp.where(same, scores, mask_fill)
            shifted = jnp.exp(scores - jnp.max(scores, axis=-1, keepdims=True))
            prob = shifted / jnp.sum(shifted, axis=-1, keepdims=True)
            probs[p] = prob
            att = one(mm(prob.astype(low), values_of(p))).astype(low)
            a_src[p, :, a_off[OUT] : a_off[OUT] + 2 * head] = att
            return carry

        lax.fori_loop(0, pairs, attend, 0)
        yield
        attended = jnp.concatenate(
            [a_src[o, :, a_off[OUT] : a_off[OUT] + 2 * head] for o in range(pairs)], axis=1
        )
        k = take()
        mixed = x1 + (mm(attended, block(k)) + vec(B_OUT))
        fetch(k + SLOTS)
        h2 = normalize(2, mixed, FFN_GAIN, FFN_SHIFT).astype(low)
        put_a(UP, h2)
        yield
        x2 = mixed + vec(B_DOWN)
        per_owner = shares[DOWN]
        for j in range(hidden // wide):
            k = take()
            before = mm(h2, block(k)) + vec(B_UP, j)
            fetch(k + SLOTS)
            active, slope = gelu_and_slope(before)
            slopes[:, j * wide : (j + 1) * wide] = slope
            active = active.astype(low)
            for o in range(wide // per_owner):
                a_src[
                    j * (wide // per_owner) + o, :, a_off[DOWN] : a_off[DOWN] + per_owner
                ] = active[:, o * per_owner : (o + 1) * per_owner]
            k = take()
            x2 += mm(active, block(k))
            fetch(k + SLOTS)
            for o in range(wide // per_owner):
                send_a_to(DOWN, j * (wide // per_owner) + o)
            yield
        x2 = x2.astype(low).astype(full)
        h3 = normalize(3, x2, BOT_GAIN, BOT_SHIFT).astype(low)
        put_a(ENC, h3)
        k_enc = take()
        moments = mm(h3, block(k_enc)) + vec(B_ENC)
        latents = width // 2
        logvar = moments[:, latents:]
        hand_arrive(1, noise_ref, noise_in)
        swing = jnp.exp(0.5 * logvar) * noise_in[...].reshape(tokens, latents).astype(full)
        latent = moments[:, :latents] + swing
        latent_low = latent.astype(low)
        put_a(LAT, latent_low)
        fetch(k_enc + SLOTS)
        k_lat = take()
        lat_active, lat_slope = gelu_and_slope(mm(latent_low, block(k_lat)) + vec(B_LAT))
        fetch(k_lat + SLOTS)
        x3 = lat_active.astype(low).astype(full)
        h4 = normalize(4, x3, DEC_GAIN, DEC_SHIFT).astype(low)
        put_a(DEC, h4)
        send_a(DEC)
        yield
        hand_arrive(2, target_ref, target_in)

        grad = jnp.zeros((tokens, width), full)
        for j in range(genes // wide):
            k = take()
            at = slice(j * wide, (j + 1) * wide)
            predicted = mm(h4, block(k)) + vec(B_DEC, j)
            wanted = target_in[:, :, at].reshape(tokens, wide).astype(full)
            d_pred = (gene_row[:, at] * (predicted - wanted)).astype(low)
            put_b(DEC, j, d_pred)
            put_sum(B_DEC, column_sums(d_pred), j)
            grad += mm_last(d_pred, block(k))
            fetch(k + SLOTS)
            yield
        d_x3 = normalize_back(4, grad, DEC_GAIN, DEC_GAIN, DEC_SHIFT).astype(low).astype(full)
        d_lat = (lat_slope * d_x3).astype(low)
        put_b(LAT, 0, d_lat)
        put_sum(B_LAT, column_sums(d_lat))
        k = take()
        d_latent = mm_last(d_lat, block(k))
        fetch(k + SLOTS)
        send_a(ENC)
        send_a(LAT)
        yield

        inverse = jnp.exp(-logvar_ref[...])
        volume = jnp.sum(logvar_ref[...], axis=-1, keepdims=True)
        count = mean_ref.shape[0]
        scaled = []
        for c in range(count):
            offset = latent - mean_ref[c : c + 1, :]
            quad = jnp.sum(offset * offset * inverse[c : c + 1], axis=-1, keepdims=True)
            scaled.append(-0.5 * (quad + volume[c : c + 1]))
        highest = functools.reduce(jnp.maximum, scaled)
        shares_c = [jnp.exp(s - highest) for s in scaled]
        whole = functools.reduce(jnp.add, shares_c)
        parts = [part / whole for part in shares_c]
        for c in range(count):
            pull = (latent - mean_ref[c : c + 1, :]) * inverse[c : c + 1]
            d_latent += parts[c] * pull
        d_moments = jnp.concatenate([d_latent, 0.5 * d_latent * swing - 0.5], axis=1).astype(low)
        put_b(ENC, 0, d_moments)
        put_sum(B_ENC, column_sums(d_moments))
        yield
        k = take()
        grad = mm_last(d_moments, block(k))
        fetch(k + SLOTS)
        g = normalize_back(3, grad, BOT_GAIN, BOT_GAIN, BOT_SHIFT).astype(low)
        put_b(DOWN, 0, g)
        put_sum(B_DOWN, column_sums(g))
        yield
        for c in range(count):
            offset = latent - mean_ref[c : c + 1, :]
            weighted = parts[c] * (offset * inverse[c : c + 1])
            mean_grad = -jnp.sum(weighted, axis=0, keepdims=True)
            logvar_grad = 0.5 * jnp.sum(parts[c] - weighted * offset, axis=0, keepdims=True)
            for o in range(GROUP):
                at = slice(o // 2 * 128, o // 2 * 128 + 128)
                row = SUM_AT[COMP_MEAN] + c
                v_src[o, row : row + 1, :] = mean_grad[:, at]
                row = SUM_AT[COMP_LOGVAR] + c
                v_src[o, row : row + 1, :] = logvar_grad[:, at]
        yield
        grad = jnp.zeros((tokens, width), full)
        for j in range(hidden // wide):
            k = take()
            d_active = mm_last(g, block(k))
            fetch(k + SLOTS)
            d_before = (slopes[:, j * wide : (j + 1) * wide] * d_active).astype(low)
            put_b(UP, j, d_before)
            put_sum(B_UP, column_sums(d_before), j)
            k = take()
            grad += mm_last(d_before, block(k))
            fetch(k + SLOTS)
            yield
        d_mixed = g.astype(full) + normalize_back(2, grad, FFN_GAIN, FFN_GAIN, FFN_SHIFT)
        mixed_grad[...] = d_mixed
        da = d_mixed.astype(low)
        put_b(OUT, 0, da)
        put_sum(B_OUT, column_sums(da))
        k = take()
        x1_in[...] = mm_last(da, block(k)).astype(low).reshape(seqs, rows, width)
        fetch(k + SLOTS)
        yield
        q_at = b_off[QKV] * wide

        def attend_back(p, carry):
            query = two(query_own[:, columns(p)])
            d_att = two(x1_in[:, :, columns(p)].reshape(tokens, 2 * head))
            prob = probs[p]
            keys = keys_of(p)
            d_value = mm_first(prob.astype(low), d_att)
            d_prob = mm_last(d_att, values_of(p))
            d_score = prob * (d_prob - jnp.sum(prob * d_prob, axis=-1, keepdims=True))
            d_score = d_score.astype(low)
            d_query = one(mm(d_score, keys)) * scale
            d_key = mm_first(d_score, query) * scale
            to = pl.ds(pl.multiple_of(q_at + p * 2 * head, 2 * head), 2 * head)
            b_all[r, :, to] = d_query.astype(low)
            dkv_part[:, :, columns(p)] = d_key.reshape(2, tokens, 2 * head)
            at = pl.ds(pl.multiple_of(width + p * 2 * head, 2 * head), 2 * head)
            dkv_part[:, :, at] = d_value.reshape(2, tokens, 2 * head)
            return carry

        lax.fori_loop(0, pairs // 2, attend_back, 0)
        yield
        lax.fori_loop(pairs // 2, pairs, attend_back, 0)
        pair(2, dkv_part.at[1 - core], dkv_in).start()
        yield
        d_query = b_all[r, :, q_at : q_at + wide]
        put_sum(B_QUERY, column_sums(d_query))
        k = take()
        grad = mm_last(d_query, block(k))
        fetch(k + SLOTS)
        pair(2, dkv_part.at[1 - core], dkv_in).wait_recv()
        for j in (1, 2):
            at = slice((j - 1) * wide, j * wide)
            d_part = (dkv_part[core, :, at] + dkv_in[:, at]).astype(low)
            put_b(QKV, j, d_part)
            if j == 2:
                put_sum(B_VALUE, column_sums(d_part))
            k = take()
            grad += mm_last(d_part, block(k))
            fetch(k + SLOTS)
        d_x1 = mixed_grad[...] + normalize_back(1, grad, ATTN_GAIN, ATTN_GAIN, ATTN_SHIFT)
        dx_out[...] = d_x1.astype(low).reshape(seqs, rows, width)
        hand_start(3, dx_out, dx_in)
        yield
        hand_arrive(3, dx_out, dx_in)
        d_x1 = dx_in[...].reshape(tokens, width).astype(full)
        d_embedded = normalize_back(0, d_x1, EMB_GAIN, EMB_GAIN, EMB_SHIFT).astype(low)
        put_b(GENE, 0, d_embedded)
        for j in range(genes // wide):
            k = take()
            at = slice(j * wide, (j + 1) * wide)
            input_grad[:, at] = mm_last(d_embedded, block(k)) * jnp.concatenate(
                [
                    jnp.broadcast_to(1.0 - masks_own[s : s + 1, at], (rows, wide))
                    for s in range(seqs)
                ],
                axis=0,
            )
        input_copy.start()
        for step in range(1, GROUP):
            v_copy(step, r).start()
        own_sums.start()
        yield
        input_copy.wait()
        hand_sent(0, x1_out, x1_in)
        hand_sent(1, noise_ref, noise_in)
        hand_sent(2, target_ref, target_in)
        hand_sent(3, dx_out, dx_in)
        pair(0, masks_own, masks_all.at[core]).wait_send()
        pair(1, kv_all.at[core], kv_all.at[core]).wait_send()
        pair(2, dkv_part.at[1 - core], dkv_in).wait_send()


    work = rows_work()
    for code in ORDER:
        kind, index = code // 100, code % 100
        if kind == 0:
            next(work)
        elif kind == 1:
            for way in (0, 1, 2):
                b_start(way, index)
        elif kind == 2:
            b_arrive(0, index)
            b_start(5, index)
            b_start(3, index)
            b_arrive(1, index)
            b_start(6, index)
            b_start(4, index)
        elif kind == 3:
            b_arrive(5, index)
            b_start(7, index)
            b_arrive(6, index)
            b_start(8, index)
        else:
            (get, end_push, middle_join, middle_total, end_land, send_late)[kind - 4](index)
    next(work, None)
    for block in range(blocks):
        for kind in range(9):
            b_copy(kind, block, goes[kind]).wait_send()
    for step in range(1, GROUP):
        v_copy(step, r).wait_send()
        for name, _, _ in layers:
            a_copy(name, step, r).wait_send()
    for index in range(len(items) + 1):
        to_middle(index, inward).wait_send()
        result(index, far, v_far).wait()

        @pl.when(middle)
        def _():
            across(index).wait_send()


SUM_LANES = dict(SUMS)


def finish(layers, core_of, *refs):
    refs = list(refs)
    count = len(layers)
    low_refs, refs = refs[:count], refs[count:]
    input_ref, tail_ref = refs[:2]
    refs = refs[2:]
    full_refs, refs = refs[:count], refs[count:]
    input_out = refs[0]
    sum_refs = dict(zip([name for name, _ in SUMS], refs[1 : 1 + len(SUMS)]))
    refs = refs[1 + len(SUMS) :]
    low_bufs, full_bufs, (in_sem, out_sem, move_sem) = refs[:count], refs[count : 2 * count], refs[2 * count :]
    move = pltpu.make_async_copy(input_ref, input_out, move_sem)
    ins = [
        pltpu.make_async_copy(src, dst, in_sem.at[i])
        for i, (src, dst) in enumerate(zip(low_refs, low_bufs))
    ]
    outs = [
        pltpu.make_async_copy(src, dst, out_sem.at[i])
        for i, (src, dst) in enumerate(zip(full_bufs, full_refs))
    ]
    for copy in ins:
        copy.start()
    move.start()
    odd = lax.axis_index("dp") % 2 == 1
    for name, rows in SUMS:
        at = SUM_AT[name]
        if name in (COMP_MEAN, COMP_LOGVAR):
            both = tail_ref[at : at + rows, :]
            sum_refs[name][...] = jnp.where(odd, both[:, 64:], both[:, :64])
        else:
            for row in range(rows):
                sum_refs[name][:, row * 128 : row * 128 + 128] = tail_ref[at + row : at + row + 1, :]
    for i in range(count):
        ins[i].wait()
        full_bufs[i][...] = low_bufs[i][...].astype(jnp.float32)
        outs[i].start()
    for copy in outs:
        copy.wait()
    move.wait()


def positions(length, width):
    frequency = np.exp(np.arange(width // 2, dtype=np.float32) * np.float32(-2.0 * math.log(10000.0) / width))
    angles = np.arange(length, dtype=np.float32)[:, None] * frequency[None, :]
    return np.stack([np.sin(angles), np.cos(angles)], axis=-1).reshape(length, width)


def body(expression, targets, noise, gene_masks, segment_ids, w_gene, emb_gain, emb_shift, attn_gain, attn_shift, w_qkv, b_qkv, w_out, b_out, ffn_gain, ffn_shift, w_up, b_up, w_down, b_down, bot_gain, bot_shift, w_enc, b_enc, comp_mean, comp_logvar, w_lat, b_lat, dec_gain, dec_shift, w_dec, b_dec):
    low, full = jnp.bfloat16, jnp.float32
    seqs, rows, genes = expression.shape
    width = w_gene.shape[1]
    hidden = w_up.shape[1]
    latents = noise.shape[2]
    length = segment_ids.shape[1]
    tokens = seqs * rows
    given = {
        EMB_GAIN: emb_gain,
        EMB_SHIFT: emb_shift,
        ATTN_GAIN: attn_gain,
        ATTN_SHIFT: attn_shift,
        B_QKV: b_qkv,
        B_OUT: b_out,
        FFN_GAIN: ffn_gain,
        FFN_SHIFT: ffn_shift,
        B_UP: b_up,
        B_DOWN: b_down,
        BOT_GAIN: bot_gain,
        BOT_SHIFT: bot_shift,
        B_ENC: b_enc,
        B_LAT: b_lat,
        DEC_GAIN: dec_gain,
        DEC_SHIFT: dec_shift,
        B_DEC: b_dec,
    }
    weights = {
        GENE: w_gene,
        QKV: w_qkv,
        OUT: w_out,
        UP: w_up,
        DOWN: w_down,
        ENC: w_enc,
        LAT: w_lat,
        DEC: w_dec,
    }
    layers = [
        (name, weights[name].shape[0] // GROUP, weights[name].shape[1] // WIDE) for name in LAYERS
    ]
    _, _, items, rows_all, a_cols, b_blocks = grad_plan(layers)
    vmem = pl.BlockSpec(memory_space=pltpu.VMEM)
    anywhere = pl.BlockSpec(memory_space=pl.ANY)
    dma = pltpu.SemaphoreType.DMA
    mask_lanes = genes + length + -length % 128
    share_shapes = [(share, count * WIDE) for _, share, count in layers]
    chunks = len(items) + 1
    results = pl.pallas_call(
        functools.partial(everything, layers, len(VECTORS)),
        out_shape=(jax.ShapeDtypeStruct((tokens, genes), full),)
        + tuple(jax.ShapeDtypeStruct(shape, low) for shape in share_shapes)
        + (jax.ShapeDtypeStruct((SUM_ROWS, 128), full),),
        in_specs=[vmem] * (5 + len(VECTORS)) + [anywhere] * 11,
        out_specs=(anywhere,) * (2 + len(layers)),
        scratch_shapes=[
            pltpu.VMEM((SLOTS, WIDE, WIDE), low),
            pltpu.VMEM((8, mask_lanes), full),
            pltpu.VMEM((2, 8, mask_lanes), full),
            pltpu.VMEM((rows, width), full),
            pltpu.VMEM((2, rows, genes), low),
            pltpu.VMEM((2, rows, latents), low),
            pltpu.VMEM((2, rows, width), low),
            pltpu.VMEM((2, rows, width), low),
            pltpu.VMEM((2, tokens, 2 * width), low),
            pltpu.VMEM((tokens, width), low),
            pltpu.VMEM((HEADS // 2, 2 * tokens, 2 * tokens), full),
            pltpu.VMEM((2, tokens, 2 * width), full),
            pltpu.VMEM((tokens, 2 * width), full),
            pltpu.VMEM((2, rows, width), low),
            pltpu.VMEM((2, rows, width), low),
            pltpu.VMEM((5, tokens, width), full),
            pltpu.VMEM((5, tokens, 128), full),
            pltpu.VMEM((tokens, hidden), full),
            pltpu.VMEM((tokens, width), full),
            pltpu.VMEM((tokens, genes), full),
            pltpu.VMEM((GROUP, tokens, a_cols), low),
            pltpu.VMEM((GROUP, tokens, a_cols), low),
            pltpu.VMEM((GROUP, tokens, b_blocks * WIDE), low),
            pltpu.VMEM((GROUP, SUM_ROWS, 128), full),
            pltpu.VMEM((GROUP, SUM_ROWS, 128), full),
            pltpu.VMEM((rows_all, WIDE), low),
            pltpu.VMEM((rows_all, WIDE), low),
            pltpu.VMEM((SUM_ROWS, 128), full),
            pltpu.VMEM((SUM_ROWS, 128), full),
            dma((SLOTS,)),
            dma((4, 2)),
            dma((4, 2)),
            dma((4,)),
            dma((3,)),
            dma((3,)),
            dma((4,)),
            dma((len(layers), GROUP)),
            dma((len(layers), GROUP)),
            dma((len(layers),)),
            dma((GROUP,)),
            dma((GROUP,)),
            dma((b_blocks, 9)),
            dma((b_blocks, 9)),
            dma((chunks, 2)),
            dma((chunks, 2)),
            dma((chunks,)),
        ],
        compiler_params=pltpu.CompilerParams(
            collective_id=0, has_side_effects=True, vmem_limit_bytes=63 * 1024 * 1024
        ),
    )(
        expression,
        gene_masks,
        segment_ids,
        comp_mean,
        comp_logvar,
        *[given[name].reshape(1, -1) for name in VECTORS],
        positions(length, width),
        targets,
        noise,
        *weights.values(),
    )
    input_grad, sums, tail = results[0], results[1:-1], results[-1]

    def sum_shape(name, count):
        return (count, 64) if name in (COMP_MEAN, COMP_LOGVAR) else (1, count * 128)

    finished = pl.pallas_call(
        functools.partial(finish, layers, None),
        out_shape=tuple(jax.ShapeDtypeStruct(shape, full) for shape in share_shapes)
        + (jax.ShapeDtypeStruct((tokens, genes), full),)
        + tuple(jax.ShapeDtypeStruct(sum_shape(name, count), full) for name, count in SUMS),
        in_specs=[anywhere] * (len(layers) + 1) + [vmem],
        out_specs=(anywhere,) * (len(layers) + 1) + (vmem,) * len(SUMS),
        scratch_shapes=[pltpu.VMEM(shape, low) for shape in share_shapes]
        + [pltpu.VMEM(shape, full) for shape in share_shapes]
        + [dma((len(layers),)), dma((len(layers),)), dma],
        compiler_params=pltpu.CompilerParams(vmem_limit_bytes=63 * 1024 * 1024),
    )(*sums, input_grad, tail)

    groups = lax.axis_size("dp") // GROUP
    d = lax.axis_index("dp")

    def shared_out(values, axis):
        if groups == 1:
            return values
        across = [[g * GROUP + r for g in range(groups)] for r in range(GROUP)]
        within = [[g * GROUP + r for r in range(GROUP)] for g in range(groups)]
        values = lax.psum(values, "dp", axis_index_groups=across)
        values = lax.all_gather(values, "dp", axis=axis, tiled=True, axis_index_groups=within)
        size = values.shape[axis] // (groups * GROUP)
        return lax.dynamic_slice_in_dim(values, d * size, size, axis=axis)

    grads = {}
    for name, values in zip(LAYERS, finished):
        grads[name] = shared_out(values, 0)
    for (name, _), values in zip(SUMS, finished[len(layers) + 1 :]):
        if name in (COMP_MEAN, COMP_LOGVAR):
            grads[name] = shared_out(values, 1)
        else:
            grads[name] = shared_out(values.reshape(-1), 0)
    return (
        finished[len(layers)].reshape(seqs, rows, genes),
        grads[GENE],
        grads[EMB_GAIN],
        grads[EMB_SHIFT],
        grads[ATTN_GAIN],
        grads[ATTN_SHIFT],
        grads[QKV],
        grads[B_QUERY],
        grads[B_VALUE],
        grads[OUT],
        grads[B_OUT],
        grads[FFN_GAIN],
        grads[FFN_SHIFT],
        grads[UP],
        grads[B_UP],
        grads[DOWN],
        grads[B_DOWN],
        grads[BOT_GAIN],
        grads[BOT_SHIFT],
        grads[ENC],
        grads[B_ENC],
        grads[COMP_MEAN],
        grads[COMP_LOGVAR],
        grads[LAT],
        grads[B_LAT],
        grads[DEC_GAIN],
        grads[DEC_SHIFT],
        grads[DEC],
        grads[B_DEC],
    )


def solution(mesh):
    rows = P("dp", "phase", None)
    return jax.shard_map(
        body,
        mesh=mesh,
        in_specs=(rows, rows, rows, P("dp", None), P("dp", None)) + (P(),) * 27,
        out_specs=(
            rows,
            P("dp", None),
            P("dp"),
            P("dp"),
            P("dp"),
            P("dp"),
            P("dp", None),
            P("dp"),
            P("dp"),
            P("dp", None),
            P("dp"),
            P("dp"),
            P("dp"),
            P("dp", None),
            P("dp"),
            P("dp", None),
            P("dp"),
            P("dp"),
            P("dp"),
            P("dp", None),
            P("dp"),
            P(None, "dp"),
            P(None, "dp"),
            P("dp", None),
            P("dp"),
            P("dp"),
            P("dp"),
            P("dp", None),
            P("dp"),
        ),
        check_vma=False,
    )
```

```python
import functools
import math

import jax
import jax.numpy as jnp
import numpy as np
from jax import lax
from jax.experimental import pallas as pl
from jax.experimental.pallas import tpu as pltpu
from jax.sharding import PartitionSpec as P

HEADS = 16
GROUP = 8
PIECE = 128
WIDE = 1024
SLOTS = 4

norm_eps = 1e-05
mask_fill = -1000000000.0
MESH = pl.DeviceIdType.MESH

(
    DOWN,
    GENE,
    UP,
    QKV,
    DEC,
    ENC,
    OUT,
    LAT,
    EMB_GAIN,
    EMB_SHIFT,
    ATTN_GAIN,
    ATTN_SHIFT,
    B_QKV,
    B_QUERY,
    B_VALUE,
    B_OUT,
    FFN_GAIN,
    FFN_SHIFT,
    B_UP,
    B_DOWN,
    BOT_GAIN,
    BOT_SHIFT,
    B_ENC,
    COMP_MEAN,
    COMP_LOGVAR,
    B_LAT,
    DEC_GAIN,
    DEC_SHIFT,
    B_DEC,
) = range(29)


LAYERS = (DEC, DOWN, LAT, ENC, UP, OUT, QKV, GENE)
VECTORS = (
    EMB_GAIN,
    EMB_SHIFT,
    ATTN_GAIN,
    ATTN_SHIFT,
    B_QKV,
    B_OUT,
    FFN_GAIN,
    FFN_SHIFT,
    B_UP,
    B_DOWN,
    BOT_GAIN,
    BOT_SHIFT,
    B_ENC,
    B_LAT,
    DEC_GAIN,
    DEC_SHIFT,
    B_DEC,
)
SUMS = (
    (COMP_MEAN, 16),
    (COMP_LOGVAR, 16),
    (EMB_GAIN, 1),
    (EMB_SHIFT, 1),
    (ATTN_GAIN, 1),
    (ATTN_SHIFT, 1),
    (B_QUERY, 1),
    (B_VALUE, 1),
    (B_OUT, 1),
    (FFN_GAIN, 1),
    (FFN_SHIFT, 1),
    (B_UP, 4),
    (B_DOWN, 1),
    (BOT_GAIN, 1),
    (BOT_SHIFT, 1),
    (B_ENC, 1),
    (B_LAT, 1),
    (DEC_GAIN, 1),
    (DEC_SHIFT, 1),
    (B_DEC, 2),
)
SUM_AT = {name: sum(n for _, n in SUMS[:i]) for i, (name, _) in enumerate(SUMS)}
SUM_ROWS = 64


def mm(left, right):
    return jnp.dot(left, right, preferred_element_type=jnp.float32)


def mm_last(left, right):
    return lax.dot_general(
        left, right, (((1,), (1,)), ((), ())), preferred_element_type=jnp.float32
    )


def mm_first(left, right):
    return lax.dot_general(
        left, right, (((0,), (0,)), ((), ())), preferred_element_type=jnp.float32
    )


def normed(values):
    center = jnp.mean(values, axis=-1, keepdims=True)
    centered = values - center
    spread = jnp.mean(centered * centered, axis=-1, keepdims=True)
    scale = lax.rsqrt(spread + norm_eps)
    return centered * scale, scale


def normed_back(grad, hat, scale, gain):
    pulled = grad * gain
    mean = jnp.mean(pulled, axis=-1, keepdims=True)
    along = jnp.mean(pulled * hat, axis=-1, keepdims=True)
    return scale * (pulled - mean - hat * along)


def column_sums(values):
    return jnp.sum(values.astype(jnp.float32), axis=0, keepdims=True)


def gelu(values):
    return values * (0.5 * (1.0 + lax.erf(values * (0.5**0.5))))


def gelu_slope(values):
    bell = 0.5 * (1.0 + lax.erf(values * (0.5**0.5)))
    return bell + values * jnp.exp(-0.5 * values * values) * (2.0 * math.pi) ** -0.5


BLOCKS = (
    (DEC, 0, 512, 512),
    (DEC, 512, 512, 512),
    (DEC, 1024, 1024, 512),
    (DOWN, 0, 512, 512),
    (DOWN, 512, 512, 512),
    (LAT, 0, 1024, 512),
    (ENC, 0, 1024, 512),
    (UP, 0, 1024, 512),
    (UP, 1024, 1024, 512),
    (UP, 2048, 1024, 512),
    (UP, 3072, 1024, 512),
    (OUT, 0, 1024, 512),
    (QKV, 0, 1024, 512),
    (QKV, 1024, 1024, 512),
    (QKV, 2048, 1024, 512),
    (GENE, 0, 1024, 256),
)


def grad_plan(layers):
    a_off, b_off, items, place = {}, {}, [], {}
    a_at, b_at, row = 0, 0, 0
    shares = {name: share for name, share, _ in layers}
    for name, share, columns in layers:
        a_off[name], b_off[name] = a_at, b_at
        for block in range(columns // WIDE):
            for start in range(0, share, PIECE):
                place[name, block, start] = row
                row += min(PIECE, share - start)
        a_at += -(-share // PIECE) * PIECE
        b_at += columns
    for block, (name, first, columns, step) in enumerate(BLOCKS):
        for start in range(0, shares[name], PIECE):
            rows = min(PIECE, shares[name] - start)
            for col in range(first, first + columns, step):
                items.append((block, start, rows, col, step, place[name, col // WIDE, start]))
    return a_off, b_off, items, row, a_at, b_at


ORDER = (
    0, 1, 2, 3, 4, 5, 6, 7, 8, 9, 100, 101, 10, 11, 12, 13, 14, 15,
    16, 17, 200, 18, 19, 201, 300, 103, 902, 903, 20, 301, 400, 500, 21, 401, 203, 104,
    102, 501, 22, 303, 600, 403, 601, 204, 105, 904, 905, 504, 505, 506, 507, 202, 106, 304,
    700, 404, 508, 604, 509, 510, 23, 205, 107, 511, 800, 701, 605, 704, 606, 801, 607, 302,
    705, 402, 416, 502, 540, 503, 804, 608, 706, 206, 108, 805, 707, 609, 305, 405, 708, 512,
    610, 513, 806, 207, 807, 109, 611, 709, 306, 808, 602, 406, 514, 710, 515, 809, 603, 640,
    208, 110, 711, 810, 612, 307, 613, 702, 407, 516, 517, 811, 614, 209, 111, 703, 712, 740,
    802, 615, 308, 713, 408, 518, 714, 519, 803, 812, 616, 210, 112, 813, 840, 715, 617, 309,
    409, 716, 520, 618, 521, 814, 211, 815, 113, 619, 717, 310, 816, 620, 410, 522, 718, 523,
    817, 212, 114, 719, 621, 311, 818, 720, 622, 411, 524, 525, 819, 721, 623, 213, 115, 820,
    624, 312, 722, 412, 526, 527, 821, 625, 723, 214, 822, 724, 626, 313, 725, 413, 528, 529,
    823, 627, 215, 824, 726, 628, 314, 825, 727, 315, 414, 530, 531, 629, 415, 826, 532, 728,
    533, 534, 535, 536, 537, 630, 538, 729, 539, 827, 828, 631, 632, 730, 829, 633, 634, 731,
    830, 635, 732, 636, 733, 831, 637, 734, 832, 638, 735, 833, 639, 736, 834, 737, 835, 738,
    836, 739, 837, 838, 839,
)


def everything(layers, n_vec, *refs):
    low, full = jnp.bfloat16, jnp.float32
    refs = list(refs)

    def pop(count):
        taken = refs[:count]
        del refs[:count]
        return taken

    expr_ref, gene_masks_ref, segments_ref, mean_ref, logvar_ref = pop(5)
    vec_refs = dict(zip(VECTORS, pop(n_vec)))
    table_ref, target_ref, noise_ref = pop(3)
    w_gene, w_qkv, w_out, w_up, w_down, w_enc, w_lat, w_dec = pop(8)
    (input_ref,) = pop(1)
    out_refs = dict(zip([name for name, _, _ in layers], pop(len(layers))))
    (tail_ref,) = pop(1)
    ring, masks_own, masks_all, table, target_in, noise_in, x1_out, x1_in = pop(8)
    kv_all, query_own, probs, dkv_part, dkv_in, dx_out, dx_in = pop(7)
    hats, scales, befores, mixed_grad, input_grad = pop(5)
    a_src, a_all, b_all, v_src, v_all, near, far, v_near, v_far = pop(9)
    ring_sem, hand_send, hand_recv, hand_local, pair_send, pair_recv = pop(6)
    one_sem, a_send, a_recv, a_local, v_send, v_recv, b_send, b_recv, c_send, c_recv, o_sem = pop(11)

    d = lax.axis_index("dp")
    z = lax.axis_index("phase")
    base = (d // GROUP) * GROUP
    r = d % GROUP
    core, cx, cy = r % 2, (r // 2) % 2, r // 4
    partner = d + 1 - 2 * core
    owner = d - core + z // 2
    own = core == z // 2
    rc, rx, ry = r + 1 - 2 * core, r + 2 - 4 * cx, r + 4 - 8 * cy
    rxc, ryc = rx + 1 - 2 * core, ry + 1 - 2 * core
    rd = rx + 4 - 8 * cy
    rdc = rd + 1 - 2 * core
    middle = (z % 3) != 0
    inward = z + 1 - 2 * (z // 2)
    outward = z - 1 + 2 * (z // 2)
    a_off, b_off, items, _, _, _ = grad_plan(layers)
    blocks = len(BLOCKS)
    shares = {name: share for name, share, _ in layers}
    index_of = {name: index for index, (name, _, _) in enumerate(layers)}
    seqs, rows, genes = expr_ref.shape
    tokens = seqs * rows
    width = table.shape[1]
    hidden = w_up.shape[1]
    length = segments_ref.shape[1]
    wide = WIDE

    barrier = pltpu.get_barrier_semaphore()

    def greet(to):
        pl.semaphore_signal(barrier, inc=1, device_id=to, device_id_type=MESH)

    for step in range(1, GROUP):
        greet((base + (r + step) % GROUP, z))
    greet((d, inward))

    @pl.when(middle)
    def _():
        greet((d, outward))

    for i in range(2):

        @pl.when(jnp.logical_not(own & (z % 2 == i)))
        def _():
            greet((owner, 2 * core + i))

    def barrier_wait():
        pl.semaphore_wait(barrier, GROUP + 1 + (z % 3 + 1) // 2 + (core + z // 2) % 2)

    def remote(src, dst, send, recv, to):
        return pltpu.make_async_remote_copy(
            src_ref=src,
            dst_ref=dst,
            send_sem=send,
            recv_sem=recv,
            device_id=to,
            device_id_type=MESH,
        )

    def columns_of(name):
        return pl.ds(a_off[name], -(-shares[name] // PIECE) * PIECE)

    def a_copy(name, step, slot):
        at, index, to = columns_of(name), index_of[name], (r + step) % GROUP
        return remote(
            a_src.at[to, :, at],
            a_all.at[slot, :, at],
            a_send.at[index, step],
            a_recv.at[index, step],
            (base + to, z),
        )

    def a_own(name):
        at = columns_of(name)
        return pltpu.make_async_copy(
            a_src.at[r, :, at], a_all.at[r, :, at], a_local.at[index_of[name]]
        )

    def send_a(name):
        for step in range(1, GROUP):
            a_copy(name, step, r).start()
        a_own(name).start()

    def send_a_to(name, to):
        step = (to - r + GROUP) % GROUP

        @pl.when(r == to)
        def _():
            a_own(name).start()

        @pl.when(r != to)
        def _():
            a_copy(name, step, r).start()

    def send_late(index):
        send_a(layers[index][0])

    def arrive_a(name):
        a_own(name).wait()
        for step in range(1, GROUP):
            a_copy(name, step, (r + GROUP - step) % GROUP).wait_recv()

    def v_copy(step, slot):
        to = (r + step) % GROUP
        return remote(
            v_src.at[to], v_all.at[slot], v_send.at[step], v_recv.at[step], (base + to, z)
        )

    own_sums = pltpu.make_async_copy(v_src.at[r], v_all.at[r], one_sem.at[0])

    comes = (rx, ry, rc, rxc, ryc, rd, rd, rdc, rdc)
    goes = (r, r, r, rx, ry, rx, ry, rd, rd)

    def b_copy(kind, block, source):
        name, first, size, _ = BLOCKS[block]
        col = b_off[name] + first
        if kind >= 5:
            size //= 2
        if kind in (6, 8):
            col += size
        to = (rx, ry, rc, rc, rc, ry, rx, rc, rc)[kind]
        view = b_all.at[source, :, pl.ds(col, size)]
        return remote(view, view, b_send.at[block, kind], b_recv.at[block, kind], (base + to, z))

    def b_start(kind, block):
        b_copy(kind, block, goes[kind]).start()

    def b_arrive(kind, block):
        b_copy(kind, block, comes[kind]).wait_recv()

    vectors = len(items)

    def place_of(ref, v_ref, index):
        if index == vectors:
            return v_ref
        _, _, count, col, size, row = items[index]
        return ref.at[pl.ds(row, count), pl.ds(col % WIDE, size)]

    def to_middle(index, to):
        ref = place_of(near, v_near, index)
        return remote(ref, ref, c_send.at[index, 0], c_recv.at[index, 0], (d, to))

    def across(index):
        src, dst = place_of(near, v_near, index), place_of(far, v_far, index)
        return remote(src, dst, c_send.at[index, 1], c_recv.at[index, 1], (d, inward))

    def to_end(index, to):
        ref = place_of(far, v_far, index)
        return remote(ref, ref, c_send.at[index, 0], c_recv.at[index, 0], (d, to))

    def result(index, ref, v_ref):
        src = place_of(ref, v_ref, index)
        if index == vectors:
            return pltpu.make_async_copy(src, tail_ref, o_sem.at[index])
        block, start, count, col, size, _ = items[index]
        to = out_refs[BLOCKS[block][0]].at[pl.ds(start, count), pl.ds(col, size)]
        return pltpu.make_async_copy(src, to, o_sem.at[index])

    def product(index):
        if index == vectors:
            return jnp.sum(v_all[...], axis=0)
        block, start, count, col, size, _ = items[index]
        name = BLOCKS[block][0]
        a_at = a_off[name] + start
        b_at = b_off[name] + col
        left = a_all[:, :, a_at : a_at + PIECE].reshape(-1, PIECE)
        right = b_all[:, :, b_at : b_at + size].reshape(-1, size)
        value = mm_first(left, right)
        if count < PIECE:
            value = jnp.where(r % 2 == 1, value[count : 2 * count], value[:count])
        return value

    def end_push(index):
        @pl.when(jnp.logical_not(middle))
        def _():
            ref = place_of(near, v_near, index)
            ref[...] = product(index).astype(ref.dtype)
            to_middle(index, inward).start()

    def middle_join(index):
        @pl.when(middle)
        def _():
            value = product(index)
            to_middle(index, inward).wait_recv()
            ref = place_of(near, v_near, index)
            ref[...] = (value + ref[...].astype(full)).astype(ref.dtype)
            across(index).start()

    def middle_total(index):
        @pl.when(middle)
        def _():
            across(index).wait_recv()
            mine, theirs = place_of(near, v_near, index), place_of(far, v_far, index)
            both = mine[...].astype(full) + theirs[...].astype(full)
            theirs[...] = both.astype(theirs.dtype)
            to_end(index, outward).start()
            result(index, far, v_far).start()

    def end_land(index):
        @pl.when(jnp.logical_not(middle))
        def _():
            to_end(index, inward).wait_recv()
            result(index, far, v_far).start()

    arrived = set()

    def get(block):
        if block == blocks:
            own_sums.wait()
            for step in range(1, GROUP):
                v_copy(step, (r + GROUP - step) % GROUP).wait_recv()
            return
        for kind in (2, 3, 4, 7, 8):
            b_arrive(kind, block)
        name = BLOCKS[block][0]
        if name not in arrived:
            arrived.add(name)
            arrive_a(name)

    table_copy = pltpu.make_async_copy(
        table_ref.at[pl.ds(z * rows, rows), :], table, one_sem.at[1]
    )
    input_copy = pltpu.make_async_copy(input_grad, input_ref, one_sem.at[2])
    pair_local = one_sem.at[3]
    table_copy.start()

    def rows_work():
        stream = []
        for j in range(genes // wide):
            stream.append(w_gene.at[pl.ds(j * wide, wide), :])
        for j in (1, 2, 0):
            stream.append(w_qkv.at[:, pl.ds(j * wide, wide)])
        stream.append(w_out)
        for j in range(hidden // wide):
            stream.append(w_up.at[:, pl.ds(j * wide, wide)])
            stream.append(w_down.at[pl.ds(j * wide, wide), :])
        stream.append(w_enc)
        stream.append(w_lat)
        for j in range(genes // wide):
            stream.append(w_dec.at[:, pl.ds(j * wide, wide)])
        stream.append(w_lat)
        stream.append(w_enc)
        for j in range(hidden // wide):
            stream.append(w_down.at[pl.ds(j * wide, wide), :])
            stream.append(w_up.at[:, pl.ds(j * wide, wide)])
        stream.append(w_out)
        for j in range(3):
            stream.append(w_qkv.at[:, pl.ds(j * wide, wide)])
        for j in range(genes // wide):
            stream.append(w_gene.at[pl.ds(j * wide, wide), :])

        def load(k):
            depth = stream[k].shape[0]
            return pltpu.make_async_copy(
                stream[k], ring.at[k % SLOTS, pl.ds(0, depth), :], ring_sem.at[k % SLOTS]
            )

        def fetch(k):
            if k < len(stream):
                load(k).start()

        place = [0]

        def take():
            k = place[0]
            place[0] += 1
            load(k).wait()
            return k

        def block(k):
            return ring[k % SLOTS, : stream[k].shape[0], :]

        for k in range(SLOTS):
            fetch(k)

        def hand(which, src, dst, i):
            return pltpu.make_async_remote_copy(
                src_ref=src.at[i],
                dst_ref=dst.at[z % 2],
                send_sem=hand_send.at[which, i],
                recv_sem=hand_recv.at[which, z % 2],
                device_id=(owner, 2 * core + i),
                device_id_type=MESH,
            )

        def hand_here(which, src, dst, i):
            return pltpu.make_async_copy(src.at[i], dst.at[i], hand_local.at[which])

        def hand_start(which, src, dst):
            for i in range(2):
                here = own & (z % 2 == i)

                @pl.when(here)
                def _():
                    hand_here(which, src, dst, i).start()

                @pl.when(jnp.logical_not(here))
                def _():
                    hand(which, src, dst, i).start()

        def hand_arrive(which, src, dst):
            for i in range(2):
                here = own & (z % 2 == i)

                @pl.when(here)
                def _():
                    hand_here(which, src, dst, i).wait()

                @pl.when(jnp.logical_not(here))
                def _():
                    pltpu.make_async_remote_copy(
                        src_ref=src.at[i],
                        dst_ref=dst.at[i],
                        send_sem=hand_send.at[which, i],
                        recv_sem=hand_recv.at[which, i],
                        device_id=(owner, 2 * core + i),
                        device_id_type=MESH,
                    ).wait_recv()

        def hand_sent(which, src, dst):
            for i in range(2):
                @pl.when(jnp.logical_not(own & (z % 2 == i)))
                def _():
                    hand(which, src, dst, i).wait_send()

        def pair(which, src, dst):
            return pltpu.make_async_remote_copy(
                src_ref=src,
                dst_ref=dst,
                send_sem=pair_send.at[which],
                recv_sem=pair_recv.at[which],
                device_id=(partner, z),
                device_id_type=MESH,
            )

        masks_own[:seqs, :genes] = gene_masks_ref[...].astype(full)
        masks_own[:seqs, genes : genes + length] = segments_ref[...].astype(full)
        own_masks = pltpu.make_async_copy(masks_own, masks_all.at[core], pair_local)
        own_masks.start()

        def vec(name, j=0):
            return vec_refs[name][:, j * wide : (j + 1) * wide]

        def put_a(name, values):
            off, share = a_off[name], shares[name]
            step = max(share, PIECE)
            for o in range(GROUP):
                start = o * share // step * step
                a_src[o, :, off : off + step] = values[:, start : start + step]

        def put_b(name, j, values):
            at = b_off[name] + j * wide
            b_all[r, :, at : at + wide] = values

        def put_sum(name, values, j=0):
            each = SUM_LANES[name]
            for o in range(values.shape[1] // 128):
                at = j * wide + o * 128
                to, row = at // (128 * each), SUM_AT[name] + at // 128 % each
                v_src[to, row : row + 1, :] = values[:, o * 128 : o * 128 + 128]

        def normalize(index, values, gain, shift):
            hat, scale = normed(values)
            hats[index] = hat
            scales[index] = jnp.broadcast_to(scale, scales.shape[1:])
            return hat * vec(gain) + vec(shift)

        def normalize_back(index, grad, gain, gain_name, shift_name):
            hat, scale = hats[index], scales[index, :, :1]
            put_sum(gain_name, jnp.sum(grad * hat, axis=0, keepdims=True))
            put_sum(shift_name, jnp.sum(grad, axis=0, keepdims=True))
            return normed_back(grad, hat, scale, vec(gain))

        keep = 1.0 - masks_own[:seqs, :genes]
        keep = jnp.concatenate(
            [jnp.broadcast_to(keep[s : s + 1], (rows, genes)) for s in range(seqs)], axis=0
        )
        masked = (expr_ref[...].reshape(tokens, genes).astype(full) * keep).astype(low)
        put_a(GENE, masked)
        table_copy.wait()
        embedded = jnp.concatenate([table[...]] * seqs, axis=0)
        for j in range(genes // wide):
            k = take()
            embedded += mm(masked[:, j * wide : (j + 1) * wide], block(k))
            fetch(k + SLOTS)
        x1_out[...] = (
            normalize(0, embedded, EMB_GAIN, EMB_SHIFT).astype(low).reshape(seqs, rows, width)
        )
        barrier_wait()
        hand_start(0, x1_out, x1_in)
        pair(0, masks_own, masks_all.at[core]).start()
        send_a(GENE)
        hand_start(1, noise_ref, noise_in)
        hand_start(2, target_ref, target_in)
        yield
        own_masks.wait()
        pair(0, masks_own, masks_all.at[1 - core]).wait_recv()
        odd = z % 2 == 1
        both_masks = masks_all[pl.ds(z // 2, 1)][0]
        mask_row = jnp.where(odd, both_masks[1:2], both_masks[0:1])
        gene_row = mask_row[:, :genes]
        segments = mask_row[:, genes : genes + length]
        place_q = lax.broadcasted_iota(jnp.int32, (tokens, length), 0) + core * tokens
        place_k = lax.broadcasted_iota(jnp.int32, (tokens, length), 1)
        own_segments = jnp.sum(
            jnp.where(place_q == place_k, segments, 0.0), axis=-1, keepdims=True
        )
        same = own_segments == segments
        same = jnp.concatenate([same.astype(full)] * 2, axis=0) > 0.5

        hand_arrive(0, x1_out, x1_in)
        x1 = x1_in[...].reshape(tokens, width).astype(full)
        h1 = normalize(1, x1, ATTN_GAIN, ATTN_SHIFT).astype(low)
        put_a(QKV, h1)
        send_a(QKV)
        head = width // HEADS
        scale = head**-0.5
        for j in (1, 2):
            k = take()
            kv_all[core, :, (j - 1) * wide : j * wide] = (
                mm(h1, block(k)) + vec(B_QKV, j)
            ).astype(low)
            fetch(k + SLOTS)
        pair(1, kv_all.at[core], kv_all.at[core]).start()
        k = take()
        query_own[...] = (mm(h1, block(k)) + vec(B_QKV, 0)).astype(low)
        fetch(k + SLOTS)
        yield
        pair(1, kv_all.at[core], kv_all.at[1 - core]).wait_recv()

        lanes = lax.broadcasted_iota(jnp.int32, (tokens, 2 * head), 1)
        first = lanes < head
        pairs = HEADS // 2

        def two(values):
            none = jnp.zeros_like(values)
            return jnp.concatenate([jnp.where(first, values, none), jnp.where(first, none, values)], axis=0)

        def one(values):
            return jnp.where(first, values[:tokens], values[tokens:])

        def columns(p):
            return pl.ds(pl.multiple_of(p * 2 * head, 2 * head), 2 * head)

        def keys_of(p):
            return kv_all[:, :, columns(p)].reshape(length, 2 * head)

        def values_of(p):
            at = pl.ds(pl.multiple_of(width + p * 2 * head, 2 * head), 2 * head)
            return kv_all[:, :, at].reshape(length, 2 * head)

        def attend(p, carry):
            scores = mm_last(two(query_own[:, columns(p)]), keys_of(p)) * scale
            scores = jnp.where(same, scores, mask_fill)
            shifted = jnp.exp(scores - jnp.max(scores, axis=-1, keepdims=True))
            prob = shifted / jnp.sum(shifted, axis=-1, keepdims=True)
            probs[p] = prob
            att = one(mm(prob.astype(low), values_of(p))).astype(low)
            a_src[p, :, a_off[OUT] : a_off[OUT] + 2 * head] = att
            return carry

        lax.fori_loop(0, pairs, attend, 0)
        yield
        attended = jnp.concatenate(
            [a_src[o, :, a_off[OUT] : a_off[OUT] + 2 * head] for o in range(pairs)], axis=1
        )
        k = take()
        mixed = x1 + (mm(attended, block(k)) + vec(B_OUT))
        fetch(k + SLOTS)
        h2 = normalize(2, mixed, FFN_GAIN, FFN_SHIFT).astype(low)
        put_a(UP, h2)
        yield
        x2 = mixed + vec(B_DOWN)
        per_owner = shares[DOWN]
        for j in range(hidden // wide):
            k = take()
            before = mm(h2, block(k)) + vec(B_UP, j)
            fetch(k + SLOTS)
            befores[:, j * wide : (j + 1) * wide] = before
            active = gelu(before).astype(low)
            for o in range(wide // per_owner):
                a_src[
                    j * (wide // per_owner) + o, :, a_off[DOWN] : a_off[DOWN] + per_owner
                ] = active[:, o * per_owner : (o + 1) * per_owner]
            k = take()
            x2 += mm(active, block(k))
            fetch(k + SLOTS)
            for o in range(wide // per_owner):
                send_a_to(DOWN, j * (wide // per_owner) + o)
            yield
        x2 = x2.astype(low).astype(full)
        h3 = normalize(3, x2, BOT_GAIN, BOT_SHIFT).astype(low)
        put_a(ENC, h3)
        k_enc = take()
        moments = mm(h3, block(k_enc)) + vec(B_ENC)
        latents = width // 2
        logvar = moments[:, latents:]
        hand_arrive(1, noise_ref, noise_in)
        swing = jnp.exp(0.5 * logvar) * noise_in[...].reshape(tokens, latents).astype(full)
        latent = moments[:, :latents] + swing
        latent_low = latent.astype(low)
        put_a(LAT, latent_low)
        fetch(k_enc + SLOTS)
        k_lat = take()
        lat_before = mm(latent_low, block(k_lat)) + vec(B_LAT)
        fetch(k_lat + SLOTS)
        x3 = gelu(lat_before).astype(low).astype(full)
        h4 = normalize(4, x3, DEC_GAIN, DEC_SHIFT).astype(low)
        put_a(DEC, h4)
        send_a(DEC)
        yield
        hand_arrive(2, target_ref, target_in)

        grad = jnp.zeros((tokens, width), full)
        for j in range(genes // wide):
            k = take()
            at = slice(j * wide, (j + 1) * wide)
            predicted = mm(h4, block(k)) + vec(B_DEC, j)
            wanted = target_in[:, :, at].reshape(tokens, wide).astype(full)
            d_pred = (gene_row[:, at] * (predicted - wanted)).astype(low)
            put_b(DEC, j, d_pred)
            put_sum(B_DEC, column_sums(d_pred), j)
            grad += mm_last(d_pred, block(k))
            fetch(k + SLOTS)
            yield
        d_x3 = normalize_back(4, grad, DEC_GAIN, DEC_GAIN, DEC_SHIFT).astype(low).astype(full)
        d_lat = (gelu_slope(lat_before) * d_x3).astype(low)
        put_b(LAT, 0, d_lat)
        put_sum(B_LAT, column_sums(d_lat))
        k = take()
        d_latent = mm_last(d_lat, block(k))
        fetch(k + SLOTS)
        yield

        inverse = jnp.exp(-logvar_ref[...])
        volume = jnp.sum(logvar_ref[...], axis=-1, keepdims=True)
        count = mean_ref.shape[0]
        scaled = []
        for c in range(count):
            offset = latent - mean_ref[c : c + 1, :]
            quad = jnp.sum(offset * offset * inverse[c : c + 1], axis=-1, keepdims=True)
            scaled.append(-0.5 * (quad + volume[c : c + 1]))
        highest = functools.reduce(jnp.maximum, scaled)
        shares_c = [jnp.exp(s - highest) for s in scaled]
        whole = functools.reduce(jnp.add, shares_c)
        parts = [part / whole for part in shares_c]
        for c in range(count):
            pull = (latent - mean_ref[c : c + 1, :]) * inverse[c : c + 1]
            d_latent += parts[c] * pull
        d_moments = jnp.concatenate([d_latent, 0.5 * d_latent * swing - 0.5], axis=1).astype(low)
        put_b(ENC, 0, d_moments)
        put_sum(B_ENC, column_sums(d_moments))
        yield
        k = take()
        grad = mm_last(d_moments, block(k))
        fetch(k + SLOTS)
        g = normalize_back(3, grad, BOT_GAIN, BOT_GAIN, BOT_SHIFT).astype(low)
        put_b(DOWN, 0, g)
        put_sum(B_DOWN, column_sums(g))
        yield
        for c in range(count):
            offset = latent - mean_ref[c : c + 1, :]
            weighted = parts[c] * (offset * inverse[c : c + 1])
            mean_grad = -jnp.sum(weighted, axis=0, keepdims=True)
            logvar_grad = 0.5 * jnp.sum(parts[c] - weighted * offset, axis=0, keepdims=True)
            for o in range(GROUP):
                at = slice(o // 2 * 128, o // 2 * 128 + 128)
                row = SUM_AT[COMP_MEAN] + c
                v_src[o, row : row + 1, :] = mean_grad[:, at]
                row = SUM_AT[COMP_LOGVAR] + c
                v_src[o, row : row + 1, :] = logvar_grad[:, at]
        yield
        grad = jnp.zeros((tokens, width), full)
        for j in range(hidden // wide):
            k = take()
            d_active = mm_last(g, block(k))
            fetch(k + SLOTS)
            slope = gelu_slope(befores[:, j * wide : (j + 1) * wide])
            d_before = (slope * d_active).astype(low)
            put_b(UP, j, d_before)
            put_sum(B_UP, column_sums(d_before), j)
            k = take()
            grad += mm_last(d_before, block(k))
            fetch(k + SLOTS)
            yield
        d_mixed = g.astype(full) + normalize_back(2, grad, FFN_GAIN, FFN_GAIN, FFN_SHIFT)
        mixed_grad[...] = d_mixed
        da = d_mixed.astype(low)
        put_b(OUT, 0, da)
        put_sum(B_OUT, column_sums(da))
        k = take()
        x1_in[...] = mm_last(da, block(k)).astype(low).reshape(seqs, rows, width)
        fetch(k + SLOTS)
        yield
        q_at = b_off[QKV]

        def attend_back(p, carry):
            query = two(query_own[:, columns(p)])
            d_att = two(x1_in[:, :, columns(p)].reshape(tokens, 2 * head))
            prob = probs[p]
            keys = keys_of(p)
            d_value = mm_first(prob.astype(low), d_att)
            d_prob = mm_last(d_att, values_of(p))
            d_score = prob * (d_prob - jnp.sum(prob * d_prob, axis=-1, keepdims=True))
            d_score = d_score.astype(low)
            d_query = one(mm(d_score, keys)) * scale
            d_key = mm_first(d_score, query) * scale
            to = pl.ds(pl.multiple_of(q_at + p * 2 * head, 2 * head), 2 * head)
            b_all[r, :, to] = d_query.astype(low)
            dkv_part[:, :, columns(p)] = d_key.reshape(2, tokens, 2 * head)
            at = pl.ds(pl.multiple_of(width + p * 2 * head, 2 * head), 2 * head)
            dkv_part[:, :, at] = d_value.reshape(2, tokens, 2 * head)
            return carry

        lax.fori_loop(0, pairs // 2, attend_back, 0)
        yield
        lax.fori_loop(pairs // 2, pairs, attend_back, 0)
        pair(2, dkv_part.at[1 - core], dkv_in).start()
        yield
        d_query = b_all[r, :, q_at : q_at + wide]
        put_sum(B_QUERY, column_sums(d_query))
        k = take()
        grad = mm_last(d_query, block(k))
        fetch(k + SLOTS)
        pair(2, dkv_part.at[1 - core], dkv_in).wait_recv()
        for j in (1, 2):
            at = slice((j - 1) * wide, j * wide)
            d_part = (dkv_part[core, :, at] + dkv_in[:, at]).astype(low)
            put_b(QKV, j, d_part)
            if j == 2:
                put_sum(B_VALUE, column_sums(d_part))
            k = take()
            grad += mm_last(d_part, block(k))
            fetch(k + SLOTS)
        d_x1 = mixed_grad[...] + normalize_back(1, grad, ATTN_GAIN, ATTN_GAIN, ATTN_SHIFT)
        dx_out[...] = d_x1.astype(low).reshape(seqs, rows, width)
        hand_start(3, dx_out, dx_in)
        yield
        hand_arrive(3, dx_out, dx_in)
        d_x1 = dx_in[...].reshape(tokens, width).astype(full)
        d_embedded = normalize_back(0, d_x1, EMB_GAIN, EMB_GAIN, EMB_SHIFT).astype(low)
        put_b(GENE, 0, d_embedded)
        for j in range(genes // wide):
            k = take()
            at = slice(j * wide, (j + 1) * wide)
            input_grad[:, at] = mm_last(d_embedded, block(k)) * jnp.concatenate(
                [
                    jnp.broadcast_to(1.0 - masks_own[s : s + 1, at], (rows, wide))
                    for s in range(seqs)
                ],
                axis=0,
            )
        input_copy.start()
        for step in range(1, GROUP):
            v_copy(step, r).start()
        own_sums.start()
        yield
        input_copy.wait()
        hand_sent(0, x1_out, x1_in)
        hand_sent(1, noise_ref, noise_in)
        hand_sent(2, target_ref, target_in)
        hand_sent(3, dx_out, dx_in)
        pair(0, masks_own, masks_all.at[core]).wait_send()
        pair(1, kv_all.at[core], kv_all.at[core]).wait_send()
        pair(2, dkv_part.at[1 - core], dkv_in).wait_send()


    work = rows_work()
    for code in ORDER:
        kind, index = code // 100, code % 100
        if kind == 0:
            next(work)
        elif kind == 1:
            for way in (0, 1, 2):
                b_start(way, index)
        elif kind == 2:
            b_arrive(0, index)
            b_start(5, index)
            b_start(3, index)
            b_arrive(1, index)
            b_start(6, index)
            b_start(4, index)
        elif kind == 3:
            b_arrive(5, index)
            b_start(7, index)
            b_arrive(6, index)
            b_start(8, index)
        else:
            (get, end_push, middle_join, middle_total, end_land, send_late)[kind - 4](index)
    next(work, None)
    for block in range(blocks):
        for kind in range(9):
            b_copy(kind, block, goes[kind]).wait_send()
    for step in range(1, GROUP):
        v_copy(step, r).wait_send()
        for name, _, _ in layers:
            a_copy(name, step, r).wait_send()
    for index in range(len(items) + 1):
        to_middle(index, inward).wait_send()
        result(index, far, v_far).wait()

        @pl.when(middle)
        def _():
            across(index).wait_send()


SUM_LANES = dict(SUMS)


def finish(layers, *refs):
    refs = list(refs)
    count = len(layers)
    low_refs, refs = refs[:count], refs[count:]
    input_ref, tail_ref = refs[:2]
    refs = refs[2:]
    full_refs, refs = refs[:count], refs[count:]
    input_out = refs[0]
    sum_refs = dict(zip([name for name, _ in SUMS], refs[1 : 1 + len(SUMS)]))
    refs = refs[1 + len(SUMS) :]
    low_bufs, full_bufs = refs[:count], refs[count : 2 * count]
    input_buf, in_sem, out_sem, move_sem = refs[2 * count :]
    move_in = pltpu.make_async_copy(input_ref, input_buf, move_sem.at[0])
    move_out = pltpu.make_async_copy(input_buf, input_out, move_sem.at[1])
    ins = [
        pltpu.make_async_copy(src, dst, in_sem.at[i])
        for i, (src, dst) in enumerate(zip(low_refs, low_bufs))
    ]
    outs = [
        pltpu.make_async_copy(src, dst, out_sem.at[i])
        for i, (src, dst) in enumerate(zip(full_bufs, full_refs))
    ]
    move_in.start()
    for copy in ins:
        copy.start()
    odd = lax.axis_index("dp") % 2 == 1
    for name, rows in SUMS:
        at = SUM_AT[name]
        if name in (COMP_MEAN, COMP_LOGVAR):
            both = tail_ref[at : at + rows, :]
            sum_refs[name][...] = jnp.where(odd, both[:, 64:], both[:, :64])
        else:
            for row in range(rows):
                sum_refs[name][:, row * 128 : row * 128 + 128] = tail_ref[at + row : at + row + 1, :]
    move_in.wait()
    move_out.start()
    for i in range(count):
        ins[i].wait()
        full_bufs[i][...] = low_bufs[i][...].astype(jnp.float32)
        outs[i].start()
    for copy in outs:
        copy.wait()
    move_out.wait()


def positions(length, width):
    frequency = np.exp(np.arange(width // 2, dtype=np.float32) * np.float32(-2.0 * math.log(10000.0) / width))
    angles = np.arange(length, dtype=np.float32)[:, None] * frequency[None, :]
    return np.stack([np.sin(angles), np.cos(angles)], axis=-1).reshape(length, width)


def body(expression, targets, noise, gene_masks, segment_ids, w_gene, emb_gain, emb_shift, attn_gain, attn_shift, w_qkv, b_qkv, w_out, b_out, ffn_gain, ffn_shift, w_up, b_up, w_down, b_down, bot_gain, bot_shift, w_enc, b_enc, comp_mean, comp_logvar, w_lat, b_lat, dec_gain, dec_shift, w_dec, b_dec):
    low, full = jnp.bfloat16, jnp.float32
    seqs, rows, genes = expression.shape
    width = w_gene.shape[1]
    hidden = w_up.shape[1]
    latents = noise.shape[2]
    length = segment_ids.shape[1]
    tokens = seqs * rows
    given = {
        EMB_GAIN: emb_gain,
        EMB_SHIFT: emb_shift,
        ATTN_GAIN: attn_gain,
        ATTN_SHIFT: attn_shift,
        B_QKV: b_qkv,
        B_OUT: b_out,
        FFN_GAIN: ffn_gain,
        FFN_SHIFT: ffn_shift,
        B_UP: b_up,
        B_DOWN: b_down,
        BOT_GAIN: bot_gain,
        BOT_SHIFT: bot_shift,
        B_ENC: b_enc,
        B_LAT: b_lat,
        DEC_GAIN: dec_gain,
        DEC_SHIFT: dec_shift,
        B_DEC: b_dec,
    }
    weights = {
        GENE: w_gene,
        QKV: w_qkv,
        OUT: w_out,
        UP: w_up,
        DOWN: w_down,
        ENC: w_enc,
        LAT: w_lat,
        DEC: w_dec,
    }
    layers = [
        (name, weights[name].shape[0] // GROUP, weights[name].shape[1]) for name in LAYERS
    ]
    _, _, items, rows_all, a_cols, b_cols = grad_plan(layers)
    vmem = pl.BlockSpec(memory_space=pltpu.VMEM)
    anywhere = pl.BlockSpec(memory_space=pl.ANY)
    dma = pltpu.SemaphoreType.DMA
    mask_lanes = genes + length + -length % 128
    share_shapes = [(share, columns) for _, share, columns in layers]
    chunks = len(items) + 1
    results = pl.pallas_call(
        functools.partial(everything, layers, len(VECTORS)),
        out_shape=(jax.ShapeDtypeStruct((tokens, genes), full),)
        + tuple(jax.ShapeDtypeStruct(shape, low) for shape in share_shapes)
        + (jax.ShapeDtypeStruct((SUM_ROWS, 128), full),),
        in_specs=[vmem] * (5 + len(VECTORS)) + [anywhere] * 11,
        out_specs=(anywhere,) * (2 + len(layers)),
        scratch_shapes=[
            pltpu.VMEM((SLOTS, WIDE, WIDE), low),
            pltpu.VMEM((8, mask_lanes), full),
            pltpu.VMEM((2, 8, mask_lanes), full),
            pltpu.VMEM((rows, width), full),
            pltpu.VMEM((2, rows, genes), low),
            pltpu.VMEM((2, rows, latents), low),
            pltpu.VMEM((2, rows, width), low),
            pltpu.VMEM((2, rows, width), low),
            pltpu.VMEM((2, tokens, 2 * width), low),
            pltpu.VMEM((tokens, width), low),
            pltpu.VMEM((HEADS // 2, 2 * tokens, 2 * tokens), full),
            pltpu.VMEM((2, tokens, 2 * width), full),
            pltpu.VMEM((tokens, 2 * width), full),
            pltpu.VMEM((2, rows, width), low),
            pltpu.VMEM((2, rows, width), low),
            pltpu.VMEM((5, tokens, width), full),
            pltpu.VMEM((5, tokens, 128), full),
            pltpu.VMEM((tokens, hidden), full),
            pltpu.VMEM((tokens, width), full),
            pltpu.VMEM((tokens, genes), full),
            pltpu.VMEM((GROUP, tokens, a_cols), low),
            pltpu.VMEM((GROUP, tokens, a_cols), low),
            pltpu.VMEM((GROUP, tokens, b_cols), low),
            pltpu.VMEM((GROUP, SUM_ROWS, 128), full),
            pltpu.VMEM((GROUP, SUM_ROWS, 128), full),
            pltpu.VMEM((rows_all, WIDE), low),
            pltpu.VMEM((rows_all, WIDE), low),
            pltpu.VMEM((SUM_ROWS, 128), full),
            pltpu.VMEM((SUM_ROWS, 128), full),
            dma((SLOTS,)),
            dma((4, 2)),
            dma((4, 2)),
            dma((4,)),
            dma((3,)),
            dma((3,)),
            dma((4,)),
            dma((len(layers), GROUP)),
            dma((len(layers), GROUP)),
            dma((len(layers),)),
            dma((GROUP,)),
            dma((GROUP,)),
            dma((len(BLOCKS), 9)),
            dma((len(BLOCKS), 9)),
            dma((chunks, 2)),
            dma((chunks, 2)),
            dma((chunks,)),
        ],
        compiler_params=pltpu.CompilerParams(
            collective_id=0, has_side_effects=True, vmem_limit_bytes=63 * 1024 * 1024
        ),
    )(
        expression,
        gene_masks,
        segment_ids,
        comp_mean,
        comp_logvar,
        *[given[name].reshape(1, -1) for name in VECTORS],
        positions(length, width),
        targets,
        noise,
        *weights.values(),
    )
    input_grad, sums, tail = results[0], results[1:-1], results[-1]

    def sum_shape(name, count):
        return (count, 64) if name in (COMP_MEAN, COMP_LOGVAR) else (1, count * 128)

    finished = pl.pallas_call(
        functools.partial(finish, layers),
        out_shape=tuple(jax.ShapeDtypeStruct(shape, full) for shape in share_shapes)
        + (jax.ShapeDtypeStruct((tokens, genes), full),)
        + tuple(jax.ShapeDtypeStruct(sum_shape(name, count), full) for name, count in SUMS),
        in_specs=[anywhere] * (len(layers) + 1) + [vmem],
        out_specs=(anywhere,) * (len(layers) + 1) + (vmem,) * len(SUMS),
        scratch_shapes=[pltpu.VMEM(shape, low) for shape in share_shapes]
        + [pltpu.VMEM(shape, full) for shape in share_shapes]
        + [pltpu.VMEM((tokens, genes), full), dma((len(layers),)), dma((len(layers),)), dma((2,))],
        compiler_params=pltpu.CompilerParams(vmem_limit_bytes=63 * 1024 * 1024),
    )(*sums, input_grad, tail)

    groups = lax.axis_size("dp") // GROUP
    d = lax.axis_index("dp")

    def shared_out(values, axis):
        if groups == 1:
            return values
        across = [[g * GROUP + r for g in range(groups)] for r in range(GROUP)]
        within = [[g * GROUP + r for r in range(GROUP)] for g in range(groups)]
        values = lax.psum(values, "dp", axis_index_groups=across)
        values = lax.all_gather(values, "dp", axis=axis, tiled=True, axis_index_groups=within)
        size = values.shape[axis] // (groups * GROUP)
        return lax.dynamic_slice_in_dim(values, d * size, size, axis=axis)

    grads = {}
    for name, values in zip(LAYERS, finished):
        grads[name] = shared_out(values, 0)
    for (name, _), values in zip(SUMS, finished[len(layers) + 1 :]):
        if name in (COMP_MEAN, COMP_LOGVAR):
            grads[name] = shared_out(values, 1)
        else:
            grads[name] = shared_out(values.reshape(-1), 0)
    return (
        finished[len(layers)].reshape(seqs, rows, genes),
        grads[GENE],
        grads[EMB_GAIN],
        grads[EMB_SHIFT],
        grads[ATTN_GAIN],
        grads[ATTN_SHIFT],
        grads[QKV],
        grads[B_QUERY],
        grads[B_VALUE],
        grads[OUT],
        grads[B_OUT],
        grads[FFN_GAIN],
        grads[FFN_SHIFT],
        grads[UP],
        grads[B_UP],
        grads[DOWN],
        grads[B_DOWN],
        grads[BOT_GAIN],
        grads[BOT_SHIFT],
        grads[ENC],
        grads[B_ENC],
        grads[COMP_MEAN],
        grads[COMP_LOGVAR],
        grads[LAT],
        grads[B_LAT],
        grads[DEC_GAIN],
        grads[DEC_SHIFT],
        grads[DEC],
        grads[B_DEC],
    )


def solution(mesh):
    rows = P("dp", "phase", None)
    return jax.shard_map(
        body,
        mesh=mesh,
        in_specs=(rows, rows, rows, P("dp", None), P("dp", None)) + (P(),) * 27,
        out_specs=(
            rows,
            P("dp", None),
            P("dp"),
            P("dp"),
            P("dp"),
            P("dp"),
            P("dp", None),
            P("dp"),
            P("dp"),
            P("dp", None),
            P("dp"),
            P("dp"),
            P("dp"),
            P("dp", None),
            P("dp"),
            P("dp", None),
            P("dp"),
            P("dp"),
            P("dp"),
            P("dp", None),
            P("dp"),
            P(None, "dp"),
            P(None, "dp"),
            P("dp", None),
            P("dp"),
            P("dp"),
            P("dp"),
            P("dp", None),
            P("dp"),
        ),
        check_vma=False,
    )
```

```python
import functools
import math

import jax
import jax.numpy as jnp
import numpy as np
from jax import lax
from jax.experimental import pallas as pl
from jax.experimental.pallas import tpu as pltpu
from jax.sharding import PartitionSpec as P

HEADS = 16
GROUP = 8
PIECE = 128
WIDE = 1024
SLOTS = 4

norm_eps = 1e-05
mask_fill = -1000000000.0
MESH = pl.DeviceIdType.MESH

(
    DOWN,
    GENE,
    UP,
    QKV,
    DEC,
    ENC,
    OUT,
    LAT,
    EMB_GAIN,
    EMB_SHIFT,
    ATTN_GAIN,
    ATTN_SHIFT,
    B_QKV,
    B_QUERY,
    B_VALUE,
    B_OUT,
    FFN_GAIN,
    FFN_SHIFT,
    B_UP,
    B_DOWN,
    BOT_GAIN,
    BOT_SHIFT,
    B_ENC,
    COMP_MEAN,
    COMP_LOGVAR,
    B_LAT,
    DEC_GAIN,
    DEC_SHIFT,
    B_DEC,
) = range(29)


LAYERS = (DEC, DOWN, LAT, ENC, UP, OUT, QKV, GENE)
VECTORS = (
    EMB_GAIN,
    EMB_SHIFT,
    ATTN_GAIN,
    ATTN_SHIFT,
    B_QKV,
    B_OUT,
    FFN_GAIN,
    FFN_SHIFT,
    B_UP,
    B_DOWN,
    BOT_GAIN,
    BOT_SHIFT,
    B_ENC,
    B_LAT,
    DEC_GAIN,
    DEC_SHIFT,
    B_DEC,
)
SUMS = (
    (COMP_MEAN, 16),
    (COMP_LOGVAR, 16),
    (EMB_GAIN, 1),
    (EMB_SHIFT, 1),
    (ATTN_GAIN, 1),
    (ATTN_SHIFT, 1),
    (B_QUERY, 1),
    (B_VALUE, 1),
    (B_OUT, 1),
    (FFN_GAIN, 1),
    (FFN_SHIFT, 1),
    (B_UP, 4),
    (B_DOWN, 1),
    (BOT_GAIN, 1),
    (BOT_SHIFT, 1),
    (B_ENC, 1),
    (B_LAT, 1),
    (DEC_GAIN, 1),
    (DEC_SHIFT, 1),
    (B_DEC, 2),
)
SUM_AT = {name: sum(n for _, n in SUMS[:i]) for i, (name, _) in enumerate(SUMS)}
SUM_ROWS = 64


def mm(left, right):
    return jnp.dot(left, right, preferred_element_type=jnp.float32)


def mm_last(left, right):
    return lax.dot_general(
        left, right, (((1,), (1,)), ((), ())), preferred_element_type=jnp.float32
    )


def mm_first(left, right):
    return lax.dot_general(
        left, right, (((0,), (0,)), ((), ())), preferred_element_type=jnp.float32
    )


def normed(values):
    center = jnp.mean(values, axis=-1, keepdims=True)
    centered = values - center
    spread = jnp.mean(centered * centered, axis=-1, keepdims=True)
    scale = lax.rsqrt(spread + norm_eps)
    return centered * scale, scale


def normed_back(grad, hat, scale, gain):
    pulled = grad * gain
    mean = jnp.mean(pulled, axis=-1, keepdims=True)
    along = jnp.mean(pulled * hat, axis=-1, keepdims=True)
    return scale * (pulled - mean - hat * along)


def column_sums(values):
    return jnp.sum(values.astype(jnp.float32), axis=0, keepdims=True)


def gelu(values):
    return values * (0.5 * (1.0 + lax.erf(values * (0.5**0.5))))


def gelu_slope(values):
    bell = 0.5 * (1.0 + lax.erf(values * (0.5**0.5)))
    return bell + values * jnp.exp(-0.5 * values * values) * (2.0 * math.pi) ** -0.5


BLOCKS = (
    (DEC, 0, 512, 512),
    (DEC, 512, 512, 512),
    (DEC, 1024, 1024, 512),
    (DOWN, 0, 1024, 512),
    (LAT, 0, 1024, 512),
    (ENC, 0, 1024, 512),
    (UP, 0, 1024, 512),
    (UP, 1024, 1024, 512),
    (UP, 2048, 1024, 512),
    (UP, 3072, 1024, 512),
    (OUT, 0, 1024, 512),
    (QKV, 0, 1024, 512),
    (QKV, 1024, 1024, 512),
    (QKV, 2048, 1024, 512),
    (GENE, 0, 1024, 256),
)


def grad_plan(layers):
    a_off, b_off, items, place = {}, {}, [], {}
    a_at, b_at, row = 0, 0, 0
    shares = {name: share for name, share, _ in layers}
    for name, share, columns in layers:
        a_off[name], b_off[name] = a_at, b_at
        for block in range(columns // WIDE):
            for start in range(0, share, PIECE):
                place[name, block, start] = row
                row += min(PIECE, share - start)
        a_at += -(-share // PIECE) * PIECE
        b_at += columns
    for block, (name, first, columns, step) in enumerate(BLOCKS):
        for start in range(0, shares[name], PIECE):
            rows = min(PIECE, shares[name] - start)
            for col in range(first, first + columns, step):
                items.append((block, start, rows, col, step, place[name, col // WIDE, start]))
    return a_off, b_off, items, row, a_at, b_at


ORDER = (
    0, 1, 2, 3, 4, 5, 6, 7, 8, 9, 100, 101, 10, 11, 12, 13, 14, 15,
    16, 17, 18, 200, 19, 201, 103, 902, 903, 20, 300, 21, 301, 400, 500, 22, 203, 102,
    104, 401, 501, 600, 303, 403, 504, 202, 105, 904, 905, 700, 505, 601, 506, 507, 23, 204,
    106, 508, 604, 302, 701, 509, 605, 402, 510, 511, 606, 205, 415, 107, 502, 540, 704, 503,
    607, 705, 608, 304, 706, 800, 609, 404, 512, 513, 707, 801, 206, 108, 610, 708, 804, 305,
    611, 709, 805, 405, 514, 515, 602, 640, 207, 109, 710, 806, 306, 603, 711, 807, 612, 406,
    516, 613, 208, 110, 702, 808, 517, 614, 307, 703, 809, 740, 810, 712, 811, 615, 407, 713,
    802, 518, 209, 111, 519, 616, 308, 714, 803, 617, 408, 715, 812, 520, 210, 112, 521, 618,
    716, 813, 309, 619, 717, 840, 409, 522, 620, 211, 113, 718, 814, 523, 310, 621, 719, 815,
    410, 524, 622, 212, 114, 720, 816, 525, 623, 311, 721, 817, 624, 411, 722, 818, 526, 213,
    527, 625, 312, 723, 819, 412, 724, 820, 528, 626, 214, 529, 627, 313, 725, 821, 314, 628,
    413, 530, 726, 822, 414, 531, 629, 727, 823, 532, 533, 534, 728, 824, 535, 536, 630, 537,
    729, 825, 538, 539, 631, 632, 633, 730, 826, 634, 635, 731, 827, 636, 732, 828, 637, 733,
    829, 638, 734, 830, 639, 735, 831, 736, 832, 737, 833, 738, 834, 739, 835, 836, 837, 838,
    839,
)


def everything(layers, n_vec, *refs):
    low, full = jnp.bfloat16, jnp.float32
    refs = list(refs)

    def pop(count):
        taken = refs[:count]
        del refs[:count]
        return taken

    expr_ref, gene_masks_ref, segments_ref, mean_ref, logvar_ref = pop(5)
    vec_refs = dict(zip(VECTORS, pop(n_vec)))
    table_ref, target_ref, noise_ref = pop(3)
    w_gene, w_qkv, w_out, w_up, w_down, w_enc, w_lat, w_dec = pop(8)
    (input_ref,) = pop(1)
    out_refs = dict(zip([name for name, _, _ in layers], pop(len(layers))))
    (tail_ref,) = pop(1)
    ring, masks_own, masks_all, table, target_in, noise_in, x1_out, x1_in = pop(8)
    kv_all, query_own, probs, dkv_part, dkv_in, dx_out, dx_in = pop(7)
    hats, scales, befores, mixed_grad, input_grad = pop(5)
    a_src, a_all, turned, b_all, v_src, v_all, near, far, v_near, v_far = pop(10)
    ring_sem, hand_send, hand_recv, hand_local, pair_send, pair_recv = pop(6)
    one_sem, a_send, a_recv, a_local, v_send, v_recv, b_send, b_recv, c_send, c_recv, o_sem = pop(11)

    d = lax.axis_index("dp")
    z = lax.axis_index("phase")
    base = (d // GROUP) * GROUP
    r = d % GROUP
    core, cx, cy = r % 2, (r // 2) % 2, r // 4
    partner = d + 1 - 2 * core
    owner = d - core + z // 2
    own = core == z // 2
    rc, rx, ry = r + 1 - 2 * core, r + 2 - 4 * cx, r + 4 - 8 * cy
    rxc, ryc = rx + 1 - 2 * core, ry + 1 - 2 * core
    rd = rx + 4 - 8 * cy
    rdc = rd + 1 - 2 * core
    middle = (z % 3) != 0
    inward = z + 1 - 2 * (z // 2)
    outward = z - 1 + 2 * (z // 2)
    a_off, b_off, items, _, _, _ = grad_plan(layers)
    blocks = len(BLOCKS)
    shares = {name: share for name, share, _ in layers}
    index_of = {name: index for index, (name, _, _) in enumerate(layers)}
    seqs, rows, genes = expr_ref.shape
    tokens = seqs * rows
    width = table.shape[1]
    hidden = w_up.shape[1]
    length = segments_ref.shape[1]
    wide = WIDE

    barrier = pltpu.get_barrier_semaphore()

    def greet(to):
        pl.semaphore_signal(barrier, inc=1, device_id=to, device_id_type=MESH)

    for step in range(1, GROUP):
        greet((base + (r + step) % GROUP, z))
    greet((d, inward))

    @pl.when(middle)
    def _():
        greet((d, outward))

    for i in range(2):

        @pl.when(jnp.logical_not(own & (z % 2 == i)))
        def _():
            greet((owner, 2 * core + i))

    def barrier_wait():
        pl.semaphore_wait(barrier, GROUP + 1 + (z % 3 + 1) // 2 + (core + z // 2) % 2)

    def remote(src, dst, send, recv, to):
        return pltpu.make_async_remote_copy(
            src_ref=src,
            dst_ref=dst,
            send_sem=send,
            recv_sem=recv,
            device_id=to,
            device_id_type=MESH,
        )

    def columns_of(name):
        return pl.ds(a_off[name], -(-shares[name] // PIECE) * PIECE)

    def a_copy(name, step, slot):
        at, index, to = columns_of(name), index_of[name], (r + step) % GROUP
        return remote(
            a_src.at[to, :, at],
            a_all.at[slot, :, at],
            a_send.at[index, step],
            a_recv.at[index, step],
            (base + to, z),
        )

    def a_own(name):
        at = columns_of(name)
        return pltpu.make_async_copy(
            a_src.at[r, :, at], a_all.at[r, :, at], a_local.at[index_of[name]]
        )

    def send_a(name):
        for step in range(1, GROUP):
            a_copy(name, step, r).start()
        a_own(name).start()

    def send_a_to(name, to):
        step = (to - r + GROUP) % GROUP

        @pl.when(r == to)
        def _():
            a_own(name).start()

        @pl.when(r != to)
        def _():
            a_copy(name, step, r).start()

    def send_late(index):
        send_a(layers[index][0])

    def arrive_a(name):
        a_own(name).wait()
        for step in range(1, GROUP):
            a_copy(name, step, (r + GROUP - step) % GROUP).wait_recv()

    def v_copy(step, slot):
        to = (r + step) % GROUP
        return remote(
            v_src.at[to], v_all.at[slot], v_send.at[step], v_recv.at[step], (base + to, z)
        )

    own_sums = pltpu.make_async_copy(v_src.at[r], v_all.at[r], one_sem.at[0])

    comes = (rx, ry, rc, rxc, ryc, rd, rd, rdc, rdc)
    goes = (r, r, r, rx, ry, rx, ry, rd, rd)

    def b_copy(kind, block, source):
        name, first, size, _ = BLOCKS[block]
        col = b_off[name] + first
        if kind >= 5:
            size //= 2
        if kind in (6, 8):
            col += size
        to = (rx, ry, rc, rc, rc, ry, rx, rc, rc)[kind]
        view = b_all.at[source, :, pl.ds(col, size)]
        return remote(view, view, b_send.at[block, kind], b_recv.at[block, kind], (base + to, z))

    def b_start(kind, block):
        b_copy(kind, block, goes[kind]).start()

    def b_arrive(kind, block):
        b_copy(kind, block, comes[kind]).wait_recv()

    vectors = len(items)

    def place_of(ref, v_ref, index):
        if index == vectors:
            return v_ref
        _, _, count, col, size, row = items[index]
        return ref.at[pl.ds(row, count), pl.ds(col % WIDE, size)]

    def to_middle(index, to):
        ref = place_of(near, v_near, index)
        return remote(ref, ref, c_send.at[index, 0], c_recv.at[index, 0], (d, to))

    def across(index):
        src, dst = place_of(near, v_near, index), place_of(far, v_far, index)
        return remote(src, dst, c_send.at[index, 1], c_recv.at[index, 1], (d, inward))

    def to_end(index, to):
        ref = place_of(far, v_far, index)
        return remote(ref, ref, c_send.at[index, 0], c_recv.at[index, 0], (d, to))

    def result(index, ref, v_ref):
        src = place_of(ref, v_ref, index)
        if index == vectors:
            return pltpu.make_async_copy(src, tail_ref, o_sem.at[index])
        block, start, count, col, size, _ = items[index]
        to = out_refs[BLOCKS[block][0]].at[pl.ds(start, count), pl.ds(col, size)]
        return pltpu.make_async_copy(src, to, o_sem.at[index])

    def product(index):
        if index == vectors:
            return jnp.sum(v_all[...], axis=0)
        block, start, count, col, size, _ = items[index]
        name = BLOCKS[block][0]
        a_at = a_off[name] + start
        b_at = b_off[name] + col
        right = b_all[:, :, b_at : b_at + size].reshape(-1, size)
        value = mm(turned[a_at : a_at + PIECE, :], right)
        if count < PIECE:
            value = jnp.where(r % 2 == 1, value[count : 2 * count], value[:count])
        return value

    def end_push(index):
        @pl.when(jnp.logical_not(middle))
        def _():
            ref = place_of(near, v_near, index)
            ref[...] = product(index).astype(ref.dtype)
            to_middle(index, inward).start()

    def middle_join(index):
        @pl.when(middle)
        def _():
            value = product(index)
            to_middle(index, inward).wait_recv()
            ref = place_of(near, v_near, index)
            ref[...] = (value + ref[...].astype(full)).astype(ref.dtype)
            across(index).start()

    def middle_total(index):
        @pl.when(middle)
        def _():
            across(index).wait_recv()
            mine, theirs = place_of(near, v_near, index), place_of(far, v_far, index)
            both = mine[...].astype(full) + theirs[...].astype(full)
            theirs[...] = both.astype(theirs.dtype)
            to_end(index, outward).start()
            result(index, far, v_far).start()

    def end_land(index):
        @pl.when(jnp.logical_not(middle))
        def _():
            to_end(index, inward).wait_recv()
            result(index, far, v_far).start()

    arrived = set()

    def get(block):
        if block == blocks:
            own_sums.wait()
            for step in range(1, GROUP):
                v_copy(step, (r + GROUP - step) % GROUP).wait_recv()
            return
        for kind in (2, 3, 4, 7, 8):
            b_arrive(kind, block)
        name = BLOCKS[block][0]
        if name not in arrived:
            arrived.add(name)
            arrive_a(name)
            for at in range(a_off[name], a_off[name] + shares[name], PIECE):
                turned[at : at + PIECE, :] = a_all[:, :, at : at + PIECE].reshape(-1, PIECE).T

    table_copy = pltpu.make_async_copy(
        table_ref.at[pl.ds(z * rows, rows), :], table, one_sem.at[1]
    )
    input_copy = pltpu.make_async_copy(input_grad, input_ref, one_sem.at[2])
    pair_local = one_sem.at[3]
    table_copy.start()

    def rows_work():
        stream = []
        for j in range(genes // wide):
            stream.append(w_gene.at[pl.ds(j * wide, wide), :])
        for j in (1, 2, 0):
            stream.append(w_qkv.at[:, pl.ds(j * wide, wide)])
        stream.append(w_out)
        for j in range(hidden // wide):
            stream.append(w_up.at[:, pl.ds(j * wide, wide)])
            stream.append(w_down.at[pl.ds(j * wide, wide), :])
        stream.append(w_enc)
        stream.append(w_lat)
        for j in range(genes // wide):
            stream.append(w_dec.at[:, pl.ds(j * wide, wide)])
        stream.append(w_lat)
        stream.append(w_enc)
        for j in range(hidden // wide):
            stream.append(w_down.at[pl.ds(j * wide, wide), :])
            stream.append(w_up.at[:, pl.ds(j * wide, wide)])
        stream.append(w_out)
        for j in range(3):
            stream.append(w_qkv.at[:, pl.ds(j * wide, wide)])
        for j in range(genes // wide):
            stream.append(w_gene.at[pl.ds(j * wide, wide), :])

        def load(k):
            depth = stream[k].shape[0]
            return pltpu.make_async_copy(
                stream[k], ring.at[k % SLOTS, pl.ds(0, depth), :], ring_sem.at[k % SLOTS]
            )

        def fetch(k):
            if k < len(stream):
                load(k).start()

        place = [0]

        def take():
            k = place[0]
            place[0] += 1
            load(k).wait()
            return k

        def block(k):
            return ring[k % SLOTS, : stream[k].shape[0], :]

        for k in range(SLOTS):
            fetch(k)

        def hand(which, src, dst, i):
            return pltpu.make_async_remote_copy(
                src_ref=src.at[i],
                dst_ref=dst.at[z % 2],
                send_sem=hand_send.at[which, i],
                recv_sem=hand_recv.at[which, z % 2],
                device_id=(owner, 2 * core + i),
                device_id_type=MESH,
            )

        def hand_here(which, src, dst, i):
            return pltpu.make_async_copy(src.at[i], dst.at[i], hand_local.at[which])

        def hand_start(which, src, dst):
            for i in range(2):
                here = own & (z % 2 == i)

                @pl.when(here)
                def _():
                    hand_here(which, src, dst, i).start()

                @pl.when(jnp.logical_not(here))
                def _():
                    hand(which, src, dst, i).start()

        def hand_arrive(which, src, dst):
            for i in range(2):
                here = own & (z % 2 == i)

                @pl.when(here)
                def _():
                    hand_here(which, src, dst, i).wait()

                @pl.when(jnp.logical_not(here))
                def _():
                    pltpu.make_async_remote_copy(
                        src_ref=src.at[i],
                        dst_ref=dst.at[i],
                        send_sem=hand_send.at[which, i],
                        recv_sem=hand_recv.at[which, i],
                        device_id=(owner, 2 * core + i),
                        device_id_type=MESH,
                    ).wait_recv()

        def hand_sent(which, src, dst):
            for i in range(2):
                @pl.when(jnp.logical_not(own & (z % 2 == i)))
                def _():
                    hand(which, src, dst, i).wait_send()

        def pair(which, src, dst):
            return pltpu.make_async_remote_copy(
                src_ref=src,
                dst_ref=dst,
                send_sem=pair_send.at[which],
                recv_sem=pair_recv.at[which],
                device_id=(partner, z),
                device_id_type=MESH,
            )

        masks_own[:seqs, :genes] = gene_masks_ref[...].astype(full)
        masks_own[:seqs, genes : genes + length] = segments_ref[...].astype(full)
        own_masks = pltpu.make_async_copy(masks_own, masks_all.at[core], pair_local)
        own_masks.start()

        def vec(name, j=0):
            return vec_refs[name][:, j * wide : (j + 1) * wide]

        def put_a(name, values):
            off, share = a_off[name], shares[name]
            step = max(share, PIECE)
            for o in range(GROUP):
                start = o * share // step * step
                a_src[o, :, off : off + step] = values[:, start : start + step]

        def put_b(name, j, values):
            at = b_off[name] + j * wide
            b_all[r, :, at : at + wide] = values

        def put_sum(name, values, j=0):
            each = SUM_LANES[name]
            for o in range(values.shape[1] // 128):
                at = j * wide + o * 128
                to, row = at // (128 * each), SUM_AT[name] + at // 128 % each
                v_src[to, row : row + 1, :] = values[:, o * 128 : o * 128 + 128]

        def normalize(index, values, gain, shift):
            hat, scale = normed(values)
            hats[index] = hat
            scales[index] = jnp.broadcast_to(scale, scales.shape[1:])
            return hat * vec(gain) + vec(shift)

        def normalize_back(index, grad, gain, gain_name, shift_name):
            hat, scale = hats[index], scales[index, :, :1]
            put_sum(gain_name, jnp.sum(grad * hat, axis=0, keepdims=True))
            put_sum(shift_name, jnp.sum(grad, axis=0, keepdims=True))
            return normed_back(grad, hat, scale, vec(gain))

        keep = 1.0 - masks_own[:seqs, :genes]
        keep = jnp.concatenate(
            [jnp.broadcast_to(keep[s : s + 1], (rows, genes)) for s in range(seqs)], axis=0
        )
        masked = (expr_ref[...].reshape(tokens, genes).astype(full) * keep).astype(low)
        put_a(GENE, masked)
        table_copy.wait()
        embedded = jnp.concatenate([table[...]] * seqs, axis=0)
        for j in range(genes // wide):
            k = take()
            embedded += mm(masked[:, j * wide : (j + 1) * wide], block(k))
            fetch(k + SLOTS)
        x1_out[...] = (
            normalize(0, embedded, EMB_GAIN, EMB_SHIFT).astype(low).reshape(seqs, rows, width)
        )
        barrier_wait()
        hand_start(0, x1_out, x1_in)
        pair(0, masks_own, masks_all.at[core]).start()
        send_a(GENE)
        hand_start(1, noise_ref, noise_in)
        hand_start(2, target_ref, target_in)
        yield
        own_masks.wait()
        pair(0, masks_own, masks_all.at[1 - core]).wait_recv()
        odd = z % 2 == 1
        both_masks = masks_all[pl.ds(z // 2, 1)][0]
        mask_row = jnp.where(odd, both_masks[1:2], both_masks[0:1])
        gene_row = mask_row[:, :genes]
        segments = mask_row[:, genes : genes + length]
        place_q = lax.broadcasted_iota(jnp.int32, (tokens, length), 0) + core * tokens
        place_k = lax.broadcasted_iota(jnp.int32, (tokens, length), 1)
        own_segments = jnp.sum(
            jnp.where(place_q == place_k, segments, 0.0), axis=-1, keepdims=True
        )
        same = own_segments == segments
        same = jnp.concatenate([same.astype(full)] * 2, axis=0) > 0.5

        hand_arrive(0, x1_out, x1_in)
        x1 = x1_in[...].reshape(tokens, width).astype(full)
        h1 = normalize(1, x1, ATTN_GAIN, ATTN_SHIFT).astype(low)
        put_a(QKV, h1)
        send_a(QKV)
        head = width // HEADS
        scale = head**-0.5
        for j in (1, 2):
            k = take()
            kv_all[core, :, (j - 1) * wide : j * wide] = (
                mm(h1, block(k)) + vec(B_QKV, j)
            ).astype(low)
            fetch(k + SLOTS)
        pair(1, kv_all.at[core], kv_all.at[core]).start()
        k = take()
        query_own[...] = (mm(h1, block(k)) + vec(B_QKV, 0)).astype(low)
        fetch(k + SLOTS)
        yield
        pair(1, kv_all.at[core], kv_all.at[1 - core]).wait_recv()

        lanes = lax.broadcasted_iota(jnp.int32, (tokens, 2 * head), 1)
        first = lanes < head
        pairs = HEADS // 2

        def two(values):
            none = jnp.zeros_like(values)
            return jnp.concatenate([jnp.where(first, values, none), jnp.where(first, none, values)], axis=0)

        def one(values):
            return jnp.where(first, values[:tokens], values[tokens:])

        def columns(p):
            return pl.ds(pl.multiple_of(p * 2 * head, 2 * head), 2 * head)

        def keys_of(p):
            return kv_all[:, :, columns(p)].reshape(length, 2 * head)

        def values_of(p):
            at = pl.ds(pl.multiple_of(width + p * 2 * head, 2 * head), 2 * head)
            return kv_all[:, :, at].reshape(length, 2 * head)

        def attend(p, carry):
            scores = mm_last(two(query_own[:, columns(p)]), keys_of(p)) * scale
            scores = jnp.where(same, scores, mask_fill)
            shifted = jnp.exp(scores - jnp.max(scores, axis=-1, keepdims=True))
            prob = shifted / jnp.sum(shifted, axis=-1, keepdims=True)
            probs[p] = prob
            att = one(mm(prob.astype(low), values_of(p))).astype(low)
            a_src[p, :, a_off[OUT] : a_off[OUT] + 2 * head] = att
            return carry

        lax.fori_loop(0, pairs, attend, 0)
        yield
        attended = jnp.concatenate(
            [a_src[o, :, a_off[OUT] : a_off[OUT] + 2 * head] for o in range(pairs)], axis=1
        )
        k = take()
        mixed = x1 + (mm(attended, block(k)) + vec(B_OUT))
        fetch(k + SLOTS)
        h2 = normalize(2, mixed, FFN_GAIN, FFN_SHIFT).astype(low)
        put_a(UP, h2)
        yield
        x2 = mixed + vec(B_DOWN)
        per_owner = shares[DOWN]
        for j in range(hidden // wide):
            k = take()
            before = mm(h2, block(k)) + vec(B_UP, j)
            fetch(k + SLOTS)
            befores[:, j * wide : (j + 1) * wide] = before
            active = gelu(before).astype(low)
            for o in range(wide // per_owner):
                a_src[
                    j * (wide // per_owner) + o, :, a_off[DOWN] : a_off[DOWN] + per_owner
                ] = active[:, o * per_owner : (o + 1) * per_owner]
            k = take()
            x2 += mm(active, block(k))
            fetch(k + SLOTS)
            for o in range(wide // per_owner):
                send_a_to(DOWN, j * (wide // per_owner) + o)
            yield
        x2 = x2.astype(low).astype(full)
        h3 = normalize(3, x2, BOT_GAIN, BOT_SHIFT).astype(low)
        put_a(ENC, h3)
        k_enc = take()
        moments = mm(h3, block(k_enc)) + vec(B_ENC)
        latents = width // 2
        logvar = moments[:, latents:]
        hand_arrive(1, noise_ref, noise_in)
        swing = jnp.exp(0.5 * logvar) * noise_in[...].reshape(tokens, latents).astype(full)
        latent = moments[:, :latents] + swing
        latent_low = latent.astype(low)
        put_a(LAT, latent_low)
        fetch(k_enc + SLOTS)
        k_lat = take()
        lat_before = mm(latent_low, block(k_lat)) + vec(B_LAT)
        fetch(k_lat + SLOTS)
        x3 = gelu(lat_before).astype(low).astype(full)
        h4 = normalize(4, x3, DEC_GAIN, DEC_SHIFT).astype(low)
        put_a(DEC, h4)
        send_a(DEC)
        yield
        hand_arrive(2, target_ref, target_in)

        grad = jnp.zeros((tokens, width), full)
        for j in range(genes // wide):
            k = take()
            at = slice(j * wide, (j + 1) * wide)
            predicted = mm(h4, block(k)) + vec(B_DEC, j)
            wanted = target_in[:, :, at].reshape(tokens, wide).astype(full)
            d_pred = (gene_row[:, at] * (predicted - wanted)).astype(low)
            put_b(DEC, j, d_pred)
            put_sum(B_DEC, column_sums(d_pred), j)
            grad += mm_last(d_pred, block(k))
            fetch(k + SLOTS)
            yield
        d_x3 = normalize_back(4, grad, DEC_GAIN, DEC_GAIN, DEC_SHIFT).astype(low).astype(full)
        d_lat = (gelu_slope(lat_before) * d_x3).astype(low)
        put_b(LAT, 0, d_lat)
        put_sum(B_LAT, column_sums(d_lat))
        k = take()
        d_latent = mm_last(d_lat, block(k))
        fetch(k + SLOTS)
        yield

        inverse = jnp.exp(-logvar_ref[...])
        volume = jnp.sum(logvar_ref[...], axis=-1, keepdims=True)
        count = mean_ref.shape[0]
        scaled = []
        for c in range(count):
            offset = latent - mean_ref[c : c + 1, :]
            quad = jnp.sum(offset * offset * inverse[c : c + 1], axis=-1, keepdims=True)
            scaled.append(-0.5 * (quad + volume[c : c + 1]))
        highest = functools.reduce(jnp.maximum, scaled)
        shares_c = [jnp.exp(s - highest) for s in scaled]
        whole = functools.reduce(jnp.add, shares_c)
        parts = [part / whole for part in shares_c]
        for c in range(count):
            pull = (latent - mean_ref[c : c + 1, :]) * inverse[c : c + 1]
            d_latent += parts[c] * pull
        d_moments = jnp.concatenate([d_latent, 0.5 * d_latent * swing - 0.5], axis=1).astype(low)
        put_b(ENC, 0, d_moments)
        put_sum(B_ENC, column_sums(d_moments))
        yield
        k = take()
        grad = mm_last(d_moments, block(k))
        fetch(k + SLOTS)
        g = normalize_back(3, grad, BOT_GAIN, BOT_GAIN, BOT_SHIFT).astype(low)
        put_b(DOWN, 0, g)
        put_sum(B_DOWN, column_sums(g))
        yield
        for c in range(count):
            offset = latent - mean_ref[c : c + 1, :]
            weighted = parts[c] * (offset * inverse[c : c + 1])
            mean_grad = -jnp.sum(weighted, axis=0, keepdims=True)
            logvar_grad = 0.5 * jnp.sum(parts[c] - weighted * offset, axis=0, keepdims=True)
            for o in range(GROUP):
                at = slice(o // 2 * 128, o // 2 * 128 + 128)
                row = SUM_AT[COMP_MEAN] + c
                v_src[o, row : row + 1, :] = mean_grad[:, at]
                row = SUM_AT[COMP_LOGVAR] + c
                v_src[o, row : row + 1, :] = logvar_grad[:, at]
        yield
        grad = jnp.zeros((tokens, width), full)
        for j in range(hidden // wide):
            k = take()
            d_active = mm_last(g, block(k))
            fetch(k + SLOTS)
            slope = gelu_slope(befores[:, j * wide : (j + 1) * wide])
            d_before = (slope * d_active).astype(low)
            put_b(UP, j, d_before)
            put_sum(B_UP, column_sums(d_before), j)
            k = take()
            grad += mm_last(d_before, block(k))
            fetch(k + SLOTS)
            yield
        d_mixed = g.astype(full) + normalize_back(2, grad, FFN_GAIN, FFN_GAIN, FFN_SHIFT)
        mixed_grad[...] = d_mixed
        da = d_mixed.astype(low)
        put_b(OUT, 0, da)
        put_sum(B_OUT, column_sums(da))
        k = take()
        x1_in[...] = mm_last(da, block(k)).astype(low).reshape(seqs, rows, width)
        fetch(k + SLOTS)
        yield
        q_at = b_off[QKV]

        def attend_back(p, carry):
            query = two(query_own[:, columns(p)])
            d_att = two(x1_in[:, :, columns(p)].reshape(tokens, 2 * head))
            prob = probs[p]
            keys = keys_of(p)
            d_value = mm_first(prob.astype(low), d_att)
            d_prob = mm_last(d_att, values_of(p))
            d_score = prob * (d_prob - jnp.sum(prob * d_prob, axis=-1, keepdims=True))
            d_score = d_score.astype(low)
            d_query = one(mm(d_score, keys)) * scale
            d_key = mm_first(d_score, query) * scale
            to = pl.ds(pl.multiple_of(q_at + p * 2 * head, 2 * head), 2 * head)
            b_all[r, :, to] = d_query.astype(low)
            dkv_part[:, :, columns(p)] = d_key.reshape(2, tokens, 2 * head)
            at = pl.ds(pl.multiple_of(width + p * 2 * head, 2 * head), 2 * head)
            dkv_part[:, :, at] = d_value.reshape(2, tokens, 2 * head)
            return carry

        lax.fori_loop(0, pairs // 2, attend_back, 0)
        yield
        lax.fori_loop(pairs // 2, pairs, attend_back, 0)
        pair(2, dkv_part.at[1 - core], dkv_in).start()
        yield
        d_query = b_all[r, :, q_at : q_at + wide]
        put_sum(B_QUERY, column_sums(d_query))
        k = take()
        grad = mm_last(d_query, block(k))
        fetch(k + SLOTS)
        pair(2, dkv_part.at[1 - core], dkv_in).wait_recv()
        for j in (1, 2):
            at = slice((j - 1) * wide, j * wide)
            d_part = (dkv_part[core, :, at] + dkv_in[:, at]).astype(low)
            put_b(QKV, j, d_part)
            if j == 2:
                put_sum(B_VALUE, column_sums(d_part))
            k = take()
            grad += mm_last(d_part, block(k))
            fetch(k + SLOTS)
        d_x1 = mixed_grad[...] + normalize_back(1, grad, ATTN_GAIN, ATTN_GAIN, ATTN_SHIFT)
        dx_out[...] = d_x1.astype(low).reshape(seqs, rows, width)
        hand_start(3, dx_out, dx_in)
        yield
        hand_arrive(3, dx_out, dx_in)
        d_x1 = dx_in[...].reshape(tokens, width).astype(full)
        d_embedded = normalize_back(0, d_x1, EMB_GAIN, EMB_GAIN, EMB_SHIFT).astype(low)
        put_b(GENE, 0, d_embedded)
        for j in range(genes // wide):
            k = take()
            at = slice(j * wide, (j + 1) * wide)
            input_grad[:, at] = mm_last(d_embedded, block(k)) * jnp.concatenate(
                [
                    jnp.broadcast_to(1.0 - masks_own[s : s + 1, at], (rows, wide))
                    for s in range(seqs)
                ],
                axis=0,
            )
        input_copy.start()
        for step in range(1, GROUP):
            v_copy(step, r).start()
        own_sums.start()
        yield
        input_copy.wait()
        hand_sent(0, x1_out, x1_in)
        hand_sent(1, noise_ref, noise_in)
        hand_sent(2, target_ref, target_in)
        hand_sent(3, dx_out, dx_in)
        pair(0, masks_own, masks_all.at[core]).wait_send()
        pair(1, kv_all.at[core], kv_all.at[core]).wait_send()
        pair(2, dkv_part.at[1 - core], dkv_in).wait_send()


    work = rows_work()
    for code in ORDER:
        kind, index = code // 100, code % 100
        if kind == 0:
            next(work)
        elif kind == 1:
            for way in (0, 1, 2):
                b_start(way, index)
        elif kind == 2:
            b_arrive(0, index)
            b_start(5, index)
            b_start(3, index)
            b_arrive(1, index)
            b_start(6, index)
            b_start(4, index)
        elif kind == 3:
            b_arrive(5, index)
            b_start(7, index)
            b_arrive(6, index)
            b_start(8, index)
        else:
            (get, end_push, middle_join, middle_total, end_land, send_late)[kind - 4](index)
    next(work, None)
    for block in range(blocks):
        for kind in range(9):
            b_copy(kind, block, goes[kind]).wait_send()
    for step in range(1, GROUP):
        v_copy(step, r).wait_send()
        for name, _, _ in layers:
            a_copy(name, step, r).wait_send()
    for index in range(len(items) + 1):
        to_middle(index, inward).wait_send()
        result(index, far, v_far).wait()

        @pl.when(middle)
        def _():
            across(index).wait_send()


SUM_LANES = dict(SUMS)


def finish(layers, *refs):
    refs = list(refs)
    count = len(layers)
    low_refs, refs = refs[:count], refs[count:]
    input_ref, tail_ref = refs[:2]
    refs = refs[2:]
    full_refs, refs = refs[:count], refs[count:]
    input_out = refs[0]
    sum_refs = dict(zip([name for name, _ in SUMS], refs[1 : 1 + len(SUMS)]))
    refs = refs[1 + len(SUMS) :]
    low_bufs, full_bufs = refs[:count], refs[count : 2 * count]
    input_buf, tail_buf, mean_buf, logvar_buf, in_sem, out_sem, move_sem, sum_sem = refs[2 * count :]
    move_in = pltpu.make_async_copy(input_ref, input_buf, move_sem.at[0])
    move_out = pltpu.make_async_copy(input_buf, input_out, move_sem.at[1])
    tail_in = pltpu.make_async_copy(tail_ref, tail_buf, move_sem.at[2])
    ins = [
        pltpu.make_async_copy(src, dst, in_sem.at[i])
        for i, (src, dst) in enumerate(zip(low_refs, low_bufs))
    ]
    outs = [
        pltpu.make_async_copy(src, dst, out_sem.at[i])
        for i, (src, dst) in enumerate(zip(full_bufs, full_refs))
    ]
    for copy in ins:
        copy.start()
    tail_in.start()
    move_in.start()
    for i in range(count):
        ins[i].wait()
        full_bufs[i][...] = low_bufs[i][...].astype(jnp.float32)
        outs[i].start()
    move_in.wait()
    move_out.start()
    tail_in.wait()
    odd = lax.axis_index("dp") % 2 == 1
    rows_of = dict(SUMS)
    for name, buf in ((COMP_MEAN, mean_buf), (COMP_LOGVAR, logvar_buf)):
        both = tail_buf[SUM_AT[name] : SUM_AT[name] + rows_of[name], :]
        buf[...] = jnp.where(odd, both[:, 64:], both[:, :64])
    sums = [
        pltpu.make_async_copy(mean_buf, sum_refs[COMP_MEAN], sum_sem.at[0]),
        pltpu.make_async_copy(logvar_buf, sum_refs[COMP_LOGVAR], sum_sem.at[1]),
    ]
    for name, rows in SUMS[2:]:
        for row in range(rows):
            sums.append(
                pltpu.make_async_copy(
                    tail_buf.at[pl.ds(SUM_AT[name] + row, 1), :],
                    sum_refs[name].at[:, pl.ds(row * 128, 128)],
                    sum_sem.at[len(sums)],
                )
            )
    for copy in sums:
        copy.start()
    for copy in sums + outs:
        copy.wait()
    move_out.wait()


def positions(length, width):
    frequency = np.exp(np.arange(width // 2, dtype=np.float32) * np.float32(-2.0 * math.log(10000.0) / width))
    angles = np.arange(length, dtype=np.float32)[:, None] * frequency[None, :]
    return np.stack([np.sin(angles), np.cos(angles)], axis=-1).reshape(length, width)


def body(expression, targets, noise, gene_masks, segment_ids, w_gene, emb_gain, emb_shift, attn_gain, attn_shift, w_qkv, b_qkv, w_out, b_out, ffn_gain, ffn_shift, w_up, b_up, w_down, b_down, bot_gain, bot_shift, w_enc, b_enc, comp_mean, comp_logvar, w_lat, b_lat, dec_gain, dec_shift, w_dec, b_dec):
    low, full = jnp.bfloat16, jnp.float32
    seqs, rows, genes = expression.shape
    width = w_gene.shape[1]
    hidden = w_up.shape[1]
    latents = noise.shape[2]
    length = segment_ids.shape[1]
    tokens = seqs * rows
    given = {
        EMB_GAIN: emb_gain,
        EMB_SHIFT: emb_shift,
        ATTN_GAIN: attn_gain,
        ATTN_SHIFT: attn_shift,
        B_QKV: b_qkv,
        B_OUT: b_out,
        FFN_GAIN: ffn_gain,
        FFN_SHIFT: ffn_shift,
        B_UP: b_up,
        B_DOWN: b_down,
        BOT_GAIN: bot_gain,
        BOT_SHIFT: bot_shift,
        B_ENC: b_enc,
        B_LAT: b_lat,
        DEC_GAIN: dec_gain,
        DEC_SHIFT: dec_shift,
        B_DEC: b_dec,
    }
    weights = {
        GENE: w_gene,
        QKV: w_qkv,
        OUT: w_out,
        UP: w_up,
        DOWN: w_down,
        ENC: w_enc,
        LAT: w_lat,
        DEC: w_dec,
    }
    layers = [
        (name, weights[name].shape[0] // GROUP, weights[name].shape[1]) for name in LAYERS
    ]
    _, _, items, rows_all, a_cols, b_cols = grad_plan(layers)
    vmem = pl.BlockSpec(memory_space=pltpu.VMEM)
    anywhere = pl.BlockSpec(memory_space=pl.ANY)
    dma = pltpu.SemaphoreType.DMA
    mask_lanes = genes + length + -length % 128
    share_shapes = [(share, columns) for _, share, columns in layers]
    chunks = len(items) + 1
    results = pl.pallas_call(
        functools.partial(everything, layers, len(VECTORS)),
        out_shape=(jax.ShapeDtypeStruct((tokens, genes), full),)
        + tuple(jax.ShapeDtypeStruct(shape, low) for shape in share_shapes)
        + (jax.ShapeDtypeStruct((SUM_ROWS, 128), full),),
        in_specs=[vmem] * (5 + len(VECTORS)) + [anywhere] * 11,
        out_specs=(anywhere,) * (2 + len(layers)),
        scratch_shapes=[
            pltpu.VMEM((SLOTS, WIDE, WIDE), low),
            pltpu.VMEM((8, mask_lanes), full),
            pltpu.VMEM((2, 8, mask_lanes), full),
            pltpu.VMEM((rows, width), full),
            pltpu.VMEM((2, rows, genes), low),
            pltpu.VMEM((2, rows, latents), low),
            pltpu.VMEM((2, rows, width), low),
            pltpu.VMEM((2, rows, width), low),
            pltpu.VMEM((2, tokens, 2 * width), low),
            pltpu.VMEM((tokens, width), low),
            pltpu.VMEM((HEADS // 2, 2 * tokens, 2 * tokens), full),
            pltpu.VMEM((2, tokens, 2 * width), full),
            pltpu.VMEM((tokens, 2 * width), full),
            pltpu.VMEM((2, rows, width), low),
            pltpu.VMEM((2, rows, width), low),
            pltpu.VMEM((5, tokens, width), full),
            pltpu.VMEM((5, tokens, 128), full),
            pltpu.VMEM((tokens, hidden), full),
            pltpu.VMEM((tokens, width), full),
            pltpu.VMEM((tokens, genes), full),
            pltpu.VMEM((GROUP, tokens, a_cols), low),
            pltpu.VMEM((GROUP, tokens, a_cols), low),
            pltpu.VMEM((a_cols, GROUP * tokens), low),
            pltpu.VMEM((GROUP, tokens, b_cols), low),
            pltpu.VMEM((GROUP, SUM_ROWS, 128), full),
            pltpu.VMEM((GROUP, SUM_ROWS, 128), full),
            pltpu.VMEM((rows_all, WIDE), low),
            pltpu.VMEM((rows_all, WIDE), low),
            pltpu.VMEM((SUM_ROWS, 128), full),
            pltpu.VMEM((SUM_ROWS, 128), full),
            dma((SLOTS,)),
            dma((4, 2)),
            dma((4, 2)),
            dma((4,)),
            dma((3,)),
            dma((3,)),
            dma((4,)),
            dma((len(layers), GROUP)),
            dma((len(layers), GROUP)),
            dma((len(layers),)),
            dma((GROUP,)),
            dma((GROUP,)),
            dma((len(BLOCKS), 9)),
            dma((len(BLOCKS), 9)),
            dma((chunks, 2)),
            dma((chunks, 2)),
            dma((chunks,)),
        ],
        compiler_params=pltpu.CompilerParams(
            collective_id=0, has_side_effects=True, vmem_limit_bytes=63 * 1024 * 1024
        ),
    )(
        expression,
        gene_masks,
        segment_ids,
        comp_mean,
        comp_logvar,
        *[given[name].reshape(1, -1) for name in VECTORS],
        positions(length, width),
        targets,
        noise,
        *weights.values(),
    )
    input_grad, sums, tail = results[0], results[1:-1], results[-1]

    def sum_shape(name, count):
        return (count, 64) if name in (COMP_MEAN, COMP_LOGVAR) else (1, count * 128)

    finished = pl.pallas_call(
        functools.partial(finish, layers),
        out_shape=tuple(jax.ShapeDtypeStruct(shape, full) for shape in share_shapes)
        + (jax.ShapeDtypeStruct((tokens, genes), full),)
        + tuple(jax.ShapeDtypeStruct(sum_shape(name, count), full) for name, count in SUMS),
        in_specs=[anywhere] * (len(layers) + 2),
        out_specs=(anywhere,) * (len(layers) + 1 + len(SUMS)),
        scratch_shapes=[pltpu.VMEM(shape, low) for shape in share_shapes]
        + [pltpu.VMEM(shape, full) for shape in share_shapes]
        + [
            pltpu.VMEM((tokens, genes), full),
            pltpu.VMEM((SUM_ROWS, 128), full),
            pltpu.VMEM((SUMS[0][1], 64), full),
            pltpu.VMEM((SUMS[1][1], 64), full),
            dma((len(layers),)),
            dma((len(layers),)),
            dma((3,)),
            dma((SUM_ROWS,)),
        ],
        compiler_params=pltpu.CompilerParams(vmem_limit_bytes=63 * 1024 * 1024),
    )(*sums, input_grad, tail)

    groups = lax.axis_size("dp") // GROUP
    d = lax.axis_index("dp")

    def shared_out(values, axis):
        if groups == 1:
            return values
        across = [[g * GROUP + r for g in range(groups)] for r in range(GROUP)]
        within = [[g * GROUP + r for r in range(GROUP)] for g in range(groups)]
        values = lax.psum(values, "dp", axis_index_groups=across)
        values = lax.all_gather(values, "dp", axis=axis, tiled=True, axis_index_groups=within)
        size = values.shape[axis] // (groups * GROUP)
        return lax.dynamic_slice_in_dim(values, d * size, size, axis=axis)

    grads = {}
    for name, values in zip(LAYERS, finished):
        grads[name] = shared_out(values, 0)
    for (name, _), values in zip(SUMS, finished[len(layers) + 1 :]):
        if name in (COMP_MEAN, COMP_LOGVAR):
            grads[name] = shared_out(values, 1)
        else:
            grads[name] = shared_out(values.reshape(-1), 0)
    return (
        finished[len(layers)].reshape(seqs, rows, genes),
        grads[GENE],
        grads[EMB_GAIN],
        grads[EMB_SHIFT],
        grads[ATTN_GAIN],
        grads[ATTN_SHIFT],
        grads[QKV],
        grads[B_QUERY],
        grads[B_VALUE],
        grads[OUT],
        grads[B_OUT],
        grads[FFN_GAIN],
        grads[FFN_SHIFT],
        grads[UP],
        grads[B_UP],
        grads[DOWN],
        grads[B_DOWN],
        grads[BOT_GAIN],
        grads[BOT_SHIFT],
        grads[ENC],
        grads[B_ENC],
        grads[COMP_MEAN],
        grads[COMP_LOGVAR],
        grads[LAT],
        grads[B_LAT],
        grads[DEC_GAIN],
        grads[DEC_SHIFT],
        grads[DEC],
        grads[B_DEC],
    )


def solution(mesh):
    rows = P("dp", "phase", None)
    return jax.shard_map(
        body,
        mesh=mesh,
        in_specs=(rows, rows, rows, P("dp", None), P("dp", None)) + (P(),) * 27,
        out_specs=(
            rows,
            P("dp", None),
            P("dp"),
            P("dp"),
            P("dp"),
            P("dp"),
            P("dp", None),
            P("dp"),
            P("dp"),
            P("dp", None),
            P("dp"),
            P("dp"),
            P("dp"),
            P("dp", None),
            P("dp"),
            P("dp", None),
            P("dp"),
            P("dp"),
            P("dp"),
            P("dp", None),
            P("dp"),
            P(None, "dp"),
            P(None, "dp"),
            P("dp", None),
            P("dp"),
            P("dp"),
            P("dp"),
            P("dp", None),
            P("dp"),
        ),
        check_vma=False,
    )
```

```python
import functools
import math

import jax
import jax.numpy as jnp
import numpy as np
from jax import lax
from jax.experimental import pallas as pl
from jax.experimental.pallas import tpu as pltpu
from jax.sharding import PartitionSpec as P

HEADS = 16
GROUP = 8
PIECE = 128
WIDE = 1024
SLOTS = 4

norm_eps = 1e-05
mask_fill = -1000000000.0
MESH = pl.DeviceIdType.MESH

(
    DOWN,
    GENE,
    UP,
    QKV,
    DEC,
    ENC,
    OUT,
    LAT,
    EMB_GAIN,
    EMB_SHIFT,
    ATTN_GAIN,
    ATTN_SHIFT,
    B_QKV,
    B_QUERY,
    B_VALUE,
    B_OUT,
    FFN_GAIN,
    FFN_SHIFT,
    B_UP,
    B_DOWN,
    BOT_GAIN,
    BOT_SHIFT,
    B_ENC,
    COMP_MEAN,
    COMP_LOGVAR,
    B_LAT,
    DEC_GAIN,
    DEC_SHIFT,
    B_DEC,
) = range(29)


LAYERS = (DEC, DOWN, LAT, ENC, UP, OUT, QKV, GENE)
VECTORS = (
    EMB_GAIN,
    EMB_SHIFT,
    ATTN_GAIN,
    ATTN_SHIFT,
    B_QKV,
    B_OUT,
    FFN_GAIN,
    FFN_SHIFT,
    B_UP,
    B_DOWN,
    BOT_GAIN,
    BOT_SHIFT,
    B_ENC,
    B_LAT,
    DEC_GAIN,
    DEC_SHIFT,
    B_DEC,
)
SUMS = (
    (COMP_MEAN, 16),
    (COMP_LOGVAR, 16),
    (EMB_GAIN, 1),
    (EMB_SHIFT, 1),
    (ATTN_GAIN, 1),
    (ATTN_SHIFT, 1),
    (B_QUERY, 1),
    (B_VALUE, 1),
    (B_OUT, 1),
    (FFN_GAIN, 1),
    (FFN_SHIFT, 1),
    (B_UP, 4),
    (B_DOWN, 1),
    (BOT_GAIN, 1),
    (BOT_SHIFT, 1),
    (B_ENC, 1),
    (B_LAT, 1),
    (DEC_GAIN, 1),
    (DEC_SHIFT, 1),
    (B_DEC, 2),
)
SUM_AT = {name: sum(n for _, n in SUMS[:i]) for i, (name, _) in enumerate(SUMS)}
SUM_ROWS = 64


def mm(left, right):
    return jnp.dot(left, right, preferred_element_type=jnp.float32)


def mm_last(left, right):
    return lax.dot_general(
        left, right, (((1,), (1,)), ((), ())), preferred_element_type=jnp.float32
    )


def mm_first(left, right):
    return lax.dot_general(
        left, right, (((0,), (0,)), ((), ())), preferred_element_type=jnp.float32
    )


def normed(values):
    center = jnp.mean(values, axis=-1, keepdims=True)
    centered = values - center
    spread = jnp.mean(centered * centered, axis=-1, keepdims=True)
    scale = lax.rsqrt(spread + norm_eps)
    return centered * scale, scale


def normed_back(grad, hat, scale, gain):
    pulled = grad * gain
    mean = jnp.mean(pulled, axis=-1, keepdims=True)
    along = jnp.mean(pulled * hat, axis=-1, keepdims=True)
    return scale * (pulled - mean - hat * along)


def column_sums(values):
    return jnp.sum(values.astype(jnp.float32), axis=0, keepdims=True)


def gelu(values):
    return values * (0.5 * (1.0 + lax.erf(values * (0.5**0.5))))


def gelu_slope(values):
    bell = 0.5 * (1.0 + lax.erf(values * (0.5**0.5)))
    return bell + values * jnp.exp(-0.5 * values * values) * (2.0 * math.pi) ** -0.5


BLOCKS = (
    (DEC, 0, 512, 512),
    (DEC, 512, 512, 512),
    (DEC, 1024, 1024, 512),
    (DOWN, 0, 1024, 512),
    (LAT, 0, 1024, 512),
    (ENC, 0, 1024, 512),
    (UP, 0, 1024, 512),
    (UP, 1024, 1024, 512),
    (UP, 2048, 1024, 512),
    (UP, 3072, 1024, 512),
    (OUT, 0, 1024, 512),
    (QKV, 0, 1024, 512),
    (QKV, 1024, 1024, 512),
    (QKV, 2048, 1024, 512),
    (GENE, 0, 1024, 256),
)


def grad_plan(layers):
    a_off, b_off, items, place = {}, {}, [], {}
    a_at, b_at, row = 0, 0, 0
    shares = {name: share for name, share, _ in layers}
    for name, share, columns in layers:
        a_off[name], b_off[name] = a_at, b_at
        for block in range(columns // WIDE):
            for start in range(0, share, PIECE):
                place[name, block, start] = row
                row += min(PIECE, share - start)
        a_at += -(-share // PIECE) * PIECE
        b_at += columns
    for block, (name, first, columns, step) in enumerate(BLOCKS):
        for start in range(0, shares[name], PIECE):
            rows = min(PIECE, shares[name] - start)
            for col in range(first, first + columns, step):
                items.append((block, start, rows, col, step, place[name, col // WIDE, start]))
    return a_off, b_off, items, row, a_at, b_at


ORDER = (
    0, 1, 2, 3, 4, 5, 6, 7, 8, 9, 100, 101, 10, 11, 12, 13, 14, 15,
    16, 17, 18, 200, 103, 19, 20, 201, 300, 102, 21, 400, 500, 22, 203, 301, 106, 600,
    905, 904, 401, 501, 202, 107, 303, 403, 504, 700, 505, 601, 506, 507, 23, 206, 508, 108,
    509, 604, 701, 510, 511, 800, 605, 302, 704, 801, 415, 606, 402, 502, 540, 705, 503, 804,
    607, 207, 109, 706, 306, 805, 608, 406, 516, 707, 517, 806, 609, 208, 110, 903, 902, 708,
    807, 610, 307, 709, 407, 518, 519, 808, 611, 209, 105, 710, 809, 602, 640, 308, 711, 408,
    520, 603, 521, 810, 702, 210, 111, 811, 616, 703, 802, 617, 309, 716, 740, 803, 618, 409,
    522, 717, 523, 816, 619, 205, 112, 718, 310, 817, 620, 410, 524, 719, 525, 818, 840, 621,
    211, 113, 720, 819, 622, 305, 721, 405, 514, 623, 515, 820, 212, 114, 722, 821, 624, 311,
    723, 411, 526, 625, 527, 822, 724, 213, 104, 823, 614, 312, 725, 615, 412, 528, 714, 529,
    824, 825, 626, 214, 715, 313, 814, 627, 413, 530, 726, 531, 815, 628, 204, 727, 826, 629,
    314, 728, 414, 532, 304, 533, 534, 630, 535, 404, 536, 537, 729, 538, 539, 631, 512, 632,
    513, 827, 828, 730, 633, 829, 634, 731, 635, 830, 732, 636, 733, 637, 831, 734, 638, 832,
    735, 639, 833, 736, 834, 612, 737, 835, 613, 738, 836, 739, 837, 712, 838, 713, 839, 812,
    813,
)


def everything(layers, n_vec, *refs):
    low, full = jnp.bfloat16, jnp.float32
    refs = list(refs)

    def pop(count):
        taken = refs[:count]
        del refs[:count]
        return taken

    expr_ref, gene_masks_ref, segments_ref, mean_ref, logvar_ref = pop(5)
    vec_refs = dict(zip(VECTORS, pop(n_vec)))
    table_ref, target_ref, noise_ref = pop(3)
    w_gene, w_qkv, w_out, w_up, w_down, w_enc, w_lat, w_dec = pop(8)
    (input_ref,) = pop(1)
    out_refs = dict(zip([name for name, _, _ in layers], pop(len(layers))))
    (tail_ref,) = pop(1)
    ring, masks_own, masks_all, table, target_in, noise_in, x1_out, x1_in = pop(8)
    kv_all, query_own, probs, dkv_part, dkv_in, dx_out, dx_in = pop(7)
    hats, scales, befores, mixed_grad, input_grad = pop(5)
    a_src, a_all, turned, b_all, v_src, v_all, near, far, v_near, v_far = pop(10)
    ring_sem, hand_send, hand_recv, hand_local, pair_send, pair_recv = pop(6)
    one_sem, a_send, a_recv, a_local, v_send, v_recv, b_send, b_recv, c_send, c_recv, o_sem = pop(11)

    d = lax.axis_index("dp")
    z = lax.axis_index("phase")
    base = (d // GROUP) * GROUP
    r = d % GROUP
    core, cx, cy = r % 2, (r // 2) % 2, r // 4
    partner = d + 1 - 2 * core
    owner = d - core + z // 2
    own = core == z // 2
    rc, rx, ry = r + 1 - 2 * core, r + 2 - 4 * cx, r + 4 - 8 * cy
    rxc, ryc = rx + 1 - 2 * core, ry + 1 - 2 * core
    rd = rx + 4 - 8 * cy
    rdc = rd + 1 - 2 * core
    middle = (z % 3) != 0
    inward = z + 1 - 2 * (z // 2)
    outward = z - 1 + 2 * (z // 2)
    a_off, b_off, items, _, _, _ = grad_plan(layers)
    blocks = len(BLOCKS)
    shares = {name: share for name, share, _ in layers}
    index_of = {name: index for index, (name, _, _) in enumerate(layers)}
    seqs, rows, genes = expr_ref.shape
    tokens = seqs * rows
    width = table.shape[1]
    hidden = w_up.shape[1]
    length = segments_ref.shape[1]
    wide = WIDE

    barrier = pltpu.get_barrier_semaphore()

    def greet(to):
        pl.semaphore_signal(barrier, inc=1, device_id=to, device_id_type=MESH)

    for step in range(1, GROUP):
        greet((base + (r + step) % GROUP, z))
    greet((d, inward))

    @pl.when(middle)
    def _():
        greet((d, outward))

    for i in range(2):

        @pl.when(jnp.logical_not(own & (z % 2 == i)))
        def _():
            greet((owner, 2 * core + i))

    def barrier_wait():
        pl.semaphore_wait(barrier, GROUP + 1 + (z % 3 + 1) // 2 + (core + z // 2) % 2)

    def remote(src, dst, send, recv, to):
        return pltpu.make_async_remote_copy(
            src_ref=src,
            dst_ref=dst,
            send_sem=send,
            recv_sem=recv,
            device_id=to,
            device_id_type=MESH,
        )

    def columns_of(name):
        return pl.ds(a_off[name], -(-shares[name] // PIECE) * PIECE)

    def a_copy(name, step, slot):
        at, index, to = columns_of(name), index_of[name], (r + step) % GROUP
        return remote(
            a_src.at[to, :, at],
            a_all.at[slot, :, at],
            a_send.at[index, step],
            a_recv.at[index, step],
            (base + to, z),
        )

    def a_own(name):
        at = columns_of(name)
        return pltpu.make_async_copy(
            a_src.at[r, :, at], a_all.at[r, :, at], a_local.at[index_of[name]]
        )

    def send_a(name):
        for step in range(1, GROUP):
            a_copy(name, step, r).start()
        a_own(name).start()

    def send_a_to(name, to):
        step = (to - r + GROUP) % GROUP

        @pl.when(r == to)
        def _():
            a_own(name).start()

        @pl.when(r != to)
        def _():
            a_copy(name, step, r).start()

    def send_late(index):
        send_a(layers[index][0])

    def arrive_a(name):
        a_own(name).wait()
        for step in range(1, GROUP):
            a_copy(name, step, (r + GROUP - step) % GROUP).wait_recv()

    def v_copy(step, slot):
        to = (r + step) % GROUP
        return remote(
            v_src.at[to], v_all.at[slot], v_send.at[step], v_recv.at[step], (base + to, z)
        )

    own_sums = pltpu.make_async_copy(v_src.at[r], v_all.at[r], one_sem.at[0])

    comes = (rx, ry, rc, rxc, ryc, rd, rd, rdc, rdc)
    goes = (r, r, r, rx, ry, rx, ry, rd, rd)

    def b_copy(kind, block, source):
        name, first, size, _ = BLOCKS[block]
        col = b_off[name] + first
        if kind >= 5:
            size //= 2
        if kind in (6, 8):
            col += size
        to = (rx, ry, rc, rc, rc, ry, rx, rc, rc)[kind]
        view = b_all.at[source, :, pl.ds(col, size)]
        return remote(view, view, b_send.at[block, kind], b_recv.at[block, kind], (base + to, z))

    def b_start(kind, block):
        b_copy(kind, block, goes[kind]).start()

    def b_arrive(kind, block):
        b_copy(kind, block, comes[kind]).wait_recv()

    vectors = len(items)

    def place_of(ref, v_ref, index):
        if index == vectors:
            return v_ref
        _, _, count, col, size, row = items[index]
        return ref.at[pl.ds(row, count), pl.ds(col % WIDE, size)]

    def to_middle(index, to):
        ref = place_of(near, v_near, index)
        return remote(ref, ref, c_send.at[index, 0], c_recv.at[index, 0], (d, to))

    def across(index):
        src, dst = place_of(near, v_near, index), place_of(far, v_far, index)
        return remote(src, dst, c_send.at[index, 1], c_recv.at[index, 1], (d, inward))

    def to_end(index, to):
        ref = place_of(far, v_far, index)
        return remote(ref, ref, c_send.at[index, 0], c_recv.at[index, 0], (d, to))

    def result(index, ref, v_ref):
        src = place_of(ref, v_ref, index)
        if index == vectors:
            return pltpu.make_async_copy(src, tail_ref, o_sem.at[index])
        block, start, count, col, size, _ = items[index]
        to = out_refs[BLOCKS[block][0]].at[pl.ds(start, count), pl.ds(col, size)]
        return pltpu.make_async_copy(src, to, o_sem.at[index])

    def product(index):
        if index == vectors:
            return jnp.sum(v_all[...], axis=0)
        block, start, count, col, size, _ = items[index]
        name = BLOCKS[block][0]
        a_at = a_off[name] + start
        b_at = b_off[name] + col
        right = b_all[:, :, b_at : b_at + size].reshape(-1, size)
        value = mm(turned[a_at : a_at + PIECE, :], right)
        if count < PIECE:
            value = jnp.where(r % 2 == 1, value[count : 2 * count], value[:count])
        return value

    def end_push(index):
        @pl.when(jnp.logical_not(middle))
        def _():
            ref = place_of(near, v_near, index)
            ref[...] = product(index).astype(ref.dtype)
            to_middle(index, inward).start()

    def middle_join(index):
        @pl.when(middle)
        def _():
            value = product(index)
            to_middle(index, inward).wait_recv()
            ref = place_of(near, v_near, index)
            ref[...] = (value + ref[...].astype(full)).astype(ref.dtype)
            across(index).start()

    totals, lands, gone = [], [], []

    def middle_sent(index):
        across(index).wait_send()
        to_end(index, outward).wait_send()
        result(index, far, v_far).wait()

    def end_sent(index):
        to_middle(index, inward).wait_send()
        result(index, far, v_far).wait()

    def middle_total(index):
        totals.append(index)

        @pl.when(middle)
        def _():
            if len(totals) > 3:
                middle_sent(totals[-4])
            across(index).wait_recv()
            mine, theirs = place_of(near, v_near, index), place_of(far, v_far, index)
            both = mine[...].astype(full) + theirs[...].astype(full)
            theirs[...] = both.astype(theirs.dtype)
            to_end(index, outward).start()
            result(index, far, v_far).start()

    def end_land(index):
        lands.append(index)

        @pl.when(jnp.logical_not(middle))
        def _():
            if len(lands) > 3:
                end_sent(lands[-4])
            to_end(index, inward).wait_recv()
            result(index, far, v_far).start()

    arrived, waited = set(), set()

    def block_sent(block):
        for kind in range(9):
            b_copy(kind, block, goes[kind]).wait_send()

    def layer_sent(name):
        for step in range(1, GROUP):
            a_copy(name, step, r).wait_send()

    def get(block):
        if len(gone) > 2 and gone[-3] not in waited:
            waited.add(gone[-3])
            block_sent(gone[-3])
        if block == blocks:
            own_sums.wait()
            for step in range(1, GROUP):
                v_copy(step, (r + GROUP - step) % GROUP).wait_recv()
            return
        gone.append(block)
        for kind in (2, 3, 4, 7, 8):
            b_arrive(kind, block)
        name = BLOCKS[block][0]
        if name not in arrived:
            arrived.add(name)
            arrive_a(name)
            layer_sent(name)
            for at in range(a_off[name], a_off[name] + shares[name], PIECE):
                turned[at : at + PIECE, :] = a_all[:, :, at : at + PIECE].reshape(-1, PIECE).T

    table_copy = pltpu.make_async_copy(
        table_ref.at[pl.ds(z * rows, rows), :], table, one_sem.at[1]
    )
    input_copy = pltpu.make_async_copy(input_grad, input_ref, one_sem.at[2])
    pair_local = one_sem.at[3]
    table_copy.start()

    def rows_work():
        stream = []
        for j in range(genes // wide):
            stream.append(w_gene.at[pl.ds(j * wide, wide), :])
        for j in (1, 2, 0):
            stream.append(w_qkv.at[:, pl.ds(j * wide, wide)])
        stream.append(w_out)
        for j in range(hidden // wide):
            stream.append(w_up.at[:, pl.ds(j * wide, wide)])
            stream.append(w_down.at[pl.ds(j * wide, wide), :])
        stream.append(w_enc)
        stream.append(w_lat)
        for j in range(genes // wide):
            stream.append(w_dec.at[:, pl.ds(j * wide, wide)])
        stream.append(w_lat)
        stream.append(w_enc)
        for j in range(hidden // wide):
            stream.append(w_down.at[pl.ds(j * wide, wide), :])
            stream.append(w_up.at[:, pl.ds(j * wide, wide)])
        stream.append(w_out)
        for j in range(3):
            stream.append(w_qkv.at[:, pl.ds(j * wide, wide)])
        for j in range(genes // wide):
            stream.append(w_gene.at[pl.ds(j * wide, wide), :])

        def load(k):
            depth = stream[k].shape[0]
            return pltpu.make_async_copy(
                stream[k], ring.at[k % SLOTS, pl.ds(0, depth), :], ring_sem.at[k % SLOTS]
            )

        def fetch(k):
            if k < len(stream):
                load(k).start()

        place = [0]

        def take():
            k = place[0]
            place[0] += 1
            load(k).wait()
            return k

        def block(k):
            return ring[k % SLOTS, : stream[k].shape[0], :]

        for k in range(SLOTS):
            fetch(k)

        def hand(which, src, dst, i):
            return pltpu.make_async_remote_copy(
                src_ref=src.at[i],
                dst_ref=dst.at[z % 2],
                send_sem=hand_send.at[which, i],
                recv_sem=hand_recv.at[which, z % 2],
                device_id=(owner, 2 * core + i),
                device_id_type=MESH,
            )

        def hand_here(which, src, dst, i):
            return pltpu.make_async_copy(src.at[i], dst.at[i], hand_local.at[which])

        def hand_start(which, src, dst):
            for i in range(2):
                here = own & (z % 2 == i)

                @pl.when(here)
                def _():
                    hand_here(which, src, dst, i).start()

                @pl.when(jnp.logical_not(here))
                def _():
                    hand(which, src, dst, i).start()

        def hand_arrive(which, src, dst):
            for i in range(2):
                here = own & (z % 2 == i)

                @pl.when(here)
                def _():
                    hand_here(which, src, dst, i).wait()

                @pl.when(jnp.logical_not(here))
                def _():
                    pltpu.make_async_remote_copy(
                        src_ref=src.at[i],
                        dst_ref=dst.at[i],
                        send_sem=hand_send.at[which, i],
                        recv_sem=hand_recv.at[which, i],
                        device_id=(owner, 2 * core + i),
                        device_id_type=MESH,
                    ).wait_recv()

        def hand_sent(which, src, dst):
            for i in range(2):
                @pl.when(jnp.logical_not(own & (z % 2 == i)))
                def _():
                    hand(which, src, dst, i).wait_send()

        def pair(which, src, dst):
            return pltpu.make_async_remote_copy(
                src_ref=src,
                dst_ref=dst,
                send_sem=pair_send.at[which],
                recv_sem=pair_recv.at[which],
                device_id=(partner, z),
                device_id_type=MESH,
            )

        masks_own[:seqs, :genes] = gene_masks_ref[...].astype(full)
        masks_own[:seqs, genes : genes + length] = segments_ref[...].astype(full)
        own_masks = pltpu.make_async_copy(masks_own, masks_all.at[core], pair_local)
        own_masks.start()

        def vec(name, j=0):
            return vec_refs[name][:, j * wide : (j + 1) * wide]

        def put_a(name, values):
            off, share = a_off[name], shares[name]
            step = max(share, PIECE)
            for o in range(GROUP):
                start = o * share // step * step
                a_src[o, :, off : off + step] = values[:, start : start + step]

        def put_b(name, j, values):
            at = b_off[name] + j * wide
            b_all[r, :, at : at + wide] = values

        def put_sum(name, values, j=0):
            each = SUM_LANES[name]
            for o in range(values.shape[1] // 128):
                at = j * wide + o * 128
                to, row = at // (128 * each), SUM_AT[name] + at // 128 % each
                v_src[to, row : row + 1, :] = values[:, o * 128 : o * 128 + 128]

        def normalize(index, values, gain, shift):
            hat, scale = normed(values)
            hats[index] = hat
            scales[index] = jnp.broadcast_to(scale, scales.shape[1:])
            return hat * vec(gain) + vec(shift)

        def normalize_back(index, grad, gain, gain_name, shift_name):
            hat, scale = hats[index], scales[index, :, :1]
            put_sum(gain_name, jnp.sum(grad * hat, axis=0, keepdims=True))
            put_sum(shift_name, jnp.sum(grad, axis=0, keepdims=True))
            return normed_back(grad, hat, scale, vec(gain))

        keep = 1.0 - masks_own[:seqs, :genes]
        keep = jnp.concatenate(
            [jnp.broadcast_to(keep[s : s + 1], (rows, genes)) for s in range(seqs)], axis=0
        )
        masked = (expr_ref[...].reshape(tokens, genes).astype(full) * keep).astype(low)
        put_a(GENE, masked)
        table_copy.wait()
        embedded = jnp.concatenate([table[...]] * seqs, axis=0)
        for j in range(genes // wide):
            k = take()
            embedded += mm(masked[:, j * wide : (j + 1) * wide], block(k))
            fetch(k + SLOTS)
        x1_out[...] = (
            normalize(0, embedded, EMB_GAIN, EMB_SHIFT).astype(low).reshape(seqs, rows, width)
        )
        barrier_wait()
        hand_start(0, x1_out, x1_in)
        pair(0, masks_own, masks_all.at[core]).start()
        send_a(GENE)
        hand_start(1, noise_ref, noise_in)
        hand_start(2, target_ref, target_in)
        yield
        own_masks.wait()
        pair(0, masks_own, masks_all.at[1 - core]).wait_recv()
        odd = z % 2 == 1
        both_masks = masks_all[pl.ds(z // 2, 1)][0]
        mask_row = jnp.where(odd, both_masks[1:2], both_masks[0:1])
        gene_row = mask_row[:, :genes]
        segments = mask_row[:, genes : genes + length]
        place_q = lax.broadcasted_iota(jnp.int32, (tokens, length), 0) + core * tokens
        place_k = lax.broadcasted_iota(jnp.int32, (tokens, length), 1)
        own_segments = jnp.sum(
            jnp.where(place_q == place_k, segments, 0.0), axis=-1, keepdims=True
        )
        same = own_segments == segments
        same = jnp.concatenate([same.astype(full)] * 2, axis=0) > 0.5

        hand_arrive(0, x1_out, x1_in)
        x1 = x1_in[...].reshape(tokens, width).astype(full)
        h1 = normalize(1, x1, ATTN_GAIN, ATTN_SHIFT).astype(low)
        put_a(QKV, h1)
        send_a(QKV)
        head = width // HEADS
        scale = head**-0.5
        for j in (1, 2):
            k = take()
            kv_all[core, :, (j - 1) * wide : j * wide] = (
                mm(h1, block(k)) + vec(B_QKV, j)
            ).astype(low)
            fetch(k + SLOTS)
        pair(1, kv_all.at[core], kv_all.at[core]).start()
        k = take()
        query_own[...] = (mm(h1, block(k)) + vec(B_QKV, 0)).astype(low)
        fetch(k + SLOTS)
        yield
        pair(1, kv_all.at[core], kv_all.at[1 - core]).wait_recv()

        lanes = lax.broadcasted_iota(jnp.int32, (tokens, 2 * head), 1)
        first = lanes < head
        pairs = HEADS // 2

        def two(values):
            none = jnp.zeros_like(values)
            return jnp.concatenate([jnp.where(first, values, none), jnp.where(first, none, values)], axis=0)

        def one(values):
            return jnp.where(first, values[:tokens], values[tokens:])

        def columns(p):
            return pl.ds(pl.multiple_of(p * 2 * head, 2 * head), 2 * head)

        def keys_of(p):
            return kv_all[:, :, columns(p)].reshape(length, 2 * head)

        def values_of(p):
            at = pl.ds(pl.multiple_of(width + p * 2 * head, 2 * head), 2 * head)
            return kv_all[:, :, at].reshape(length, 2 * head)

        def attend(p, carry):
            scores = mm_last(two(query_own[:, columns(p)]), keys_of(p)) * scale
            scores = jnp.where(same, scores, mask_fill)
            shifted = jnp.exp(scores - jnp.max(scores, axis=-1, keepdims=True))
            prob = shifted / jnp.sum(shifted, axis=-1, keepdims=True)
            probs[p] = prob
            att = one(mm(prob.astype(low), values_of(p))).astype(low)
            a_src[p, :, a_off[OUT] : a_off[OUT] + 2 * head] = att
            return carry

        lax.fori_loop(0, pairs, attend, 0)
        yield
        attended = jnp.concatenate(
            [a_src[o, :, a_off[OUT] : a_off[OUT] + 2 * head] for o in range(pairs)], axis=1
        )
        k = take()
        mixed = x1 + (mm(attended, block(k)) + vec(B_OUT))
        fetch(k + SLOTS)
        h2 = normalize(2, mixed, FFN_GAIN, FFN_SHIFT).astype(low)
        put_a(UP, h2)
        yield
        x2 = mixed + vec(B_DOWN)
        per_owner = shares[DOWN]
        for j in range(hidden // wide):
            k = take()
            before = mm(h2, block(k)) + vec(B_UP, j)
            fetch(k + SLOTS)
            befores[:, j * wide : (j + 1) * wide] = before
            active = gelu(before).astype(low)
            for o in range(wide // per_owner):
                a_src[
                    j * (wide // per_owner) + o, :, a_off[DOWN] : a_off[DOWN] + per_owner
                ] = active[:, o * per_owner : (o + 1) * per_owner]
            k = take()
            x2 += mm(active, block(k))
            fetch(k + SLOTS)
            for o in range(wide // per_owner):
                send_a_to(DOWN, j * (wide // per_owner) + o)
            yield
        x2 = x2.astype(low).astype(full)
        h3 = normalize(3, x2, BOT_GAIN, BOT_SHIFT).astype(low)
        put_a(ENC, h3)
        k_enc = take()
        moments = mm(h3, block(k_enc)) + vec(B_ENC)
        latents = width // 2
        logvar = moments[:, latents:]
        hand_arrive(1, noise_ref, noise_in)
        swing = jnp.exp(0.5 * logvar) * noise_in[...].reshape(tokens, latents).astype(full)
        latent = moments[:, :latents] + swing
        latent_low = latent.astype(low)
        put_a(LAT, latent_low)
        fetch(k_enc + SLOTS)
        k_lat = take()
        lat_before = mm(latent_low, block(k_lat)) + vec(B_LAT)
        fetch(k_lat + SLOTS)
        x3 = gelu(lat_before).astype(low).astype(full)
        h4 = normalize(4, x3, DEC_GAIN, DEC_SHIFT).astype(low)
        put_a(DEC, h4)
        send_a(DEC)
        yield
        hand_arrive(2, target_ref, target_in)

        grad = jnp.zeros((tokens, width), full)
        for j in range(genes // wide):
            k = take()
            at = slice(j * wide, (j + 1) * wide)
            predicted = mm(h4, block(k)) + vec(B_DEC, j)
            wanted = target_in[:, :, at].reshape(tokens, wide).astype(full)
            d_pred = (gene_row[:, at] * (predicted - wanted)).astype(low)
            put_b(DEC, j, d_pred)
            put_sum(B_DEC, column_sums(d_pred), j)
            grad += mm_last(d_pred, block(k))
            fetch(k + SLOTS)
            yield
        d_x3 = normalize_back(4, grad, DEC_GAIN, DEC_GAIN, DEC_SHIFT).astype(low).astype(full)
        d_lat = (gelu_slope(lat_before) * d_x3).astype(low)
        put_b(LAT, 0, d_lat)
        put_sum(B_LAT, column_sums(d_lat))
        k = take()
        d_latent = mm_last(d_lat, block(k))
        fetch(k + SLOTS)
        yield

        inverse = jnp.exp(-logvar_ref[...])
        volume = jnp.sum(logvar_ref[...], axis=-1, keepdims=True)
        count = mean_ref.shape[0]
        scaled = []
        for c in range(count):
            offset = latent - mean_ref[c : c + 1, :]
            quad = jnp.sum(offset * offset * inverse[c : c + 1], axis=-1, keepdims=True)
            scaled.append(-0.5 * (quad + volume[c : c + 1]))
        highest = functools.reduce(jnp.maximum, scaled)
        shares_c = [jnp.exp(s - highest) for s in scaled]
        whole = functools.reduce(jnp.add, shares_c)
        parts = [part / whole for part in shares_c]
        for c in range(count):
            pull = (latent - mean_ref[c : c + 1, :]) * inverse[c : c + 1]
            d_latent += parts[c] * pull
        d_moments = jnp.concatenate([d_latent, 0.5 * d_latent * swing - 0.5], axis=1).astype(low)
        put_b(ENC, 0, d_moments)
        put_sum(B_ENC, column_sums(d_moments))
        yield
        k = take()
        grad = mm_last(d_moments, block(k))
        fetch(k + SLOTS)
        g = normalize_back(3, grad, BOT_GAIN, BOT_GAIN, BOT_SHIFT).astype(low)
        put_b(DOWN, 0, g)
        put_sum(B_DOWN, column_sums(g))
        yield
        for c in range(count):
            offset = latent - mean_ref[c : c + 1, :]
            weighted = parts[c] * (offset * inverse[c : c + 1])
            mean_grad = -jnp.sum(weighted, axis=0, keepdims=True)
            logvar_grad = 0.5 * jnp.sum(parts[c] - weighted * offset, axis=0, keepdims=True)
            for o in range(GROUP):
                at = slice(o // 2 * 128, o // 2 * 128 + 128)
                row = SUM_AT[COMP_MEAN] + c
                v_src[o, row : row + 1, :] = mean_grad[:, at]
                row = SUM_AT[COMP_LOGVAR] + c
                v_src[o, row : row + 1, :] = logvar_grad[:, at]
        yield
        grad = jnp.zeros((tokens, width), full)
        for j in range(hidden // wide):
            k = take()
            d_active = mm_last(g, block(k))
            fetch(k + SLOTS)
            slope = gelu_slope(befores[:, j * wide : (j + 1) * wide])
            d_before = (slope * d_active).astype(low)
            put_b(UP, j, d_before)
            put_sum(B_UP, column_sums(d_before), j)
            k = take()
            grad += mm_last(d_before, block(k))
            fetch(k + SLOTS)
            yield
        d_mixed = g.astype(full) + normalize_back(2, grad, FFN_GAIN, FFN_GAIN, FFN_SHIFT)
        mixed_grad[...] = d_mixed
        da = d_mixed.astype(low)
        put_b(OUT, 0, da)
        put_sum(B_OUT, column_sums(da))
        k = take()
        x1_in[...] = mm_last(da, block(k)).astype(low).reshape(seqs, rows, width)
        fetch(k + SLOTS)
        yield
        q_at = b_off[QKV]

        def attend_back(p, carry):
            query = two(query_own[:, columns(p)])
            d_att = two(x1_in[:, :, columns(p)].reshape(tokens, 2 * head))
            prob = probs[p]
            keys = keys_of(p)
            d_value = mm_first(prob.astype(low), d_att)
            d_prob = mm_last(d_att, values_of(p))
            d_score = prob * (d_prob - jnp.sum(prob * d_prob, axis=-1, keepdims=True))
            d_score = d_score.astype(low)
            d_query = one(mm(d_score, keys)) * scale
            d_key = mm_first(d_score, query) * scale
            to = pl.ds(pl.multiple_of(q_at + p * 2 * head, 2 * head), 2 * head)
            b_all[r, :, to] = d_query.astype(low)
            dkv_part[:, :, columns(p)] = d_key.reshape(2, tokens, 2 * head)
            at = pl.ds(pl.multiple_of(width + p * 2 * head, 2 * head), 2 * head)
            dkv_part[:, :, at] = d_value.reshape(2, tokens, 2 * head)
            return carry

        lax.fori_loop(0, pairs // 2, attend_back, 0)
        yield
        lax.fori_loop(pairs // 2, pairs, attend_back, 0)
        pair(2, dkv_part.at[1 - core], dkv_in).start()
        yield
        d_query = b_all[r, :, q_at : q_at + wide]
        put_sum(B_QUERY, column_sums(d_query))
        k = take()
        grad = mm_last(d_query, block(k))
        fetch(k + SLOTS)
        pair(2, dkv_part.at[1 - core], dkv_in).wait_recv()
        for j in (1, 2):
            at = slice((j - 1) * wide, j * wide)
            d_part = (dkv_part[core, :, at] + dkv_in[:, at]).astype(low)
            put_b(QKV, j, d_part)
            if j == 2:
                put_sum(B_VALUE, column_sums(d_part))
            k = take()
            grad += mm_last(d_part, block(k))
            fetch(k + SLOTS)
        d_x1 = mixed_grad[...] + normalize_back(1, grad, ATTN_GAIN, ATTN_GAIN, ATTN_SHIFT)
        dx_out[...] = d_x1.astype(low).reshape(seqs, rows, width)
        hand_start(3, dx_out, dx_in)
        yield
        hand_arrive(3, dx_out, dx_in)
        d_x1 = dx_in[...].reshape(tokens, width).astype(full)
        d_embedded = normalize_back(0, d_x1, EMB_GAIN, EMB_GAIN, EMB_SHIFT).astype(low)
        put_b(GENE, 0, d_embedded)
        for j in range(genes // wide):
            k = take()
            at = slice(j * wide, (j + 1) * wide)
            input_grad[:, at] = mm_last(d_embedded, block(k)) * jnp.concatenate(
                [
                    jnp.broadcast_to(1.0 - masks_own[s : s + 1, at], (rows, wide))
                    for s in range(seqs)
                ],
                axis=0,
            )
        input_copy.start()
        for step in range(1, GROUP):
            v_copy(step, r).start()
        own_sums.start()
        yield
        input_copy.wait()
        hand_sent(0, x1_out, x1_in)
        hand_sent(1, noise_ref, noise_in)
        hand_sent(2, target_ref, target_in)
        hand_sent(3, dx_out, dx_in)
        pair(0, masks_own, masks_all.at[core]).wait_send()
        pair(1, kv_all.at[core], kv_all.at[core]).wait_send()
        pair(2, dkv_part.at[1 - core], dkv_in).wait_send()


    work = rows_work()
    for code in ORDER:
        kind, index = code // 100, code % 100
        if kind == 0:
            next(work)
        elif kind == 1:
            for way in (0, 1, 2):
                b_start(way, index)
        elif kind == 2:
            b_arrive(0, index)
            b_start(5, index)
            b_start(3, index)
            b_arrive(1, index)
            b_start(6, index)
            b_start(4, index)
        elif kind == 3:
            b_arrive(5, index)
            b_start(7, index)
            b_arrive(6, index)
            b_start(8, index)
        else:
            (get, end_push, middle_join, middle_total, end_land, send_late)[kind - 4](index)
    next(work, None)
    for block in gone[-3:]:
        if block not in waited:
            block_sent(block)
    for step in range(1, GROUP):
        v_copy(step, r).wait_send()

    @pl.when(middle)
    def _():
        for index in totals[-3:]:
            middle_sent(index)

    @pl.when(jnp.logical_not(middle))
    def _():
        for index in lands[-3:]:
            end_sent(index)


SUM_LANES = dict(SUMS)


def finish(layers, *refs):
    refs = list(refs)
    count = len(layers)
    low_refs, refs = refs[:count], refs[count:]
    input_ref, tail_ref = refs[:2]
    refs = refs[2:]
    full_refs, refs = refs[:count], refs[count:]
    input_out = refs[0]
    sum_refs = dict(zip([name for name, _ in SUMS], refs[1 : 1 + len(SUMS)]))
    refs = refs[1 + len(SUMS) :]
    low_bufs, full_bufs = refs[:count], refs[count : 2 * count]
    input_buf, tail_buf, mean_buf, logvar_buf, in_sem, out_sem, move_sem, sum_sem = refs[2 * count :]
    move_in = pltpu.make_async_copy(input_ref, input_buf, move_sem.at[0])
    move_out = pltpu.make_async_copy(input_buf, input_out, move_sem.at[1])
    tail_in = pltpu.make_async_copy(tail_ref, tail_buf, move_sem.at[2])
    ins = [
        pltpu.make_async_copy(src, dst, in_sem.at[i])
        for i, (src, dst) in enumerate(zip(low_refs, low_bufs))
    ]
    outs = [
        pltpu.make_async_copy(src, dst, out_sem.at[i])
        for i, (src, dst) in enumerate(zip(full_bufs, full_refs))
    ]
    for copy in ins:
        copy.start()
    tail_in.start()
    move_in.start()
    for i in range(count):
        ins[i].wait()
        full_bufs[i][...] = low_bufs[i][...].astype(jnp.float32)
        outs[i].start()
    move_in.wait()
    move_out.start()
    tail_in.wait()
    odd = lax.axis_index("dp") % 2 == 1
    rows_of = dict(SUMS)
    for name, buf in ((COMP_MEAN, mean_buf), (COMP_LOGVAR, logvar_buf)):
        both = tail_buf[SUM_AT[name] : SUM_AT[name] + rows_of[name], :]
        buf[...] = jnp.where(odd, both[:, 64:], both[:, :64])
    sums = [
        pltpu.make_async_copy(mean_buf, sum_refs[COMP_MEAN], sum_sem.at[0]),
        pltpu.make_async_copy(logvar_buf, sum_refs[COMP_LOGVAR], sum_sem.at[1]),
    ]
    for name, rows in SUMS[2:]:
        for row in range(rows):
            sums.append(
                pltpu.make_async_copy(
                    tail_buf.at[pl.ds(SUM_AT[name] + row, 1), :],
                    sum_refs[name].at[:, pl.ds(row * 128, 128)],
                    sum_sem.at[len(sums)],
                )
            )
    for copy in sums:
        copy.start()
    for copy in sums + outs:
        copy.wait()
    move_out.wait()


def positions(length, width):
    frequency = np.exp(np.arange(width // 2, dtype=np.float32) * np.float32(-2.0 * math.log(10000.0) / width))
    angles = np.arange(length, dtype=np.float32)[:, None] * frequency[None, :]
    return np.stack([np.sin(angles), np.cos(angles)], axis=-1).reshape(length, width)


def body(expression, targets, noise, gene_masks, segment_ids, w_gene, emb_gain, emb_shift, attn_gain, attn_shift, w_qkv, b_qkv, w_out, b_out, ffn_gain, ffn_shift, w_up, b_up, w_down, b_down, bot_gain, bot_shift, w_enc, b_enc, comp_mean, comp_logvar, w_lat, b_lat, dec_gain, dec_shift, w_dec, b_dec):
    low, full = jnp.bfloat16, jnp.float32
    seqs, rows, genes = expression.shape
    width = w_gene.shape[1]
    hidden = w_up.shape[1]
    latents = noise.shape[2]
    length = segment_ids.shape[1]
    tokens = seqs * rows
    given = {
        EMB_GAIN: emb_gain,
        EMB_SHIFT: emb_shift,
        ATTN_GAIN: attn_gain,
        ATTN_SHIFT: attn_shift,
        B_QKV: b_qkv,
        B_OUT: b_out,
        FFN_GAIN: ffn_gain,
        FFN_SHIFT: ffn_shift,
        B_UP: b_up,
        B_DOWN: b_down,
        BOT_GAIN: bot_gain,
        BOT_SHIFT: bot_shift,
        B_ENC: b_enc,
        B_LAT: b_lat,
        DEC_GAIN: dec_gain,
        DEC_SHIFT: dec_shift,
        B_DEC: b_dec,
    }
    weights = {
        GENE: w_gene,
        QKV: w_qkv,
        OUT: w_out,
        UP: w_up,
        DOWN: w_down,
        ENC: w_enc,
        LAT: w_lat,
        DEC: w_dec,
    }
    layers = [
        (name, weights[name].shape[0] // GROUP, weights[name].shape[1]) for name in LAYERS
    ]
    _, _, items, rows_all, a_cols, b_cols = grad_plan(layers)
    vmem = pl.BlockSpec(memory_space=pltpu.VMEM)
    anywhere = pl.BlockSpec(memory_space=pl.ANY)
    dma = pltpu.SemaphoreType.DMA
    mask_lanes = genes + length + -length % 128
    share_shapes = [(share, columns) for _, share, columns in layers]
    chunks = len(items) + 1
    results = pl.pallas_call(
        functools.partial(everything, layers, len(VECTORS)),
        out_shape=(jax.ShapeDtypeStruct((tokens, genes), full),)
        + tuple(jax.ShapeDtypeStruct(shape, low) for shape in share_shapes)
        + (jax.ShapeDtypeStruct((SUM_ROWS, 128), full),),
        in_specs=[vmem] * (5 + len(VECTORS)) + [anywhere] * 11,
        out_specs=(anywhere,) * (2 + len(layers)),
        scratch_shapes=[
            pltpu.VMEM((SLOTS, WIDE, WIDE), low),
            pltpu.VMEM((8, mask_lanes), full),
            pltpu.VMEM((2, 8, mask_lanes), full),
            pltpu.VMEM((rows, width), full),
            pltpu.VMEM((2, rows, genes), low),
            pltpu.VMEM((2, rows, latents), low),
            pltpu.VMEM((2, rows, width), low),
            pltpu.VMEM((2, rows, width), low),
            pltpu.VMEM((2, tokens, 2 * width), low),
            pltpu.VMEM((tokens, width), low),
            pltpu.VMEM((HEADS // 2, 2 * tokens, 2 * tokens), full),
            pltpu.VMEM((2, tokens, 2 * width), full),
            pltpu.VMEM((tokens, 2 * width), full),
            pltpu.VMEM((2, rows, width), low),
            pltpu.VMEM((2, rows, width), low),
            pltpu.VMEM((5, tokens, width), full),
            pltpu.VMEM((5, tokens, 128), full),
            pltpu.VMEM((tokens, hidden), full),
            pltpu.VMEM((tokens, width), full),
            pltpu.VMEM((tokens, genes), full),
            pltpu.VMEM((GROUP, tokens, a_cols), low),
            pltpu.VMEM((GROUP, tokens, a_cols), low),
            pltpu.VMEM((a_cols, GROUP * tokens), low),
            pltpu.VMEM((GROUP, tokens, b_cols), low),
            pltpu.VMEM((GROUP, SUM_ROWS, 128), full),
            pltpu.VMEM((GROUP, SUM_ROWS, 128), full),
            pltpu.VMEM((rows_all, WIDE), low),
            pltpu.VMEM((rows_all, WIDE), low),
            pltpu.VMEM((SUM_ROWS, 128), full),
            pltpu.VMEM((SUM_ROWS, 128), full),
            dma((SLOTS,)),
            dma((4, 2)),
            dma((4, 2)),
            dma((4,)),
            dma((3,)),
            dma((3,)),
            dma((4,)),
            dma((len(layers), GROUP)),
            dma((len(layers), GROUP)),
            dma((len(layers),)),
            dma((GROUP,)),
            dma((GROUP,)),
            dma((len(BLOCKS), 9)),
            dma((len(BLOCKS), 9)),
            dma((chunks, 2)),
            dma((chunks, 2)),
            dma((chunks,)),
        ],
        compiler_params=pltpu.CompilerParams(
            collective_id=0, has_side_effects=True, vmem_limit_bytes=63 * 1024 * 1024
        ),
    )(
        expression,
        gene_masks,
        segment_ids,
        comp_mean,
        comp_logvar,
        *[given[name].reshape(1, -1) for name in VECTORS],
        positions(length, width),
        targets,
        noise,
        *weights.values(),
    )
    input_grad, sums, tail = results[0], results[1:-1], results[-1]

    def sum_shape(name, count):
        return (count, 64) if name in (COMP_MEAN, COMP_LOGVAR) else (1, count * 128)

    finished = pl.pallas_call(
        functools.partial(finish, layers),
        out_shape=tuple(jax.ShapeDtypeStruct(shape, full) for shape in share_shapes)
        + (jax.ShapeDtypeStruct((tokens, genes), full),)
        + tuple(jax.ShapeDtypeStruct(sum_shape(name, count), full) for name, count in SUMS),
        in_specs=[anywhere] * (len(layers) + 2),
        out_specs=(anywhere,) * (len(layers) + 1 + len(SUMS)),
        scratch_shapes=[pltpu.VMEM(shape, low) for shape in share_shapes]
        + [pltpu.VMEM(shape, full) for shape in share_shapes]
        + [
            pltpu.VMEM((tokens, genes), full),
            pltpu.VMEM((SUM_ROWS, 128), full),
            pltpu.VMEM((SUMS[0][1], 64), full),
            pltpu.VMEM((SUMS[1][1], 64), full),
            dma((len(layers),)),
            dma((len(layers),)),
            dma((3,)),
            dma((SUM_ROWS,)),
        ],
        compiler_params=pltpu.CompilerParams(vmem_limit_bytes=63 * 1024 * 1024),
    )(*sums, input_grad, tail)

    groups = lax.axis_size("dp") // GROUP
    d = lax.axis_index("dp")

    def shared_out(values, axis):
        if groups == 1:
            return values
        across = [[g * GROUP + r for g in range(groups)] for r in range(GROUP)]
        within = [[g * GROUP + r for r in range(GROUP)] for g in range(groups)]
        values = lax.psum(values, "dp", axis_index_groups=across)
        values = lax.all_gather(values, "dp", axis=axis, tiled=True, axis_index_groups=within)
        size = values.shape[axis] // (groups * GROUP)
        return lax.dynamic_slice_in_dim(values, d * size, size, axis=axis)

    grads = {}
    for name, values in zip(LAYERS, finished):
        grads[name] = shared_out(values, 0)
    for (name, _), values in zip(SUMS, finished[len(layers) + 1 :]):
        if name in (COMP_MEAN, COMP_LOGVAR):
            grads[name] = shared_out(values, 1)
        else:
            grads[name] = shared_out(values.reshape(-1), 0)
    return (
        finished[len(layers)].reshape(seqs, rows, genes),
        grads[GENE],
        grads[EMB_GAIN],
        grads[EMB_SHIFT],
        grads[ATTN_GAIN],
        grads[ATTN_SHIFT],
        grads[QKV],
        grads[B_QUERY],
        grads[B_VALUE],
        grads[OUT],
        grads[B_OUT],
        grads[FFN_GAIN],
        grads[FFN_SHIFT],
        grads[UP],
        grads[B_UP],
        grads[DOWN],
        grads[B_DOWN],
        grads[BOT_GAIN],
        grads[BOT_SHIFT],
        grads[ENC],
        grads[B_ENC],
        grads[COMP_MEAN],
        grads[COMP_LOGVAR],
        grads[LAT],
        grads[B_LAT],
        grads[DEC_GAIN],
        grads[DEC_SHIFT],
        grads[DEC],
        grads[B_DEC],
    )


def solution(mesh):
    rows = P("dp", "phase", None)
    return jax.shard_map(
        body,
        mesh=mesh,
        in_specs=(rows, rows, rows, P("dp", None), P("dp", None)) + (P(),) * 27,
        out_specs=(
            rows,
            P("dp", None),
            P("dp"),
            P("dp"),
            P("dp"),
            P("dp"),
            P("dp", None),
            P("dp"),
            P("dp"),
            P("dp", None),
            P("dp"),
            P("dp"),
            P("dp"),
            P("dp", None),
            P("dp"),
            P("dp", None),
            P("dp"),
            P("dp"),
            P("dp"),
            P("dp", None),
            P("dp"),
            P(None, "dp"),
            P(None, "dp"),
            P("dp", None),
            P("dp"),
            P("dp"),
            P("dp"),
            P("dp", None),
            P("dp"),
        ),
        check_vma=False,
    )
```

```python
import functools
import math

import jax
import jax.numpy as jnp
import numpy as np
from jax import lax
from jax.experimental import pallas as pl
from jax.experimental.pallas import tpu as pltpu
from jax.sharding import PartitionSpec as P

HEADS = 16
GROUP = 8
PIECE = 128
WIDE = 1024
SLOTS = 4

norm_eps = 1e-05
mask_fill = -1000000000.0
MESH = pl.DeviceIdType.MESH

(
    H2,
    DOWN,
    GENE,
    UP,
    QKV,
    DEC,
    ENC,
    OUT,
    LAT,
    EMB_GAIN,
    EMB_SHIFT,
    ATTN_GAIN,
    ATTN_SHIFT,
    B_QKV,
    B_QUERY,
    B_VALUE,
    B_OUT,
    FFN_GAIN,
    FFN_SHIFT,
    B_UP,
    B_DOWN,
    BOT_GAIN,
    BOT_SHIFT,
    B_ENC,
    COMP_MEAN,
    COMP_LOGVAR,
    B_LAT,
    DEC_GAIN,
    DEC_SHIFT,
    B_DEC,
) = range(30)


LAYERS = (DEC, DOWN, LAT, ENC, UP, OUT, QKV, GENE)
VECTORS = (
    EMB_GAIN,
    EMB_SHIFT,
    ATTN_GAIN,
    ATTN_SHIFT,
    B_QKV,
    B_OUT,
    FFN_GAIN,
    FFN_SHIFT,
    B_UP,
    B_DOWN,
    BOT_GAIN,
    BOT_SHIFT,
    B_ENC,
    B_LAT,
    DEC_GAIN,
    DEC_SHIFT,
    B_DEC,
)
SUMS = (
    (COMP_MEAN, 16),
    (COMP_LOGVAR, 16),
    (EMB_GAIN, 1),
    (EMB_SHIFT, 1),
    (ATTN_GAIN, 1),
    (ATTN_SHIFT, 1),
    (B_QUERY, 1),
    (B_VALUE, 1),
    (B_OUT, 1),
    (FFN_GAIN, 1),
    (FFN_SHIFT, 1),
    (B_UP, 4),
    (B_DOWN, 1),
    (BOT_GAIN, 1),
    (BOT_SHIFT, 1),
    (B_ENC, 1),
    (B_LAT, 1),
    (DEC_GAIN, 1),
    (DEC_SHIFT, 1),
    (B_DEC, 2),
)
SUM_AT = {name: sum(n for _, n in SUMS[:i]) for i, (name, _) in enumerate(SUMS)}
SUM_ROWS = 64


def mm(left, right):
    return jnp.dot(left, right, preferred_element_type=jnp.float32)


def mm_last(left, right):
    return lax.dot_general(
        left, right, (((1,), (1,)), ((), ())), preferred_element_type=jnp.float32
    )


def mm_first(left, right):
    return lax.dot_general(
        left, right, (((0,), (0,)), ((), ())), preferred_element_type=jnp.float32
    )


def normed(values):
    center = jnp.mean(values, axis=-1, keepdims=True)
    centered = values - center
    spread = jnp.mean(centered * centered, axis=-1, keepdims=True)
    scale = lax.rsqrt(spread + norm_eps)
    return centered * scale, scale


def normed_back(grad, hat, scale, gain):
    pulled = grad * gain
    mean = jnp.mean(pulled, axis=-1, keepdims=True)
    along = jnp.mean(pulled * hat, axis=-1, keepdims=True)
    return scale * (pulled - mean - hat * along)


def column_sums(values):
    return jnp.sum(values.astype(jnp.float32), axis=0, keepdims=True)


def gelu(values):
    return values * (0.5 * (1.0 + lax.erf(values * (0.5**0.5))))


def gelu_slope(values):
    bell = 0.5 * (1.0 + lax.erf(values * (0.5**0.5)))
    return bell + values * jnp.exp(-0.5 * values * values) * (2.0 * math.pi) ** -0.5


MADE_HERE = (DOWN, UP)

BLOCKS = (
    (H2, 0, 1024, 512),
    (DEC, 0, 512, 128),
    (DEC, 512, 512, 256),
    (DEC, 1024, 1024, 512),
    (DOWN, 0, 1024, 512),
    (LAT, 0, 1024, 512),
    (ENC, 0, 1024, 512),
    (UP, 0, 1024, 512),
    (UP, 1024, 1024, 512),
    (UP, 2048, 1024, 512),
    (UP, 3072, 1024, 512),
    (OUT, 0, 1024, 512),
    (QKV, 0, 1024, 512),
    (QKV, 1024, 1024, 512),
    (QKV, 2048, 1024, 512),
    (GENE, 0, 1024, 256),
)


def grad_plan(layers):
    a_off, b_off, t_off, items, place = {}, {}, {}, [], {}
    a_at, b_at, t_at, row = 0, 0, 0, 0
    shares = {name: share for name, share, _ in layers}
    for name, share, columns in layers:
        b_off[name], t_off[name] = b_at, t_at
        if name not in MADE_HERE:
            a_off[name] = a_at
            a_at += -(-share // PIECE) * PIECE
        for block in range(columns // WIDE):
            for start in range(0, share, PIECE):
                place[name, block, start] = row
                row += min(PIECE, share - start)
        t_at += -(-share // PIECE) * PIECE
        b_at += columns
    b_off[H2] = b_at
    shares[H2] = 0
    for block, (name, first, columns, step) in enumerate(BLOCKS):
        for start in range(0, shares[name], PIECE):
            rows = min(PIECE, shares[name] - start)
            for col in range(first, first + columns, step):
                items.append((block, start, rows, col, step, place[name, col // WIDE, start]))
    return a_off, b_off, t_off, items, row, a_at, b_at + WIDE, t_at


ORDER = (
    0, 1, 2, 3, 100, 4, 5, 6, 7, 8, 9, 200, 101, 102, 10, 11, 12, 13,
    300, 14, 15, 201, 400, 1000, 202, 301, 104, 16, 401, 500, 302, 501, 502, 503, 402, 600,
    504, 601, 505, 17, 204, 103, 107, 700, 701, 602, 603, 604, 605, 304, 800, 801, 18, 702,
    703, 404, 704, 508, 509, 19, 510, 203, 108, 705, 511, 512, 905, 513, 514, 20, 515, 207,
    109, 802, 803, 804, 805, 608, 609, 303, 21, 610, 403, 708, 506, 611, 208, 110, 507, 903,
    709, 612, 808, 902, 307, 710, 613, 809, 22, 209, 111, 407, 520, 521, 711, 308, 810, 712,
    713, 614, 615, 408, 522, 523, 811, 210, 112, 606, 812, 714, 607, 813, 23, 309, 715, 814,
    620, 706, 621, 409, 524, 525, 211, 113, 815, 707, 416, 622, 310, 720, 806, 623, 410, 526,
    544, 721, 527, 807, 624, 212, 114, 722, 820, 625, 311, 723, 626, 411, 528, 529, 821, 724,
    213, 115, 822, 627, 312, 725, 823, 628, 412, 726, 530, 531, 629, 644, 824, 214, 106, 727,
    825, 313, 630, 728, 826, 413, 532, 631, 533, 729, 827, 215, 105, 730, 744, 314, 828, 632,
    731, 414, 534, 535, 633, 829, 206, 830, 732, 315, 634, 831, 844, 733, 415, 536, 537, 538,
    635, 539, 540, 541, 205, 734, 542, 543, 636, 832, 833, 306, 637, 735, 638, 305, 406, 736,
    518, 639, 519, 737, 834, 640, 405, 738, 516, 641, 517, 835, 739, 836, 642, 740, 837, 643,
    741, 838, 742, 839, 618, 743, 840, 841, 619, 842, 616, 843, 718, 617, 719, 716, 818, 717,
    819, 816, 817,
)


def everything(layers, n_vec, *refs):
    low, full = jnp.bfloat16, jnp.float32
    refs = list(refs)

    def pop(count):
        taken = refs[:count]
        del refs[:count]
        return taken

    expr_ref, gene_masks_ref, segments_ref, mean_ref, logvar_ref = pop(5)
    vec_refs = dict(zip(VECTORS, pop(n_vec)))
    table_ref, target_ref, noise_ref = pop(3)
    w_gene, w_qkv, w_out, w_up, w_down, w_enc, w_lat, w_dec = pop(8)
    (input_ref,) = pop(1)
    out_refs = dict(zip([name for name, _, _ in layers], pop(len(layers))))
    (tail_ref,) = pop(1)
    ring, masks_own, masks_all, table, target_in, noise_in, x1_out, x1_in = pop(8)
    kv_all, query_own, probs, dkv_part, dkv_in, dx_out, dx_in = pop(7)
    hats, scales, befores, mixed_grad, input_grad = pop(5)
    a_src, a_all, turned, up_part, b_all, v_src, v_all, near, far, v_near, v_far = pop(11)
    ring_sem, hand_send, hand_recv, hand_local, pair_send, pair_recv = pop(6)
    one_sem, a_send, a_recv, a_local, v_send, v_recv, b_send, b_recv, c_send, c_recv, o_sem = pop(11)

    d = lax.axis_index("dp")
    z = lax.axis_index("phase")
    base = (d // GROUP) * GROUP
    r = d % GROUP
    core, cx, cy = r % 2, (r // 2) % 2, r // 4
    partner = d + 1 - 2 * core
    owner = d - core + z // 2
    own = core == z // 2
    rc, rx, ry = r + 1 - 2 * core, r + 2 - 4 * cx, r + 4 - 8 * cy
    rxc, ryc = rx + 1 - 2 * core, ry + 1 - 2 * core
    rd = rx + 4 - 8 * cy
    rdc = rd + 1 - 2 * core
    middle = (z % 3) != 0
    inward = z + 1 - 2 * (z // 2)
    outward = z - 1 + 2 * (z // 2)
    a_off, b_off, t_off, items, _, _, _, _ = grad_plan(layers)
    blocks = len(BLOCKS)
    shares = {name: share for name, share, _ in layers}
    index_of = {name: index for index, (name, _, _) in enumerate(layers)}
    seqs, rows, genes = expr_ref.shape
    tokens = seqs * rows
    width = table.shape[1]
    hidden = w_up.shape[1]
    length = segments_ref.shape[1]
    wide = WIDE

    barrier = pltpu.get_barrier_semaphore()

    def greet(to):
        pl.semaphore_signal(barrier, inc=1, device_id=to, device_id_type=MESH)

    for step in range(1, GROUP):
        greet((base + (r + step) % GROUP, z))
    greet((d, inward))

    @pl.when(middle)
    def _():
        greet((d, outward))

    for i in range(2):

        @pl.when(jnp.logical_not(own & (z % 2 == i)))
        def _():
            greet((owner, 2 * core + i))

    def barrier_wait():
        pl.semaphore_wait(barrier, GROUP + 1 + (z % 3 + 1) // 2 + (core + z // 2) % 2)

    def remote(src, dst, send, recv, to):
        return pltpu.make_async_remote_copy(
            src_ref=src,
            dst_ref=dst,
            send_sem=send,
            recv_sem=recv,
            device_id=to,
            device_id_type=MESH,
        )

    def columns_of(name):
        return pl.ds(a_off[name], -(-shares[name] // PIECE) * PIECE)

    def a_copy(name, step, slot):
        at, index, to = columns_of(name), index_of[name], (r + step) % GROUP
        return remote(
            a_src.at[to, :, at],
            a_all.at[slot, :, at],
            a_send.at[index, step],
            a_recv.at[index, step],
            (base + to, z),
        )

    def a_own(name):
        at = columns_of(name)
        return pltpu.make_async_copy(
            a_src.at[r, :, at], a_all.at[r, :, at], a_local.at[index_of[name]]
        )

    def send_a(name):
        for step in range(1, GROUP):
            a_copy(name, step, r).start()
        a_own(name).start()

    def send_late(index):
        send_a(layers[index][0])

    def arrive_a(name):
        a_own(name).wait()
        for step in range(1, GROUP):
            a_copy(name, step, (r + GROUP - step) % GROUP).wait_recv()

    def v_copy(step, slot):
        to = (r + step) % GROUP
        return remote(
            v_src.at[to], v_all.at[slot], v_send.at[step], v_recv.at[step], (base + to, z)
        )

    own_sums = pltpu.make_async_copy(v_src.at[r], v_all.at[r], one_sem.at[0])

    comes = (rx, ry, rc, rxc, ryc, rd, rd, rdc, rdc)
    goes = (r, r, r, rx, ry, rx, ry, rd, rd)

    def b_copy(kind, block, source):
        name, first, size, _ = BLOCKS[block]
        col = b_off[name] + first
        if kind >= 5:
            size //= 2
        if kind in (6, 8):
            col += size
        to = (rx, ry, rc, rc, rc, ry, rx, rc, rc)[kind]
        view = b_all.at[source, :, pl.ds(col, size)]
        return remote(view, view, b_send.at[block, kind], b_recv.at[block, kind], (base + to, z))

    def b_start(kind, block):
        b_copy(kind, block, goes[kind]).start()

    def b_arrive(kind, block):
        b_copy(kind, block, comes[kind]).wait_recv()

    vectors = len(items)

    def place_of(ref, v_ref, index):
        if index == vectors:
            return v_ref
        _, _, count, col, size, row = items[index]
        return ref.at[pl.ds(row, count), pl.ds(col % WIDE, size)]

    def to_middle(index, to):
        ref = place_of(near, v_near, index)
        return remote(ref, ref, c_send.at[index, 0], c_recv.at[index, 0], (d, to))

    def across(index):
        src, dst = place_of(near, v_near, index), place_of(far, v_far, index)
        return remote(src, dst, c_send.at[index, 1], c_recv.at[index, 1], (d, inward))

    def to_end(index, to):
        ref = place_of(far, v_far, index)
        return remote(ref, ref, c_send.at[index, 0], c_recv.at[index, 0], (d, to))

    def result(index, ref, v_ref):
        src = place_of(ref, v_ref, index)
        if index == vectors:
            return pltpu.make_async_copy(src, tail_ref, o_sem.at[index])
        block, start, count, col, size, _ = items[index]
        to = out_refs[BLOCKS[block][0]].at[pl.ds(start, count), pl.ds(col, size)]
        return pltpu.make_async_copy(src, to, o_sem.at[index])

    def product(index):
        if index == vectors:
            return jnp.sum(v_all[...], axis=0)
        block, start, count, col, size, _ = items[index]
        name = BLOCKS[block][0]
        a_at = t_off[name] + start
        b_at = b_off[name] + col
        right = b_all[:, :, b_at : b_at + size].reshape(-1, size)
        value = mm(turned[a_at : a_at + PIECE, :], right)
        if count < PIECE:
            value = jnp.where(r % 2 == 1, value[count : 2 * count], value[:count])
        return value

    def end_push(index):
        @pl.when(jnp.logical_not(middle))
        def _():
            ref = place_of(near, v_near, index)
            ref[...] = product(index).astype(ref.dtype)
            to_middle(index, inward).start()

    def middle_join(index):
        @pl.when(middle)
        def _():
            value = product(index)
            to_middle(index, inward).wait_recv()
            ref = place_of(near, v_near, index)
            ref[...] = (value + ref[...].astype(full)).astype(ref.dtype)
            across(index).start()

    totals, lands, gone = [], [], []

    def middle_sent(index):
        across(index).wait_send()
        to_end(index, outward).wait_send()
        result(index, far, v_far).wait()

    def end_sent(index):
        to_middle(index, inward).wait_send()
        result(index, far, v_far).wait()

    def middle_total(index):
        totals.append(index)

        @pl.when(middle)
        def _():
            if len(totals) > 3:
                middle_sent(totals[-4])
            across(index).wait_recv()
            mine, theirs = place_of(near, v_near, index), place_of(far, v_far, index)
            both = mine[...].astype(full) + theirs[...].astype(full)
            theirs[...] = both.astype(theirs.dtype)
            to_end(index, outward).start()
            result(index, far, v_far).start()

    def end_land(index):
        lands.append(index)

        @pl.when(jnp.logical_not(middle))
        def _():
            if len(lands) > 3:
                end_sent(lands[-4])
            to_end(index, inward).wait_recv()
            result(index, far, v_far).start()

    arrived, waited = set(), set()

    up_columns = pl.ds(pl.multiple_of(r * shares[DOWN], PIECE), shares[DOWN])
    up_copy = pltpu.make_async_copy(w_up.at[:, up_columns], up_part, one_sem.at[4])
    up_copy.start()

    def make_lefts(_):
        own_columns = pl.ds(pl.multiple_of(b_off[H2] + r * PIECE, PIECE), PIECE)
        at = t_off[UP]
        turned[at : at + PIECE, :] = b_all[:, :, own_columns].reshape(-1, PIECE).T
        up_copy.wait()
        bias = vec_refs[B_UP][:, up_columns]
        count = GROUP // 2
        for slot in range(0, GROUP, count):
            h2 = b_all[slot : slot + count, :, b_off[H2] : b_off[H2] + width].reshape(-1, width)
            active = gelu(mm(h2, up_part[...]) + bias).astype(low)
            turned[
                t_off[DOWN] : t_off[DOWN] + shares[DOWN],
                slot * tokens : (slot + count) * tokens,
            ] = active.T

    def block_sent(block):
        for kind in range(9):
            b_copy(kind, block, goes[kind]).wait_send()

    def layer_sent(name):
        for step in range(1, GROUP):
            a_copy(name, step, r).wait_send()

    def get(block):
        if len(gone) > 2 and gone[-3] not in waited:
            waited.add(gone[-3])
            block_sent(gone[-3])
        if block == blocks:
            own_sums.wait()
            for step in range(1, GROUP):
                v_copy(step, (r + GROUP - step) % GROUP).wait_recv()
            return
        gone.append(block)
        for kind in (2, 3, 4, 7, 8):
            b_arrive(kind, block)
        name = BLOCKS[block][0]
        if name in a_off and name not in arrived:
            arrived.add(name)
            arrive_a(name)
            layer_sent(name)
            for start in range(0, shares[name], PIECE):
                at, to = a_off[name] + start, t_off[name] + start
                turned[to : to + PIECE, :] = a_all[:, :, at : at + PIECE].reshape(-1, PIECE).T

    table_copy = pltpu.make_async_copy(
        table_ref.at[pl.ds(z * rows, rows), :], table, one_sem.at[1]
    )
    input_copy = pltpu.make_async_copy(input_grad, input_ref, one_sem.at[2])
    pair_local = one_sem.at[3]
    table_copy.start()

    def rows_work():
        stream = []
        for j in range(genes // wide):
            stream.append(w_gene.at[pl.ds(j * wide, wide), :])
        for j in (1, 2, 0):
            stream.append(w_qkv.at[:, pl.ds(j * wide, wide)])
        stream.append(w_out)
        for j in range(hidden // wide):
            stream.append(w_up.at[:, pl.ds(j * wide, wide)])
            stream.append(w_down.at[pl.ds(j * wide, wide), :])
        stream.append(w_enc)
        stream.append(w_lat)
        for j in range(genes // wide):
            stream.append(w_dec.at[:, pl.ds(j * wide, wide)])
        stream.append(w_lat)
        stream.append(w_enc)
        for j in range(hidden // wide):
            stream.append(w_down.at[pl.ds(j * wide, wide), :])
            stream.append(w_up.at[:, pl.ds(j * wide, wide)])
        stream.append(w_out)
        for j in range(3):
            stream.append(w_qkv.at[:, pl.ds(j * wide, wide)])
        for j in range(genes // wide):
            stream.append(w_gene.at[pl.ds(j * wide, wide), :])

        def load(k):
            depth = stream[k].shape[0]
            return pltpu.make_async_copy(
                stream[k], ring.at[k % SLOTS, pl.ds(0, depth), :], ring_sem.at[k % SLOTS]
            )

        def fetch(k):
            if k < len(stream):
                load(k).start()

        place = [0]

        def take():
            k = place[0]
            place[0] += 1
            load(k).wait()
            return k

        def block(k):
            return ring[k % SLOTS, : stream[k].shape[0], :]

        for k in range(SLOTS):
            fetch(k)

        def hand(which, src, dst, i):
            return pltpu.make_async_remote_copy(
                src_ref=src.at[i],
                dst_ref=dst.at[z % 2],
                send_sem=hand_send.at[which, i],
                recv_sem=hand_recv.at[which, z % 2],
                device_id=(owner, 2 * core + i),
                device_id_type=MESH,
            )

        def hand_here(which, src, dst, i):
            return pltpu.make_async_copy(src.at[i], dst.at[i], hand_local.at[which])

        def hand_start(which, src, dst):
            for i in range(2):
                here = own & (z % 2 == i)

                @pl.when(here)
                def _():
                    hand_here(which, src, dst, i).start()

                @pl.when(jnp.logical_not(here))
                def _():
                    hand(which, src, dst, i).start()

        def hand_arrive(which, src, dst):
            for i in range(2):
                here = own & (z % 2 == i)

                @pl.when(here)
                def _():
                    hand_here(which, src, dst, i).wait()

                @pl.when(jnp.logical_not(here))
                def _():
                    pltpu.make_async_remote_copy(
                        src_ref=src.at[i],
                        dst_ref=dst.at[i],
                        send_sem=hand_send.at[which, i],
                        recv_sem=hand_recv.at[which, i],
                        device_id=(owner, 2 * core + i),
                        device_id_type=MESH,
                    ).wait_recv()

        def hand_sent(which, src, dst):
            for i in range(2):
                @pl.when(jnp.logical_not(own & (z % 2 == i)))
                def _():
                    hand(which, src, dst, i).wait_send()

        def pair(which, src, dst):
            return pltpu.make_async_remote_copy(
                src_ref=src,
                dst_ref=dst,
                send_sem=pair_send.at[which],
                recv_sem=pair_recv.at[which],
                device_id=(partner, z),
                device_id_type=MESH,
            )

        masks_own[:seqs, :genes] = gene_masks_ref[...].astype(full)
        masks_own[:seqs, genes : genes + length] = segments_ref[...].astype(full)
        own_masks = pltpu.make_async_copy(masks_own, masks_all.at[core], pair_local)
        own_masks.start()

        def vec(name, j=0):
            return vec_refs[name][:, j * wide : (j + 1) * wide]

        def put_a(name, values):
            off, share = a_off[name], shares[name]
            step = max(share, PIECE)
            for o in range(GROUP):
                start = o * share // step * step
                a_src[o, :, off : off + step] = values[:, start : start + step]

        def put_b(name, j, values):
            at = b_off[name] + j * wide
            b_all[r, :, at : at + wide] = values

        def put_sum(name, values, j=0):
            each = SUM_LANES[name]
            for o in range(values.shape[1] // 128):
                at = j * wide + o * 128
                to, row = at // (128 * each), SUM_AT[name] + at // 128 % each
                v_src[to, row : row + 1, :] = values[:, o * 128 : o * 128 + 128]

        def normalize(index, values, gain, shift):
            hat, scale = normed(values)
            hats[index] = hat
            scales[index] = jnp.broadcast_to(scale, scales.shape[1:])
            return hat * vec(gain) + vec(shift)

        def normalize_back(index, grad, gain, gain_name, shift_name):
            hat, scale = hats[index], scales[index, :, :1]
            put_sum(gain_name, jnp.sum(grad * hat, axis=0, keepdims=True))
            put_sum(shift_name, jnp.sum(grad, axis=0, keepdims=True))
            return normed_back(grad, hat, scale, vec(gain))

        keep = 1.0 - masks_own[:seqs, :genes]
        keep = jnp.concatenate(
            [jnp.broadcast_to(keep[s : s + 1], (rows, genes)) for s in range(seqs)], axis=0
        )
        masked = (expr_ref[...].reshape(tokens, genes).astype(full) * keep).astype(low)
        put_a(GENE, masked)
        table_copy.wait()
        embedded = jnp.concatenate([table[...]] * seqs, axis=0)
        for j in range(genes // wide):
            k = take()
            embedded += mm(masked[:, j * wide : (j + 1) * wide], block(k))
            fetch(k + SLOTS)
        x1_out[...] = (
            normalize(0, embedded, EMB_GAIN, EMB_SHIFT).astype(low).reshape(seqs, rows, width)
        )
        barrier_wait()
        hand_start(0, x1_out, x1_in)
        pair(0, masks_own, masks_all.at[core]).start()
        send_a(GENE)
        hand_start(1, noise_ref, noise_in)
        hand_start(2, target_ref, target_in)
        yield
        own_masks.wait()
        pair(0, masks_own, masks_all.at[1 - core]).wait_recv()
        odd = z % 2 == 1
        both_masks = masks_all[pl.ds(z // 2, 1)][0]
        mask_row = jnp.where(odd, both_masks[1:2], both_masks[0:1])
        gene_row = mask_row[:, :genes]
        segments = mask_row[:, genes : genes + length]
        place_q = lax.broadcasted_iota(jnp.int32, (tokens, length), 0) + core * tokens
        place_k = lax.broadcasted_iota(jnp.int32, (tokens, length), 1)
        own_segments = jnp.sum(
            jnp.where(place_q == place_k, segments, 0.0), axis=-1, keepdims=True
        )
        same = own_segments == segments
        same = jnp.concatenate([same.astype(full)] * 2, axis=0) > 0.5

        hand_arrive(0, x1_out, x1_in)
        x1 = x1_in[...].reshape(tokens, width).astype(full)
        h1 = normalize(1, x1, ATTN_GAIN, ATTN_SHIFT).astype(low)
        put_a(QKV, h1)
        send_a(QKV)
        head = width // HEADS
        scale = head**-0.5
        for j in (1, 2):
            k = take()
            kv_all[core, :, (j - 1) * wide : j * wide] = (
                mm(h1, block(k)) + vec(B_QKV, j)
            ).astype(low)
            fetch(k + SLOTS)
        pair(1, kv_all.at[core], kv_all.at[core]).start()
        k = take()
        query_own[...] = (mm(h1, block(k)) + vec(B_QKV, 0)).astype(low)
        fetch(k + SLOTS)
        yield
        pair(1, kv_all.at[core], kv_all.at[1 - core]).wait_recv()

        lanes = lax.broadcasted_iota(jnp.int32, (tokens, 2 * head), 1)
        first = lanes < head
        pairs = HEADS // 2

        def two(values):
            none = jnp.zeros_like(values)
            return jnp.concatenate([jnp.where(first, values, none), jnp.where(first, none, values)], axis=0)

        def one(values):
            return jnp.where(first, values[:tokens], values[tokens:])

        def columns(p):
            return pl.ds(pl.multiple_of(p * 2 * head, 2 * head), 2 * head)

        def keys_of(p):
            return kv_all[:, :, columns(p)].reshape(length, 2 * head)

        def values_of(p):
            at = pl.ds(pl.multiple_of(width + p * 2 * head, 2 * head), 2 * head)
            return kv_all[:, :, at].reshape(length, 2 * head)

        def attend(p, carry):
            scores = mm_last(two(query_own[:, columns(p)]), keys_of(p)) * scale
            scores = jnp.where(same, scores, mask_fill)
            shifted = jnp.exp(scores - jnp.max(scores, axis=-1, keepdims=True))
            prob = shifted / jnp.sum(shifted, axis=-1, keepdims=True)
            probs[p] = prob
            att = one(mm(prob.astype(low), values_of(p))).astype(low)
            a_src[p, :, a_off[OUT] : a_off[OUT] + 2 * head] = att
            return carry

        lax.fori_loop(0, pairs, attend, 0)
        yield
        attended = jnp.concatenate(
            [a_src[o, :, a_off[OUT] : a_off[OUT] + 2 * head] for o in range(pairs)], axis=1
        )
        k = take()
        mixed = x1 + (mm(attended, block(k)) + vec(B_OUT))
        fetch(k + SLOTS)
        h2 = normalize(2, mixed, FFN_GAIN, FFN_SHIFT).astype(low)
        b_all[r, :, b_off[H2] : b_off[H2] + width] = h2
        yield
        x2 = mixed + vec(B_DOWN)
        for j in range(hidden // wide):
            k = take()
            before = mm(h2, block(k)) + vec(B_UP, j)
            fetch(k + SLOTS)
            befores[:, j * wide : (j + 1) * wide] = before
            active = gelu(before).astype(low)
            k = take()
            x2 += mm(active, block(k))
            fetch(k + SLOTS)
            yield
        x2 = x2.astype(low).astype(full)
        h3 = normalize(3, x2, BOT_GAIN, BOT_SHIFT).astype(low)
        put_a(ENC, h3)
        k_enc = take()
        moments = mm(h3, block(k_enc)) + vec(B_ENC)
        latents = width // 2
        logvar = moments[:, latents:]
        hand_arrive(1, noise_ref, noise_in)
        swing = jnp.exp(0.5 * logvar) * noise_in[...].reshape(tokens, latents).astype(full)
        latent = moments[:, :latents] + swing
        latent_low = latent.astype(low)
        put_a(LAT, latent_low)
        fetch(k_enc + SLOTS)
        k_lat = take()
        lat_before = mm(latent_low, block(k_lat)) + vec(B_LAT)
        fetch(k_lat + SLOTS)
        x3 = gelu(lat_before).astype(low).astype(full)
        h4 = normalize(4, x3, DEC_GAIN, DEC_SHIFT).astype(low)
        put_a(DEC, h4)
        send_a(DEC)
        yield
        hand_arrive(2, target_ref, target_in)

        grad = jnp.zeros((tokens, width), full)
        for j in range(genes // wide):
            k = take()
            at = slice(j * wide, (j + 1) * wide)
            predicted = mm(h4, block(k)) + vec(B_DEC, j)
            wanted = target_in[:, :, at].reshape(tokens, wide).astype(full)
            d_pred = (gene_row[:, at] * (predicted - wanted)).astype(low)
            put_b(DEC, j, d_pred)
            put_sum(B_DEC, column_sums(d_pred), j)
            grad += mm_last(d_pred, block(k))
            fetch(k + SLOTS)
            yield
        d_x3 = normalize_back(4, grad, DEC_GAIN, DEC_GAIN, DEC_SHIFT).astype(low).astype(full)
        d_lat = (gelu_slope(lat_before) * d_x3).astype(low)
        put_b(LAT, 0, d_lat)
        put_sum(B_LAT, column_sums(d_lat))
        k = take()
        d_latent = mm_last(d_lat, block(k))
        fetch(k + SLOTS)
        yield

        inverse = jnp.exp(-logvar_ref[...])
        volume = jnp.sum(logvar_ref[...], axis=-1, keepdims=True)
        count = mean_ref.shape[0]
        scaled = []
        for c in range(count):
            offset = latent - mean_ref[c : c + 1, :]
            quad = jnp.sum(offset * offset * inverse[c : c + 1], axis=-1, keepdims=True)
            scaled.append(-0.5 * (quad + volume[c : c + 1]))
        highest = functools.reduce(jnp.maximum, scaled)
        shares_c = [jnp.exp(s - highest) for s in scaled]
        whole = functools.reduce(jnp.add, shares_c)
        parts = [part / whole for part in shares_c]
        for c in range(count):
            pull = (latent - mean_ref[c : c + 1, :]) * inverse[c : c + 1]
            d_latent += parts[c] * pull
        d_moments = jnp.concatenate([d_latent, 0.5 * d_latent * swing - 0.5], axis=1).astype(low)
        put_b(ENC, 0, d_moments)
        put_sum(B_ENC, column_sums(d_moments))
        yield
        k = take()
        grad = mm_last(d_moments, block(k))
        fetch(k + SLOTS)
        g = normalize_back(3, grad, BOT_GAIN, BOT_GAIN, BOT_SHIFT).astype(low)
        put_b(DOWN, 0, g)
        put_sum(B_DOWN, column_sums(g))
        yield
        for c in range(count):
            offset = latent - mean_ref[c : c + 1, :]
            weighted = parts[c] * (offset * inverse[c : c + 1])
            mean_grad = -jnp.sum(weighted, axis=0, keepdims=True)
            logvar_grad = 0.5 * jnp.sum(parts[c] - weighted * offset, axis=0, keepdims=True)
            for o in range(GROUP):
                at = slice(o // 2 * 128, o // 2 * 128 + 128)
                row = SUM_AT[COMP_MEAN] + c
                v_src[o, row : row + 1, :] = mean_grad[:, at]
                row = SUM_AT[COMP_LOGVAR] + c
                v_src[o, row : row + 1, :] = logvar_grad[:, at]
        yield
        grad = jnp.zeros((tokens, width), full)
        for j in range(hidden // wide):
            k = take()
            d_active = mm_last(g, block(k))
            fetch(k + SLOTS)
            slope = gelu_slope(befores[:, j * wide : (j + 1) * wide])
            d_before = (slope * d_active).astype(low)
            put_b(UP, j, d_before)
            put_sum(B_UP, column_sums(d_before), j)
            k = take()
            grad += mm_last(d_before, block(k))
            fetch(k + SLOTS)
            yield
        d_mixed = g.astype(full) + normalize_back(2, grad, FFN_GAIN, FFN_GAIN, FFN_SHIFT)
        mixed_grad[...] = d_mixed
        da = d_mixed.astype(low)
        put_b(OUT, 0, da)
        put_sum(B_OUT, column_sums(da))
        k = take()
        x1_in[...] = mm_last(da, block(k)).astype(low).reshape(seqs, rows, width)
        fetch(k + SLOTS)
        yield
        q_at = b_off[QKV]

        def attend_back(p, carry):
            query = two(query_own[:, columns(p)])
            d_att = two(x1_in[:, :, columns(p)].reshape(tokens, 2 * head))
            prob = probs[p]
            keys = keys_of(p)
            d_value = mm_first(prob.astype(low), d_att)
            d_prob = mm_last(d_att, values_of(p))
            d_score = prob * (d_prob - jnp.sum(prob * d_prob, axis=-1, keepdims=True))
            d_score = d_score.astype(low)
            d_query = one(mm(d_score, keys)) * scale
            d_key = mm_first(d_score, query) * scale
            to = pl.ds(pl.multiple_of(q_at + p * 2 * head, 2 * head), 2 * head)
            b_all[r, :, to] = d_query.astype(low)
            dkv_part[:, :, columns(p)] = d_key.reshape(2, tokens, 2 * head)
            at = pl.ds(pl.multiple_of(width + p * 2 * head, 2 * head), 2 * head)
            dkv_part[:, :, at] = d_value.reshape(2, tokens, 2 * head)
            return carry

        lax.fori_loop(0, pairs // 2, attend_back, 0)
        yield
        lax.fori_loop(pairs // 2, pairs, attend_back, 0)
        pair(2, dkv_part.at[1 - core], dkv_in).start()
        yield
        d_query = b_all[r, :, q_at : q_at + wide]
        put_sum(B_QUERY, column_sums(d_query))
        k = take()
        grad = mm_last(d_query, block(k))
        fetch(k + SLOTS)
        pair(2, dkv_part.at[1 - core], dkv_in).wait_recv()
        for j in (1, 2):
            at = slice((j - 1) * wide, j * wide)
            d_part = (dkv_part[core, :, at] + dkv_in[:, at]).astype(low)
            put_b(QKV, j, d_part)
            if j == 2:
                put_sum(B_VALUE, column_sums(d_part))
            k = take()
            grad += mm_last(d_part, block(k))
            fetch(k + SLOTS)
        d_x1 = mixed_grad[...] + normalize_back(1, grad, ATTN_GAIN, ATTN_GAIN, ATTN_SHIFT)
        dx_out[...] = d_x1.astype(low).reshape(seqs, rows, width)
        hand_start(3, dx_out, dx_in)
        yield
        hand_arrive(3, dx_out, dx_in)
        d_x1 = dx_in[...].reshape(tokens, width).astype(full)
        d_embedded = normalize_back(0, d_x1, EMB_GAIN, EMB_GAIN, EMB_SHIFT).astype(low)
        put_b(GENE, 0, d_embedded)
        for j in range(genes // wide):
            k = take()
            at = slice(j * wide, (j + 1) * wide)
            input_grad[:, at] = mm_last(d_embedded, block(k)) * jnp.concatenate(
                [
                    jnp.broadcast_to(1.0 - masks_own[s : s + 1, at], (rows, wide))
                    for s in range(seqs)
                ],
                axis=0,
            )
        input_copy.start()
        for step in range(1, GROUP):
            v_copy(step, r).start()
        own_sums.start()
        yield
        input_copy.wait()
        hand_sent(0, x1_out, x1_in)
        hand_sent(1, noise_ref, noise_in)
        hand_sent(2, target_ref, target_in)
        hand_sent(3, dx_out, dx_in)
        pair(0, masks_own, masks_all.at[core]).wait_send()
        pair(1, kv_all.at[core], kv_all.at[core]).wait_send()
        pair(2, dkv_part.at[1 - core], dkv_in).wait_send()


    work = rows_work()
    for code in ORDER:
        kind, index = code // 100, code % 100
        if kind == 0:
            next(work)
        elif kind == 1:
            for way in (0, 1, 2):
                b_start(way, index)
        elif kind == 2:
            b_arrive(0, index)
            b_start(5, index)
            b_start(3, index)
            b_arrive(1, index)
            b_start(6, index)
            b_start(4, index)
        elif kind == 3:
            b_arrive(5, index)
            b_start(7, index)
            b_arrive(6, index)
            b_start(8, index)
        else:
            (get, end_push, middle_join, middle_total, end_land, send_late, make_lefts)[kind - 4](index)
    next(work, None)
    for block in gone[-3:]:
        if block not in waited:
            block_sent(block)
    for step in range(1, GROUP):
        v_copy(step, r).wait_send()

    @pl.when(middle)
    def _():
        for index in totals[-3:]:
            middle_sent(index)

    @pl.when(jnp.logical_not(middle))
    def _():
        for index in lands[-3:]:
            end_sent(index)


SUM_LANES = dict(SUMS)


def finish(layers, *refs):
    refs = list(refs)
    count = len(layers)
    low_refs, refs = refs[:count], refs[count:]
    input_ref, tail_ref = refs[:2]
    refs = refs[2:]
    full_refs, refs = refs[:count], refs[count:]
    input_out = refs[0]
    sum_refs = dict(zip([name for name, _ in SUMS], refs[1 : 1 + len(SUMS)]))
    refs = refs[1 + len(SUMS) :]
    low_bufs, full_bufs = refs[:count], refs[count : 2 * count]
    input_buf, tail_buf, mean_buf, logvar_buf, in_sem, out_sem, move_sem, sum_sem = refs[2 * count :]
    move_in = pltpu.make_async_copy(input_ref, input_buf, move_sem.at[0])
    move_out = pltpu.make_async_copy(input_buf, input_out, move_sem.at[1])
    tail_in = pltpu.make_async_copy(tail_ref, tail_buf, move_sem.at[2])
    ins = [
        pltpu.make_async_copy(src, dst, in_sem.at[i])
        for i, (src, dst) in enumerate(zip(low_refs, low_bufs))
    ]
    outs = [
        pltpu.make_async_copy(src, dst, out_sem.at[i])
        for i, (src, dst) in enumerate(zip(full_bufs, full_refs))
    ]
    for copy in ins:
        copy.start()
    tail_in.start()
    move_in.start()
    for i in range(count):
        ins[i].wait()
        full_bufs[i][...] = low_bufs[i][...].astype(jnp.float32)
        outs[i].start()
    move_in.wait()
    move_out.start()
    tail_in.wait()
    odd = lax.axis_index("dp") % 2 == 1
    rows_of = dict(SUMS)
    for name, buf in ((COMP_MEAN, mean_buf), (COMP_LOGVAR, logvar_buf)):
        both = tail_buf[SUM_AT[name] : SUM_AT[name] + rows_of[name], :]
        buf[...] = jnp.where(odd, both[:, 64:], both[:, :64])
    sums = [
        pltpu.make_async_copy(mean_buf, sum_refs[COMP_MEAN], sum_sem.at[0]),
        pltpu.make_async_copy(logvar_buf, sum_refs[COMP_LOGVAR], sum_sem.at[1]),
    ]
    for name, rows in SUMS[2:]:
        for row in range(rows):
            sums.append(
                pltpu.make_async_copy(
                    tail_buf.at[pl.ds(SUM_AT[name] + row, 1), :],
                    sum_refs[name].at[:, pl.ds(row * 128, 128)],
                    sum_sem.at[len(sums)],
                )
            )
    for copy in sums:
        copy.start()
    for copy in sums + outs:
        copy.wait()
    move_out.wait()


def positions(length, width):
    frequency = np.exp(np.arange(width // 2, dtype=np.float32) * np.float32(-2.0 * math.log(10000.0) / width))
    angles = np.arange(length, dtype=np.float32)[:, None] * frequency[None, :]
    return np.stack([np.sin(angles), np.cos(angles)], axis=-1).reshape(length, width)


def body(expression, targets, noise, gene_masks, segment_ids, w_gene, emb_gain, emb_shift, attn_gain, attn_shift, w_qkv, b_qkv, w_out, b_out, ffn_gain, ffn_shift, w_up, b_up, w_down, b_down, bot_gain, bot_shift, w_enc, b_enc, comp_mean, comp_logvar, w_lat, b_lat, dec_gain, dec_shift, w_dec, b_dec):
    low, full = jnp.bfloat16, jnp.float32
    seqs, rows, genes = expression.shape
    width = w_gene.shape[1]
    hidden = w_up.shape[1]
    latents = noise.shape[2]
    length = segment_ids.shape[1]
    tokens = seqs * rows
    given = {
        EMB_GAIN: emb_gain,
        EMB_SHIFT: emb_shift,
        ATTN_GAIN: attn_gain,
        ATTN_SHIFT: attn_shift,
        B_QKV: b_qkv,
        B_OUT: b_out,
        FFN_GAIN: ffn_gain,
        FFN_SHIFT: ffn_shift,
        B_UP: b_up,
        B_DOWN: b_down,
        BOT_GAIN: bot_gain,
        BOT_SHIFT: bot_shift,
        B_ENC: b_enc,
        B_LAT: b_lat,
        DEC_GAIN: dec_gain,
        DEC_SHIFT: dec_shift,
        B_DEC: b_dec,
    }
    weights = {
        GENE: w_gene,
        QKV: w_qkv,
        OUT: w_out,
        UP: w_up,
        DOWN: w_down,
        ENC: w_enc,
        LAT: w_lat,
        DEC: w_dec,
    }
    layers = [
        (name, weights[name].shape[0] // GROUP, weights[name].shape[1]) for name in LAYERS
    ]
    _, _, _, items, rows_all, a_cols, b_cols, t_rows = grad_plan(layers)
    vmem = pl.BlockSpec(memory_space=pltpu.VMEM)
    anywhere = pl.BlockSpec(memory_space=pl.ANY)
    dma = pltpu.SemaphoreType.DMA
    mask_lanes = genes + length + -length % 128
    share_shapes = [(share, columns) for _, share, columns in layers]
    chunks = len(items) + 1
    results = pl.pallas_call(
        functools.partial(everything, layers, len(VECTORS)),
        out_shape=(jax.ShapeDtypeStruct((tokens, genes), full),)
        + tuple(jax.ShapeDtypeStruct(shape, low) for shape in share_shapes)
        + (jax.ShapeDtypeStruct((SUM_ROWS, 128), full),),
        in_specs=[vmem] * (5 + len(VECTORS)) + [anywhere] * 11,
        out_specs=(anywhere,) * (2 + len(layers)),
        scratch_shapes=[
            pltpu.VMEM((SLOTS, WIDE, WIDE), low),
            pltpu.VMEM((8, mask_lanes), full),
            pltpu.VMEM((2, 8, mask_lanes), full),
            pltpu.VMEM((rows, width), full),
            pltpu.VMEM((2, rows, genes), low),
            pltpu.VMEM((2, rows, latents), low),
            pltpu.VMEM((2, rows, width), low),
            pltpu.VMEM((2, rows, width), low),
            pltpu.VMEM((2, tokens, 2 * width), low),
            pltpu.VMEM((tokens, width), low),
            pltpu.VMEM((HEADS // 2, 2 * tokens, 2 * tokens), full),
            pltpu.VMEM((2, tokens, 2 * width), full),
            pltpu.VMEM((tokens, 2 * width), full),
            pltpu.VMEM((2, rows, width), low),
            pltpu.VMEM((2, rows, width), low),
            pltpu.VMEM((5, tokens, width), full),
            pltpu.VMEM((5, tokens, 128), full),
            pltpu.VMEM((tokens, hidden), full),
            pltpu.VMEM((tokens, width), full),
            pltpu.VMEM((tokens, genes), full),
            pltpu.VMEM((GROUP, tokens, a_cols), low),
            pltpu.VMEM((GROUP, tokens, a_cols), low),
            pltpu.VMEM((t_rows, GROUP * tokens), low),
            pltpu.VMEM((width, hidden // GROUP), low),
            pltpu.VMEM((GROUP, tokens, b_cols), low),
            pltpu.VMEM((GROUP, SUM_ROWS, 128), full),
            pltpu.VMEM((GROUP, SUM_ROWS, 128), full),
            pltpu.VMEM((rows_all, WIDE), low),
            pltpu.VMEM((rows_all, WIDE), low),
            pltpu.VMEM((SUM_ROWS, 128), full),
            pltpu.VMEM((SUM_ROWS, 128), full),
            dma((SLOTS,)),
            dma((4, 2)),
            dma((4, 2)),
            dma((4,)),
            dma((3,)),
            dma((3,)),
            dma((5,)),
            dma((len(layers), GROUP)),
            dma((len(layers), GROUP)),
            dma((len(layers),)),
            dma((GROUP,)),
            dma((GROUP,)),
            dma((len(BLOCKS), 9)),
            dma((len(BLOCKS), 9)),
            dma((chunks, 2)),
            dma((chunks, 2)),
            dma((chunks,)),
        ],
        compiler_params=pltpu.CompilerParams(
            collective_id=0, has_side_effects=True, vmem_limit_bytes=63 * 1024 * 1024
        ),
    )(
        expression,
        gene_masks,
        segment_ids,
        comp_mean,
        comp_logvar,
        *[given[name].reshape(1, -1) for name in VECTORS],
        positions(length, width),
        targets,
        noise,
        *weights.values(),
    )
    input_grad, sums, tail = results[0], results[1:-1], results[-1]

    def sum_shape(name, count):
        return (count, 64) if name in (COMP_MEAN, COMP_LOGVAR) else (1, count * 128)

    finished = pl.pallas_call(
        functools.partial(finish, layers),
        out_shape=tuple(jax.ShapeDtypeStruct(shape, full) for shape in share_shapes)
        + (jax.ShapeDtypeStruct((tokens, genes), full),)
        + tuple(jax.ShapeDtypeStruct(sum_shape(name, count), full) for name, count in SUMS),
        in_specs=[anywhere] * (len(layers) + 2),
        out_specs=(anywhere,) * (len(layers) + 1 + len(SUMS)),
        scratch_shapes=[pltpu.VMEM(shape, low) for shape in share_shapes]
        + [pltpu.VMEM(shape, full) for shape in share_shapes]
        + [
            pltpu.VMEM((tokens, genes), full),
            pltpu.VMEM((SUM_ROWS, 128), full),
            pltpu.VMEM((SUMS[0][1], 64), full),
            pltpu.VMEM((SUMS[1][1], 64), full),
            dma((len(layers),)),
            dma((len(layers),)),
            dma((3,)),
            dma((SUM_ROWS,)),
        ],
        compiler_params=pltpu.CompilerParams(vmem_limit_bytes=63 * 1024 * 1024),
    )(*sums, input_grad, tail)

    groups = lax.axis_size("dp") // GROUP
    d = lax.axis_index("dp")

    def shared_out(values, axis):
        if groups == 1:
            return values
        across = [[g * GROUP + r for g in range(groups)] for r in range(GROUP)]
        within = [[g * GROUP + r for r in range(GROUP)] for g in range(groups)]
        values = lax.psum(values, "dp", axis_index_groups=across)
        values = lax.all_gather(values, "dp", axis=axis, tiled=True, axis_index_groups=within)
        size = values.shape[axis] // (groups * GROUP)
        return lax.dynamic_slice_in_dim(values, d * size, size, axis=axis)

    grads = {}
    for name, values in zip(LAYERS, finished):
        grads[name] = shared_out(values, 0)
    for (name, _), values in zip(SUMS, finished[len(layers) + 1 :]):
        if name in (COMP_MEAN, COMP_LOGVAR):
            grads[name] = shared_out(values, 1)
        else:
            grads[name] = shared_out(values.reshape(-1), 0)
    return (
        finished[len(layers)].reshape(seqs, rows, genes),
        grads[GENE],
        grads[EMB_GAIN],
        grads[EMB_SHIFT],
        grads[ATTN_GAIN],
        grads[ATTN_SHIFT],
        grads[QKV],
        grads[B_QUERY],
        grads[B_VALUE],
        grads[OUT],
        grads[B_OUT],
        grads[FFN_GAIN],
        grads[FFN_SHIFT],
        grads[UP],
        grads[B_UP],
        grads[DOWN],
        grads[B_DOWN],
        grads[BOT_GAIN],
        grads[BOT_SHIFT],
        grads[ENC],
        grads[B_ENC],
        grads[COMP_MEAN],
        grads[COMP_LOGVAR],
        grads[LAT],
        grads[B_LAT],
        grads[DEC_GAIN],
        grads[DEC_SHIFT],
        grads[DEC],
        grads[B_DEC],
    )


def solution(mesh):
    rows = P("dp", "phase", None)
    return jax.shard_map(
        body,
        mesh=mesh,
        in_specs=(rows, rows, rows, P("dp", None), P("dp", None)) + (P(),) * 27,
        out_specs=(
            rows,
            P("dp", None),
            P("dp"),
            P("dp"),
            P("dp"),
            P("dp"),
            P("dp", None),
            P("dp"),
            P("dp"),
            P("dp", None),
            P("dp"),
            P("dp"),
            P("dp"),
            P("dp", None),
            P("dp"),
            P("dp", None),
            P("dp"),
            P("dp"),
            P("dp"),
            P("dp", None),
            P("dp"),
            P(None, "dp"),
            P(None, "dp"),
            P("dp", None),
            P("dp"),
            P("dp"),
            P("dp"),
            P("dp", None),
            P("dp"),
        ),
        check_vma=False,
    )
```

```python
import functools
import math

import jax
import jax.numpy as jnp
import numpy as np
from jax import lax
from jax.experimental import pallas as pl
from jax.experimental.pallas import tpu as pltpu
from jax.sharding import PartitionSpec as P

HEADS = 16
GROUP = 8
PIECE = 128
WIDE = 1024
SLOTS = 4

norm_eps = 1e-05
mask_fill = -1000000000.0
MESH = pl.DeviceIdType.MESH

(
    H2,
    DOWN,
    GENE,
    UP,
    QKV,
    DEC,
    ENC,
    OUT,
    LAT,
    EMB_GAIN,
    EMB_SHIFT,
    ATTN_GAIN,
    ATTN_SHIFT,
    B_QKV,
    B_QUERY,
    B_VALUE,
    B_OUT,
    FFN_GAIN,
    FFN_SHIFT,
    B_UP,
    B_DOWN,
    BOT_GAIN,
    BOT_SHIFT,
    B_ENC,
    COMP_MEAN,
    COMP_LOGVAR,
    B_LAT,
    DEC_GAIN,
    DEC_SHIFT,
    B_DEC,
) = range(30)


LAYERS = (DEC, DOWN, LAT, ENC, UP, OUT, QKV, GENE)
VECTORS = (
    EMB_GAIN,
    EMB_SHIFT,
    ATTN_GAIN,
    ATTN_SHIFT,
    B_QKV,
    B_OUT,
    FFN_GAIN,
    FFN_SHIFT,
    B_UP,
    B_DOWN,
    BOT_GAIN,
    BOT_SHIFT,
    B_ENC,
    B_LAT,
    DEC_GAIN,
    DEC_SHIFT,
    B_DEC,
)
SUMS = (
    (COMP_MEAN, 16),
    (COMP_LOGVAR, 16),
    (EMB_GAIN, 1),
    (EMB_SHIFT, 1),
    (ATTN_GAIN, 1),
    (ATTN_SHIFT, 1),
    (B_QUERY, 1),
    (B_VALUE, 1),
    (B_OUT, 1),
    (FFN_GAIN, 1),
    (FFN_SHIFT, 1),
    (B_UP, 4),
    (B_DOWN, 1),
    (BOT_GAIN, 1),
    (BOT_SHIFT, 1),
    (B_ENC, 1),
    (B_LAT, 1),
    (DEC_GAIN, 1),
    (DEC_SHIFT, 1),
    (B_DEC, 2),
)
SUM_AT = {name: sum(n for _, n in SUMS[:i]) for i, (name, _) in enumerate(SUMS)}
SUM_ROWS = 64


def mm(left, right):
    return jnp.dot(left, right, preferred_element_type=jnp.float32)


def mm_last(left, right):
    return lax.dot_general(
        left, right, (((1,), (1,)), ((), ())), preferred_element_type=jnp.float32
    )


def mm_first(left, right):
    return lax.dot_general(
        left, right, (((0,), (0,)), ((), ())), preferred_element_type=jnp.float32
    )


def normed(values):
    center = jnp.mean(values, axis=-1, keepdims=True)
    centered = values - center
    spread = jnp.mean(centered * centered, axis=-1, keepdims=True)
    scale = lax.rsqrt(spread + norm_eps)
    return centered * scale, scale


def normed_back(grad, hat, scale, gain):
    pulled = grad * gain
    mean = jnp.mean(pulled, axis=-1, keepdims=True)
    along = jnp.mean(pulled * hat, axis=-1, keepdims=True)
    return scale * (pulled - mean - hat * along)


def column_sums(values):
    return jnp.sum(values.astype(jnp.float32), axis=0, keepdims=True)


def gelu(values):
    return values * (0.5 * (1.0 + lax.erf(values * (0.5**0.5))))


def gelu_slope(values):
    bell = 0.5 * (1.0 + lax.erf(values * (0.5**0.5)))
    return bell + values * jnp.exp(-0.5 * values * values) * (2.0 * math.pi) ** -0.5


LEFT_GROUPS = ((GENE,), (DEC,), (QKV, OUT, ENC, LAT))

BLOCKS = (
    (H2, 0, 1024, 512),
    (DEC, 0, 512, 128),
    (DEC, 512, 512, 256),
    (DEC, 1024, 1024, 512),
    (DOWN, 0, 1024, 512),
    (LAT, 0, 1024, 512),
    (ENC, 0, 1024, 512),
    (UP, 0, 1024, 512),
    (UP, 1024, 1024, 512),
    (UP, 2048, 1024, 512),
    (UP, 3072, 1024, 512),
    (OUT, 0, 1024, 512),
    (QKV, 0, 1024, 512),
    (QKV, 1024, 1024, 512),
    (QKV, 2048, 1024, 512),
    (GENE, 0, 1024, 256),
)


def grad_plan(layers):
    a_off, b_off, t_off, items, place = {}, {}, {}, [], {}
    a_at, b_at, t_at, row = 0, 0, 0, 0
    shares = {name: share for name, share, _ in layers}
    for name, share, columns in layers:
        b_off[name], t_off[name] = b_at, t_at
        for block in range(columns // WIDE):
            for start in range(0, share, PIECE):
                place[name, block, start] = row
                row += min(PIECE, share - start)
        t_at += -(-share // PIECE) * PIECE
        b_at += columns
    groups = []
    for names in LEFT_GROUPS:
        first = a_at
        for name in names:
            a_off[name] = a_at
            a_at += -(-shares[name] // PIECE) * PIECE
        groups.append((first, a_at - first))
    b_off[H2] = b_at
    shares[H2] = 0
    for block, (name, first, columns, step) in enumerate(BLOCKS):
        for start in range(0, shares[name], PIECE):
            rows = min(PIECE, shares[name] - start)
            for col in range(first, first + columns, step):
                items.append((block, start, rows, col, step, place[name, col // WIDE, start]))
    return a_off, b_off, t_off, items, row, groups, b_at + WIDE, t_at


ORDER = (
    0, 1, 2, 3, 100, 4, 5, 6, 7, 8, 9, 200, 101, 102, 10, 11, 12, 13,
    300, 14, 15, 201, 400, 1000, 202, 301, 104, 16, 401, 500, 302, 501, 502, 503, 402, 600,
    504, 601, 505, 17, 204, 103, 107, 700, 701, 602, 603, 604, 605, 304, 800, 801, 18, 702,
    703, 404, 704, 508, 509, 19, 510, 203, 108, 705, 511, 512, 902, 513, 514, 20, 515, 207,
    109, 802, 803, 804, 805, 608, 609, 303, 21, 610, 403, 708, 506, 611, 208, 110, 507, 709,
    612, 808, 307, 710, 613, 809, 22, 209, 111, 407, 520, 521, 711, 308, 810, 712, 713, 614,
    615, 408, 522, 523, 811, 210, 112, 606, 812, 714, 607, 813, 23, 309, 715, 814, 620, 706,
    621, 409, 524, 525, 211, 113, 815, 707, 416, 622, 310, 720, 806, 623, 410, 526, 544, 721,
    527, 807, 624, 212, 114, 722, 820, 625, 311, 723, 626, 411, 528, 529, 821, 724, 213, 115,
    822, 627, 312, 725, 823, 628, 412, 726, 530, 531, 629, 644, 824, 214, 106, 727, 825, 313,
    630, 728, 826, 413, 532, 631, 533, 729, 827, 215, 105, 730, 744, 314, 828, 632, 731, 414,
    534, 535, 633, 829, 206, 830, 732, 315, 634, 831, 844, 733, 415, 536, 537, 538, 635, 539,
    540, 541, 205, 734, 542, 543, 636, 832, 833, 306, 637, 735, 638, 305, 406, 736, 518, 639,
    519, 737, 834, 640, 405, 738, 516, 641, 517, 835, 739, 836, 642, 740, 837, 643, 741, 838,
    742, 839, 618, 743, 840, 841, 619, 842, 616, 843, 718, 617, 719, 716, 818, 717, 819, 816,
    817,
)


def everything(layers, n_vec, *refs):
    low, full = jnp.bfloat16, jnp.float32
    refs = list(refs)

    def pop(count):
        taken = refs[:count]
        del refs[:count]
        return taken

    expr_ref, gene_masks_ref, segments_ref, mean_ref, logvar_ref = pop(5)
    vec_refs = dict(zip(VECTORS, pop(n_vec)))
    table_ref, target_ref, noise_ref = pop(3)
    w_gene, w_qkv, w_out, w_up, w_down, w_enc, w_lat, w_dec = pop(8)
    (input_ref,) = pop(1)
    out_refs = dict(zip([name for name, _, _ in layers], pop(len(layers))))
    (tail_ref,) = pop(1)
    ring, masks_own, masks_all, table, target_in, noise_in, x1_out, x1_in = pop(8)
    kv_all, query_own, probs, dkv_part, dkv_in, dx_out, dx_in = pop(7)
    hats, scales, befores, mixed_grad, input_grad = pop(5)
    a_src, a_all, turned, up_part, b_all, v_src, v_all, near, far, v_near, v_far = pop(11)
    ring_sem, hand_send, hand_recv, hand_local, pair_send, pair_recv = pop(6)
    one_sem, a_send, a_recv, a_local, v_send, v_recv, b_send, b_recv, c_send, c_recv, o_sem = pop(11)

    d = lax.axis_index("dp")
    z = lax.axis_index("phase")
    base = (d // GROUP) * GROUP
    r = d % GROUP
    core, cx, cy = r % 2, (r // 2) % 2, r // 4
    partner = d + 1 - 2 * core
    owner = d - core + z // 2
    own = core == z // 2
    rc, rx, ry = r + 1 - 2 * core, r + 2 - 4 * cx, r + 4 - 8 * cy
    rxc, ryc = rx + 1 - 2 * core, ry + 1 - 2 * core
    rd = rx + 4 - 8 * cy
    rdc = rd + 1 - 2 * core
    middle = (z % 3) != 0
    inward = z + 1 - 2 * (z // 2)
    outward = z - 1 + 2 * (z // 2)
    a_off, b_off, t_off, items, _, left_groups, _, _ = grad_plan(layers)
    blocks = len(BLOCKS)
    shares = {name: share for name, share, _ in layers}
    seqs, rows, genes = expr_ref.shape
    tokens = seqs * rows
    width = table.shape[1]
    hidden = w_up.shape[1]
    length = segments_ref.shape[1]
    wide = WIDE

    barrier = pltpu.get_barrier_semaphore()

    def greet(to):
        pl.semaphore_signal(barrier, inc=1, device_id=to, device_id_type=MESH)

    for step in range(1, GROUP):
        greet((base + (r + step) % GROUP, z))
    greet((d, inward))

    @pl.when(middle)
    def _():
        greet((d, outward))

    for i in range(2):

        @pl.when(jnp.logical_not(own & (z % 2 == i)))
        def _():
            greet((owner, 2 * core + i))

    def barrier_wait():
        pl.semaphore_wait(barrier, GROUP + 1 + (z % 3 + 1) // 2 + (core + z // 2) % 2)

    def remote(src, dst, send, recv, to):
        return pltpu.make_async_remote_copy(
            src_ref=src,
            dst_ref=dst,
            send_sem=send,
            recv_sem=recv,
            device_id=to,
            device_id_type=MESH,
        )

    def columns_of(index):
        return pl.ds(*left_groups[index])

    def a_copy(index, step):
        at, to = columns_of(index), (r + step) % GROUP
        return remote(
            a_src.at[to, :, at],
            a_all.at[r, :, at],
            a_send.at[index],
            a_recv.at[index],
            (base + to, z),
        )

    def a_seven(index):
        part = a_all.at[pl.ds(0, GROUP - 1), :, columns_of(index)]
        return remote(part, part, a_send.at[index], a_recv.at[index], (base + rc, z))

    def a_own(index):
        at = columns_of(index)
        return pltpu.make_async_copy(a_src.at[r, :, at], a_all.at[r, :, at], a_local.at[index])

    def send_a(index):
        for step in range(1, GROUP):
            a_copy(index, step).start()
        a_own(index).start()

    def arrive_a(index):
        a_own(index).wait()
        a_seven(index).wait_recv()
        a_seven(index).wait_send()

    def v_copy(step):
        to = (r + step) % GROUP
        return remote(v_src.at[to], v_all.at[r], v_send.at[0], v_recv.at[0], (base + to, z))

    def v_seven():
        part = v_all.at[pl.ds(0, GROUP - 1)]
        return remote(part, part, v_send.at[0], v_recv.at[0], (base + rc, z))

    own_sums = pltpu.make_async_copy(v_src.at[r], v_all.at[r], one_sem.at[0])

    goes = (r, r, r, rx, ry, rx, ry, rd)
    counts = (0, 0, 2, 2, 2, 1, 1, 2)

    def b_start(kind, block):
        name, first, size, _ = BLOCKS[block]
        col = b_off[name] + first
        if kind in (5, 6):
            size //= 2
        if kind == 6:
            col += size
        to = (rx, ry, rc, rc, rc, ry, rx, rc)[kind]
        view = b_all.at[goes[kind], :, pl.ds(col, size)]
        recv = b_recv.at[block, counts[kind]]
        remote(view, view, b_send.at[block], recv, (base + to, z)).start()

    def b_bytes(block, way, many):
        name, first, size, _ = BLOCKS[block]
        part = b_all.at[pl.ds(0, many), :, pl.ds(b_off[name] + first, size)]
        return remote(part, part, b_send.at[block], b_recv.at[block, way], (base + rc, z))

    def neighbours_here(block):
        b_bytes(block, 0, 2).wait_recv()

    def halves_here(block):
        b_bytes(block, 1, 1).wait_recv()

    def beside_here(block):
        b_bytes(block, 2, 4).wait_recv()

    def block_sent(block):
        b_bytes(block, 0, GROUP - 1).wait_send()

    vectors = len(items)

    def place_of(ref, v_ref, index):
        if index == vectors:
            return v_ref
        _, _, count, col, size, row = items[index]
        return ref.at[pl.ds(row, count), pl.ds(col % WIDE, size)]

    def is_vec(index):
        return 1 if index == vectors else 0

    def to_middle(index, to):
        ref = place_of(near, v_near, index)
        return remote(ref, ref, c_send.at[0, is_vec(index)], c_recv.at[index, 0], (d, to))

    def across(index):
        src, dst = place_of(near, v_near, index), place_of(far, v_far, index)
        return remote(src, dst, c_send.at[1, is_vec(index)], c_recv.at[index, 1], (d, inward))

    def to_end(index, to):
        ref = place_of(far, v_far, index)
        return remote(ref, ref, c_send.at[0, is_vec(index)], c_recv.at[index, 0], (d, to))

    def result(index, ref, v_ref):
        src = place_of(ref, v_ref, index)
        if index == vectors:
            return pltpu.make_async_copy(src, tail_ref, o_sem.at[1])
        block, start, count, col, size, _ = items[index]
        to = out_refs[BLOCKS[block][0]].at[pl.ds(start, count), pl.ds(col, size)]
        return pltpu.make_async_copy(src, to, o_sem.at[0])

    def product(index):
        if index == vectors:
            return jnp.sum(v_all[...], axis=0)
        block, start, count, col, size, _ = items[index]
        name = BLOCKS[block][0]
        a_at = t_off[name] + start
        b_at = b_off[name] + col
        right = b_all[:, :, b_at : b_at + size].reshape(-1, size)
        value = mm(turned[a_at : a_at + PIECE, :], right)
        if count < PIECE:
            value = jnp.where(r % 2 == 1, value[count : 2 * count], value[:count])
        return value

    def end_push(index):
        @pl.when(jnp.logical_not(middle))
        def _():
            ref = place_of(near, v_near, index)
            ref[...] = product(index).astype(ref.dtype)
            to_middle(index, inward).start()

    def middle_join(index):
        @pl.when(middle)
        def _():
            value = product(index)
            to_middle(index, inward).wait_recv()
            ref = place_of(near, v_near, index)
            ref[...] = (value + ref[...].astype(full)).astype(ref.dtype)
            across(index).start()

    def middle_total(index):
        @pl.when(middle)
        def _():
            across(index).wait_recv()
            mine, theirs = place_of(near, v_near, index), place_of(far, v_far, index)
            both = mine[...].astype(full) + theirs[...].astype(full)
            theirs[...] = both.astype(theirs.dtype)
            to_end(index, outward).start()
            result(index, far, v_far).start()

    def end_land(index):
        @pl.when(jnp.logical_not(middle))
        def _():
            to_end(index, inward).wait_recv()
            result(index, far, v_far).start()


    up_columns = pl.ds(pl.multiple_of(r * shares[DOWN], PIECE), shares[DOWN])
    up_copy = pltpu.make_async_copy(w_up.at[:, up_columns], up_part, one_sem.at[4])
    up_copy.start()

    def make_lefts(_):
        own_columns = pl.ds(pl.multiple_of(b_off[H2] + r * PIECE, PIECE), PIECE)
        at = t_off[UP]
        turned[at : at + PIECE, :] = b_all[:, :, own_columns].reshape(-1, PIECE).T
        up_copy.wait()
        bias = vec_refs[B_UP][:, up_columns]
        count = GROUP // 2
        for slot in range(0, GROUP, count):
            h2 = b_all[slot : slot + count, :, b_off[H2] : b_off[H2] + width].reshape(-1, width)
            active = gelu(mm(h2, up_part[...]) + bias).astype(low)
            turned[
                t_off[DOWN] : t_off[DOWN] + shares[DOWN],
                slot * tokens : (slot + count) * tokens,
            ] = active.T

    group_of = {name: index for index, names in enumerate(LEFT_GROUPS) for name in names}
    gone, arrived, turned_already = [], set(), set()

    def get(block):
        if block == blocks:
            own_sums.wait()
            v_seven().wait_recv()
            return
        gone.append(block)
        beside_here(block)
        if len(gone) > 3:
            block_sent(gone[-4])
        name = BLOCKS[block][0]
        if name not in a_off or name in turned_already:
            return
        turned_already.add(name)
        if group_of[name] not in arrived:
            arrived.add(group_of[name])
            arrive_a(group_of[name])
        for start in range(0, shares[name], PIECE):
            at, to = a_off[name] + start, t_off[name] + start
            turned[to : to + PIECE, :] = a_all[:, :, at : at + PIECE].reshape(-1, PIECE).T

    table_copy = pltpu.make_async_copy(
        table_ref.at[pl.ds(z * rows, rows), :], table, one_sem.at[1]
    )
    input_copy = pltpu.make_async_copy(input_grad, input_ref, one_sem.at[2])
    pair_local = one_sem.at[3]
    table_copy.start()

    def rows_work():
        stream = []
        for j in range(genes // wide):
            stream.append(w_gene.at[pl.ds(j * wide, wide), :])
        for j in (1, 2, 0):
            stream.append(w_qkv.at[:, pl.ds(j * wide, wide)])
        stream.append(w_out)
        for j in range(hidden // wide):
            stream.append(w_up.at[:, pl.ds(j * wide, wide)])
            stream.append(w_down.at[pl.ds(j * wide, wide), :])
        stream.append(w_enc)
        stream.append(w_lat)
        for j in range(genes // wide):
            stream.append(w_dec.at[:, pl.ds(j * wide, wide)])
        stream.append(w_lat)
        stream.append(w_enc)
        for j in range(hidden // wide):
            stream.append(w_down.at[pl.ds(j * wide, wide), :])
            stream.append(w_up.at[:, pl.ds(j * wide, wide)])
        stream.append(w_out)
        for j in range(3):
            stream.append(w_qkv.at[:, pl.ds(j * wide, wide)])
        for j in range(genes // wide):
            stream.append(w_gene.at[pl.ds(j * wide, wide), :])

        def load(k):
            depth = stream[k].shape[0]
            return pltpu.make_async_copy(
                stream[k], ring.at[k % SLOTS, pl.ds(0, depth), :], ring_sem.at[k % SLOTS]
            )

        def fetch(k):
            if k < len(stream):
                load(k).start()

        place = [0]

        def take():
            k = place[0]
            place[0] += 1
            load(k).wait()
            return k

        def block(k):
            return ring[k % SLOTS, : stream[k].shape[0], :]

        for k in range(SLOTS):
            fetch(k)

        def hand(which, src, dst, i):
            return pltpu.make_async_remote_copy(
                src_ref=src.at[i],
                dst_ref=dst.at[z % 2],
                send_sem=hand_send.at[which, i],
                recv_sem=hand_recv.at[which, z % 2],
                device_id=(owner, 2 * core + i),
                device_id_type=MESH,
            )

        def hand_here(which, src, dst, i):
            return pltpu.make_async_copy(src.at[i], dst.at[i], hand_local.at[which])

        def hand_start(which, src, dst):
            for i in range(2):
                here = own & (z % 2 == i)

                @pl.when(here)
                def _():
                    hand_here(which, src, dst, i).start()

                @pl.when(jnp.logical_not(here))
                def _():
                    hand(which, src, dst, i).start()

        def hand_arrive(which, src, dst):
            for i in range(2):
                here = own & (z % 2 == i)

                @pl.when(here)
                def _():
                    hand_here(which, src, dst, i).wait()

                @pl.when(jnp.logical_not(here))
                def _():
                    pltpu.make_async_remote_copy(
                        src_ref=src.at[i],
                        dst_ref=dst.at[i],
                        send_sem=hand_send.at[which, i],
                        recv_sem=hand_recv.at[which, i],
                        device_id=(owner, 2 * core + i),
                        device_id_type=MESH,
                    ).wait_recv()

        def hand_sent(which, src, dst):
            for i in range(2):
                @pl.when(jnp.logical_not(own & (z % 2 == i)))
                def _():
                    hand(which, src, dst, i).wait_send()

        def pair(which, src, dst):
            return pltpu.make_async_remote_copy(
                src_ref=src,
                dst_ref=dst,
                send_sem=pair_send.at[which],
                recv_sem=pair_recv.at[which],
                device_id=(partner, z),
                device_id_type=MESH,
            )

        masks_own[:seqs, :genes] = gene_masks_ref[...].astype(full)
        masks_own[:seqs, genes : genes + length] = segments_ref[...].astype(full)
        own_masks = pltpu.make_async_copy(masks_own, masks_all.at[core], pair_local)
        own_masks.start()

        def vec(name, j=0):
            return vec_refs[name][:, j * wide : (j + 1) * wide]

        def put_a(name, values):
            off, share = a_off[name], shares[name]
            step = max(share, PIECE)
            for o in range(GROUP):
                start = o * share // step * step
                a_src[o, :, off : off + step] = values[:, start : start + step]

        def put_b(name, j, values):
            at = b_off[name] + j * wide
            b_all[r, :, at : at + wide] = values

        def put_sum(name, values, j=0):
            each = SUM_LANES[name]
            for o in range(values.shape[1] // 128):
                at = j * wide + o * 128
                to, row = at // (128 * each), SUM_AT[name] + at // 128 % each
                v_src[to, row : row + 1, :] = values[:, o * 128 : o * 128 + 128]

        def normalize(index, values, gain, shift):
            hat, scale = normed(values)
            hats[index] = hat
            scales[index] = jnp.broadcast_to(scale, scales.shape[1:])
            return hat * vec(gain) + vec(shift)

        def normalize_back(index, grad, gain, gain_name, shift_name):
            hat, scale = hats[index], scales[index, :, :1]
            put_sum(gain_name, jnp.sum(grad * hat, axis=0, keepdims=True))
            put_sum(shift_name, jnp.sum(grad, axis=0, keepdims=True))
            return normed_back(grad, hat, scale, vec(gain))

        keep = 1.0 - masks_own[:seqs, :genes]
        keep = jnp.concatenate(
            [jnp.broadcast_to(keep[s : s + 1], (rows, genes)) for s in range(seqs)], axis=0
        )
        masked = (expr_ref[...].reshape(tokens, genes).astype(full) * keep).astype(low)
        put_a(GENE, masked)
        table_copy.wait()
        embedded = jnp.concatenate([table[...]] * seqs, axis=0)
        for j in range(genes // wide):
            k = take()
            embedded += mm(masked[:, j * wide : (j + 1) * wide], block(k))
            fetch(k + SLOTS)
        x1_out[...] = (
            normalize(0, embedded, EMB_GAIN, EMB_SHIFT).astype(low).reshape(seqs, rows, width)
        )
        barrier_wait()
        hand_start(0, x1_out, x1_in)
        pair(0, masks_own, masks_all.at[core]).start()
        send_a(0)
        hand_start(1, noise_ref, noise_in)
        hand_start(2, target_ref, target_in)
        yield
        own_masks.wait()
        pair(0, masks_own, masks_all.at[1 - core]).wait_recv()
        odd = z % 2 == 1
        both_masks = masks_all[pl.ds(z // 2, 1)][0]
        mask_row = jnp.where(odd, both_masks[1:2], both_masks[0:1])
        gene_row = mask_row[:, :genes]
        segments = mask_row[:, genes : genes + length]
        place_q = lax.broadcasted_iota(jnp.int32, (tokens, length), 0) + core * tokens
        place_k = lax.broadcasted_iota(jnp.int32, (tokens, length), 1)
        own_segments = jnp.sum(
            jnp.where(place_q == place_k, segments, 0.0), axis=-1, keepdims=True
        )
        same = own_segments == segments
        same = jnp.concatenate([same.astype(full)] * 2, axis=0) > 0.5

        hand_arrive(0, x1_out, x1_in)
        x1 = x1_in[...].reshape(tokens, width).astype(full)
        h1 = normalize(1, x1, ATTN_GAIN, ATTN_SHIFT).astype(low)
        put_a(QKV, h1)
        head = width // HEADS
        scale = head**-0.5
        for j in (1, 2):
            k = take()
            kv_all[core, :, (j - 1) * wide : j * wide] = (
                mm(h1, block(k)) + vec(B_QKV, j)
            ).astype(low)
            fetch(k + SLOTS)
        pair(1, kv_all.at[core], kv_all.at[core]).start()
        k = take()
        query_own[...] = (mm(h1, block(k)) + vec(B_QKV, 0)).astype(low)
        fetch(k + SLOTS)
        yield
        pair(1, kv_all.at[core], kv_all.at[1 - core]).wait_recv()

        lanes = lax.broadcasted_iota(jnp.int32, (tokens, 2 * head), 1)
        first = lanes < head
        pairs = HEADS // 2

        def two(values):
            none = jnp.zeros_like(values)
            return jnp.concatenate([jnp.where(first, values, none), jnp.where(first, none, values)], axis=0)

        def one(values):
            return jnp.where(first, values[:tokens], values[tokens:])

        def columns(p):
            return pl.ds(pl.multiple_of(p * 2 * head, 2 * head), 2 * head)

        def keys_of(p):
            return kv_all[:, :, columns(p)].reshape(length, 2 * head)

        def values_of(p):
            at = pl.ds(pl.multiple_of(width + p * 2 * head, 2 * head), 2 * head)
            return kv_all[:, :, at].reshape(length, 2 * head)

        def attend(p, carry):
            scores = mm_last(two(query_own[:, columns(p)]), keys_of(p)) * scale
            scores = jnp.where(same, scores, mask_fill)
            shifted = jnp.exp(scores - jnp.max(scores, axis=-1, keepdims=True))
            prob = shifted / jnp.sum(shifted, axis=-1, keepdims=True)
            probs[p] = prob
            att = one(mm(prob.astype(low), values_of(p))).astype(low)
            a_src[p, :, a_off[OUT] : a_off[OUT] + 2 * head] = att
            return carry

        lax.fori_loop(0, pairs, attend, 0)
        yield
        attended = jnp.concatenate(
            [a_src[o, :, a_off[OUT] : a_off[OUT] + 2 * head] for o in range(pairs)], axis=1
        )
        k = take()
        mixed = x1 + (mm(attended, block(k)) + vec(B_OUT))
        fetch(k + SLOTS)
        h2 = normalize(2, mixed, FFN_GAIN, FFN_SHIFT).astype(low)
        b_all[r, :, b_off[H2] : b_off[H2] + width] = h2
        yield
        x2 = mixed + vec(B_DOWN)
        for j in range(hidden // wide):
            k = take()
            before = mm(h2, block(k)) + vec(B_UP, j)
            fetch(k + SLOTS)
            befores[:, j * wide : (j + 1) * wide] = before
            active = gelu(before).astype(low)
            k = take()
            x2 += mm(active, block(k))
            fetch(k + SLOTS)
            yield
        x2 = x2.astype(low).astype(full)
        h3 = normalize(3, x2, BOT_GAIN, BOT_SHIFT).astype(low)
        put_a(ENC, h3)
        k_enc = take()
        moments = mm(h3, block(k_enc)) + vec(B_ENC)
        latents = width // 2
        logvar = moments[:, latents:]
        hand_arrive(1, noise_ref, noise_in)
        swing = jnp.exp(0.5 * logvar) * noise_in[...].reshape(tokens, latents).astype(full)
        latent = moments[:, :latents] + swing
        latent_low = latent.astype(low)
        put_a(LAT, latent_low)
        fetch(k_enc + SLOTS)
        k_lat = take()
        lat_before = mm(latent_low, block(k_lat)) + vec(B_LAT)
        fetch(k_lat + SLOTS)
        x3 = gelu(lat_before).astype(low).astype(full)
        h4 = normalize(4, x3, DEC_GAIN, DEC_SHIFT).astype(low)
        put_a(DEC, h4)
        send_a(1)
        yield
        hand_arrive(2, target_ref, target_in)

        grad = jnp.zeros((tokens, width), full)
        for j in range(genes // wide):
            k = take()
            at = slice(j * wide, (j + 1) * wide)
            predicted = mm(h4, block(k)) + vec(B_DEC, j)
            wanted = target_in[:, :, at].reshape(tokens, wide).astype(full)
            d_pred = (gene_row[:, at] * (predicted - wanted)).astype(low)
            put_b(DEC, j, d_pred)
            put_sum(B_DEC, column_sums(d_pred), j)
            grad += mm_last(d_pred, block(k))
            fetch(k + SLOTS)
            yield
        d_x3 = normalize_back(4, grad, DEC_GAIN, DEC_GAIN, DEC_SHIFT).astype(low).astype(full)
        d_lat = (gelu_slope(lat_before) * d_x3).astype(low)
        put_b(LAT, 0, d_lat)
        put_sum(B_LAT, column_sums(d_lat))
        k = take()
        d_latent = mm_last(d_lat, block(k))
        fetch(k + SLOTS)
        yield

        inverse = jnp.exp(-logvar_ref[...])
        volume = jnp.sum(logvar_ref[...], axis=-1, keepdims=True)
        count = mean_ref.shape[0]
        scaled = []
        for c in range(count):
            offset = latent - mean_ref[c : c + 1, :]
            quad = jnp.sum(offset * offset * inverse[c : c + 1], axis=-1, keepdims=True)
            scaled.append(-0.5 * (quad + volume[c : c + 1]))
        highest = functools.reduce(jnp.maximum, scaled)
        shares_c = [jnp.exp(s - highest) for s in scaled]
        whole = functools.reduce(jnp.add, shares_c)
        parts = [part / whole for part in shares_c]
        for c in range(count):
            pull = (latent - mean_ref[c : c + 1, :]) * inverse[c : c + 1]
            d_latent += parts[c] * pull
        d_moments = jnp.concatenate([d_latent, 0.5 * d_latent * swing - 0.5], axis=1).astype(low)
        put_b(ENC, 0, d_moments)
        put_sum(B_ENC, column_sums(d_moments))
        yield
        k = take()
        grad = mm_last(d_moments, block(k))
        fetch(k + SLOTS)
        g = normalize_back(3, grad, BOT_GAIN, BOT_GAIN, BOT_SHIFT).astype(low)
        put_b(DOWN, 0, g)
        put_sum(B_DOWN, column_sums(g))
        yield
        for c in range(count):
            offset = latent - mean_ref[c : c + 1, :]
            weighted = parts[c] * (offset * inverse[c : c + 1])
            mean_grad = -jnp.sum(weighted, axis=0, keepdims=True)
            logvar_grad = 0.5 * jnp.sum(parts[c] - weighted * offset, axis=0, keepdims=True)
            for o in range(GROUP):
                at = slice(o // 2 * 128, o // 2 * 128 + 128)
                row = SUM_AT[COMP_MEAN] + c
                v_src[o, row : row + 1, :] = mean_grad[:, at]
                row = SUM_AT[COMP_LOGVAR] + c
                v_src[o, row : row + 1, :] = logvar_grad[:, at]
        yield
        grad = jnp.zeros((tokens, width), full)
        for j in range(hidden // wide):
            k = take()
            d_active = mm_last(g, block(k))
            fetch(k + SLOTS)
            slope = gelu_slope(befores[:, j * wide : (j + 1) * wide])
            d_before = (slope * d_active).astype(low)
            put_b(UP, j, d_before)
            put_sum(B_UP, column_sums(d_before), j)
            k = take()
            grad += mm_last(d_before, block(k))
            fetch(k + SLOTS)
            yield
        d_mixed = g.astype(full) + normalize_back(2, grad, FFN_GAIN, FFN_GAIN, FFN_SHIFT)
        mixed_grad[...] = d_mixed
        da = d_mixed.astype(low)
        put_b(OUT, 0, da)
        put_sum(B_OUT, column_sums(da))
        k = take()
        x1_in[...] = mm_last(da, block(k)).astype(low).reshape(seqs, rows, width)
        fetch(k + SLOTS)
        yield
        q_at = b_off[QKV]

        def attend_back(p, carry):
            query = two(query_own[:, columns(p)])
            d_att = two(x1_in[:, :, columns(p)].reshape(tokens, 2 * head))
            prob = probs[p]
            keys = keys_of(p)
            d_value = mm_first(prob.astype(low), d_att)
            d_prob = mm_last(d_att, values_of(p))
            d_score = prob * (d_prob - jnp.sum(prob * d_prob, axis=-1, keepdims=True))
            d_score = d_score.astype(low)
            d_query = one(mm(d_score, keys)) * scale
            d_key = mm_first(d_score, query) * scale
            to = pl.ds(pl.multiple_of(q_at + p * 2 * head, 2 * head), 2 * head)
            b_all[r, :, to] = d_query.astype(low)
            dkv_part[:, :, columns(p)] = d_key.reshape(2, tokens, 2 * head)
            at = pl.ds(pl.multiple_of(width + p * 2 * head, 2 * head), 2 * head)
            dkv_part[:, :, at] = d_value.reshape(2, tokens, 2 * head)
            return carry

        lax.fori_loop(0, pairs // 2, attend_back, 0)
        yield
        lax.fori_loop(pairs // 2, pairs, attend_back, 0)
        pair(2, dkv_part.at[1 - core], dkv_in).start()
        yield
        d_query = b_all[r, :, q_at : q_at + wide]
        put_sum(B_QUERY, column_sums(d_query))
        k = take()
        grad = mm_last(d_query, block(k))
        fetch(k + SLOTS)
        pair(2, dkv_part.at[1 - core], dkv_in).wait_recv()
        for j in (1, 2):
            at = slice((j - 1) * wide, j * wide)
            d_part = (dkv_part[core, :, at] + dkv_in[:, at]).astype(low)
            put_b(QKV, j, d_part)
            if j == 2:
                put_sum(B_VALUE, column_sums(d_part))
            k = take()
            grad += mm_last(d_part, block(k))
            fetch(k + SLOTS)
        d_x1 = mixed_grad[...] + normalize_back(1, grad, ATTN_GAIN, ATTN_GAIN, ATTN_SHIFT)
        dx_out[...] = d_x1.astype(low).reshape(seqs, rows, width)
        hand_start(3, dx_out, dx_in)
        yield
        hand_arrive(3, dx_out, dx_in)
        d_x1 = dx_in[...].reshape(tokens, width).astype(full)
        d_embedded = normalize_back(0, d_x1, EMB_GAIN, EMB_GAIN, EMB_SHIFT).astype(low)
        put_b(GENE, 0, d_embedded)
        for j in range(genes // wide):
            k = take()
            at = slice(j * wide, (j + 1) * wide)
            input_grad[:, at] = mm_last(d_embedded, block(k)) * jnp.concatenate(
                [
                    jnp.broadcast_to(1.0 - masks_own[s : s + 1, at], (rows, wide))
                    for s in range(seqs)
                ],
                axis=0,
            )
        input_copy.start()
        for step in range(1, GROUP):
            v_copy(step).start()
        own_sums.start()
        yield
        input_copy.wait()
        hand_sent(0, x1_out, x1_in)
        hand_sent(1, noise_ref, noise_in)
        hand_sent(2, target_ref, target_in)
        hand_sent(3, dx_out, dx_in)
        pair(0, masks_own, masks_all.at[core]).wait_send()
        pair(1, kv_all.at[core], kv_all.at[core]).wait_send()
        pair(2, dkv_part.at[1 - core], dkv_in).wait_send()


    work = rows_work()
    for code in ORDER:
        kind, index = code // 100, code % 100
        if kind == 0:
            next(work)
        elif kind == 1:
            for way in (0, 1, 2):
                b_start(way, index)
        elif kind == 2:
            neighbours_here(index)
            for way in (5, 6, 3, 4):
                b_start(way, index)
        elif kind == 3:
            halves_here(index)
            b_start(7, index)
        else:
            (get, end_push, middle_join, middle_total, end_land, send_a, make_lefts)[kind - 4](index)
    next(work, None)
    for block in gone[-3:]:
        block_sent(block)
    v_seven().wait_send()

    def sums_sent(leg):
        for vec_too, ref in ((0, near), (1, v_near)):
            remote(ref, ref, c_send.at[leg, vec_too], c_recv.at[0, 0], (d, inward)).wait_send()

    sums_sent(0)

    @pl.when(middle)
    def _():
        sums_sent(1)

    pltpu.make_async_copy(near, far, o_sem.at[0]).wait()
    pltpu.make_async_copy(v_near, v_far, o_sem.at[1]).wait()


SUM_LANES = dict(SUMS)


def finish(layers, *refs):
    refs = list(refs)
    count = len(layers)
    low_refs, refs = refs[:count], refs[count:]
    input_ref, tail_ref = refs[:2]
    refs = refs[2:]
    full_refs, refs = refs[:count], refs[count:]
    input_out = refs[0]
    sum_refs = dict(zip([name for name, _ in SUMS], refs[1 : 1 + len(SUMS)]))
    refs = refs[1 + len(SUMS) :]
    low_bufs, full_bufs = refs[:count], refs[count : 2 * count]
    input_buf, tail_buf, mean_buf, logvar_buf, in_sem, out_sem, move_sem, sum_sem = refs[2 * count :]
    move_in = pltpu.make_async_copy(input_ref, input_buf, move_sem.at[0])
    move_out = pltpu.make_async_copy(input_buf, input_out, move_sem.at[1])
    tail_in = pltpu.make_async_copy(tail_ref, tail_buf, move_sem.at[2])
    ins = [
        pltpu.make_async_copy(src, dst, in_sem.at[i])
        for i, (src, dst) in enumerate(zip(low_refs, low_bufs))
    ]
    outs = [
        pltpu.make_async_copy(src, dst, out_sem.at[i])
        for i, (src, dst) in enumerate(zip(full_bufs, full_refs))
    ]
    for copy in ins:
        copy.start()
    tail_in.start()
    move_in.start()
    for i in range(count):
        ins[i].wait()
        full_bufs[i][...] = low_bufs[i][...].astype(jnp.float32)
        outs[i].start()
    move_in.wait()
    move_out.start()
    tail_in.wait()
    odd = lax.axis_index("dp") % 2 == 1
    rows_of = dict(SUMS)
    for name, buf in ((COMP_MEAN, mean_buf), (COMP_LOGVAR, logvar_buf)):
        both = tail_buf[SUM_AT[name] : SUM_AT[name] + rows_of[name], :]
        buf[...] = jnp.where(odd, both[:, 64:], both[:, :64])
    sums = [
        pltpu.make_async_copy(mean_buf, sum_refs[COMP_MEAN], sum_sem.at[0]),
        pltpu.make_async_copy(logvar_buf, sum_refs[COMP_LOGVAR], sum_sem.at[1]),
    ]
    for name, rows in SUMS[2:]:
        for row in range(rows):
            sums.append(
                pltpu.make_async_copy(
                    tail_buf.at[pl.ds(SUM_AT[name] + row, 1), :],
                    sum_refs[name].at[:, pl.ds(row * 128, 128)],
                    sum_sem.at[len(sums)],
                )
            )
    for copy in sums:
        copy.start()
    for copy in sums + outs:
        copy.wait()
    move_out.wait()


def positions(length, width):
    frequency = np.exp(np.arange(width // 2, dtype=np.float32) * np.float32(-2.0 * math.log(10000.0) / width))
    angles = np.arange(length, dtype=np.float32)[:, None] * frequency[None, :]
    return np.stack([np.sin(angles), np.cos(angles)], axis=-1).reshape(length, width)


def body(expression, targets, noise, gene_masks, segment_ids, w_gene, emb_gain, emb_shift, attn_gain, attn_shift, w_qkv, b_qkv, w_out, b_out, ffn_gain, ffn_shift, w_up, b_up, w_down, b_down, bot_gain, bot_shift, w_enc, b_enc, comp_mean, comp_logvar, w_lat, b_lat, dec_gain, dec_shift, w_dec, b_dec):
    low, full = jnp.bfloat16, jnp.float32
    seqs, rows, genes = expression.shape
    width = w_gene.shape[1]
    hidden = w_up.shape[1]
    latents = noise.shape[2]
    length = segment_ids.shape[1]
    tokens = seqs * rows
    given = {
        EMB_GAIN: emb_gain,
        EMB_SHIFT: emb_shift,
        ATTN_GAIN: attn_gain,
        ATTN_SHIFT: attn_shift,
        B_QKV: b_qkv,
        B_OUT: b_out,
        FFN_GAIN: ffn_gain,
        FFN_SHIFT: ffn_shift,
        B_UP: b_up,
        B_DOWN: b_down,
        BOT_GAIN: bot_gain,
        BOT_SHIFT: bot_shift,
        B_ENC: b_enc,
        B_LAT: b_lat,
        DEC_GAIN: dec_gain,
        DEC_SHIFT: dec_shift,
        B_DEC: b_dec,
    }
    weights = {
        GENE: w_gene,
        QKV: w_qkv,
        OUT: w_out,
        UP: w_up,
        DOWN: w_down,
        ENC: w_enc,
        LAT: w_lat,
        DEC: w_dec,
    }
    layers = [
        (name, weights[name].shape[0] // GROUP, weights[name].shape[1]) for name in LAYERS
    ]
    _, _, _, items, rows_all, left_groups, b_cols, t_rows = grad_plan(layers)
    a_cols = sum(size for _, size in left_groups)
    vmem = pl.BlockSpec(memory_space=pltpu.VMEM)
    anywhere = pl.BlockSpec(memory_space=pl.ANY)
    dma = pltpu.SemaphoreType.DMA
    mask_lanes = genes + length + -length % 128
    share_shapes = [(share, columns) for _, share, columns in layers]
    chunks = len(items) + 1
    results = pl.pallas_call(
        functools.partial(everything, layers, len(VECTORS)),
        out_shape=(jax.ShapeDtypeStruct((tokens, genes), full),)
        + tuple(jax.ShapeDtypeStruct(shape, low) for shape in share_shapes)
        + (jax.ShapeDtypeStruct((SUM_ROWS, 128), full),),
        in_specs=[vmem] * (5 + len(VECTORS)) + [anywhere] * 11,
        out_specs=(anywhere,) * (2 + len(layers)),
        scratch_shapes=[
            pltpu.VMEM((SLOTS, WIDE, WIDE), low),
            pltpu.VMEM((8, mask_lanes), full),
            pltpu.VMEM((2, 8, mask_lanes), full),
            pltpu.VMEM((rows, width), full),
            pltpu.VMEM((2, rows, genes), low),
            pltpu.VMEM((2, rows, latents), low),
            pltpu.VMEM((2, rows, width), low),
            pltpu.VMEM((2, rows, width), low),
            pltpu.VMEM((2, tokens, 2 * width), low),
            pltpu.VMEM((tokens, width), low),
            pltpu.VMEM((HEADS // 2, 2 * tokens, 2 * tokens), full),
            pltpu.VMEM((2, tokens, 2 * width), full),
            pltpu.VMEM((tokens, 2 * width), full),
            pltpu.VMEM((2, rows, width), low),
            pltpu.VMEM((2, rows, width), low),
            pltpu.VMEM((5, tokens, width), full),
            pltpu.VMEM((5, tokens, 128), full),
            pltpu.VMEM((tokens, hidden), full),
            pltpu.VMEM((tokens, width), full),
            pltpu.VMEM((tokens, genes), full),
            pltpu.VMEM((GROUP, tokens, a_cols), low),
            pltpu.VMEM((GROUP, tokens, a_cols), low),
            pltpu.VMEM((t_rows, GROUP * tokens), low),
            pltpu.VMEM((width, hidden // GROUP), low),
            pltpu.VMEM((GROUP, tokens, b_cols), low),
            pltpu.VMEM((GROUP, SUM_ROWS, 128), full),
            pltpu.VMEM((GROUP, SUM_ROWS, 128), full),
            pltpu.VMEM((rows_all, WIDE), low),
            pltpu.VMEM((rows_all, WIDE), low),
            pltpu.VMEM((SUM_ROWS, 128), full),
            pltpu.VMEM((SUM_ROWS, 128), full),
            dma((SLOTS,)),
            dma((4, 2)),
            dma((4, 2)),
            dma((4,)),
            dma((3,)),
            dma((3,)),
            dma((5,)),
            dma((len(LEFT_GROUPS),)),
            dma((len(LEFT_GROUPS),)),
            dma((len(LEFT_GROUPS),)),
            dma((1,)),
            dma((1,)),
            dma((len(BLOCKS),)),
            dma((len(BLOCKS), 3)),
            dma((2, 2)),
            dma((chunks, 2)),
            dma((2,)),
        ],
        compiler_params=pltpu.CompilerParams(
            collective_id=0, has_side_effects=True, vmem_limit_bytes=63 * 1024 * 1024
        ),
    )(
        expression,
        gene_masks,
        segment_ids,
        comp_mean,
        comp_logvar,
        *[given[name].reshape(1, -1) for name in VECTORS],
        positions(length, width),
        targets,
        noise,
        *weights.values(),
    )
    input_grad, sums, tail = results[0], results[1:-1], results[-1]

    def sum_shape(name, count):
        return (count, 64) if name in (COMP_MEAN, COMP_LOGVAR) else (1, count * 128)

    finished = pl.pallas_call(
        functools.partial(finish, layers),
        out_shape=tuple(jax.ShapeDtypeStruct(shape, full) for shape in share_shapes)
        + (jax.ShapeDtypeStruct((tokens, genes), full),)
        + tuple(jax.ShapeDtypeStruct(sum_shape(name, count), full) for name, count in SUMS),
        in_specs=[anywhere] * (len(layers) + 2),
        out_specs=(anywhere,) * (len(layers) + 1 + len(SUMS)),
        scratch_shapes=[pltpu.VMEM(shape, low) for shape in share_shapes]
        + [pltpu.VMEM(shape, full) for shape in share_shapes]
        + [
            pltpu.VMEM((tokens, genes), full),
            pltpu.VMEM((SUM_ROWS, 128), full),
            pltpu.VMEM((SUMS[0][1], 64), full),
            pltpu.VMEM((SUMS[1][1], 64), full),
            dma((len(layers),)),
            dma((len(layers),)),
            dma((3,)),
            dma((SUM_ROWS,)),
        ],
        compiler_params=pltpu.CompilerParams(vmem_limit_bytes=63 * 1024 * 1024),
    )(*sums, input_grad, tail)

    groups = lax.axis_size("dp") // GROUP
    d = lax.axis_index("dp")

    def shared_out(values, axis):
        if groups == 1:
            return values
        across = [[g * GROUP + r for g in range(groups)] for r in range(GROUP)]
        within = [[g * GROUP + r for r in range(GROUP)] for g in range(groups)]
        values = lax.psum(values, "dp", axis_index_groups=across)
        values = lax.all_gather(values, "dp", axis=axis, tiled=True, axis_index_groups=within)
        size = values.shape[axis] // (groups * GROUP)
        return lax.dynamic_slice_in_dim(values, d * size, size, axis=axis)

    grads = {}
    for name, values in zip(LAYERS, finished):
        grads[name] = shared_out(values, 0)
    for (name, _), values in zip(SUMS, finished[len(layers) + 1 :]):
        if name in (COMP_MEAN, COMP_LOGVAR):
            grads[name] = shared_out(values, 1)
        else:
            grads[name] = shared_out(values.reshape(-1), 0)
    return (
        finished[len(layers)].reshape(seqs, rows, genes),
        grads[GENE],
        grads[EMB_GAIN],
        grads[EMB_SHIFT],
        grads[ATTN_GAIN],
        grads[ATTN_SHIFT],
        grads[QKV],
        grads[B_QUERY],
        grads[B_VALUE],
        grads[OUT],
        grads[B_OUT],
        grads[FFN_GAIN],
        grads[FFN_SHIFT],
        grads[UP],
        grads[B_UP],
        grads[DOWN],
        grads[B_DOWN],
        grads[BOT_GAIN],
        grads[BOT_SHIFT],
        grads[ENC],
        grads[B_ENC],
        grads[COMP_MEAN],
        grads[COMP_LOGVAR],
        grads[LAT],
        grads[B_LAT],
        grads[DEC_GAIN],
        grads[DEC_SHIFT],
        grads[DEC],
        grads[B_DEC],
    )


def solution(mesh):
    rows = P("dp", "phase", None)
    return jax.shard_map(
        body,
        mesh=mesh,
        in_specs=(rows, rows, rows, P("dp", None), P("dp", None)) + (P(),) * 27,
        out_specs=(
            rows,
            P("dp", None),
            P("dp"),
            P("dp"),
            P("dp"),
            P("dp"),
            P("dp", None),
            P("dp"),
            P("dp"),
            P("dp", None),
            P("dp"),
            P("dp"),
            P("dp"),
            P("dp", None),
            P("dp"),
            P("dp", None),
            P("dp"),
            P("dp"),
            P("dp"),
            P("dp", None),
            P("dp"),
            P(None, "dp"),
            P(None, "dp"),
            P("dp", None),
            P("dp"),
            P("dp"),
            P("dp"),
            P("dp", None),
            P("dp"),
        ),
        check_vma=False,
    )
```

```python
import functools
import math

import jax
import jax.numpy as jnp
import numpy as np
from jax import lax
from jax.experimental import pallas as pl
from jax.experimental.pallas import tpu as pltpu
from jax.sharding import PartitionSpec as P

HEADS = 16
GROUP = 8
CHIPS = 4
PIECE = 128
WIDE = 1024
SLOTS = 4

norm_eps = 1e-05
mask_fill = -1000000000.0
MESH = pl.DeviceIdType.MESH

(
    H2,
    DOWN,
    GENE,
    UP,
    QKV,
    DEC,
    ENC,
    OUT,
    LAT,
    EMB_GAIN,
    EMB_SHIFT,
    ATTN_GAIN,
    ATTN_SHIFT,
    B_QKV,
    B_QUERY,
    B_VALUE,
    B_OUT,
    FFN_GAIN,
    FFN_SHIFT,
    B_UP,
    B_DOWN,
    BOT_GAIN,
    BOT_SHIFT,
    B_ENC,
    COMP_MEAN,
    COMP_LOGVAR,
    B_LAT,
    DEC_GAIN,
    DEC_SHIFT,
    B_DEC,
) = range(30)


LAYERS = (DEC, DOWN, LAT, ENC, UP, OUT, QKV, GENE)
VECTORS = (
    EMB_GAIN,
    EMB_SHIFT,
    ATTN_GAIN,
    ATTN_SHIFT,
    B_QKV,
    B_OUT,
    FFN_GAIN,
    FFN_SHIFT,
    B_UP,
    B_DOWN,
    BOT_GAIN,
    BOT_SHIFT,
    B_ENC,
    B_LAT,
    DEC_GAIN,
    DEC_SHIFT,
    B_DEC,
)
SUMS = (
    (COMP_MEAN, 16),
    (COMP_LOGVAR, 16),
    (EMB_GAIN, 1),
    (EMB_SHIFT, 1),
    (ATTN_GAIN, 1),
    (ATTN_SHIFT, 1),
    (B_QUERY, 1),
    (B_VALUE, 1),
    (B_OUT, 1),
    (FFN_GAIN, 1),
    (FFN_SHIFT, 1),
    (B_UP, 4),
    (B_DOWN, 1),
    (BOT_GAIN, 1),
    (BOT_SHIFT, 1),
    (B_ENC, 1),
    (B_LAT, 1),
    (DEC_GAIN, 1),
    (DEC_SHIFT, 1),
    (B_DEC, 2),
)
SUM_AT = {name: sum(n for _, n in SUMS[:i]) for i, (name, _) in enumerate(SUMS)}
SUM_ROWS = 64


def mm(left, right):
    return jnp.dot(left, right, preferred_element_type=jnp.float32)


def mm_last(left, right):
    return lax.dot_general(
        left, right, (((1,), (1,)), ((), ())), preferred_element_type=jnp.float32
    )


def mm_first(left, right):
    return lax.dot_general(
        left, right, (((0,), (0,)), ((), ())), preferred_element_type=jnp.float32
    )


def normed(values):
    center = jnp.mean(values, axis=-1, keepdims=True)
    centered = values - center
    spread = jnp.mean(centered * centered, axis=-1, keepdims=True)
    scale = lax.rsqrt(spread + norm_eps)
    return centered * scale, scale


def normed_back(grad, hat, scale, gain):
    pulled = grad * gain
    mean = jnp.mean(pulled, axis=-1, keepdims=True)
    along = jnp.mean(pulled * hat, axis=-1, keepdims=True)
    return scale * (pulled - mean - hat * along)


def column_sums(values):
    return jnp.sum(values.astype(jnp.float32), axis=0, keepdims=True)


def gelu(values):
    return values * (0.5 * (1.0 + lax.erf(values * (0.5**0.5))))


def gelu_slope(values):
    bell = 0.5 * (1.0 + lax.erf(values * (0.5**0.5)))
    return bell + values * jnp.exp(-0.5 * values * values) * (2.0 * math.pi) ** -0.5


LEFT_GROUPS = ((GENE,), (DOWN,), (DEC,), (QKV, UP, OUT, ENC, LAT))

BLOCKS = (
    (DEC, 0, 512, 256),
    (DEC, 512, 512, 256),
    (DEC, 1024, 1024, 512),
    (DOWN, 0, 1024, 512),
    (LAT, 0, 1024, 512),
    (ENC, 0, 1024, 512),
    (UP, 0, 1024, 512),
    (UP, 1024, 1024, 512),
    (UP, 2048, 1024, 512),
    (UP, 3072, 1024, 512),
    (OUT, 0, 1024, 512),
    (QKV, 0, 1024, 512),
    (QKV, 1024, 1024, 512),
    (QKV, 2048, 1024, 512),
    (GENE, 0, 1024, 256),
)


def grad_plan(layers):
    a_off, b_off, t_off, items, place = {}, {}, {}, [], {}
    a_at, b_at, t_at, row = 0, 0, 0, 0
    many = {name: 2 * share for name, share, _ in layers}
    for name, _, columns in layers:
        b_off[name], t_off[name] = b_at, t_at
        for block in range(columns // WIDE):
            for start in range(0, many[name], PIECE):
                place[name, block, start] = row
                row += PIECE
        t_at += many[name]
        b_at += columns
    groups = []
    for names in LEFT_GROUPS:
        first = a_at
        for name in names:
            a_off[name] = a_at
            a_at += many[name]
        groups.append((first, a_at - first))
    for block, (name, first, columns, step) in enumerate(BLOCKS):
        for start in range(0, many[name], PIECE):
            for col in range(0, columns // 2, step):
                items.append((block, start, col, step, place[name, first // WIDE, start]))
    return a_off, b_off, t_off, items, row, groups, b_at, t_at


ORDER = (
    0, 1, 2, 3, 4, 5, 6, 7, 8, 9, 100, 101, 10, 11, 12, 13, 14, 15,
    16, 17, 1002, 1001, 18, 19, 200, 103, 20, 201, 102, 400, 500, 501, 21, 600, 203, 106,
    401, 502, 503, 601, 22, 700, 202, 107, 701, 602, 403, 506, 603, 507, 903, 508, 509, 510,
    511, 702, 512, 206, 108, 703, 513, 800, 801, 606, 402, 504, 505, 802, 23, 607, 803, 608,
    207, 109, 706, 609, 707, 610, 806, 708, 415, 611, 807, 709, 612, 1003, 1000, 808, 710, 613,
    809, 711, 604, 406, 517, 541, 518, 810, 712, 208, 110, 605, 811, 713, 407, 519, 520, 617,
    812, 704, 618, 209, 111, 813, 705, 619, 408, 521, 717, 522, 804, 620, 805, 718, 210, 112,
    817, 621, 641, 719, 409, 523, 524, 622, 818, 720, 819, 721, 211, 113, 623, 410, 722, 741,
    525, 526, 624, 820, 821, 723, 212, 114, 822, 625, 724, 411, 527, 626, 528, 823, 841, 725,
    824, 213, 105, 627, 726, 412, 529, 530, 628, 825, 727, 826, 214, 104, 629, 728, 413, 531,
    532, 630, 827, 729, 828, 205, 631, 730, 414, 533, 534, 535, 632, 536, 537, 538, 539, 540,
    731, 829, 633, 830, 204, 634, 732, 635, 405, 733, 515, 636, 516, 831, 734, 637, 404, 514,
    735, 832, 638, 736, 833, 639, 737, 834, 640, 738, 835, 739, 836, 615, 740, 837, 838, 616,
    839, 715, 840, 614, 716, 815, 714, 816, 814,
)


def everything(layers, n_vec, *refs):
    low, full = jnp.bfloat16, jnp.float32
    refs = list(refs)

    def pop(count):
        taken = refs[:count]
        del refs[:count]
        return taken

    expr_ref, gene_masks_ref, segments_ref, mean_ref, logvar_ref = pop(5)
    vec_refs = dict(zip(VECTORS, pop(n_vec)))
    table_ref, target_ref, noise_ref = pop(3)
    w_gene, w_qkv, w_out, w_up, w_down, w_enc, w_lat, w_dec = pop(8)
    (input_ref,) = pop(1)
    out_refs = dict(zip([name for name, _, _ in layers], pop(len(layers))))
    (tail_ref,) = pop(1)
    ring, masks_own, masks_all, table, target_in, noise_in, x1_out, x1_in = pop(8)
    kv_all, query_own, probs, dkv_part, dkv_in, dx_out, dx_in = pop(7)
    hats, scales, befores, mixed_grad, input_grad = pop(5)
    a_src, a_all, turned, b_own, b_all, v_src, v_all, near, far, v_near, v_far = pop(11)
    ring_sem, hand_send, hand_recv, hand_local, pair_send, pair_recv = pop(6)
    one_sem, a_send, a_recv, a_local, v_send, v_recv, b_send, b_recv, c_send, c_recv = pop(10)
    b_local, o_sem, far_send, far_recv = pop(4)

    d = lax.axis_index("dp")
    z = lax.axis_index("phase")
    base = (d // GROUP) * GROUP
    r = d % GROUP
    core, cx, cy = r % 2, (r // 2) % 2, r // 4
    partner = d + 1 - 2 * core
    owner = d - core + z // 2
    own = core == z // 2
    chip = r // 2
    kx, ky = chip + 1 - 2 * cx, chip + 2 - 4 * cy

    def member(to_chip, to_core):
        return (base + 2 * to_chip + to_core, z)

    beside = member(chip, 1 - core)
    middle = (z % 3) != 0
    inward = z + 1 - 2 * (z // 2)
    outward = z - 1 + 2 * (z // 2)
    a_off, b_off, t_off, items, _, left_groups, _, _ = grad_plan(layers)
    blocks = len(BLOCKS)
    shares = {name: share for name, share, _ in layers}
    seqs, rows, genes = expr_ref.shape
    tokens = seqs * rows
    width = table.shape[1]
    hidden = w_up.shape[1]
    length = segments_ref.shape[1]
    wide = WIDE

    barrier = pltpu.get_barrier_semaphore()

    def greet(to):
        pl.semaphore_signal(barrier, inc=1, device_id=to, device_id_type=MESH)

    for step in range(1, GROUP):
        greet((base + (r + step) % GROUP, z))
    greet((d, inward))

    @pl.when(middle)
    def _():
        greet((d, outward))

    for i in range(2):

        @pl.when(jnp.logical_not(own & (z % 2 == i)))
        def _():
            greet((owner, 2 * core + i))

    def barrier_wait():
        pl.semaphore_wait(barrier, GROUP + 1 + (z % 3 + 1) // 2 + (core + z // 2) % 2)

    def remote(src, dst, send, recv, to):
        return pltpu.make_async_remote_copy(
            src_ref=src,
            dst_ref=dst,
            send_sem=send,
            recv_sem=recv,
            device_id=to,
            device_id_type=MESH,
        )

    def columns_of(index):
        return pl.ds(*left_groups[index])

    def a_copy(index, step):
        at, to = columns_of(index), (chip + step) % CHIPS
        return remote(
            a_src.at[to, :, at],
            a_all.at[core, chip, :, at],
            a_send.at[index, 0],
            a_recv.at[index, 0],
            member(to, core),
        )

    def a_three(index):
        part = a_all.at[core, pl.ds(0, CHIPS - 1), :, columns_of(index)]
        return remote(part, part, a_send.at[index, 0], a_recv.at[index, 0], beside)

    def a_beside(index):
        part = a_all.at[core, :, :, columns_of(index)]
        return remote(part, part, a_send.at[index, 1], a_recv.at[index, 1], beside)

    def a_own(index):
        at = columns_of(index)
        return pltpu.make_async_copy(
            a_src.at[chip, :, at], a_all.at[core, chip, :, at], a_local.at[index]
        )

    def send_a(index):
        for step in range(1, CHIPS):
            a_copy(index, step).start()
        a_own(index).start()

    def pass_a(index):
        a_own(index).wait()
        a_three(index).wait_recv()
        a_beside(index).start()

    def arrive_a(index):
        part = a_all.at[1 - core, :, :, columns_of(index)]
        remote(part, part, a_send.at[index, 1], a_recv.at[index, 1], beside).wait_recv()
        a_three(index).wait_send()
        a_beside(index).wait_send()

    def v_copy(step):
        to = (r + step) % GROUP
        return remote(v_src.at[to], v_all.at[r], v_send.at[0], v_recv.at[0], (base + to, z))

    def v_seven():
        part = v_all.at[pl.ds(0, GROUP - 1)]
        return remote(part, part, v_send.at[0], v_recv.at[0], beside)

    own_sums = pltpu.make_async_copy(v_src.at[r], v_all.at[r], one_sem.at[0])

    def half_of(block, of_core):
        name, first, size, _ = BLOCKS[block]
        start = pl.multiple_of(b_off[name] + first + of_core * (size // 2), 128)
        return b_own.at[:, pl.ds(start, size // 2)]

    def landing(block):
        name, first, size, _ = BLOCKS[block]
        return pl.ds((b_off[name] + first) // 2, size // 2)

    def b_keep(block):
        return pltpu.make_async_copy(
            half_of(block, core), b_all.at[core, chip, :, landing(block)], b_local.at[block]
        )

    def own_block(block):
        dst = b_all.at[core, chip, :, landing(block)]
        for to_chip in (kx, ky):
            for to_core in (core, 1 - core):
                remote(
                    half_of(block, to_core),
                    dst,
                    b_send.at[block],
                    b_recv.at[block, 0],
                    member(to_chip, to_core),
                ).start()
        remote(
            half_of(block, 1 - core), dst, b_send.at[block], b_recv.at[block, 1], beside
        ).start()
        b_keep(block).start()

    def b_bytes(block, way, many):
        part = b_all.at[0, pl.ds(0, many), :, landing(block)]
        return remote(part, part, b_send.at[block], b_recv.at[block, way], beside)

    def pass_block(block):
        part = b_all.at[:, :, :, landing(block)]
        pltpu.make_async_remote_copy(
            src_ref=part.at[0],
            dst_ref=part.at[0],
            send_sem=b_send.at[block],
            recv_sem=b_recv.at[block, 0],
            device_id=beside,
            device_id_type=MESH,
        ).wait_recv()
        name, first, size, _ = BLOCKS[block]
        at = (b_off[name] + first) // 2
        for from_chip, to_chip, start in ((kx, ky, at), (ky, kx, at + size // 4)):
            view = b_all.at[:, from_chip, :, pl.ds(start, size // 4)]
            remote(
                view, view, b_send.at[block], b_recv.at[block, 1], member(to_chip, core)
            ).start()

    def block_here(block):
        b_keep(block).wait()
        b_bytes(block, 1, 3).wait_recv()

    def block_sent(block):
        for many in (4, 3):
            b_bytes(block, 1, many).wait_send()

    vectors = len(items)

    def place_of(ref, v_ref, index):
        if index == vectors:
            return v_ref
        block, _, col, size, row = items[index]
        col += BLOCKS[block][1] % WIDE // 2
        return ref.at[pl.ds(row, PIECE), pl.ds(col, size)]

    def is_vec(index):
        return 1 if index == vectors else 0

    def to_middle(index, to):
        ref = place_of(near, v_near, index)
        return remote(ref, ref, c_send.at[0, is_vec(index)], c_recv.at[index, 0], (d, to))

    def across(index):
        src, dst = place_of(near, v_near, index), place_of(far, v_far, index)
        return remote(src, dst, c_send.at[1, is_vec(index)], c_recv.at[index, 1], (d, inward))

    def to_end(index, to):
        ref = place_of(far, v_far, index)
        return remote(ref, ref, c_send.at[0, is_vec(index)], c_recv.at[index, 0], (d, to))

    def result(index):
        if index == vectors:
            pltpu.make_async_copy(v_far, tail_ref, o_sem.at[1]).start()
            return
        block, start, col, size, row = items[index]
        name, first, columns, _ = BLOCKS[block]
        share, at = shares[name], first % WIDE // 2 + col
        to_columns = pl.ds(pl.multiple_of(first + core * (columns // 2) + col, 128), size)
        count = min(PIECE, share)
        for offset in range(0, PIECE, count):
            owner_core, to_row = (start + offset) // share, (start + offset) % share
            src = far.at[pl.ds(row + offset, count), pl.ds(at, size)]
            dst = out_refs[name].at[pl.ds(to_row, count), to_columns]

            @pl.when(core == owner_core)
            def _():
                pltpu.make_async_copy(src, dst, o_sem.at[0]).start()

            @pl.when(core != owner_core)
            def _():
                remote(src, dst, far_send.at[0], far_recv.at[0], beside).start()

    def product(index):
        if index == vectors:
            return jnp.sum(v_all[...], axis=0)
        block, start, col, size, _ = items[index]
        name, first, _, _ = BLOCKS[block]
        a_at = t_off[name] + start
        b_at = (b_off[name] + first) // 2 + col
        right = b_all[:, :, :, b_at : b_at + size].reshape(-1, size)
        return mm(turned[a_at : a_at + PIECE, :], right)

    def end_push(index):
        @pl.when(jnp.logical_not(middle))
        def _():
            ref = place_of(near, v_near, index)
            ref[...] = product(index).astype(ref.dtype)
            to_middle(index, inward).start()

    def middle_join(index):
        @pl.when(middle)
        def _():
            value = product(index)
            to_middle(index, inward).wait_recv()
            ref = place_of(near, v_near, index)
            ref[...] = (value + ref[...].astype(full)).astype(ref.dtype)
            across(index).start()

    def middle_total(index):
        @pl.when(middle)
        def _():
            across(index).wait_recv()
            mine, theirs = place_of(near, v_near, index), place_of(far, v_far, index)
            both = mine[...].astype(full) + theirs[...].astype(full)
            theirs[...] = both.astype(theirs.dtype)
            to_end(index, outward).start()
            result(index)

    def end_land(index):
        @pl.when(jnp.logical_not(middle))
        def _():
            to_end(index, inward).wait_recv()
            result(index)


    group_of = {name: index for index, names in enumerate(LEFT_GROUPS) for name in names}
    gone, arrived, turned_already = [], set(), set()

    def get(block):
        if block == blocks:
            own_sums.wait()
            v_seven().wait_recv()
            return
        gone.append(block)
        block_here(block)
        if len(gone) > 3:
            block_sent(gone[-4])
        name = BLOCKS[block][0]
        if name in turned_already:
            return
        turned_already.add(name)
        if group_of[name] not in arrived:
            arrived.add(group_of[name])
            arrive_a(group_of[name])
        for start in range(0, 2 * shares[name], PIECE):
            at, to = a_off[name] + start, t_off[name] + start
            turned[to : to + PIECE, :] = a_all[:, :, :, at : at + PIECE].reshape(-1, PIECE).T

    table_copy = pltpu.make_async_copy(
        table_ref.at[pl.ds(z * rows, rows), :], table, one_sem.at[1]
    )
    input_copy = pltpu.make_async_copy(input_grad, input_ref, one_sem.at[2])
    pair_local = one_sem.at[3]
    table_copy.start()

    def rows_work():
        stream = []
        for j in range(genes // wide):
            stream.append(w_gene.at[pl.ds(j * wide, wide), :])
        for j in (1, 2, 0):
            stream.append(w_qkv.at[:, pl.ds(j * wide, wide)])
        stream.append(w_out)
        for j in range(hidden // wide):
            stream.append(w_up.at[:, pl.ds(j * wide, wide)])
            stream.append(w_down.at[pl.ds(j * wide, wide), :])
        stream.append(w_enc)
        stream.append(w_lat)
        for j in range(genes // wide):
            stream.append(w_dec.at[:, pl.ds(j * wide, wide)])
        stream.append(w_lat)
        stream.append(w_enc)
        for j in range(hidden // wide):
            stream.append(w_down.at[pl.ds(j * wide, wide), :])
            stream.append(w_up.at[:, pl.ds(j * wide, wide)])
        stream.append(w_out)
        for j in range(3):
            stream.append(w_qkv.at[:, pl.ds(j * wide, wide)])
        for j in range(genes // wide):
            stream.append(w_gene.at[pl.ds(j * wide, wide), :])

        def load(k):
            depth = stream[k].shape[0]
            return pltpu.make_async_copy(
                stream[k], ring.at[k % SLOTS, pl.ds(0, depth), :], ring_sem.at[k % SLOTS]
            )

        def fetch(k):
            if k < len(stream):
                load(k).start()

        place = [0]

        def take():
            k = place[0]
            place[0] += 1
            load(k).wait()
            return k

        def block(k):
            return ring[k % SLOTS, : stream[k].shape[0], :]

        for k in range(SLOTS):
            fetch(k)

        def hand(which, src, dst, i):
            return pltpu.make_async_remote_copy(
                src_ref=src.at[i],
                dst_ref=dst.at[z % 2],
                send_sem=hand_send.at[which, i],
                recv_sem=hand_recv.at[which, z % 2],
                device_id=(owner, 2 * core + i),
                device_id_type=MESH,
            )

        def hand_here(which, src, dst, i):
            return pltpu.make_async_copy(src.at[i], dst.at[i], hand_local.at[which])

        def hand_start(which, src, dst):
            for i in range(2):
                here = own & (z % 2 == i)

                @pl.when(here)
                def _():
                    hand_here(which, src, dst, i).start()

                @pl.when(jnp.logical_not(here))
                def _():
                    hand(which, src, dst, i).start()

        def hand_arrive(which, src, dst):
            for i in range(2):
                here = own & (z % 2 == i)

                @pl.when(here)
                def _():
                    hand_here(which, src, dst, i).wait()

                @pl.when(jnp.logical_not(here))
                def _():
                    pltpu.make_async_remote_copy(
                        src_ref=src.at[i],
                        dst_ref=dst.at[i],
                        send_sem=hand_send.at[which, i],
                        recv_sem=hand_recv.at[which, i],
                        device_id=(owner, 2 * core + i),
                        device_id_type=MESH,
                    ).wait_recv()

        def hand_sent(which, src, dst):
            for i in range(2):
                @pl.when(jnp.logical_not(own & (z % 2 == i)))
                def _():
                    hand(which, src, dst, i).wait_send()

        def pair(which, src, dst):
            return pltpu.make_async_remote_copy(
                src_ref=src,
                dst_ref=dst,
                send_sem=pair_send.at[which],
                recv_sem=pair_recv.at[which],
                device_id=(partner, z),
                device_id_type=MESH,
            )

        masks_own[:seqs, :genes] = gene_masks_ref[...].astype(full)
        masks_own[:seqs, genes : genes + length] = segments_ref[...].astype(full)
        own_masks = pltpu.make_async_copy(masks_own, masks_all.at[core], pair_local)
        own_masks.start()

        def vec(name, j=0):
            return vec_refs[name][:, j * wide : (j + 1) * wide]

        def put_a(name, values):
            off, many = a_off[name], 2 * shares[name]
            for o in range(CHIPS):
                a_src[o, :, off : off + many] = values[:, o * many : (o + 1) * many]

        def put_b(name, j, values):
            at = b_off[name] + j * wide
            b_own[:, at : at + wide] = values

        def put_sum(name, values, j=0):
            each = SUM_LANES[name]
            for o in range(values.shape[1] // 128):
                at = j * wide + o * 128
                to, row = at // (128 * each), SUM_AT[name] + at // 128 % each
                v_src[to, row : row + 1, :] = values[:, o * 128 : o * 128 + 128]

        def normalize(index, values, gain, shift):
            hat, scale = normed(values)
            hats[index] = hat
            scales[index] = jnp.broadcast_to(scale, scales.shape[1:])
            return hat * vec(gain) + vec(shift)

        def normalize_back(index, grad, gain, gain_name, shift_name):
            hat, scale = hats[index], scales[index, :, :1]
            put_sum(gain_name, jnp.sum(grad * hat, axis=0, keepdims=True))
            put_sum(shift_name, jnp.sum(grad, axis=0, keepdims=True))
            return normed_back(grad, hat, scale, vec(gain))

        keep = 1.0 - masks_own[:seqs, :genes]
        keep = jnp.concatenate(
            [jnp.broadcast_to(keep[s : s + 1], (rows, genes)) for s in range(seqs)], axis=0
        )
        masked = (expr_ref[...].reshape(tokens, genes).astype(full) * keep).astype(low)
        put_a(GENE, masked)
        table_copy.wait()
        embedded = jnp.concatenate([table[...]] * seqs, axis=0)
        for j in range(genes // wide):
            k = take()
            embedded += mm(masked[:, j * wide : (j + 1) * wide], block(k))
            fetch(k + SLOTS)
        x1_out[...] = (
            normalize(0, embedded, EMB_GAIN, EMB_SHIFT).astype(low).reshape(seqs, rows, width)
        )
        barrier_wait()
        hand_start(0, x1_out, x1_in)
        pair(0, masks_own, masks_all.at[core]).start()
        send_a(0)
        hand_start(1, noise_ref, noise_in)
        hand_start(2, target_ref, target_in)
        yield
        own_masks.wait()
        pair(0, masks_own, masks_all.at[1 - core]).wait_recv()
        odd = z % 2 == 1
        both_masks = masks_all[pl.ds(z // 2, 1)][0]
        mask_row = jnp.where(odd, both_masks[1:2], both_masks[0:1])
        gene_row = mask_row[:, :genes]
        segments = mask_row[:, genes : genes + length]
        place_q = lax.broadcasted_iota(jnp.int32, (tokens, length), 0) + core * tokens
        place_k = lax.broadcasted_iota(jnp.int32, (tokens, length), 1)
        own_segments = jnp.sum(
            jnp.where(place_q == place_k, segments, 0.0), axis=-1, keepdims=True
        )
        same = own_segments == segments
        same = jnp.concatenate([same.astype(full)] * 2, axis=0) > 0.5

        hand_arrive(0, x1_out, x1_in)
        x1 = x1_in[...].reshape(tokens, width).astype(full)
        h1 = normalize(1, x1, ATTN_GAIN, ATTN_SHIFT).astype(low)
        put_a(QKV, h1)
        head = width // HEADS
        scale = head**-0.5
        for j in (1, 2):
            k = take()
            kv_all[core, :, (j - 1) * wide : j * wide] = (
                mm(h1, block(k)) + vec(B_QKV, j)
            ).astype(low)
            fetch(k + SLOTS)
        pair(1, kv_all.at[core], kv_all.at[core]).start()
        k = take()
        query_own[...] = (mm(h1, block(k)) + vec(B_QKV, 0)).astype(low)
        fetch(k + SLOTS)
        yield
        pair(1, kv_all.at[core], kv_all.at[1 - core]).wait_recv()

        lanes = lax.broadcasted_iota(jnp.int32, (tokens, 2 * head), 1)
        first = lanes < head
        pairs = HEADS // 2

        def two(values):
            none = jnp.zeros_like(values)
            return jnp.concatenate([jnp.where(first, values, none), jnp.where(first, none, values)], axis=0)

        def one(values):
            return jnp.where(first, values[:tokens], values[tokens:])

        def columns(p):
            return pl.ds(pl.multiple_of(p * 2 * head, 2 * head), 2 * head)

        def keys_of(p):
            return kv_all[:, :, columns(p)].reshape(length, 2 * head)

        def values_of(p):
            at = pl.ds(pl.multiple_of(width + p * 2 * head, 2 * head), 2 * head)
            return kv_all[:, :, at].reshape(length, 2 * head)

        def attend(p, carry):
            scores = mm_last(two(query_own[:, columns(p)]), keys_of(p)) * scale
            scores = jnp.where(same, scores, mask_fill)
            shifted = jnp.exp(scores - jnp.max(scores, axis=-1, keepdims=True))
            prob = shifted / jnp.sum(shifted, axis=-1, keepdims=True)
            probs[p] = prob
            att = one(mm(prob.astype(low), values_of(p))).astype(low)
            to = pl.ds(pl.multiple_of(a_off[OUT] + p % 2 * 2 * head, 2 * head), 2 * head)
            a_src[p // 2, :, to] = att
            return carry

        lax.fori_loop(0, pairs, attend, 0)
        yield
        attended = jnp.concatenate(
            [a_src[o, :, a_off[OUT] : a_off[OUT] + 4 * head] for o in range(CHIPS)], axis=1
        )
        k = take()
        mixed = x1 + (mm(attended, block(k)) + vec(B_OUT))
        fetch(k + SLOTS)
        h2 = normalize(2, mixed, FFN_GAIN, FFN_SHIFT).astype(low)
        put_a(UP, h2)
        yield
        x2 = mixed + vec(B_DOWN)
        per_chip = 2 * shares[DOWN]
        for j in range(hidden // wide):
            k = take()
            before = mm(h2, block(k)) + vec(B_UP, j)
            fetch(k + SLOTS)
            befores[:, j * wide : (j + 1) * wide] = before
            active = gelu(before).astype(low)
            for o in range(wide // per_chip):
                a_src[
                    j * (wide // per_chip) + o, :, a_off[DOWN] : a_off[DOWN] + per_chip
                ] = active[:, o * per_chip : (o + 1) * per_chip]
            k = take()
            x2 += mm(active, block(k))
            fetch(k + SLOTS)
            if j == hidden // wide - 1:
                send_a(1)
            yield
        x2 = x2.astype(low).astype(full)
        h3 = normalize(3, x2, BOT_GAIN, BOT_SHIFT).astype(low)
        put_a(ENC, h3)
        k_enc = take()
        moments = mm(h3, block(k_enc)) + vec(B_ENC)
        latents = width // 2
        logvar = moments[:, latents:]
        hand_arrive(1, noise_ref, noise_in)
        swing = jnp.exp(0.5 * logvar) * noise_in[...].reshape(tokens, latents).astype(full)
        latent = moments[:, :latents] + swing
        latent_low = latent.astype(low)
        put_a(LAT, latent_low)
        fetch(k_enc + SLOTS)
        k_lat = take()
        lat_before = mm(latent_low, block(k_lat)) + vec(B_LAT)
        fetch(k_lat + SLOTS)
        x3 = gelu(lat_before).astype(low).astype(full)
        h4 = normalize(4, x3, DEC_GAIN, DEC_SHIFT).astype(low)
        put_a(DEC, h4)
        send_a(2)
        yield
        hand_arrive(2, target_ref, target_in)

        grad = jnp.zeros((tokens, width), full)
        for j in range(genes // wide):
            k = take()
            at = slice(j * wide, (j + 1) * wide)
            predicted = mm(h4, block(k)) + vec(B_DEC, j)
            wanted = target_in[:, :, at].reshape(tokens, wide).astype(full)
            d_pred = (gene_row[:, at] * (predicted - wanted)).astype(low)
            put_b(DEC, j, d_pred)
            put_sum(B_DEC, column_sums(d_pred), j)
            grad += mm_last(d_pred, block(k))
            fetch(k + SLOTS)
            yield
        d_x3 = normalize_back(4, grad, DEC_GAIN, DEC_GAIN, DEC_SHIFT).astype(low).astype(full)
        d_lat = (gelu_slope(lat_before) * d_x3).astype(low)
        put_b(LAT, 0, d_lat)
        put_sum(B_LAT, column_sums(d_lat))
        k = take()
        d_latent = mm_last(d_lat, block(k))
        fetch(k + SLOTS)
        yield

        inverse = jnp.exp(-logvar_ref[...])
        volume = jnp.sum(logvar_ref[...], axis=-1, keepdims=True)
        count = mean_ref.shape[0]
        scaled = []
        for c in range(count):
            offset = latent - mean_ref[c : c + 1, :]
            quad = jnp.sum(offset * offset * inverse[c : c + 1], axis=-1, keepdims=True)
            scaled.append(-0.5 * (quad + volume[c : c + 1]))
        highest = functools.reduce(jnp.maximum, scaled)
        shares_c = [jnp.exp(s - highest) for s in scaled]
        whole = functools.reduce(jnp.add, shares_c)
        parts = [part / whole for part in shares_c]
        for c in range(count):
            pull = (latent - mean_ref[c : c + 1, :]) * inverse[c : c + 1]
            d_latent += parts[c] * pull
        d_moments = jnp.concatenate([d_latent, 0.5 * d_latent * swing - 0.5], axis=1).astype(low)
        put_b(ENC, 0, d_moments)
        put_sum(B_ENC, column_sums(d_moments))
        yield
        k = take()
        grad = mm_last(d_moments, block(k))
        fetch(k + SLOTS)
        g = normalize_back(3, grad, BOT_GAIN, BOT_GAIN, BOT_SHIFT).astype(low)
        put_b(DOWN, 0, g)
        put_sum(B_DOWN, column_sums(g))
        yield
        for c in range(count):
            offset = latent - mean_ref[c : c + 1, :]
            weighted = parts[c] * (offset * inverse[c : c + 1])
            mean_grad = -jnp.sum(weighted, axis=0, keepdims=True)
            logvar_grad = 0.5 * jnp.sum(parts[c] - weighted * offset, axis=0, keepdims=True)
            for o in range(GROUP):
                at = slice(o // 2 * 128, o // 2 * 128 + 128)
                row = SUM_AT[COMP_MEAN] + c
                v_src[o, row : row + 1, :] = mean_grad[:, at]
                row = SUM_AT[COMP_LOGVAR] + c
                v_src[o, row : row + 1, :] = logvar_grad[:, at]
        yield
        grad = jnp.zeros((tokens, width), full)
        for j in range(hidden // wide):
            k = take()
            d_active = mm_last(g, block(k))
            fetch(k + SLOTS)
            slope = gelu_slope(befores[:, j * wide : (j + 1) * wide])
            d_before = (slope * d_active).astype(low)
            put_b(UP, j, d_before)
            put_sum(B_UP, column_sums(d_before), j)
            k = take()
            grad += mm_last(d_before, block(k))
            fetch(k + SLOTS)
            yield
        d_mixed = g.astype(full) + normalize_back(2, grad, FFN_GAIN, FFN_GAIN, FFN_SHIFT)
        mixed_grad[...] = d_mixed
        da = d_mixed.astype(low)
        put_b(OUT, 0, da)
        put_sum(B_OUT, column_sums(da))
        k = take()
        x1_in[...] = mm_last(da, block(k)).astype(low).reshape(seqs, rows, width)
        fetch(k + SLOTS)
        yield
        q_at = b_off[QKV]

        def attend_back(p, carry):
            query = two(query_own[:, columns(p)])
            d_att = two(x1_in[:, :, columns(p)].reshape(tokens, 2 * head))
            prob = probs[p]
            keys = keys_of(p)
            d_value = mm_first(prob.astype(low), d_att)
            d_prob = mm_last(d_att, values_of(p))
            d_score = prob * (d_prob - jnp.sum(prob * d_prob, axis=-1, keepdims=True))
            d_score = d_score.astype(low)
            d_query = one(mm(d_score, keys)) * scale
            d_key = mm_first(d_score, query) * scale
            to = pl.ds(pl.multiple_of(q_at + p * 2 * head, 2 * head), 2 * head)
            b_own[:, to] = d_query.astype(low)
            dkv_part[:, :, columns(p)] = d_key.reshape(2, tokens, 2 * head)
            at = pl.ds(pl.multiple_of(width + p * 2 * head, 2 * head), 2 * head)
            dkv_part[:, :, at] = d_value.reshape(2, tokens, 2 * head)
            return carry

        lax.fori_loop(0, pairs // 2, attend_back, 0)
        yield
        lax.fori_loop(pairs // 2, pairs, attend_back, 0)
        pair(2, dkv_part.at[1 - core], dkv_in).start()
        yield
        d_query = b_own[:, q_at : q_at + wide]
        put_sum(B_QUERY, column_sums(d_query))
        k = take()
        grad = mm_last(d_query, block(k))
        fetch(k + SLOTS)
        pair(2, dkv_part.at[1 - core], dkv_in).wait_recv()
        for j in (1, 2):
            at = slice((j - 1) * wide, j * wide)
            d_part = (dkv_part[core, :, at] + dkv_in[:, at]).astype(low)
            put_b(QKV, j, d_part)
            if j == 2:
                put_sum(B_VALUE, column_sums(d_part))
            k = take()
            grad += mm_last(d_part, block(k))
            fetch(k + SLOTS)
        d_x1 = mixed_grad[...] + normalize_back(1, grad, ATTN_GAIN, ATTN_GAIN, ATTN_SHIFT)
        dx_out[...] = d_x1.astype(low).reshape(seqs, rows, width)
        hand_start(3, dx_out, dx_in)
        yield
        hand_arrive(3, dx_out, dx_in)
        d_x1 = dx_in[...].reshape(tokens, width).astype(full)
        d_embedded = normalize_back(0, d_x1, EMB_GAIN, EMB_GAIN, EMB_SHIFT).astype(low)
        put_b(GENE, 0, d_embedded)
        for j in range(genes // wide):
            k = take()
            at = slice(j * wide, (j + 1) * wide)
            input_grad[:, at] = mm_last(d_embedded, block(k)) * jnp.concatenate(
                [
                    jnp.broadcast_to(1.0 - masks_own[s : s + 1, at], (rows, wide))
                    for s in range(seqs)
                ],
                axis=0,
            )
        input_copy.start()
        for step in range(1, GROUP):
            v_copy(step).start()
        own_sums.start()
        yield
        input_copy.wait()
        hand_sent(0, x1_out, x1_in)
        hand_sent(1, noise_ref, noise_in)
        hand_sent(2, target_ref, target_in)
        hand_sent(3, dx_out, dx_in)
        pair(0, masks_own, masks_all.at[core]).wait_send()
        pair(1, kv_all.at[core], kv_all.at[core]).wait_send()
        pair(2, dkv_part.at[1 - core], dkv_in).wait_send()


    work = rows_work()
    for code in ORDER:
        kind, index = code // 100, code % 100
        if kind == 0:
            next(work)
        elif kind == 1:
            own_block(index)
        elif kind == 2:
            pass_block(index)
        else:
            (get, end_push, middle_join, middle_total, end_land, send_a, pass_a)[kind - 4](index)
    next(work, None)
    for block in gone[-3:]:
        block_sent(block)
    v_seven().wait_send()

    def sums_sent(leg):
        for vec_too, ref in ((0, near), (1, v_near)):
            remote(ref, ref, c_send.at[leg, vec_too], c_recv.at[0, 0], (d, inward)).wait_send()

    sums_sent(0)

    @pl.when(middle)
    def _():
        sums_sent(1)

    half = pl.ds(0, near.shape[0] // 2)
    pltpu.make_async_copy(near.at[half], far.at[half], o_sem.at[0]).wait()
    passed = remote(far.at[half], far.at[half], far_send.at[0], far_recv.at[0], beside)
    passed.wait_send()
    passed.wait_recv()
    pltpu.make_async_copy(v_near, v_far, o_sem.at[1]).wait()


SUM_LANES = dict(SUMS)


def finish(layers, *refs):
    refs = list(refs)
    count = len(layers)
    low_refs, refs = refs[:count], refs[count:]
    input_ref, tail_ref = refs[:2]
    refs = refs[2:]
    full_refs, refs = refs[:count], refs[count:]
    input_out = refs[0]
    sum_refs = dict(zip([name for name, _ in SUMS], refs[1 : 1 + len(SUMS)]))
    refs = refs[1 + len(SUMS) :]
    low_bufs, full_bufs = refs[:count], refs[count : 2 * count]
    input_buf, tail_buf, mean_buf, logvar_buf, in_sem, out_sem, move_sem, sum_sem = refs[2 * count :]
    move_in = pltpu.make_async_copy(input_ref, input_buf, move_sem.at[0])
    move_out = pltpu.make_async_copy(input_buf, input_out, move_sem.at[1])
    tail_in = pltpu.make_async_copy(tail_ref, tail_buf, move_sem.at[2])
    ins = [
        pltpu.make_async_copy(src, dst, in_sem.at[i])
        for i, (src, dst) in enumerate(zip(low_refs, low_bufs))
    ]
    outs = [
        pltpu.make_async_copy(src, dst, out_sem.at[i])
        for i, (src, dst) in enumerate(zip(full_bufs, full_refs))
    ]
    for copy in ins:
        copy.start()
    tail_in.start()
    move_in.start()
    for i in range(count):
        ins[i].wait()
        full_bufs[i][...] = low_bufs[i][...].astype(jnp.float32)
        outs[i].start()
    move_in.wait()
    move_out.start()
    tail_in.wait()
    odd = lax.axis_index("dp") % 2 == 1
    rows_of = dict(SUMS)
    for name, buf in ((COMP_MEAN, mean_buf), (COMP_LOGVAR, logvar_buf)):
        both = tail_buf[SUM_AT[name] : SUM_AT[name] + rows_of[name], :]
        buf[...] = jnp.where(odd, both[:, 64:], both[:, :64])
    sums = [
        pltpu.make_async_copy(mean_buf, sum_refs[COMP_MEAN], sum_sem.at[0]),
        pltpu.make_async_copy(logvar_buf, sum_refs[COMP_LOGVAR], sum_sem.at[1]),
    ]
    for name, rows in SUMS[2:]:
        for row in range(rows):
            sums.append(
                pltpu.make_async_copy(
                    tail_buf.at[pl.ds(SUM_AT[name] + row, 1), :],
                    sum_refs[name].at[:, pl.ds(row * 128, 128)],
                    sum_sem.at[len(sums)],
                )
            )
    for copy in sums:
        copy.start()
    for copy in sums + outs:
        copy.wait()
    move_out.wait()


def positions(length, width):
    frequency = np.exp(np.arange(width // 2, dtype=np.float32) * np.float32(-2.0 * math.log(10000.0) / width))
    angles = np.arange(length, dtype=np.float32)[:, None] * frequency[None, :]
    return np.stack([np.sin(angles), np.cos(angles)], axis=-1).reshape(length, width)


def body(expression, targets, noise, gene_masks, segment_ids, w_gene, emb_gain, emb_shift, attn_gain, attn_shift, w_qkv, b_qkv, w_out, b_out, ffn_gain, ffn_shift, w_up, b_up, w_down, b_down, bot_gain, bot_shift, w_enc, b_enc, comp_mean, comp_logvar, w_lat, b_lat, dec_gain, dec_shift, w_dec, b_dec):
    low, full = jnp.bfloat16, jnp.float32
    seqs, rows, genes = expression.shape
    width = w_gene.shape[1]
    hidden = w_up.shape[1]
    latents = noise.shape[2]
    length = segment_ids.shape[1]
    tokens = seqs * rows
    given = {
        EMB_GAIN: emb_gain,
        EMB_SHIFT: emb_shift,
        ATTN_GAIN: attn_gain,
        ATTN_SHIFT: attn_shift,
        B_QKV: b_qkv,
        B_OUT: b_out,
        FFN_GAIN: ffn_gain,
        FFN_SHIFT: ffn_shift,
        B_UP: b_up,
        B_DOWN: b_down,
        BOT_GAIN: bot_gain,
        BOT_SHIFT: bot_shift,
        B_ENC: b_enc,
        B_LAT: b_lat,
        DEC_GAIN: dec_gain,
        DEC_SHIFT: dec_shift,
        B_DEC: b_dec,
    }
    weights = {
        GENE: w_gene,
        QKV: w_qkv,
        OUT: w_out,
        UP: w_up,
        DOWN: w_down,
        ENC: w_enc,
        LAT: w_lat,
        DEC: w_dec,
    }
    layers = [
        (name, weights[name].shape[0] // GROUP, weights[name].shape[1]) for name in LAYERS
    ]
    _, _, _, items, rows_all, left_groups, b_cols, t_rows = grad_plan(layers)
    a_cols = sum(size for _, size in left_groups)
    vmem = pl.BlockSpec(memory_space=pltpu.VMEM)
    anywhere = pl.BlockSpec(memory_space=pl.ANY)
    dma = pltpu.SemaphoreType.DMA
    mask_lanes = genes + length + -length % 128
    share_shapes = [(share, columns) for _, share, columns in layers]
    chunks = len(items) + 1
    results = pl.pallas_call(
        functools.partial(everything, layers, len(VECTORS)),
        out_shape=(jax.ShapeDtypeStruct((tokens, genes), full),)
        + tuple(jax.ShapeDtypeStruct(shape, low) for shape in share_shapes)
        + (jax.ShapeDtypeStruct((SUM_ROWS, 128), full),),
        in_specs=[vmem] * (5 + len(VECTORS)) + [anywhere] * 11,
        out_specs=(anywhere,) * (2 + len(layers)),
        scratch_shapes=[
            pltpu.VMEM((SLOTS, WIDE, WIDE), low),
            pltpu.VMEM((8, mask_lanes), full),
            pltpu.VMEM((2, 8, mask_lanes), full),
            pltpu.VMEM((rows, width), full),
            pltpu.VMEM((2, rows, genes), low),
            pltpu.VMEM((2, rows, latents), low),
            pltpu.VMEM((2, rows, width), low),
            pltpu.VMEM((2, rows, width), low),
            pltpu.VMEM((2, tokens, 2 * width), low),
            pltpu.VMEM((tokens, width), low),
            pltpu.VMEM((HEADS // 2, 2 * tokens, 2 * tokens), full),
            pltpu.VMEM((2, tokens, 2 * width), full),
            pltpu.VMEM((tokens, 2 * width), full),
            pltpu.VMEM((2, rows, width), low),
            pltpu.VMEM((2, rows, width), low),
            pltpu.VMEM((5, tokens, width), full),
            pltpu.VMEM((5, tokens, 128), full),
            pltpu.VMEM((tokens, hidden), full),
            pltpu.VMEM((tokens, width), full),
            pltpu.VMEM((tokens, genes), full),
            pltpu.VMEM((CHIPS, tokens, a_cols), low),
            pltpu.VMEM((2, CHIPS, tokens, a_cols), low),
            pltpu.VMEM((t_rows, GROUP * tokens), low),
            pltpu.VMEM((tokens, b_cols), low),
            pltpu.VMEM((2, CHIPS, tokens, b_cols // 2), low),
            pltpu.VMEM((GROUP, SUM_ROWS, 128), full),
            pltpu.VMEM((GROUP, SUM_ROWS, 128), full),
            pltpu.VMEM((rows_all, WIDE // 2), low),
            pltpu.VMEM((rows_all, WIDE // 2), low),
            pltpu.VMEM((SUM_ROWS, 128), full),
            pltpu.VMEM((SUM_ROWS, 128), full),
            dma((SLOTS,)),
            dma((4, 2)),
            dma((4, 2)),
            dma((4,)),
            dma((3,)),
            dma((3,)),
            dma((5,)),
            dma((len(LEFT_GROUPS), 2)),
            dma((len(LEFT_GROUPS), 2)),
            dma((len(LEFT_GROUPS),)),
            dma((1,)),
            dma((1,)),
            dma((len(BLOCKS),)),
            dma((len(BLOCKS), 2)),
            dma((2, 2)),
            dma((chunks, 2)),
            dma((len(BLOCKS),)),
            dma((2,)),
            dma((1,)),
            dma((1,)),
        ],
        compiler_params=pltpu.CompilerParams(
            collective_id=0, has_side_effects=True, vmem_limit_bytes=63 * 1024 * 1024
        ),
    )(
        expression,
        gene_masks,
        segment_ids,
        comp_mean,
        comp_logvar,
        *[given[name].reshape(1, -1) for name in VECTORS],
        positions(length, width),
        targets,
        noise,
        *weights.values(),
    )
    input_grad, sums, tail = results[0], results[1:-1], results[-1]

    def sum_shape(name, count):
        return (count, 64) if name in (COMP_MEAN, COMP_LOGVAR) else (1, count * 128)

    finished = pl.pallas_call(
        functools.partial(finish, layers),
        out_shape=tuple(jax.ShapeDtypeStruct(shape, full) for shape in share_shapes)
        + (jax.ShapeDtypeStruct((tokens, genes), full),)
        + tuple(jax.ShapeDtypeStruct(sum_shape(name, count), full) for name, count in SUMS),
        in_specs=[anywhere] * (len(layers) + 2),
        out_specs=(anywhere,) * (len(layers) + 1 + len(SUMS)),
        scratch_shapes=[pltpu.VMEM(shape, low) for shape in share_shapes]
        + [pltpu.VMEM(shape, full) for shape in share_shapes]
        + [
            pltpu.VMEM((tokens, genes), full),
            pltpu.VMEM((SUM_ROWS, 128), full),
            pltpu.VMEM((SUMS[0][1], 64), full),
            pltpu.VMEM((SUMS[1][1], 64), full),
            dma((len(layers),)),
            dma((len(layers),)),
            dma((3,)),
            dma((SUM_ROWS,)),
        ],
        compiler_params=pltpu.CompilerParams(vmem_limit_bytes=63 * 1024 * 1024),
    )(*sums, input_grad, tail)

    groups = lax.axis_size("dp") // GROUP
    d = lax.axis_index("dp")

    def shared_out(values, axis):
        if groups == 1:
            return values
        across = [[g * GROUP + r for g in range(groups)] for r in range(GROUP)]
        within = [[g * GROUP + r for r in range(GROUP)] for g in range(groups)]
        values = lax.psum(values, "dp", axis_index_groups=across)
        values = lax.all_gather(values, "dp", axis=axis, tiled=True, axis_index_groups=within)
        size = values.shape[axis] // (groups * GROUP)
        return lax.dynamic_slice_in_dim(values, d * size, size, axis=axis)

    grads = {}
    for name, values in zip(LAYERS, finished):
        grads[name] = shared_out(values, 0)
    for (name, _), values in zip(SUMS, finished[len(layers) + 1 :]):
        if name in (COMP_MEAN, COMP_LOGVAR):
            grads[name] = shared_out(values, 1)
        else:
            grads[name] = shared_out(values.reshape(-1), 0)
    return (
        finished[len(layers)].reshape(seqs, rows, genes),
        grads[GENE],
        grads[EMB_GAIN],
        grads[EMB_SHIFT],
        grads[ATTN_GAIN],
        grads[ATTN_SHIFT],
        grads[QKV],
        grads[B_QUERY],
        grads[B_VALUE],
        grads[OUT],
        grads[B_OUT],
        grads[FFN_GAIN],
        grads[FFN_SHIFT],
        grads[UP],
        grads[B_UP],
        grads[DOWN],
        grads[B_DOWN],
        grads[BOT_GAIN],
        grads[BOT_SHIFT],
        grads[ENC],
        grads[B_ENC],
        grads[COMP_MEAN],
        grads[COMP_LOGVAR],
        grads[LAT],
        grads[B_LAT],
        grads[DEC_GAIN],
        grads[DEC_SHIFT],
        grads[DEC],
        grads[B_DEC],
    )


def solution(mesh):
    rows = P("dp", "phase", None)
    return jax.shard_map(
        body,
        mesh=mesh,
        in_specs=(rows, rows, rows, P("dp", None), P("dp", None)) + (P(),) * 27,
        out_specs=(
            rows,
            P("dp", None),
            P("dp"),
            P("dp"),
            P("dp"),
            P("dp"),
            P("dp", None),
            P("dp"),
            P("dp"),
            P("dp", None),
            P("dp"),
            P("dp"),
            P("dp"),
            P("dp", None),
            P("dp"),
            P("dp", None),
            P("dp"),
            P("dp"),
            P("dp"),
            P("dp", None),
            P("dp"),
            P(None, "dp"),
            P(None, "dp"),
            P("dp", None),
            P("dp"),
            P("dp"),
            P("dp"),
            P("dp", None),
            P("dp"),
        ),
        check_vma=False,
    )
```

```python
import functools
import math

import jax
import jax.numpy as jnp
import numpy as np
from jax import lax
from jax.experimental import pallas as pl
from jax.experimental.pallas import tpu as pltpu
from jax.sharding import PartitionSpec as P

HEADS = 16
GROUP = 8
PIECE = 128
WIDE = 1024
SLOTS = 5

norm_eps = 1e-05
mask_fill = -1000000000.0
MESH = pl.DeviceIdType.MESH

(
    H2,
    DOWN,
    GENE,
    UP,
    QKV,
    DEC,
    ENC,
    OUT,
    LAT,
    EMB_GAIN,
    EMB_SHIFT,
    ATTN_GAIN,
    ATTN_SHIFT,
    B_QKV,
    B_QUERY,
    B_VALUE,
    B_OUT,
    FFN_GAIN,
    FFN_SHIFT,
    B_UP,
    B_DOWN,
    BOT_GAIN,
    BOT_SHIFT,
    B_ENC,
    COMP_MEAN,
    COMP_LOGVAR,
    B_LAT,
    DEC_GAIN,
    DEC_SHIFT,
    B_DEC,
) = range(30)


LAYERS = (DEC, DOWN, LAT, ENC, UP, OUT, QKV, GENE)
VECTORS = (
    EMB_GAIN,
    EMB_SHIFT,
    ATTN_GAIN,
    ATTN_SHIFT,
    B_QKV,
    B_OUT,
    FFN_GAIN,
    FFN_SHIFT,
    B_UP,
    B_DOWN,
    BOT_GAIN,
    BOT_SHIFT,
    B_ENC,
    B_LAT,
    DEC_GAIN,
    DEC_SHIFT,
    B_DEC,
)

VECTOR_ROWS = {B_QKV: 3, B_UP: 4, B_DEC: 2}
VECTOR_AT = {
    name: sum(VECTOR_ROWS.get(other, 1) for other in VECTORS[:i]) for i, name in enumerate(VECTORS)
}
SUMS = (
    (COMP_MEAN, 16),
    (COMP_LOGVAR, 16),
    (EMB_GAIN, 1),
    (EMB_SHIFT, 1),
    (ATTN_GAIN, 1),
    (ATTN_SHIFT, 1),
    (B_QUERY, 1),
    (B_VALUE, 1),
    (B_OUT, 1),
    (FFN_GAIN, 1),
    (FFN_SHIFT, 1),
    (B_UP, 4),
    (B_DOWN, 1),
    (BOT_GAIN, 1),
    (BOT_SHIFT, 1),
    (B_ENC, 1),
    (B_LAT, 1),
    (DEC_GAIN, 1),
    (DEC_SHIFT, 1),
    (B_DEC, 2),
)
SUM_AT = {name: sum(n for _, n in SUMS[:i]) for i, (name, _) in enumerate(SUMS)}
SUM_ROWS = 64


def mm(left, right):
    return jnp.dot(left, right, preferred_element_type=jnp.float32)


def mm_last(left, right):
    return lax.dot_general(
        left, right, (((1,), (1,)), ((), ())), preferred_element_type=jnp.float32
    )


def mm_first(left, right):
    return lax.dot_general(
        left, right, (((0,), (0,)), ((), ())), preferred_element_type=jnp.float32
    )


def normed(values):
    center = jnp.mean(values, axis=-1, keepdims=True)
    centered = values - center
    spread = jnp.mean(centered * centered, axis=-1, keepdims=True)
    scale = lax.rsqrt(spread + norm_eps)
    return centered * scale, scale


def normed_back(grad, hat, scale, gain):
    pulled = grad * gain
    mean = jnp.mean(pulled, axis=-1, keepdims=True)
    along = jnp.mean(pulled * hat, axis=-1, keepdims=True)
    return scale * (pulled - mean - hat * along)


def column_sums(values):
    return jnp.sum(values.astype(jnp.float32), axis=0, keepdims=True)


def gelu(values):
    return values * (0.5 * (1.0 + lax.erf(values * (0.5**0.5))))


def gelu_slope(values):
    bell = 0.5 * (1.0 + lax.erf(values * (0.5**0.5)))
    return bell + values * jnp.exp(-0.5 * values * values) * (2.0 * math.pi) ** -0.5


LEFT_GROUPS = ((GENE,), (DEC,), (QKV, OUT, ENC, LAT))

BLOCKS = (
    (H2, 0, 1024, 512),
    (DEC, 0, 512, 128),
    (DEC, 512, 512, 256),
    (DEC, 1024, 1024, 512),
    (DOWN, 0, 1024, 512),
    (LAT, 0, 1024, 512),
    (ENC, 0, 1024, 512),
    (UP, 0, 1024, 512),
    (UP, 1024, 1024, 512),
    (UP, 2048, 1024, 512),
    (UP, 3072, 1024, 512),
    (OUT, 0, 1024, 512),
    (QKV, 0, 1024, 512),
    (QKV, 1024, 1024, 512),
    (QKV, 2048, 1024, 512),
    (GENE, 0, 1024, 256),
)


def grad_plan(layers):
    a_off, b_off, t_off, items, place = {}, {}, {}, [], {}
    a_at, b_at, t_at, row = 0, 0, 0, 0
    shares = {name: share for name, share, _ in layers}
    for name, share, columns in layers:
        b_off[name], t_off[name] = b_at, t_at
        for block in range(columns // WIDE):
            for start in range(0, share, PIECE):
                place[name, block, start] = row
                row += min(PIECE, share - start)
        t_at += -(-share // PIECE) * PIECE
        b_at += columns
    groups = []
    for names in LEFT_GROUPS:
        first = a_at
        for name in names:
            a_off[name] = a_at
            a_at += -(-shares[name] // PIECE) * PIECE
        groups.append((first, a_at - first))
    b_off[H2] = b_at
    shares[H2] = 0
    for block, (name, first, columns, step) in enumerate(BLOCKS):
        for start in range(0, shares[name], PIECE):
            rows = min(PIECE, shares[name] - start)
            for col in range(first, first + columns, step):
                items.append((block, start, rows, col, step, place[name, col // WIDE, start]))
    return a_off, b_off, t_off, items, row, groups, b_at + WIDE, t_at


ORDER = (
    0, 1, 2, 3, 100, 4, 5, 6, 7, 8, 9, 200, 101, 102, 10, 11, 12, 13,
    300, 14, 15, 201, 400, 1000, 202, 301, 104, 16, 401, 500, 302, 501, 502, 503, 402, 600,
    504, 601, 505, 17, 204, 103, 107, 700, 701, 602, 603, 604, 605, 304, 800, 801, 18, 702,
    703, 404, 704, 508, 509, 19, 510, 203, 108, 705, 511, 512, 902, 513, 514, 20, 515, 207,
    109, 802, 803, 804, 805, 608, 609, 303, 21, 610, 403, 708, 506, 611, 208, 110, 507, 709,
    612, 808, 307, 710, 613, 809, 22, 209, 111, 407, 520, 521, 711, 308, 810, 712, 713, 614,
    615, 408, 522, 523, 811, 210, 112, 606, 812, 714, 607, 813, 23, 309, 715, 814, 620, 706,
    621, 409, 524, 525, 211, 113, 815, 707, 416, 622, 310, 720, 806, 623, 410, 526, 544, 721,
    527, 807, 624, 212, 114, 722, 820, 625, 311, 723, 626, 411, 528, 529, 821, 724, 213, 115,
    822, 627, 312, 725, 823, 628, 412, 726, 530, 531, 629, 644, 824, 214, 106, 727, 825, 313,
    630, 728, 826, 413, 532, 631, 533, 729, 827, 215, 105, 730, 744, 314, 828, 632, 731, 414,
    534, 535, 633, 829, 206, 830, 732, 315, 634, 831, 844, 733, 415, 536, 537, 538, 635, 539,
    540, 541, 205, 734, 542, 543, 636, 832, 833, 306, 637, 735, 638, 305, 406, 736, 518, 639,
    519, 737, 834, 640, 405, 738, 516, 641, 517, 835, 739, 836, 642, 740, 837, 643, 741, 838,
    742, 839, 618, 743, 840, 841, 619, 842, 616, 843, 718, 617, 719, 716, 818, 717, 819, 816,
    817,
)


def everything(layers, n_vec, *refs):
    low, full = jnp.bfloat16, jnp.float32
    refs = list(refs)

    def pop(count):
        taken = refs[:count]
        del refs[:count]
        return taken

    expr_in, gene_masks_in, segments_in, mean_in, logvar_in = pop(5)
    vectors_in = pop(n_vec)
    table_ref, target_ref, noise_ref = pop(3)
    w_gene, w_qkv, w_out, w_up, w_down, w_enc, w_lat, w_dec = pop(8)
    (input_ref,) = pop(1)
    out_refs = dict(zip([name for name, _, _ in layers], pop(len(layers))))
    (tail_ref,) = pop(1)
    expr_ref, gene_masks_ref, segments_ref, tables, vec_all, in_sem = pop(6)
    ring, masks_own, masks_all, table, target_in, noise_in, x1_out, x1_in = pop(8)
    kv_all, query_own, probs, dkv_part, dkv_in, dx_out, dx_in = pop(7)
    hats, scales = pop(2)
    a_src, a_all, turned, up_part, b_all, v_src, v_all, near, far, v_near, v_far = pop(11)
    ring_sem, hand_send, hand_recv, hand_local, pair_send, pair_recv = pop(6)
    one_sem, a_send, a_recv, a_local, v_send, v_recv, b_send, b_recv, c_send, c_recv, o_sem = pop(11)

    expr_copy = pltpu.make_async_copy(expr_in, expr_ref, in_sem.at[0])
    mask_copies = (
        pltpu.make_async_copy(gene_masks_in, gene_masks_ref, in_sem.at[1]),
        pltpu.make_async_copy(segments_in, segments_ref, in_sem.at[2]),
    )
    mean_ref, logvar_ref = tables.at[0], tables.at[1]

    def start_inputs():
        for name, src in zip(VECTORS, vectors_in):
            at = pl.ds(VECTOR_AT[name] * WIDE, src.shape[1])
            pltpu.make_async_copy(src, vec_all.at[:, at], in_sem.at[3]).start()
        pltpu.make_async_copy(mean_in, mean_ref, in_sem.at[4]).start()
        pltpu.make_async_copy(logvar_in, logvar_ref, in_sem.at[4]).start()

    expr_copy.start()
    for copy in mask_copies:
        copy.start()

    d = lax.axis_index("dp")
    z = lax.axis_index("phase")
    base = (d // GROUP) * GROUP
    r = d % GROUP
    core, cx, cy = r % 2, (r // 2) % 2, r // 4
    partner = d + 1 - 2 * core
    owner = d - core + z // 2
    own = core == z // 2
    rc, rx, ry = r + 1 - 2 * core, r + 2 - 4 * cx, r + 4 - 8 * cy
    rxc, ryc = rx + 1 - 2 * core, ry + 1 - 2 * core
    rd = rx + 4 - 8 * cy
    rdc = rd + 1 - 2 * core
    middle = (z % 3) != 0
    inward = z + 1 - 2 * (z // 2)
    outward = z - 1 + 2 * (z // 2)
    a_off, b_off, t_off, items, _, left_groups, _, _ = grad_plan(layers)
    blocks = len(BLOCKS)
    shares = {name: share for name, share, _ in layers}
    seqs, rows, genes = expr_ref.shape
    tokens = seqs * rows
    width = table.shape[1]
    hidden = w_up.shape[1]
    length = segments_ref.shape[1]
    wide = WIDE

    barrier = pltpu.get_barrier_semaphore()

    def greet(to):
        pl.semaphore_signal(barrier, inc=1, device_id=to, device_id_type=MESH)

    for step in range(1, GROUP):
        greet((base + (r + step) % GROUP, z))
    greet((d, inward))

    @pl.when(middle)
    def _():
        greet((d, outward))

    for i in range(2):

        @pl.when(jnp.logical_not(own & (z % 2 == i)))
        def _():
            greet((owner, 2 * core + i))

    def barrier_wait():
        pl.semaphore_wait(barrier, GROUP + 1 + (z % 3 + 1) // 2 + (core + z // 2) % 2)

    def remote(src, dst, send, recv, to):
        return pltpu.make_async_remote_copy(
            src_ref=src,
            dst_ref=dst,
            send_sem=send,
            recv_sem=recv,
            device_id=to,
            device_id_type=MESH,
        )

    def columns_of(index):
        return pl.ds(*left_groups[index])

    def a_copy(index, step):
        at, to = columns_of(index), (r + step) % GROUP
        return remote(
            a_src.at[to, :, at],
            a_all.at[r, :, at],
            a_send.at[index],
            a_recv.at[index],
            (base + to, z),
        )

    def a_seven(index):
        part = a_all.at[pl.ds(0, GROUP - 1), :, columns_of(index)]
        return remote(part, part, a_send.at[index], a_recv.at[index], (base + rc, z))

    def a_own(index):
        at = columns_of(index)
        return pltpu.make_async_copy(a_src.at[r, :, at], a_all.at[r, :, at], a_local.at[index])

    def send_a(index):
        for step in range(1, GROUP):
            a_copy(index, step).start()
        a_own(index).start()

    def arrive_a(index):
        a_own(index).wait()
        a_seven(index).wait_recv()
        a_seven(index).wait_send()

    def v_copy(step):
        to = (r + step) % GROUP
        return remote(v_src.at[to], v_all.at[r], v_send.at[0], v_recv.at[0], (base + to, z))

    def v_seven():
        part = v_all.at[pl.ds(0, GROUP - 1)]
        return remote(part, part, v_send.at[0], v_recv.at[0], (base + rc, z))

    own_sums = pltpu.make_async_copy(v_src.at[r], v_all.at[r], one_sem.at[0])

    goes = (r, r, r, rx, ry, rx, ry, rd)
    counts = (0, 0, 2, 2, 2, 1, 1, 2)

    def b_start(kind, block):
        name, first, size, _ = BLOCKS[block]
        col = b_off[name] + first
        if kind in (5, 6):
            size //= 2
        if kind == 6:
            col += size
        to = (rx, ry, rc, rc, rc, ry, rx, rc)[kind]
        view = b_all.at[goes[kind], :, pl.ds(col, size)]
        recv = b_recv.at[block, counts[kind]]
        remote(view, view, b_send.at[block], recv, (base + to, z)).start()

    def b_bytes(block, way, many):
        name, first, size, _ = BLOCKS[block]
        part = b_all.at[pl.ds(0, many), :, pl.ds(b_off[name] + first, size)]
        return remote(part, part, b_send.at[block], b_recv.at[block, way], (base + rc, z))

    def neighbours_here(block):
        b_bytes(block, 0, 2).wait_recv()

    def halves_here(block):
        b_bytes(block, 1, 1).wait_recv()

    def beside_here(block):
        b_bytes(block, 2, 4).wait_recv()

    def block_sent(block):
        b_bytes(block, 0, GROUP - 1).wait_send()

    vectors = len(items)

    def place_of(ref, v_ref, index):
        if index == vectors:
            return v_ref
        _, _, count, col, size, row = items[index]
        return ref.at[pl.ds(row, count), pl.ds(col % WIDE, size)]

    def is_vec(index):
        return 1 if index == vectors else 0

    def to_middle(index, to):
        ref = place_of(near, v_near, index)
        return remote(ref, ref, c_send.at[0, is_vec(index)], c_recv.at[index, 0], (d, to))

    def across(index):
        src, dst = place_of(near, v_near, index), place_of(far, v_far, index)
        return remote(src, dst, c_send.at[1, is_vec(index)], c_recv.at[index, 1], (d, inward))

    def to_end(index, to):
        ref = place_of(far, v_far, index)
        return remote(ref, ref, c_send.at[0, is_vec(index)], c_recv.at[index, 0], (d, to))

    def result(index, ref, v_ref):
        src = place_of(ref, v_ref, index)
        if index == vectors:
            return pltpu.make_async_copy(src, tail_ref, o_sem.at[1])
        block, start, count, col, size, _ = items[index]
        to = out_refs[BLOCKS[block][0]].at[pl.ds(start, count), pl.ds(col, size)]
        return pltpu.make_async_copy(src, to, o_sem.at[0])

    def product(index):
        if index == vectors:
            return jnp.sum(v_all[...], axis=0)
        block, start, count, col, size, _ = items[index]
        name = BLOCKS[block][0]
        a_at = t_off[name] + start
        b_at = b_off[name] + col
        right = b_all[:, :, b_at : b_at + size].reshape(-1, size)
        value = mm(turned[a_at : a_at + PIECE, :], right)
        if count < PIECE:
            value = jnp.where(r % 2 == 1, value[count : 2 * count], value[:count])
        return value

    def end_push(index):
        @pl.when(jnp.logical_not(middle))
        def _():
            ref = place_of(near, v_near, index)
            ref[...] = product(index).astype(ref.dtype)
            to_middle(index, inward).start()

    def middle_join(index):
        @pl.when(middle)
        def _():
            value = product(index)
            to_middle(index, inward).wait_recv()
            ref = place_of(near, v_near, index)
            ref[...] = (value + ref[...].astype(full)).astype(ref.dtype)
            across(index).start()

    def middle_total(index):
        @pl.when(middle)
        def _():
            across(index).wait_recv()
            mine, theirs = place_of(near, v_near, index), place_of(far, v_far, index)
            both = mine[...].astype(full) + theirs[...].astype(full)
            theirs[...] = both.astype(theirs.dtype)
            to_end(index, outward).start()
            result(index, far, v_far).start()

    def end_land(index):
        @pl.when(jnp.logical_not(middle))
        def _():
            to_end(index, inward).wait_recv()
            result(index, far, v_far).start()


    up_columns = pl.ds(pl.multiple_of(r * shares[DOWN], PIECE), shares[DOWN])
    up_copy = pltpu.make_async_copy(w_up.at[:, up_columns], up_part, one_sem.at[4])
    up_copy.start()

    def make_lefts(_):
        own_columns = pl.ds(pl.multiple_of(b_off[H2] + r * PIECE, PIECE), PIECE)
        at = t_off[UP]
        turned[at : at + PIECE, :] = b_all[:, :, own_columns].reshape(-1, PIECE).T
        up_copy.wait()
        own_bias = pl.multiple_of(VECTOR_AT[B_UP] * WIDE + r * shares[DOWN], PIECE)
        bias = vec_all[:, pl.ds(own_bias, shares[DOWN])]
        count = GROUP // 2
        for slot in range(0, GROUP, count):
            h2 = b_all[slot : slot + count, :, b_off[H2] : b_off[H2] + width].reshape(-1, width)
            active = gelu(mm(h2, up_part[...]) + bias).astype(low)
            turned[
                t_off[DOWN] : t_off[DOWN] + shares[DOWN],
                slot * tokens : (slot + count) * tokens,
            ] = active.T

    group_of = {name: index for index, names in enumerate(LEFT_GROUPS) for name in names}
    gone, arrived, turned_already = [], set(), set()

    def get(block):
        if block == blocks:
            own_sums.wait()
            v_seven().wait_recv()
            return
        gone.append(block)
        beside_here(block)
        if len(gone) > 3:
            block_sent(gone[-4])
        name = BLOCKS[block][0]
        if name not in a_off or name in turned_already:
            return
        turned_already.add(name)
        if group_of[name] not in arrived:
            arrived.add(group_of[name])
            arrive_a(group_of[name])
        for start in range(0, shares[name], PIECE):
            at, to = a_off[name] + start, t_off[name] + start
            turned[to : to + PIECE, :] = a_all[:, :, at : at + PIECE].reshape(-1, PIECE).T

    table_copy = pltpu.make_async_copy(
        table_ref.at[pl.ds(z * rows, rows), :], table, one_sem.at[1]
    )
    input_copies = [
        pltpu.make_async_copy(
            hats.at[1 + j], input_ref.at[:, pl.ds(j * wide, wide)], one_sem.at[(2, 5)[j]]
        )
        for j in range(genes // wide)
    ]

    def held(j):
        each = 2 * width // wide
        return dkv_part.at[j // each, :, pl.ds(j % each * wide, wide)]

    pair_local = one_sem.at[3]
    table_copy.start()
    start_inputs()

    def rows_work():
        stream = []
        for j in range(genes // wide):
            stream.append(w_gene.at[pl.ds(j * wide, wide), :])
        for j in (1, 2, 0):
            stream.append(w_qkv.at[:, pl.ds(j * wide, wide)])
        stream.append(w_out)
        for j in range(hidden // wide):
            stream.append(w_up.at[:, pl.ds(j * wide, wide)])
            stream.append(w_down.at[pl.ds(j * wide, wide), :])
        stream.append(w_enc)
        stream.append(w_lat)
        for j in range(genes // wide):
            stream.append(w_dec.at[:, pl.ds(j * wide, wide)])
        stream.append(w_lat)
        stream.append(w_enc)
        for j in range(hidden // wide):
            stream.append(w_down.at[pl.ds(j * wide, wide), :])
            stream.append(w_up.at[:, pl.ds(j * wide, wide)])
        stream.append(w_out)
        for j in range(3):
            stream.append(w_qkv.at[:, pl.ds(j * wide, wide)])
        for j in range(genes // wide):
            stream.append(w_gene.at[pl.ds(j * wide, wide), :])

        def load(k):
            depth = stream[k].shape[0]
            return pltpu.make_async_copy(
                stream[k], ring.at[k % SLOTS, pl.ds(0, depth), :], ring_sem.at[k % SLOTS]
            )

        def fetch(k):
            if k < len(stream):
                load(k).start()

        place = [0]

        def take():
            k = place[0]
            place[0] += 1
            load(k).wait()
            return k

        def block(k):
            return ring[k % SLOTS, : stream[k].shape[0], :]

        for k in range(SLOTS):
            fetch(k)

        def hand(which, src, dst, i):
            return pltpu.make_async_remote_copy(
                src_ref=src.at[i],
                dst_ref=dst.at[z % 2],
                send_sem=hand_send.at[which, i],
                recv_sem=hand_recv.at[which, z % 2],
                device_id=(owner, 2 * core + i),
                device_id_type=MESH,
            )

        def hand_here(which, src, dst, i):
            return pltpu.make_async_copy(src.at[i], dst.at[i], hand_local.at[which])

        def hand_start(which, src, dst):
            for i in range(2):
                here = own & (z % 2 == i)

                @pl.when(here)
                def _():
                    hand_here(which, src, dst, i).start()

                @pl.when(jnp.logical_not(here))
                def _():
                    hand(which, src, dst, i).start()

        def hand_arrive(which, src, dst):
            for i in range(2):
                here = own & (z % 2 == i)

                @pl.when(here)
                def _():
                    hand_here(which, src, dst, i).wait()

                @pl.when(jnp.logical_not(here))
                def _():
                    pltpu.make_async_remote_copy(
                        src_ref=src.at[i],
                        dst_ref=dst.at[i],
                        send_sem=hand_send.at[which, i],
                        recv_sem=hand_recv.at[which, i],
                        device_id=(owner, 2 * core + i),
                        device_id_type=MESH,
                    ).wait_recv()

        def hand_sent(which, src, dst):
            for i in range(2):
                @pl.when(jnp.logical_not(own & (z % 2 == i)))
                def _():
                    hand(which, src, dst, i).wait_send()

        def pair(which, src, dst):
            return pltpu.make_async_remote_copy(
                src_ref=src,
                dst_ref=dst,
                send_sem=pair_send.at[which],
                recv_sem=pair_recv.at[which],
                device_id=(partner, z),
                device_id_type=MESH,
            )

        expr_copy.wait()
        for copy in mask_copies:
            copy.wait()
        masks_own[:seqs, :genes] = gene_masks_ref[...].astype(full)
        masks_own[:seqs, genes : genes + length] = segments_ref[...].astype(full)
        own_masks = pltpu.make_async_copy(masks_own, masks_all.at[core], pair_local)
        own_masks.start()

        def vec(name, j=0):
            at = (VECTOR_AT[name] + j) * wide
            return vec_all[:, at : at + wide]

        def put_a(name, values):
            off, share = a_off[name], shares[name]
            step = max(share, PIECE)
            for o in range(GROUP):
                start = o * share // step * step
                a_src[o, :, off : off + step] = values[:, start : start + step]

        def put_b(name, j, values):
            at = b_off[name] + j * wide
            b_all[r, :, at : at + wide] = values

        def put_sum(name, values, j=0):
            each = SUM_LANES[name]
            for o in range(values.shape[1] // 128):
                at = j * wide + o * 128
                to, row = at // (128 * each), SUM_AT[name] + at // 128 % each
                v_src[to, row : row + 1, :] = values[:, o * 128 : o * 128 + 128]

        def normalize(index, values, gain, shift):
            hat, scale = normed(values)
            hats[index] = hat
            scales[index] = jnp.broadcast_to(scale, scales.shape[1:])
            return hat * vec(gain) + vec(shift)

        def normalize_back(index, grad, gain, gain_name, shift_name):
            hat, scale = hats[index], scales[index, :, :1]
            put_sum(gain_name, jnp.sum(grad * hat, axis=0, keepdims=True))
            put_sum(shift_name, jnp.sum(grad, axis=0, keepdims=True))
            return normed_back(grad, hat, scale, vec(gain))

        keep = 1.0 - masks_own[:seqs, :genes]
        keep = jnp.concatenate(
            [jnp.broadcast_to(keep[s : s + 1], (rows, genes)) for s in range(seqs)], axis=0
        )
        masked = (expr_ref[...].reshape(tokens, genes).astype(full) * keep).astype(low)
        put_a(GENE, masked)
        table_copy.wait()
        embedded = jnp.concatenate([table[...]] * seqs, axis=0)
        for j in range(genes // wide):
            k = take()
            embedded += mm(masked[:, j * wide : (j + 1) * wide], block(k))
            fetch(k + SLOTS)
        pltpu.make_async_copy(vec_all, vec_all, in_sem.at[3]).wait()
        x1_out[...] = (
            normalize(0, embedded, EMB_GAIN, EMB_SHIFT).astype(low).reshape(seqs, rows, width)
        )
        barrier_wait()
        hand_start(0, x1_out, x1_in)
        pair(0, masks_own, masks_all.at[core]).start()
        send_a(0)
        hand_start(1, noise_ref, noise_in)
        hand_start(2, target_ref, target_in)
        yield
        own_masks.wait()
        pair(0, masks_own, masks_all.at[1 - core]).wait_recv()
        odd = z % 2 == 1
        both_masks = masks_all[pl.ds(z // 2, 1)][0]
        mask_row = jnp.where(odd, both_masks[1:2], both_masks[0:1])
        gene_row = mask_row[:, :genes]
        segments = mask_row[:, genes : genes + length]
        place_q = lax.broadcasted_iota(jnp.int32, (tokens, length), 0) + core * tokens
        place_k = lax.broadcasted_iota(jnp.int32, (tokens, length), 1)
        own_segments = jnp.sum(
            jnp.where(place_q == place_k, segments, 0.0), axis=-1, keepdims=True
        )
        same = own_segments == segments
        same = jnp.concatenate([same.astype(full)] * 2, axis=0) > 0.5

        hand_arrive(0, x1_out, x1_in)
        x1 = x1_in[...].reshape(tokens, width).astype(full)
        h1 = normalize(1, x1, ATTN_GAIN, ATTN_SHIFT).astype(low)
        put_a(QKV, h1)
        head = width // HEADS
        scale = head**-0.5
        for j in (1, 2):
            k = take()
            kv_all[core, :, (j - 1) * wide : j * wide] = (
                mm(h1, block(k)) + vec(B_QKV, j)
            ).astype(low)
            fetch(k + SLOTS)
        pair(1, kv_all.at[core], kv_all.at[core]).start()
        k = take()
        query_own[...] = (mm(h1, block(k)) + vec(B_QKV, 0)).astype(low)
        fetch(k + SLOTS)
        yield
        pair(1, kv_all.at[core], kv_all.at[1 - core]).wait_recv()

        lanes = lax.broadcasted_iota(jnp.int32, (tokens, 2 * head), 1)
        first = lanes < head
        pairs = HEADS // 2

        def two(values):
            none = jnp.zeros_like(values)
            return jnp.concatenate([jnp.where(first, values, none), jnp.where(first, none, values)], axis=0)

        def one(values):
            return jnp.where(first, values[:tokens], values[tokens:])

        def columns(p):
            return pl.ds(pl.multiple_of(p * 2 * head, 2 * head), 2 * head)

        def keys_of(p):
            return kv_all[:, :, columns(p)].reshape(length, 2 * head)

        def values_of(p):
            at = pl.ds(pl.multiple_of(width + p * 2 * head, 2 * head), 2 * head)
            return kv_all[:, :, at].reshape(length, 2 * head)

        def attend(p, carry):
            scores = mm_last(two(query_own[:, columns(p)]), keys_of(p)) * scale
            scores = jnp.where(same, scores, mask_fill)
            shifted = jnp.exp(scores - jnp.max(scores, axis=-1, keepdims=True))
            prob = shifted / jnp.sum(shifted, axis=-1, keepdims=True)
            probs[p] = prob
            att = one(mm(prob.astype(low), values_of(p))).astype(low)
            a_src[p, :, a_off[OUT] : a_off[OUT] + 2 * head] = att
            return carry

        lax.fori_loop(0, pairs, attend, 0)
        yield
        attended = jnp.concatenate(
            [a_src[o, :, a_off[OUT] : a_off[OUT] + 2 * head] for o in range(pairs)], axis=1
        )
        k = take()
        mixed = x1 + (mm(attended, block(k)) + vec(B_OUT))
        fetch(k + SLOTS)
        h2 = normalize(2, mixed, FFN_GAIN, FFN_SHIFT).astype(low)
        b_all[r, :, b_off[H2] : b_off[H2] + width] = h2
        yield
        x2 = mixed + vec(B_DOWN)
        for j in range(hidden // wide):
            k = take()
            before = mm(h2, block(k)) + vec(B_UP, j)
            fetch(k + SLOTS)
            held(j)[...] = before
            active = gelu(before).astype(low)
            k = take()
            x2 += mm(active, block(k))
            fetch(k + SLOTS)
            yield
        x2 = x2.astype(low).astype(full)
        h3 = normalize(3, x2, BOT_GAIN, BOT_SHIFT).astype(low)
        put_a(ENC, h3)
        k_enc = take()
        moments = mm(h3, block(k_enc)) + vec(B_ENC)
        latents = width // 2
        logvar = moments[:, latents:]
        hand_arrive(1, noise_ref, noise_in)
        swing = jnp.exp(0.5 * logvar) * noise_in[...].reshape(tokens, latents).astype(full)
        latent = moments[:, :latents] + swing
        latent_low = latent.astype(low)
        put_a(LAT, latent_low)
        fetch(k_enc + SLOTS)
        k_lat = take()
        lat_before = mm(latent_low, block(k_lat)) + vec(B_LAT)
        fetch(k_lat + SLOTS)
        x3 = gelu(lat_before).astype(low).astype(full)
        h4 = normalize(4, x3, DEC_GAIN, DEC_SHIFT).astype(low)
        put_a(DEC, h4)
        send_a(1)
        yield
        hand_arrive(2, target_ref, target_in)

        grad = jnp.zeros((tokens, width), full)
        for j in range(genes // wide):
            k = take()
            at = slice(j * wide, (j + 1) * wide)
            predicted = mm(h4, block(k)) + vec(B_DEC, j)
            wanted = target_in[:, :, at].reshape(tokens, wide).astype(full)
            d_pred = (gene_row[:, at] * (predicted - wanted)).astype(low)
            put_b(DEC, j, d_pred)
            put_sum(B_DEC, column_sums(d_pred), j)
            grad += mm_last(d_pred, block(k))
            fetch(k + SLOTS)
            yield
        d_x3 = normalize_back(4, grad, DEC_GAIN, DEC_GAIN, DEC_SHIFT).astype(low).astype(full)
        d_lat = (gelu_slope(lat_before) * d_x3).astype(low)
        put_b(LAT, 0, d_lat)
        put_sum(B_LAT, column_sums(d_lat))
        k = take()
        d_latent = mm_last(d_lat, block(k))
        fetch(k + SLOTS)
        yield

        pltpu.make_async_copy(tables, tables, in_sem.at[4]).wait()
        inverse = jnp.exp(-logvar_ref[...])
        volume = jnp.sum(logvar_ref[...], axis=-1, keepdims=True)
        count = mean_ref.shape[0]
        scaled = []
        for c in range(count):
            offset = latent - mean_ref[c : c + 1, :]
            quad = jnp.sum(offset * offset * inverse[c : c + 1], axis=-1, keepdims=True)
            scaled.append(-0.5 * (quad + volume[c : c + 1]))
        highest = functools.reduce(jnp.maximum, scaled)
        shares_c = [jnp.exp(s - highest) for s in scaled]
        whole = functools.reduce(jnp.add, shares_c)
        parts = [part / whole for part in shares_c]
        for c in range(count):
            pull = (latent - mean_ref[c : c + 1, :]) * inverse[c : c + 1]
            d_latent += parts[c] * pull
        d_moments = jnp.concatenate([d_latent, 0.5 * d_latent * swing - 0.5], axis=1).astype(low)
        put_b(ENC, 0, d_moments)
        put_sum(B_ENC, column_sums(d_moments))
        yield
        k = take()
        grad = mm_last(d_moments, block(k))
        fetch(k + SLOTS)
        g = normalize_back(3, grad, BOT_GAIN, BOT_GAIN, BOT_SHIFT).astype(low)
        put_b(DOWN, 0, g)
        put_sum(B_DOWN, column_sums(g))
        yield
        for c in range(count):
            offset = latent - mean_ref[c : c + 1, :]
            weighted = parts[c] * (offset * inverse[c : c + 1])
            mean_grad = -jnp.sum(weighted, axis=0, keepdims=True)
            logvar_grad = 0.5 * jnp.sum(parts[c] - weighted * offset, axis=0, keepdims=True)
            for o in range(GROUP):
                at = slice(o // 2 * 128, o // 2 * 128 + 128)
                row = SUM_AT[COMP_MEAN] + c
                v_src[o, row : row + 1, :] = mean_grad[:, at]
                row = SUM_AT[COMP_LOGVAR] + c
                v_src[o, row : row + 1, :] = logvar_grad[:, at]
        yield
        grad = jnp.zeros((tokens, width), full)
        for j in range(hidden // wide):
            k = take()
            d_active = mm_last(g, block(k))
            fetch(k + SLOTS)
            slope = gelu_slope(held(j)[...])
            d_before = (slope * d_active).astype(low)
            put_b(UP, j, d_before)
            put_sum(B_UP, column_sums(d_before), j)
            k = take()
            grad += mm_last(d_before, block(k))
            fetch(k + SLOTS)
            yield
        d_mixed = g.astype(full) + normalize_back(2, grad, FFN_GAIN, FFN_GAIN, FFN_SHIFT)
        hats[3] = d_mixed
        da = d_mixed.astype(low)
        put_b(OUT, 0, da)
        put_sum(B_OUT, column_sums(da))
        k = take()
        x1_in[...] = mm_last(da, block(k)).astype(low).reshape(seqs, rows, width)
        fetch(k + SLOTS)
        yield
        q_at = b_off[QKV]

        def attend_back(p, carry):
            query = two(query_own[:, columns(p)])
            d_att = two(x1_in[:, :, columns(p)].reshape(tokens, 2 * head))
            prob = probs[p]
            keys = keys_of(p)
            d_value = mm_first(prob.astype(low), d_att)
            d_prob = mm_last(d_att, values_of(p))
            d_score = prob * (d_prob - jnp.sum(prob * d_prob, axis=-1, keepdims=True))
            d_score = d_score.astype(low)
            d_query = one(mm(d_score, keys)) * scale
            d_key = mm_first(d_score, query) * scale
            to = pl.ds(pl.multiple_of(q_at + p * 2 * head, 2 * head), 2 * head)
            b_all[r, :, to] = d_query.astype(low)
            dkv_part[:, :, columns(p)] = d_key.reshape(2, tokens, 2 * head)
            at = pl.ds(pl.multiple_of(width + p * 2 * head, 2 * head), 2 * head)
            dkv_part[:, :, at] = d_value.reshape(2, tokens, 2 * head)
            return carry

        lax.fori_loop(0, pairs // 2, attend_back, 0)
        yield
        lax.fori_loop(pairs // 2, pairs, attend_back, 0)
        pair(2, dkv_part.at[1 - core], dkv_in).start()
        yield
        d_query = b_all[r, :, q_at : q_at + wide]
        put_sum(B_QUERY, column_sums(d_query))
        k = take()
        grad = mm_last(d_query, block(k))
        fetch(k + SLOTS)
        pair(2, dkv_part.at[1 - core], dkv_in).wait_recv()
        for j in (1, 2):
            at = slice((j - 1) * wide, j * wide)
            d_part = (dkv_part[core, :, at] + dkv_in[:, at]).astype(low)
            put_b(QKV, j, d_part)
            if j == 2:
                put_sum(B_VALUE, column_sums(d_part))
            k = take()
            grad += mm_last(d_part, block(k))
            fetch(k + SLOTS)
        d_x1 = hats[3] + normalize_back(1, grad, ATTN_GAIN, ATTN_GAIN, ATTN_SHIFT)
        dx_out[...] = d_x1.astype(low).reshape(seqs, rows, width)
        hand_start(3, dx_out, dx_in)
        yield
        hand_arrive(3, dx_out, dx_in)
        d_x1 = dx_in[...].reshape(tokens, width).astype(full)
        d_embedded = normalize_back(0, d_x1, EMB_GAIN, EMB_GAIN, EMB_SHIFT).astype(low)
        put_b(GENE, 0, d_embedded)
        for j in range(genes // wide):
            k = take()
            at = slice(j * wide, (j + 1) * wide)
            hats[1 + j] = mm_last(d_embedded, block(k)) * jnp.concatenate(
                [
                    jnp.broadcast_to(1.0 - masks_own[s : s + 1, at], (rows, wide))
                    for s in range(seqs)
                ],
                axis=0,
            )
        for copy in input_copies:
            copy.start()
        for step in range(1, GROUP):
            v_copy(step).start()
        own_sums.start()
        yield
        for copy in input_copies:
            copy.wait()
        hand_sent(0, x1_out, x1_in)
        hand_sent(1, noise_ref, noise_in)
        hand_sent(2, target_ref, target_in)
        hand_sent(3, dx_out, dx_in)
        pair(0, masks_own, masks_all.at[core]).wait_send()
        pair(1, kv_all.at[core], kv_all.at[core]).wait_send()
        pair(2, dkv_part.at[1 - core], dkv_in).wait_send()


    work = rows_work()
    for code in ORDER:
        kind, index = code // 100, code % 100
        if kind == 0:
            next(work)
        elif kind == 1:
            for way in (0, 1, 2):
                b_start(way, index)
        elif kind == 2:
            neighbours_here(index)
            for way in (5, 6, 3, 4):
                b_start(way, index)
        elif kind == 3:
            halves_here(index)
            b_start(7, index)
        else:
            (get, end_push, middle_join, middle_total, end_land, send_a, make_lefts)[kind - 4](index)
    next(work, None)
    for block in gone[-3:]:
        block_sent(block)
    v_seven().wait_send()

    def sums_sent(leg):
        for vec_too, ref in ((0, near), (1, v_near)):
            remote(ref, ref, c_send.at[leg, vec_too], c_recv.at[0, 0], (d, inward)).wait_send()

    sums_sent(0)

    @pl.when(middle)
    def _():
        sums_sent(1)

    pltpu.make_async_copy(near, far, o_sem.at[0]).wait()
    pltpu.make_async_copy(v_near, v_far, o_sem.at[1]).wait()


SUM_LANES = dict(SUMS)


def finish(layers, *refs):
    refs = list(refs)
    count = len(layers)
    low_refs, refs = refs[:count], refs[count:]
    input_ref, tail_ref = refs[:2]
    refs = refs[2:]
    full_refs, refs = refs[:count], refs[count:]
    input_out = refs[0]
    sum_refs = dict(zip([name for name, _ in SUMS], refs[1 : 1 + len(SUMS)]))
    refs = refs[1 + len(SUMS) :]
    low_bufs, full_bufs = refs[:count], refs[count : 2 * count]
    input_buf, tail_buf, mean_buf, logvar_buf, in_sem, out_sem, move_sem, sum_sem = refs[2 * count :]
    move_in = pltpu.make_async_copy(input_ref, input_buf, move_sem.at[0])
    move_out = pltpu.make_async_copy(input_buf, input_out, move_sem.at[1])
    tail_in = pltpu.make_async_copy(tail_ref, tail_buf, move_sem.at[2])
    ins = [
        pltpu.make_async_copy(src, dst, in_sem.at[i])
        for i, (src, dst) in enumerate(zip(low_refs, low_bufs))
    ]
    outs = [
        pltpu.make_async_copy(src, dst, out_sem.at[i])
        for i, (src, dst) in enumerate(zip(full_bufs, full_refs))
    ]
    for copy in ins:
        copy.start()
    tail_in.start()
    move_in.start()
    for i in range(count):
        ins[i].wait()
        full_bufs[i][...] = low_bufs[i][...].astype(jnp.float32)
        outs[i].start()
    move_in.wait()
    move_out.start()
    tail_in.wait()
    odd = lax.axis_index("dp") % 2 == 1
    rows_of = dict(SUMS)
    for name, buf in ((COMP_MEAN, mean_buf), (COMP_LOGVAR, logvar_buf)):
        both = tail_buf[SUM_AT[name] : SUM_AT[name] + rows_of[name], :]
        buf[...] = jnp.where(odd, both[:, 64:], both[:, :64])
    sums = [
        pltpu.make_async_copy(mean_buf, sum_refs[COMP_MEAN], sum_sem.at[0]),
        pltpu.make_async_copy(logvar_buf, sum_refs[COMP_LOGVAR], sum_sem.at[1]),
    ]
    for name, rows in SUMS[2:]:
        for row in range(rows):
            sums.append(
                pltpu.make_async_copy(
                    tail_buf.at[pl.ds(SUM_AT[name] + row, 1), :],
                    sum_refs[name].at[:, pl.ds(row * 128, 128)],
                    sum_sem.at[len(sums)],
                )
            )
    for copy in sums:
        copy.start()
    for copy in sums + outs:
        copy.wait()
    move_out.wait()


def positions(length, width):
    frequency = np.exp(np.arange(width // 2, dtype=np.float32) * np.float32(-2.0 * math.log(10000.0) / width))
    angles = np.arange(length, dtype=np.float32)[:, None] * frequency[None, :]
    return np.stack([np.sin(angles), np.cos(angles)], axis=-1).reshape(length, width)


def body(expression, targets, noise, gene_masks, segment_ids, w_gene, emb_gain, emb_shift, attn_gain, attn_shift, w_qkv, b_qkv, w_out, b_out, ffn_gain, ffn_shift, w_up, b_up, w_down, b_down, bot_gain, bot_shift, w_enc, b_enc, comp_mean, comp_logvar, w_lat, b_lat, dec_gain, dec_shift, w_dec, b_dec):
    low, full = jnp.bfloat16, jnp.float32
    seqs, rows, genes = expression.shape
    width = w_gene.shape[1]
    hidden = w_up.shape[1]
    latents = noise.shape[2]
    length = segment_ids.shape[1]
    tokens = seqs * rows
    given = {
        EMB_GAIN: emb_gain,
        EMB_SHIFT: emb_shift,
        ATTN_GAIN: attn_gain,
        ATTN_SHIFT: attn_shift,
        B_QKV: b_qkv,
        B_OUT: b_out,
        FFN_GAIN: ffn_gain,
        FFN_SHIFT: ffn_shift,
        B_UP: b_up,
        B_DOWN: b_down,
        BOT_GAIN: bot_gain,
        BOT_SHIFT: bot_shift,
        B_ENC: b_enc,
        B_LAT: b_lat,
        DEC_GAIN: dec_gain,
        DEC_SHIFT: dec_shift,
        B_DEC: b_dec,
    }
    weights = {
        GENE: w_gene,
        QKV: w_qkv,
        OUT: w_out,
        UP: w_up,
        DOWN: w_down,
        ENC: w_enc,
        LAT: w_lat,
        DEC: w_dec,
    }
    layers = [
        (name, weights[name].shape[0] // GROUP, weights[name].shape[1]) for name in LAYERS
    ]
    _, _, _, items, rows_all, left_groups, b_cols, t_rows = grad_plan(layers)
    a_cols = sum(size for _, size in left_groups)
    anywhere = pl.BlockSpec(memory_space=pl.ANY)
    dma = pltpu.SemaphoreType.DMA
    mask_lanes = genes + length + -length % 128
    share_shapes = [(share, columns) for _, share, columns in layers]
    chunks = len(items) + 1
    results = pl.pallas_call(
        functools.partial(everything, layers, len(VECTORS)),
        out_shape=(jax.ShapeDtypeStruct((tokens, genes), full),)
        + tuple(jax.ShapeDtypeStruct(shape, low) for shape in share_shapes)
        + (jax.ShapeDtypeStruct((SUM_ROWS, 128), full),),
        in_specs=[anywhere] * (16 + len(VECTORS)),
        out_specs=(anywhere,) * (2 + len(layers)),
        scratch_shapes=[
            pltpu.VMEM(expression.shape, low),
            pltpu.VMEM(gene_masks.shape, jnp.int32),
            pltpu.VMEM(segment_ids.shape, jnp.int32),
            pltpu.VMEM((2,) + comp_mean.shape, full),
            pltpu.VMEM((1, sum(given[name].shape[0] for name in VECTORS)), full),
            dma((5,)),
            pltpu.VMEM((SLOTS, WIDE, WIDE), low),
            pltpu.VMEM((8, mask_lanes), full),
            pltpu.VMEM((2, 8, mask_lanes), full),
            pltpu.VMEM((rows, width), full),
            pltpu.VMEM((2, rows, genes), low),
            pltpu.VMEM((2, rows, latents), low),
            pltpu.VMEM((2, rows, width), low),
            pltpu.VMEM((2, rows, width), low),
            pltpu.VMEM((2, tokens, 2 * width), low),
            pltpu.VMEM((tokens, width), low),
            pltpu.VMEM((HEADS // 2, 2 * tokens, 2 * tokens), full),
            pltpu.VMEM((2, tokens, 2 * width), full),
            pltpu.VMEM((tokens, 2 * width), full),
            pltpu.VMEM((2, rows, width), low),
            pltpu.VMEM((2, rows, width), low),
            pltpu.VMEM((5, tokens, width), full),
            pltpu.VMEM((5, tokens, 128), full),
            pltpu.VMEM((GROUP, tokens, a_cols), low),
            pltpu.VMEM((GROUP, tokens, a_cols), low),
            pltpu.VMEM((t_rows, GROUP * tokens), low),
            pltpu.VMEM((width, hidden // GROUP), low),
            pltpu.VMEM((GROUP, tokens, b_cols), low),
            pltpu.VMEM((GROUP, SUM_ROWS, 128), full),
            pltpu.VMEM((GROUP, SUM_ROWS, 128), full),
            pltpu.VMEM((rows_all, WIDE), low),
            pltpu.VMEM((rows_all, WIDE), low),
            pltpu.VMEM((SUM_ROWS, 128), full),
            pltpu.VMEM((SUM_ROWS, 128), full),
            dma((SLOTS,)),
            dma((4, 2)),
            dma((4, 2)),
            dma((4,)),
            dma((3,)),
            dma((3,)),
            dma((6,)),
            dma((len(LEFT_GROUPS),)),
            dma((len(LEFT_GROUPS),)),
            dma((len(LEFT_GROUPS),)),
            dma((1,)),
            dma((1,)),
            dma((len(BLOCKS),)),
            dma((len(BLOCKS), 3)),
            dma((2, 2)),
            dma((chunks, 2)),
            dma((2,)),
        ],
        compiler_params=pltpu.CompilerParams(
            collective_id=0, has_side_effects=True, vmem_limit_bytes=63 * 1024 * 1024
        ),
    )(
        expression,
        gene_masks,
        segment_ids,
        comp_mean,
        comp_logvar,
        *[given[name].reshape(1, -1) for name in VECTORS],
        positions(length, width),
        targets,
        noise,
        *weights.values(),
    )
    input_grad, sums, tail = results[0], results[1:-1], results[-1]

    def sum_shape(name, count):
        return (count, 64) if name in (COMP_MEAN, COMP_LOGVAR) else (1, count * 128)

    finished = pl.pallas_call(
        functools.partial(finish, layers),
        out_shape=tuple(jax.ShapeDtypeStruct(shape, full) for shape in share_shapes)
        + (jax.ShapeDtypeStruct((tokens, genes), full),)
        + tuple(jax.ShapeDtypeStruct(sum_shape(name, count), full) for name, count in SUMS),
        in_specs=[anywhere] * (len(layers) + 2),
        out_specs=(anywhere,) * (len(layers) + 1 + len(SUMS)),
        scratch_shapes=[pltpu.VMEM(shape, low) for shape in share_shapes]
        + [pltpu.VMEM(shape, full) for shape in share_shapes]
        + [
            pltpu.VMEM((tokens, genes), full),
            pltpu.VMEM((SUM_ROWS, 128), full),
            pltpu.VMEM((SUMS[0][1], 64), full),
            pltpu.VMEM((SUMS[1][1], 64), full),
            dma((len(layers),)),
            dma((len(layers),)),
            dma((3,)),
            dma((SUM_ROWS,)),
        ],
        compiler_params=pltpu.CompilerParams(vmem_limit_bytes=63 * 1024 * 1024),
    )(*sums, input_grad, tail)

    groups = lax.axis_size("dp") // GROUP
    d = lax.axis_index("dp")

    def shared_out(values, axis):
        if groups == 1:
            return values
        across = [[g * GROUP + r for g in range(groups)] for r in range(GROUP)]
        within = [[g * GROUP + r for r in range(GROUP)] for g in range(groups)]
        values = lax.psum(values, "dp", axis_index_groups=across)
        values = lax.all_gather(values, "dp", axis=axis, tiled=True, axis_index_groups=within)
        size = values.shape[axis] // (groups * GROUP)
        return lax.dynamic_slice_in_dim(values, d * size, size, axis=axis)

    grads = {}
    for name, values in zip(LAYERS, finished):
        grads[name] = shared_out(values, 0)
    for (name, _), values in zip(SUMS, finished[len(layers) + 1 :]):
        if name in (COMP_MEAN, COMP_LOGVAR):
            grads[name] = shared_out(values, 1)
        else:
            grads[name] = shared_out(values.reshape(-1), 0)
    return (
        finished[len(layers)].reshape(seqs, rows, genes),
        grads[GENE],
        grads[EMB_GAIN],
        grads[EMB_SHIFT],
        grads[ATTN_GAIN],
        grads[ATTN_SHIFT],
        grads[QKV],
        grads[B_QUERY],
        grads[B_VALUE],
        grads[OUT],
        grads[B_OUT],
        grads[FFN_GAIN],
        grads[FFN_SHIFT],
        grads[UP],
        grads[B_UP],
        grads[DOWN],
        grads[B_DOWN],
        grads[BOT_GAIN],
        grads[BOT_SHIFT],
        grads[ENC],
        grads[B_ENC],
        grads[COMP_MEAN],
        grads[COMP_LOGVAR],
        grads[LAT],
        grads[B_LAT],
        grads[DEC_GAIN],
        grads[DEC_SHIFT],
        grads[DEC],
        grads[B_DEC],
    )


def solution(mesh):
    rows = P("dp", "phase", None)
    return jax.shard_map(
        body,
        mesh=mesh,
        in_specs=(rows, rows, rows, P("dp", None), P("dp", None)) + (P(),) * 27,
        out_specs=(
            rows,
            P("dp", None),
            P("dp"),
            P("dp"),
            P("dp"),
            P("dp"),
            P("dp", None),
            P("dp"),
            P("dp"),
            P("dp", None),
            P("dp"),
            P("dp"),
            P("dp"),
            P("dp", None),
            P("dp"),
            P("dp", None),
            P("dp"),
            P("dp"),
            P("dp"),
            P("dp", None),
            P("dp"),
            P(None, "dp"),
            P(None, "dp"),
            P("dp", None),
            P("dp"),
            P("dp"),
            P("dp"),
            P("dp", None),
            P("dp"),
        ),
        check_vma=False,
    )
```

```python
import functools
import math

import jax
import jax.numpy as jnp
import numpy as np
from jax import lax
from jax.experimental import pallas as pl
from jax.experimental.pallas import tpu as pltpu
from jax.sharding import PartitionSpec as P

HEADS = 16
GROUP = 8
PIECE = 128
WIDE = 1024
SLOTS = 5

norm_eps = 1e-05
mask_fill = -1000000000.0
MESH = pl.DeviceIdType.MESH

(
    H2,
    DOWN,
    GENE,
    UP,
    QKV,
    DEC,
    ENC,
    OUT,
    LAT,
    EMB_GAIN,
    EMB_SHIFT,
    ATTN_GAIN,
    ATTN_SHIFT,
    B_QKV,
    B_QUERY,
    B_VALUE,
    B_OUT,
    FFN_GAIN,
    FFN_SHIFT,
    B_UP,
    B_DOWN,
    BOT_GAIN,
    BOT_SHIFT,
    B_ENC,
    COMP_MEAN,
    COMP_LOGVAR,
    B_LAT,
    DEC_GAIN,
    DEC_SHIFT,
    B_DEC,
) = range(30)


LAYERS = (DEC, DOWN, LAT, ENC, UP, OUT, QKV, GENE)
VECTORS = (
    EMB_GAIN,
    EMB_SHIFT,
    ATTN_GAIN,
    ATTN_SHIFT,
    B_QKV,
    B_OUT,
    FFN_GAIN,
    FFN_SHIFT,
    B_UP,
    B_DOWN,
    BOT_GAIN,
    BOT_SHIFT,
    B_ENC,
    B_LAT,
    DEC_GAIN,
    DEC_SHIFT,
    B_DEC,
)

VECTOR_ROWS = {B_QKV: 3, B_UP: 4, B_DEC: 2}
VECTOR_AT = {
    name: sum(VECTOR_ROWS.get(other, 1) for other in VECTORS[:i]) for i, name in enumerate(VECTORS)
}
SUMS = (
    (COMP_MEAN, 16),
    (COMP_LOGVAR, 16),
    (EMB_GAIN, 1),
    (EMB_SHIFT, 1),
    (ATTN_GAIN, 1),
    (ATTN_SHIFT, 1),
    (B_QUERY, 1),
    (B_VALUE, 1),
    (B_OUT, 1),
    (FFN_GAIN, 1),
    (FFN_SHIFT, 1),
    (B_UP, 4),
    (B_DOWN, 1),
    (BOT_GAIN, 1),
    (BOT_SHIFT, 1),
    (B_ENC, 1),
    (B_LAT, 1),
    (DEC_GAIN, 1),
    (DEC_SHIFT, 1),
    (B_DEC, 2),
)
SUM_AT = {name: sum(n for _, n in SUMS[:i]) for i, (name, _) in enumerate(SUMS)}
SUM_ROWS = 64


def mm(left, right):
    return jnp.dot(left, right, preferred_element_type=jnp.float32)


def mm_last(left, right):
    return lax.dot_general(
        left, right, (((1,), (1,)), ((), ())), preferred_element_type=jnp.float32
    )


def mm_first(left, right):
    return lax.dot_general(
        left, right, (((0,), (0,)), ((), ())), preferred_element_type=jnp.float32
    )


def normed(values):
    center = jnp.mean(values, axis=-1, keepdims=True)
    centered = values - center
    spread = jnp.mean(centered * centered, axis=-1, keepdims=True)
    scale = lax.rsqrt(spread + norm_eps)
    return centered * scale, scale


def normed_back(grad, hat, scale, gain):
    pulled = grad * gain
    mean = jnp.mean(pulled, axis=-1, keepdims=True)
    along = jnp.mean(pulled * hat, axis=-1, keepdims=True)
    return scale * (pulled - mean - hat * along)


def column_sums(values):
    return jnp.sum(values.astype(jnp.float32), axis=0, keepdims=True)


def gelu(values):
    return values * (0.5 * (1.0 + lax.erf(values * (0.5**0.5))))


def gelu_slope(values):
    bell = 0.5 * (1.0 + lax.erf(values * (0.5**0.5)))
    return bell + values * jnp.exp(-0.5 * values * values) * (2.0 * math.pi) ** -0.5


LEFT_GROUPS = ((GENE,), (DEC,), (QKV, OUT, ENC, LAT))

BLOCKS = (
    (H2, 0, 1024, 512),
    (DEC, 0, 512, 128),
    (DEC, 512, 512, 256),
    (DEC, 1024, 1024, 512),
    (DOWN, 0, 1024, 512),
    (LAT, 0, 1024, 512),
    (ENC, 0, 1024, 512),
    (UP, 0, 1024, 512),
    (UP, 1024, 1024, 512),
    (UP, 2048, 1024, 512),
    (UP, 3072, 1024, 512),
    (OUT, 0, 1024, 512),
    (QKV, 0, 1024, 512),
    (QKV, 1024, 1024, 512),
    (QKV, 2048, 1024, 512),
    (GENE, 0, 1024, 256),
)


def grad_plan(layers):
    a_off, b_off, t_off, items, place = {}, {}, {}, [], {}
    a_at, b_at, t_at, row = 0, 0, 0, 0
    shares = {name: share for name, share, _ in layers}
    for name, share, columns in layers:
        b_off[name], t_off[name] = b_at, t_at
        for block in range(columns // WIDE):
            for start in range(0, share, PIECE):
                place[name, block, start] = row
                row += min(PIECE, share - start)
        t_at += -(-share // PIECE) * PIECE
        b_at += columns
    groups = []
    for names in LEFT_GROUPS:
        first = a_at
        for name in names:
            a_off[name] = a_at
            a_at += -(-shares[name] // PIECE) * PIECE
        groups.append((first, a_at - first))
    b_off[H2] = b_at
    shares[H2] = 0
    for block, (name, first, columns, step) in enumerate(BLOCKS):
        for start in range(0, shares[name], PIECE):
            rows = min(PIECE, shares[name] - start)
            for col in range(first, first + columns, step):
                items.append((block, start, rows, col, step, place[name, col // WIDE, start]))
    return a_off, b_off, t_off, items, row, groups, b_at + WIDE, t_at


ORDER = (
    0, 1, 2, 3, 100, 4, 5, 6, 7, 8, 9, 200, 101, 102, 10, 11, 12, 13,
    300, 14, 15, 201, 400, 1000, 202, 301, 104, 16, 401, 500, 302, 501, 502, 503, 402, 600,
    504, 601, 505, 17, 204, 103, 107, 700, 701, 602, 603, 604, 605, 304, 800, 801, 18, 702,
    703, 404, 704, 508, 509, 19, 510, 203, 108, 705, 511, 512, 902, 513, 514, 20, 515, 207,
    109, 802, 803, 804, 805, 608, 609, 303, 21, 610, 403, 708, 506, 611, 208, 110, 507, 709,
    612, 808, 307, 710, 613, 809, 22, 209, 111, 407, 520, 521, 711, 308, 810, 712, 713, 614,
    615, 408, 522, 523, 811, 210, 112, 606, 812, 714, 607, 813, 23, 309, 715, 814, 620, 706,
    621, 409, 524, 525, 211, 113, 815, 707, 416, 622, 310, 720, 806, 623, 410, 526, 544, 721,
    527, 807, 624, 212, 114, 722, 820, 625, 311, 723, 626, 411, 528, 529, 821, 724, 213, 115,
    822, 627, 312, 725, 823, 628, 412, 726, 530, 531, 629, 644, 824, 214, 106, 727, 825, 313,
    630, 728, 826, 413, 532, 631, 533, 729, 827, 215, 105, 730, 744, 314, 828, 632, 731, 414,
    534, 535, 633, 829, 206, 830, 732, 315, 634, 831, 844, 733, 415, 536, 537, 538, 635, 539,
    540, 541, 205, 734, 542, 543, 636, 832, 833, 306, 637, 735, 638, 305, 406, 736, 518, 639,
    519, 737, 834, 640, 405, 738, 516, 641, 517, 835, 739, 836, 642, 740, 837, 643, 741, 838,
    742, 839, 618, 743, 840, 841, 619, 842, 616, 843, 718, 617, 719, 716, 818, 717, 819, 816,
    817,
)


def everything(layers, n_vec, *refs):
    low, full = jnp.bfloat16, jnp.float32
    refs = list(refs)

    def pop(count):
        taken = refs[:count]
        del refs[:count]
        return taken

    expr_in, gene_masks_in, segments_in, mean_in, logvar_in = pop(5)
    vectors_in = pop(n_vec)
    table_ref, target_ref, noise_ref = pop(3)
    w_gene, w_qkv, w_out, w_up, w_down, w_enc, w_lat, w_dec = pop(8)
    (input_ref,) = pop(1)
    out_refs = dict(zip([name for name, _, _ in layers], pop(len(layers))))
    (tail_ref,) = pop(1)
    expr_ref, gene_masks_ref, segments_ref, tables, vec_all, in_sem = pop(6)
    ring, masks_own, masks_all, table, target_in, noise_in, x1_out, x1_in = pop(8)
    kv_all, query_own, probs, dkv_part, dkv_in, dx_out, dx_in = pop(7)
    hats, scales = pop(2)
    a_src, a_all, turned, up_part, b_all, v_src, v_all, near, far, v_near, v_far = pop(11)
    ring_sem, hand_send, hand_recv, hand_local, pair_send, pair_recv = pop(6)
    one_sem, a_send, a_recv, a_local, v_send, v_recv, b_send, b_recv, c_send, c_recv, o_sem = pop(11)

    expr_copy = pltpu.make_async_copy(expr_in, expr_ref, in_sem.at[0])
    mask_copies = (
        pltpu.make_async_copy(gene_masks_in, gene_masks_ref, in_sem.at[1]),
        pltpu.make_async_copy(segments_in, segments_ref, in_sem.at[2]),
    )
    mean_ref, logvar_ref = tables.at[0], tables.at[1]

    def start_inputs():
        for name, src in zip(VECTORS, vectors_in):
            at = pl.ds(VECTOR_AT[name] * WIDE, src.shape[1])
            pltpu.make_async_copy(src, vec_all.at[:, at], in_sem.at[3]).start()
        pltpu.make_async_copy(mean_in, mean_ref, in_sem.at[4]).start()
        pltpu.make_async_copy(logvar_in, logvar_ref, in_sem.at[4]).start()

    expr_copy.start()
    for copy in mask_copies:
        copy.start()

    d = lax.axis_index("dp")
    z = lax.axis_index("phase")
    base = (d // GROUP) * GROUP
    r = d % GROUP
    core, cx, cy = r % 2, (r // 2) % 2, r // 4
    partner = d + 1 - 2 * core
    owner = d - core + z // 2
    own = core == z // 2
    rc, rx, ry = r + 1 - 2 * core, r + 2 - 4 * cx, r + 4 - 8 * cy
    rxc, ryc = rx + 1 - 2 * core, ry + 1 - 2 * core
    rd = rx + 4 - 8 * cy
    rdc = rd + 1 - 2 * core
    middle = (z % 3) != 0
    inward = z + 1 - 2 * (z // 2)
    outward = z - 1 + 2 * (z // 2)
    a_off, b_off, t_off, items, _, left_groups, _, _ = grad_plan(layers)
    blocks = len(BLOCKS)
    shares = {name: share for name, share, _ in layers}
    seqs, rows, genes = expr_ref.shape
    tokens = seqs * rows
    width = table.shape[1]
    hidden = w_up.shape[1]
    length = segments_ref.shape[1]
    wide = WIDE

    barrier = pltpu.get_barrier_semaphore()

    def greet(to):
        pl.semaphore_signal(barrier, inc=1, device_id=to, device_id_type=MESH)

    for step in range(1, GROUP):
        greet((base + (r + step) % GROUP, z))
    greet((d, inward))

    @pl.when(middle)
    def _():
        greet((d, outward))

    for i in range(2):

        @pl.when(jnp.logical_not(own & (z % 2 == i)))
        def _():
            greet((owner, 2 * core + i))

    def barrier_wait():
        pl.semaphore_wait(barrier, GROUP + 1 + (z % 3 + 1) // 2 + (core + z // 2) % 2)

    def remote(src, dst, send, recv, to):
        return pltpu.make_async_remote_copy(
            src_ref=src,
            dst_ref=dst,
            send_sem=send,
            recv_sem=recv,
            device_id=to,
            device_id_type=MESH,
        )

    def columns_of(index):
        return pl.ds(*left_groups[index])

    def a_copy(index, step):
        at, to = columns_of(index), (r + step) % GROUP
        return remote(
            a_src.at[to, :, at],
            a_all.at[r, :, at],
            a_send.at[index],
            a_recv.at[index],
            (base + to, z),
        )

    def a_seven(index):
        part = a_all.at[pl.ds(0, GROUP - 1), :, columns_of(index)]
        return remote(part, part, a_send.at[index], a_recv.at[index], (base + rc, z))

    def a_own(index):
        at = columns_of(index)
        return pltpu.make_async_copy(a_src.at[r, :, at], a_all.at[r, :, at], a_local.at[index])

    def send_a(index):
        for step in range(1, GROUP):
            a_copy(index, step).start()
        a_own(index).start()

    def arrive_a(index):
        a_own(index).wait()
        a_seven(index).wait_recv()
        a_seven(index).wait_send()

    def v_copy(step):
        to = (r + step) % GROUP
        return remote(v_src.at[to], v_all.at[r], v_send.at[0], v_recv.at[0], (base + to, z))

    def v_seven():
        part = v_all.at[pl.ds(0, GROUP - 1)]
        return remote(part, part, v_send.at[0], v_recv.at[0], (base + rc, z))

    own_sums = pltpu.make_async_copy(v_src.at[r], v_all.at[r], one_sem.at[0])

    goes = (r, r, r, rx, ry, rx, ry, rd)
    counts = (0, 0, 2, 2, 2, 1, 1, 2)

    def b_start(kind, block):
        name, first, size, _ = BLOCKS[block]
        col = b_off[name] + first
        if kind in (5, 6):
            size //= 2
        if kind == 6:
            col += size
        to = (rx, ry, rc, rc, rc, ry, rx, rc)[kind]
        view = b_all.at[goes[kind], :, pl.ds(col, size)]
        recv = b_recv.at[block, counts[kind]]
        remote(view, view, b_send.at[block], recv, (base + to, z)).start()

    def b_bytes(block, way, many):
        name, first, size, _ = BLOCKS[block]
        part = b_all.at[pl.ds(0, many), :, pl.ds(b_off[name] + first, size)]
        return remote(part, part, b_send.at[block], b_recv.at[block, way], (base + rc, z))

    def neighbours_here(block):
        b_bytes(block, 0, 2).wait_recv()

    def halves_here(block):
        b_bytes(block, 1, 1).wait_recv()

    def beside_here(block):
        b_bytes(block, 2, 4).wait_recv()

    def block_sent(block):
        b_bytes(block, 0, GROUP - 1).wait_send()

    vectors = len(items)

    def place_of(ref, v_ref, index):
        if index == vectors:
            return v_ref
        _, _, count, col, size, row = items[index]
        return ref.at[pl.ds(row, count), pl.ds(col % WIDE, size)]

    def is_vec(index):
        return 1 if index == vectors else 0

    def to_middle(index, to):
        ref = place_of(near, v_near, index)
        return remote(ref, ref, c_send.at[0, is_vec(index)], c_recv.at[index, 0], (d, to))

    def across(index):
        src, dst = place_of(near, v_near, index), place_of(far, v_far, index)
        return remote(src, dst, c_send.at[1, is_vec(index)], c_recv.at[index, 1], (d, inward))

    def to_end(index, to):
        ref = place_of(far, v_far, index)
        return remote(ref, ref, c_send.at[0, is_vec(index)], c_recv.at[index, 0], (d, to))

    def result(index, ref, v_ref):
        src = place_of(ref, v_ref, index)
        if index == vectors:
            return pltpu.make_async_copy(src, tail_ref, o_sem.at[1])
        block, start, count, col, size, _ = items[index]
        to = out_refs[BLOCKS[block][0]].at[pl.ds(start, count), pl.ds(col, size)]
        return pltpu.make_async_copy(src, to, o_sem.at[0])

    def product(index):
        if index == vectors:
            return jnp.sum(v_all[...], axis=0)
        block, start, count, col, size, _ = items[index]
        name = BLOCKS[block][0]
        a_at = t_off[name] + start
        b_at = b_off[name] + col
        right = b_all[:, :, b_at : b_at + size].reshape(-1, size)
        value = mm(turned[a_at : a_at + PIECE, :], right)
        if count < PIECE:
            value = jnp.where(r % 2 == 1, value[count : 2 * count], value[:count])
        return value

    def end_push(index):
        @pl.when(jnp.logical_not(middle))
        def _():
            ref = place_of(near, v_near, index)
            ref[...] = product(index).astype(ref.dtype)
            to_middle(index, inward).start()

    def middle_join(index):
        @pl.when(middle)
        def _():
            value = product(index)
            to_middle(index, inward).wait_recv()
            ref = place_of(near, v_near, index)
            ref[...] = (value + ref[...].astype(full)).astype(ref.dtype)
            across(index).start()

    def middle_total(index):
        @pl.when(middle)
        def _():
            across(index).wait_recv()
            mine, theirs = place_of(near, v_near, index), place_of(far, v_far, index)
            both = mine[...].astype(full) + theirs[...].astype(full)
            theirs[...] = both.astype(theirs.dtype)
            to_end(index, outward).start()
            result(index, far, v_far).start()

    def end_land(index):
        @pl.when(jnp.logical_not(middle))
        def _():
            to_end(index, inward).wait_recv()
            result(index, far, v_far).start()


    up_columns = pl.ds(pl.multiple_of(r * shares[DOWN], PIECE), shares[DOWN])
    up_copy = pltpu.make_async_copy(w_up.at[:, up_columns], up_part, one_sem.at[4])
    up_copy.start()

    def make_lefts(_):
        own_columns = pl.ds(pl.multiple_of(b_off[H2] + r * PIECE, PIECE), PIECE)
        at = t_off[UP]
        turned[at : at + PIECE, :] = b_all[:, :, own_columns].reshape(-1, PIECE).T
        up_copy.wait()
        own_bias = pl.multiple_of(VECTOR_AT[B_UP] * WIDE + r * shares[DOWN], PIECE)
        bias = vec_all[:, pl.ds(own_bias, shares[DOWN])]
        count = GROUP // 2
        for slot in range(0, GROUP, count):
            h2 = b_all[slot : slot + count, :, b_off[H2] : b_off[H2] + width].reshape(-1, width)
            active = gelu(mm(h2, up_part[...]) + bias).astype(low)
            turned[
                t_off[DOWN] : t_off[DOWN] + shares[DOWN],
                slot * tokens : (slot + count) * tokens,
            ] = active.T

    group_of = {name: index for index, names in enumerate(LEFT_GROUPS) for name in names}
    gone, arrived, turned_already = [], set(), set()

    def get(block):
        if block == blocks:
            own_sums.wait()
            v_seven().wait_recv()
            return
        gone.append(block)
        beside_here(block)
        if len(gone) > 3:
            block_sent(gone[-4])
        name = BLOCKS[block][0]
        if name not in a_off or name in turned_already:
            return
        turned_already.add(name)
        if group_of[name] not in arrived:
            arrived.add(group_of[name])
            arrive_a(group_of[name])
        for start in range(0, shares[name], PIECE):
            at, to = a_off[name] + start, t_off[name] + start
            turned[to : to + PIECE, :] = a_all[:, :, at : at + PIECE].reshape(-1, PIECE).T

    table_copy = pltpu.make_async_copy(
        table_ref.at[pl.ds(z * rows, rows), :], table, one_sem.at[1]
    )
    input_copies = [
        pltpu.make_async_copy(
            hats.at[1 + j], input_ref.at[:, pl.ds(j * wide, wide)], one_sem.at[(2, 5)[j]]
        )
        for j in range(genes // wide)
    ]

    def held(j):
        each = 2 * width // wide
        return dkv_part.at[j // each, :, pl.ds(j % each * wide, wide)]

    pair_local = one_sem.at[3]
    table_copy.start()
    start_inputs()

    def rows_work():
        stream = []
        for j in range(genes // wide):
            stream.append(w_gene.at[pl.ds(j * wide, wide), :])
        for j in (1, 2, 0):
            stream.append(w_qkv.at[:, pl.ds(j * wide, wide)])
        stream.append(w_out)
        for j in range(hidden // wide):
            stream.append(w_up.at[:, pl.ds(j * wide, wide)])
            stream.append(w_down.at[pl.ds(j * wide, wide), :])
        stream.append(w_enc)
        stream.append(w_lat)
        for j in range(genes // wide):
            stream.append(w_dec.at[:, pl.ds(j * wide, wide)])
        stream.append(w_lat)
        stream.append(w_enc)
        for j in range(hidden // wide):
            stream.append(w_down.at[pl.ds(j * wide, wide), :])
            stream.append(w_up.at[:, pl.ds(j * wide, wide)])
        stream.append(w_out)
        for j in range(3):
            stream.append(w_qkv.at[:, pl.ds(j * wide, wide)])
        for j in range(genes // wide):
            stream.append(w_gene.at[pl.ds(j * wide, wide), :])

        def load(k):
            depth = stream[k].shape[0]
            return pltpu.make_async_copy(
                stream[k], ring.at[k % SLOTS, pl.ds(0, depth), :], ring_sem.at[k % SLOTS]
            )

        def fetch(k):
            if k < len(stream):
                load(k).start()

        place = [0]

        def take():
            k = place[0]
            place[0] += 1
            load(k).wait()
            return k

        def block(k):
            return ring[k % SLOTS, : stream[k].shape[0], :]

        for k in range(SLOTS):
            fetch(k)

        def hand(which, src, dst, i):
            return pltpu.make_async_remote_copy(
                src_ref=src.at[i],
                dst_ref=dst.at[z % 2],
                send_sem=hand_send.at[which, i],
                recv_sem=hand_recv.at[which, z % 2],
                device_id=(owner, 2 * core + i),
                device_id_type=MESH,
            )

        def hand_here(which, src, dst, i):
            return pltpu.make_async_copy(src.at[i], dst.at[i], hand_local.at[which])

        def hand_start(which, src, dst):
            for i in range(2):
                here = own & (z % 2 == i)

                @pl.when(here)
                def _():
                    hand_here(which, src, dst, i).start()

                @pl.when(jnp.logical_not(here))
                def _():
                    hand(which, src, dst, i).start()

        def hand_arrive(which, src, dst):
            for i in range(2):
                here = own & (z % 2 == i)

                @pl.when(here)
                def _():
                    hand_here(which, src, dst, i).wait()

                @pl.when(jnp.logical_not(here))
                def _():
                    pltpu.make_async_remote_copy(
                        src_ref=src.at[i],
                        dst_ref=dst.at[i],
                        send_sem=hand_send.at[which, i],
                        recv_sem=hand_recv.at[which, i],
                        device_id=(owner, 2 * core + i),
                        device_id_type=MESH,
                    ).wait_recv()

        def hand_sent(which, src, dst):
            for i in range(2):
                @pl.when(jnp.logical_not(own & (z % 2 == i)))
                def _():
                    hand(which, src, dst, i).wait_send()

        def pair(which, src, dst):
            return pltpu.make_async_remote_copy(
                src_ref=src,
                dst_ref=dst,
                send_sem=pair_send.at[which],
                recv_sem=pair_recv.at[which],
                device_id=(partner, z),
                device_id_type=MESH,
            )

        expr_copy.wait()
        for copy in mask_copies:
            copy.wait()
        masks_own[:seqs, :genes] = gene_masks_ref[...].astype(full)
        masks_own[:seqs, genes : genes + length] = segments_ref[...].astype(full)
        own_masks = pltpu.make_async_copy(masks_own, masks_all.at[core], pair_local)
        own_masks.start()

        def vec(name, j=0):
            at = (VECTOR_AT[name] + j) * wide
            return vec_all[:, at : at + wide]

        def put_a(name, values):
            off, share = a_off[name], shares[name]
            step = max(share, PIECE)
            for o in range(GROUP):
                start = o * share // step * step
                a_src[o, :, off : off + step] = values[:, start : start + step]

        def put_b(name, j, values):
            at = b_off[name] + j * wide
            b_all[r, :, at : at + wide] = values

        def put_sum(name, values, j=0):
            each = SUM_LANES[name]
            for o in range(values.shape[1] // 128):
                at = j * wide + o * 128
                to, row = at // (128 * each), SUM_AT[name] + at // 128 % each
                v_src[to, row : row + 1, :] = values[:, o * 128 : o * 128 + 128]

        def normalize(index, values, gain, shift):
            hat, scale = normed(values)
            hats[index] = hat
            scales[index] = jnp.broadcast_to(scale, scales.shape[1:])
            return hat * vec(gain) + vec(shift)

        def normalize_back(index, grad, gain, gain_name, shift_name):
            hat, scale = hats[index], scales[index, :, :1]
            put_sum(gain_name, jnp.sum(grad * hat, axis=0, keepdims=True))
            put_sum(shift_name, jnp.sum(grad, axis=0, keepdims=True))
            return normed_back(grad, hat, scale, vec(gain))

        keep = 1.0 - masks_own[:seqs, :genes]
        keep = jnp.concatenate(
            [jnp.broadcast_to(keep[s : s + 1], (rows, genes)) for s in range(seqs)], axis=0
        )
        masked = (expr_ref[...].reshape(tokens, genes).astype(full) * keep).astype(low)
        put_a(GENE, masked)
        table_copy.wait()
        embedded = jnp.concatenate([table[...]] * seqs, axis=0)
        for j in range(genes // wide):
            k = take()
            embedded += mm(masked[:, j * wide : (j + 1) * wide], block(k))
            fetch(k + SLOTS)
        pltpu.make_async_copy(vec_all, vec_all, in_sem.at[3]).wait()
        x1_out[...] = (
            normalize(0, embedded, EMB_GAIN, EMB_SHIFT).astype(low).reshape(seqs, rows, width)
        )
        barrier_wait()
        hand_start(0, x1_out, x1_in)
        pair(0, masks_own, masks_all.at[core]).start()
        send_a(0)
        yield
        own_masks.wait()
        pair(0, masks_own, masks_all.at[1 - core]).wait_recv()
        odd = z % 2 == 1
        both_masks = masks_all[pl.ds(z // 2, 1)][0]
        mask_row = jnp.where(odd, both_masks[1:2], both_masks[0:1])
        gene_row = mask_row[:, :genes]
        segments = mask_row[:, genes : genes + length]
        place_q = lax.broadcasted_iota(jnp.int32, (tokens, length), 0) + core * tokens
        place_k = lax.broadcasted_iota(jnp.int32, (tokens, length), 1)
        own_segments = jnp.sum(
            jnp.where(place_q == place_k, segments, 0.0), axis=-1, keepdims=True
        )
        same = own_segments == segments
        same = jnp.concatenate([same.astype(full)] * 2, axis=0) > 0.5

        hand_arrive(0, x1_out, x1_in)
        hand_start(1, noise_ref, noise_in)
        hand_start(2, target_ref, target_in)
        x1 = x1_in[...].reshape(tokens, width).astype(full)
        h1 = normalize(1, x1, ATTN_GAIN, ATTN_SHIFT).astype(low)
        put_a(QKV, h1)
        head = width // HEADS
        scale = head**-0.5
        for j in (1, 2):
            k = take()
            kv_all[core, :, (j - 1) * wide : j * wide] = (
                mm(h1, block(k)) + vec(B_QKV, j)
            ).astype(low)
            fetch(k + SLOTS)
        pair(1, kv_all.at[core], kv_all.at[core]).start()
        k = take()
        query_own[...] = (mm(h1, block(k)) + vec(B_QKV, 0)).astype(low)
        fetch(k + SLOTS)
        yield
        pair(1, kv_all.at[core], kv_all.at[1 - core]).wait_recv()

        lanes = lax.broadcasted_iota(jnp.int32, (tokens, 2 * head), 1)
        first = lanes < head
        pairs = HEADS // 2

        def two(values):
            none = jnp.zeros_like(values)
            return jnp.concatenate([jnp.where(first, values, none), jnp.where(first, none, values)], axis=0)

        def one(values):
            return jnp.where(first, values[:tokens], values[tokens:])

        def columns(p):
            return pl.ds(pl.multiple_of(p * 2 * head, 2 * head), 2 * head)

        def keys_of(p):
            return kv_all[:, :, columns(p)].reshape(length, 2 * head)

        def values_of(p):
            at = pl.ds(pl.multiple_of(width + p * 2 * head, 2 * head), 2 * head)
            return kv_all[:, :, at].reshape(length, 2 * head)

        def attend(p, carry):
            scores = mm_last(two(query_own[:, columns(p)]), keys_of(p)) * scale
            scores = jnp.where(same, scores, mask_fill)
            shifted = jnp.exp(scores - jnp.max(scores, axis=-1, keepdims=True))
            prob = shifted / jnp.sum(shifted, axis=-1, keepdims=True)
            probs[p] = prob
            att = one(mm(prob.astype(low), values_of(p))).astype(low)
            a_src[p, :, a_off[OUT] : a_off[OUT] + 2 * head] = att
            return carry

        lax.fori_loop(0, pairs, attend, 0)
        yield
        attended = jnp.concatenate(
            [a_src[o, :, a_off[OUT] : a_off[OUT] + 2 * head] for o in range(pairs)], axis=1
        )
        k = take()
        mixed = x1 + (mm(attended, block(k)) + vec(B_OUT))
        fetch(k + SLOTS)
        h2 = normalize(2, mixed, FFN_GAIN, FFN_SHIFT).astype(low)
        b_all[r, :, b_off[H2] : b_off[H2] + width] = h2
        yield
        x2 = mixed + vec(B_DOWN)
        for j in range(hidden // wide):
            k = take()
            before = mm(h2, block(k)) + vec(B_UP, j)
            fetch(k + SLOTS)
            held(j)[...] = before
            active = gelu(before).astype(low)
            k = take()
            x2 += mm(active, block(k))
            fetch(k + SLOTS)
            yield
        x2 = x2.astype(low).astype(full)
        h3 = normalize(3, x2, BOT_GAIN, BOT_SHIFT).astype(low)
        put_a(ENC, h3)
        k_enc = take()
        moments = mm(h3, block(k_enc)) + vec(B_ENC)
        latents = width // 2
        logvar = moments[:, latents:]
        hand_arrive(1, noise_ref, noise_in)
        swing = jnp.exp(0.5 * logvar) * noise_in[...].reshape(tokens, latents).astype(full)
        latent = moments[:, :latents] + swing
        latent_low = latent.astype(low)
        put_a(LAT, latent_low)
        fetch(k_enc + SLOTS)
        k_lat = take()
        lat_before = mm(latent_low, block(k_lat)) + vec(B_LAT)
        fetch(k_lat + SLOTS)
        x3 = gelu(lat_before).astype(low).astype(full)
        h4 = normalize(4, x3, DEC_GAIN, DEC_SHIFT).astype(low)
        put_a(DEC, h4)
        send_a(1)
        yield
        hand_arrive(2, target_ref, target_in)

        grad = jnp.zeros((tokens, width), full)
        for j in range(genes // wide):
            k = take()
            at = slice(j * wide, (j + 1) * wide)
            predicted = mm(h4, block(k)) + vec(B_DEC, j)
            wanted = target_in[:, :, at].reshape(tokens, wide).astype(full)
            d_pred = (gene_row[:, at] * (predicted - wanted)).astype(low)
            put_b(DEC, j, d_pred)
            put_sum(B_DEC, column_sums(d_pred), j)
            grad += mm_last(d_pred, block(k))
            fetch(k + SLOTS)
            yield
        d_x3 = normalize_back(4, grad, DEC_GAIN, DEC_GAIN, DEC_SHIFT).astype(low).astype(full)
        d_lat = (gelu_slope(lat_before) * d_x3).astype(low)
        put_b(LAT, 0, d_lat)
        put_sum(B_LAT, column_sums(d_lat))
        k = take()
        d_latent = mm_last(d_lat, block(k))
        fetch(k + SLOTS)
        yield

        pltpu.make_async_copy(tables, tables, in_sem.at[4]).wait()
        inverse = jnp.exp(-logvar_ref[...])
        volume = jnp.sum(logvar_ref[...], axis=-1, keepdims=True)
        count = mean_ref.shape[0]
        scaled = []
        for c in range(count):
            offset = latent - mean_ref[c : c + 1, :]
            quad = jnp.sum(offset * offset * inverse[c : c + 1], axis=-1, keepdims=True)
            scaled.append(-0.5 * (quad + volume[c : c + 1]))
        highest = functools.reduce(jnp.maximum, scaled)
        shares_c = [jnp.exp(s - highest) for s in scaled]
        whole = functools.reduce(jnp.add, shares_c)
        parts = [part / whole for part in shares_c]
        for c in range(count):
            pull = (latent - mean_ref[c : c + 1, :]) * inverse[c : c + 1]
            d_latent += parts[c] * pull
        d_moments = jnp.concatenate([d_latent, 0.5 * d_latent * swing - 0.5], axis=1).astype(low)
        put_b(ENC, 0, d_moments)
        put_sum(B_ENC, column_sums(d_moments))
        yield
        k = take()
        grad = mm_last(d_moments, block(k))
        fetch(k + SLOTS)
        g = normalize_back(3, grad, BOT_GAIN, BOT_GAIN, BOT_SHIFT).astype(low)
        put_b(DOWN, 0, g)
        put_sum(B_DOWN, column_sums(g))
        yield
        for c in range(count):
            offset = latent - mean_ref[c : c + 1, :]
            weighted = parts[c] * (offset * inverse[c : c + 1])
            mean_grad = -jnp.sum(weighted, axis=0, keepdims=True)
            logvar_grad = 0.5 * jnp.sum(parts[c] - weighted * offset, axis=0, keepdims=True)
            for o in range(GROUP):
                at = slice(o // 2 * 128, o // 2 * 128 + 128)
                row = SUM_AT[COMP_MEAN] + c
                v_src[o, row : row + 1, :] = mean_grad[:, at]
                row = SUM_AT[COMP_LOGVAR] + c
                v_src[o, row : row + 1, :] = logvar_grad[:, at]
        yield
        grad = jnp.zeros((tokens, width), full)
        for j in range(hidden // wide):
            k = take()
            d_active = mm_last(g, block(k))
            fetch(k + SLOTS)
            slope = gelu_slope(held(j)[...])
            d_before = (slope * d_active).astype(low)
            put_b(UP, j, d_before)
            put_sum(B_UP, column_sums(d_before), j)
            k = take()
            grad += mm_last(d_before, block(k))
            fetch(k + SLOTS)
            yield
        d_mixed = g.astype(full) + normalize_back(2, grad, FFN_GAIN, FFN_GAIN, FFN_SHIFT)
        hats[3] = d_mixed
        da = d_mixed.astype(low)
        put_b(OUT, 0, da)
        put_sum(B_OUT, column_sums(da))
        k = take()
        x1_in[...] = mm_last(da, block(k)).astype(low).reshape(seqs, rows, width)
        fetch(k + SLOTS)
        yield
        q_at = b_off[QKV]

        def attend_back(p, carry):
            query = two(query_own[:, columns(p)])
            d_att = two(x1_in[:, :, columns(p)].reshape(tokens, 2 * head))
            prob = probs[p]
            keys = keys_of(p)
            d_value = mm_first(prob.astype(low), d_att)
            d_prob = mm_last(d_att, values_of(p))
            d_score = prob * (d_prob - jnp.sum(prob * d_prob, axis=-1, keepdims=True))
            d_score = d_score.astype(low)
            d_query = one(mm(d_score, keys)) * scale
            d_key = mm_first(d_score, query) * scale
            to = pl.ds(pl.multiple_of(q_at + p * 2 * head, 2 * head), 2 * head)
            b_all[r, :, to] = d_query.astype(low)
            dkv_part[:, :, columns(p)] = d_key.reshape(2, tokens, 2 * head)
            at = pl.ds(pl.multiple_of(width + p * 2 * head, 2 * head), 2 * head)
            dkv_part[:, :, at] = d_value.reshape(2, tokens, 2 * head)
            return carry

        lax.fori_loop(0, pairs // 2, attend_back, 0)
        yield
        lax.fori_loop(pairs // 2, pairs, attend_back, 0)
        pair(2, dkv_part.at[1 - core], dkv_in).start()
        yield
        d_query = b_all[r, :, q_at : q_at + wide]
        put_sum(B_QUERY, column_sums(d_query))
        k = take()
        grad = mm_last(d_query, block(k))
        fetch(k + SLOTS)
        pair(2, dkv_part.at[1 - core], dkv_in).wait_recv()
        for j in (1, 2):
            at = slice((j - 1) * wide, j * wide)
            d_part = (dkv_part[core, :, at] + dkv_in[:, at]).astype(low)
            put_b(QKV, j, d_part)
            if j == 2:
                put_sum(B_VALUE, column_sums(d_part))
            k = take()
            grad += mm_last(d_part, block(k))
            fetch(k + SLOTS)
        d_x1 = hats[3] + normalize_back(1, grad, ATTN_GAIN, ATTN_GAIN, ATTN_SHIFT)
        dx_out[...] = d_x1.astype(low).reshape(seqs, rows, width)
        hand_start(3, dx_out, dx_in)
        yield
        hand_arrive(3, dx_out, dx_in)
        d_x1 = dx_in[...].reshape(tokens, width).astype(full)
        d_embedded = normalize_back(0, d_x1, EMB_GAIN, EMB_GAIN, EMB_SHIFT).astype(low)
        put_b(GENE, 0, d_embedded)
        for j in range(genes // wide):
            k = take()
            at = slice(j * wide, (j + 1) * wide)
            hats[1 + j] = mm_last(d_embedded, block(k)) * jnp.concatenate(
                [
                    jnp.broadcast_to(1.0 - masks_own[s : s + 1, at], (rows, wide))
                    for s in range(seqs)
                ],
                axis=0,
            )
        for copy in input_copies:
            copy.start()
        for step in range(1, GROUP):
            v_copy(step).start()
        own_sums.start()
        yield
        for copy in input_copies:
            copy.wait()
        hand_sent(0, x1_out, x1_in)
        hand_sent(1, noise_ref, noise_in)
        hand_sent(2, target_ref, target_in)
        hand_sent(3, dx_out, dx_in)
        pair(0, masks_own, masks_all.at[core]).wait_send()
        pair(1, kv_all.at[core], kv_all.at[core]).wait_send()
        pair(2, dkv_part.at[1 - core], dkv_in).wait_send()


    work = rows_work()
    for code in ORDER:
        kind, index = code // 100, code % 100
        if kind == 0:
            next(work)
        elif kind == 1:
            for way in (0, 1, 2):
                b_start(way, index)
        elif kind == 2:
            neighbours_here(index)
            for way in (5, 6, 3, 4):
                b_start(way, index)
        elif kind == 3:
            halves_here(index)
            b_start(7, index)
        else:
            (get, end_push, middle_join, middle_total, end_land, send_a, make_lefts)[kind - 4](index)
    next(work, None)
    for block in gone[-3:]:
        block_sent(block)
    v_seven().wait_send()

    def sums_sent(leg):
        for vec_too, ref in ((0, near), (1, v_near)):
            remote(ref, ref, c_send.at[leg, vec_too], c_recv.at[0, 0], (d, inward)).wait_send()

    sums_sent(0)

    @pl.when(middle)
    def _():
        sums_sent(1)

    pltpu.make_async_copy(near, far, o_sem.at[0]).wait()
    pltpu.make_async_copy(v_near, v_far, o_sem.at[1]).wait()


SUM_LANES = dict(SUMS)


def finish(layers, *refs):
    refs = list(refs)
    count = len(layers)
    low_refs, refs = refs[:count], refs[count:]
    input_ref, tail_ref = refs[:2]
    refs = refs[2:]
    full_refs, refs = refs[:count], refs[count:]
    input_out = refs[0]
    sum_refs = dict(zip([name for name, _ in SUMS], refs[1 : 1 + len(SUMS)]))
    refs = refs[1 + len(SUMS) :]
    low_bufs, full_bufs = refs[:count], refs[count : 2 * count]
    input_buf, tail_buf, mean_buf, logvar_buf, in_sem, out_sem, move_sem, sum_sem = refs[2 * count :]
    move_in = pltpu.make_async_copy(input_ref, input_buf, move_sem.at[0])
    move_out = pltpu.make_async_copy(input_buf, input_out, move_sem.at[1])
    tail_in = pltpu.make_async_copy(tail_ref, tail_buf, move_sem.at[2])
    ins = [
        pltpu.make_async_copy(src, dst, in_sem.at[i])
        for i, (src, dst) in enumerate(zip(low_refs, low_bufs))
    ]
    outs = [
        pltpu.make_async_copy(src, dst, out_sem.at[i])
        for i, (src, dst) in enumerate(zip(full_bufs, full_refs))
    ]
    for copy in ins:
        copy.start()
    tail_in.start()
    move_in.start()
    for i in range(count):
        ins[i].wait()
        full_bufs[i][...] = low_bufs[i][...].astype(jnp.float32)
        outs[i].start()
    move_in.wait()
    move_out.start()
    tail_in.wait()
    odd = lax.axis_index("dp") % 2 == 1
    rows_of = dict(SUMS)
    for name, buf in ((COMP_MEAN, mean_buf), (COMP_LOGVAR, logvar_buf)):
        both = tail_buf[SUM_AT[name] : SUM_AT[name] + rows_of[name], :]
        buf[...] = jnp.where(odd, both[:, 64:], both[:, :64])
    sums = [
        pltpu.make_async_copy(mean_buf, sum_refs[COMP_MEAN], sum_sem.at[0]),
        pltpu.make_async_copy(logvar_buf, sum_refs[COMP_LOGVAR], sum_sem.at[1]),
    ]
    for name, rows in SUMS[2:]:
        for row in range(rows):
            sums.append(
                pltpu.make_async_copy(
                    tail_buf.at[pl.ds(SUM_AT[name] + row, 1), :],
                    sum_refs[name].at[:, pl.ds(row * 128, 128)],
                    sum_sem.at[len(sums)],
                )
            )
    for copy in sums:
        copy.start()
    for copy in sums + outs:
        copy.wait()
    move_out.wait()


def positions(length, width):
    frequency = np.exp(np.arange(width // 2, dtype=np.float32) * np.float32(-2.0 * math.log(10000.0) / width))
    angles = np.arange(length, dtype=np.float32)[:, None] * frequency[None, :]
    return np.stack([np.sin(angles), np.cos(angles)], axis=-1).reshape(length, width)


def body(expression, targets, noise, gene_masks, segment_ids, w_gene, emb_gain, emb_shift, attn_gain, attn_shift, w_qkv, b_qkv, w_out, b_out, ffn_gain, ffn_shift, w_up, b_up, w_down, b_down, bot_gain, bot_shift, w_enc, b_enc, comp_mean, comp_logvar, w_lat, b_lat, dec_gain, dec_shift, w_dec, b_dec):
    low, full = jnp.bfloat16, jnp.float32
    seqs, rows, genes = expression.shape
    width = w_gene.shape[1]
    hidden = w_up.shape[1]
    latents = noise.shape[2]
    length = segment_ids.shape[1]
    tokens = seqs * rows
    given = {
        EMB_GAIN: emb_gain,
        EMB_SHIFT: emb_shift,
        ATTN_GAIN: attn_gain,
        ATTN_SHIFT: attn_shift,
        B_QKV: b_qkv,
        B_OUT: b_out,
        FFN_GAIN: ffn_gain,
        FFN_SHIFT: ffn_shift,
        B_UP: b_up,
        B_DOWN: b_down,
        BOT_GAIN: bot_gain,
        BOT_SHIFT: bot_shift,
        B_ENC: b_enc,
        B_LAT: b_lat,
        DEC_GAIN: dec_gain,
        DEC_SHIFT: dec_shift,
        B_DEC: b_dec,
    }
    weights = {
        GENE: w_gene,
        QKV: w_qkv,
        OUT: w_out,
        UP: w_up,
        DOWN: w_down,
        ENC: w_enc,
        LAT: w_lat,
        DEC: w_dec,
    }
    layers = [
        (name, weights[name].shape[0] // GROUP, weights[name].shape[1]) for name in LAYERS
    ]
    _, _, _, items, rows_all, left_groups, b_cols, t_rows = grad_plan(layers)
    a_cols = sum(size for _, size in left_groups)
    anywhere = pl.BlockSpec(memory_space=pl.ANY)
    dma = pltpu.SemaphoreType.DMA
    mask_lanes = genes + length + -length % 128
    share_shapes = [(share, columns) for _, share, columns in layers]
    chunks = len(items) + 1
    results = pl.pallas_call(
        functools.partial(everything, layers, len(VECTORS)),
        out_shape=(jax.ShapeDtypeStruct((tokens, genes), full),)
        + tuple(jax.ShapeDtypeStruct(shape, low) for shape in share_shapes)
        + (jax.ShapeDtypeStruct((SUM_ROWS, 128), full),),
        in_specs=[anywhere] * (16 + len(VECTORS)),
        out_specs=(anywhere,) * (2 + len(layers)),
        scratch_shapes=[
            pltpu.VMEM(expression.shape, low),
            pltpu.VMEM(gene_masks.shape, jnp.int32),
            pltpu.VMEM(segment_ids.shape, jnp.int32),
            pltpu.VMEM((2,) + comp_mean.shape, full),
            pltpu.VMEM((1, sum(given[name].shape[0] for name in VECTORS)), full),
            dma((5,)),
            pltpu.VMEM((SLOTS, WIDE, WIDE), low),
            pltpu.VMEM((8, mask_lanes), full),
            pltpu.VMEM((2, 8, mask_lanes), full),
            pltpu.VMEM((rows, width), full),
            pltpu.VMEM((2, rows, genes), low),
            pltpu.VMEM((2, rows, latents), low),
            pltpu.VMEM((2, rows, width), low),
            pltpu.VMEM((2, rows, width), low),
            pltpu.VMEM((2, tokens, 2 * width), low),
            pltpu.VMEM((tokens, width), low),
            pltpu.VMEM((HEADS // 2, 2 * tokens, 2 * tokens), full),
            pltpu.VMEM((2, tokens, 2 * width), full),
            pltpu.VMEM((tokens, 2 * width), full),
            pltpu.VMEM((2, rows, width), low),
            pltpu.VMEM((2, rows, width), low),
            pltpu.VMEM((5, tokens, width), full),
            pltpu.VMEM((5, tokens, 128), full),
            pltpu.VMEM((GROUP, tokens, a_cols), low),
            pltpu.VMEM((GROUP, tokens, a_cols), low),
            pltpu.VMEM((t_rows, GROUP * tokens), low),
            pltpu.VMEM((width, hidden // GROUP), low),
            pltpu.VMEM((GROUP, tokens, b_cols), low),
            pltpu.VMEM((GROUP, SUM_ROWS, 128), full),
            pltpu.VMEM((GROUP, SUM_ROWS, 128), full),
            pltpu.VMEM((rows_all, WIDE), low),
            pltpu.VMEM((rows_all, WIDE), low),
            pltpu.VMEM((SUM_ROWS, 128), full),
            pltpu.VMEM((SUM_ROWS, 128), full),
            dma((SLOTS,)),
            dma((4, 2)),
            dma((4, 2)),
            dma((4,)),
            dma((3,)),
            dma((3,)),
            dma((6,)),
            dma((len(LEFT_GROUPS),)),
            dma((len(LEFT_GROUPS),)),
            dma((len(LEFT_GROUPS),)),
            dma((1,)),
            dma((1,)),
            dma((len(BLOCKS),)),
            dma((len(BLOCKS), 3)),
            dma((2, 2)),
            dma((chunks, 2)),
            dma((2,)),
        ],
        compiler_params=pltpu.CompilerParams(
            collective_id=0, has_side_effects=True, vmem_limit_bytes=63 * 1024 * 1024
        ),
    )(
        expression,
        gene_masks,
        segment_ids,
        comp_mean,
        comp_logvar,
        *[given[name].reshape(1, -1) for name in VECTORS],
        positions(length, width),
        targets,
        noise,
        *weights.values(),
    )
    input_grad, sums, tail = results[0], results[1:-1], results[-1]

    def sum_shape(name, count):
        return (count, 64) if name in (COMP_MEAN, COMP_LOGVAR) else (1, count * 128)

    finished = pl.pallas_call(
        functools.partial(finish, layers),
        out_shape=tuple(jax.ShapeDtypeStruct(shape, full) for shape in share_shapes)
        + (jax.ShapeDtypeStruct((tokens, genes), full),)
        + tuple(jax.ShapeDtypeStruct(sum_shape(name, count), full) for name, count in SUMS),
        in_specs=[anywhere] * (len(layers) + 2),
        out_specs=(anywhere,) * (len(layers) + 1 + len(SUMS)),
        scratch_shapes=[pltpu.VMEM(shape, low) for shape in share_shapes]
        + [pltpu.VMEM(shape, full) for shape in share_shapes]
        + [
            pltpu.VMEM((tokens, genes), full),
            pltpu.VMEM((SUM_ROWS, 128), full),
            pltpu.VMEM((SUMS[0][1], 64), full),
            pltpu.VMEM((SUMS[1][1], 64), full),
            dma((len(layers),)),
            dma((len(layers),)),
            dma((3,)),
            dma((SUM_ROWS,)),
        ],
        compiler_params=pltpu.CompilerParams(vmem_limit_bytes=63 * 1024 * 1024),
    )(*sums, input_grad, tail)

    groups = lax.axis_size("dp") // GROUP
    d = lax.axis_index("dp")

    def shared_out(values, axis):
        if groups == 1:
            return values
        across = [[g * GROUP + r for g in range(groups)] for r in range(GROUP)]
        within = [[g * GROUP + r for r in range(GROUP)] for g in range(groups)]
        values = lax.psum(values, "dp", axis_index_groups=across)
        values = lax.all_gather(values, "dp", axis=axis, tiled=True, axis_index_groups=within)
        size = values.shape[axis] // (groups * GROUP)
        return lax.dynamic_slice_in_dim(values, d * size, size, axis=axis)

    grads = {}
    for name, values in zip(LAYERS, finished):
        grads[name] = shared_out(values, 0)
    for (name, _), values in zip(SUMS, finished[len(layers) + 1 :]):
        if name in (COMP_MEAN, COMP_LOGVAR):
            grads[name] = shared_out(values, 1)
        else:
            grads[name] = shared_out(values.reshape(-1), 0)
    return (
        finished[len(layers)].reshape(seqs, rows, genes),
        grads[GENE],
        grads[EMB_GAIN],
        grads[EMB_SHIFT],
        grads[ATTN_GAIN],
        grads[ATTN_SHIFT],
        grads[QKV],
        grads[B_QUERY],
        grads[B_VALUE],
        grads[OUT],
        grads[B_OUT],
        grads[FFN_GAIN],
        grads[FFN_SHIFT],
        grads[UP],
        grads[B_UP],
        grads[DOWN],
        grads[B_DOWN],
        grads[BOT_GAIN],
        grads[BOT_SHIFT],
        grads[ENC],
        grads[B_ENC],
        grads[COMP_MEAN],
        grads[COMP_LOGVAR],
        grads[LAT],
        grads[B_LAT],
        grads[DEC_GAIN],
        grads[DEC_SHIFT],
        grads[DEC],
        grads[B_DEC],
    )


def solution(mesh):
    rows = P("dp", "phase", None)
    return jax.shard_map(
        body,
        mesh=mesh,
        in_specs=(rows, rows, rows, P("dp", None), P("dp", None)) + (P(),) * 27,
        out_specs=(
            rows,
            P("dp", None),
            P("dp"),
            P("dp"),
            P("dp"),
            P("dp"),
            P("dp", None),
            P("dp"),
            P("dp"),
            P("dp", None),
            P("dp"),
            P("dp"),
            P("dp"),
            P("dp", None),
            P("dp"),
            P("dp", None),
            P("dp"),
            P("dp"),
            P("dp"),
            P("dp", None),
            P("dp"),
            P(None, "dp"),
            P(None, "dp"),
            P("dp", None),
            P("dp"),
            P("dp"),
            P("dp"),
            P("dp", None),
            P("dp"),
        ),
        check_vma=False,
    )
```

```python
import functools
import math

import jax
import jax.numpy as jnp
import numpy as np
from jax import lax
from jax.experimental import pallas as pl
from jax.experimental.pallas import tpu as pltpu
from jax.sharding import PartitionSpec as P

HEADS = 16
GROUP = 8
PIECE = 128
WIDE = 1024
SLOTS = 5

norm_eps = 1e-05
mask_fill = -1000000000.0
MESH = pl.DeviceIdType.MESH

(
    H2,
    DOWN,
    GENE,
    UP,
    QKV,
    DEC,
    ENC,
    OUT,
    LAT,
    EMB_GAIN,
    EMB_SHIFT,
    ATTN_GAIN,
    ATTN_SHIFT,
    B_QKV,
    B_QUERY,
    B_VALUE,
    B_OUT,
    FFN_GAIN,
    FFN_SHIFT,
    B_UP,
    B_DOWN,
    BOT_GAIN,
    BOT_SHIFT,
    B_ENC,
    COMP_MEAN,
    COMP_LOGVAR,
    B_LAT,
    DEC_GAIN,
    DEC_SHIFT,
    B_DEC,
) = range(30)


LAYERS = (DEC, DOWN, LAT, ENC, UP, OUT, QKV, GENE)
VECTORS = (
    EMB_GAIN,
    EMB_SHIFT,
    ATTN_GAIN,
    ATTN_SHIFT,
    B_QKV,
    B_OUT,
    FFN_GAIN,
    FFN_SHIFT,
    B_UP,
    B_DOWN,
    BOT_GAIN,
    BOT_SHIFT,
    B_ENC,
    B_LAT,
    DEC_GAIN,
    DEC_SHIFT,
    B_DEC,
)

VECTOR_ROWS = {B_QKV: 3, B_UP: 4, B_DEC: 2}
VECTOR_AT = {
    name: sum(VECTOR_ROWS.get(other, 1) for other in VECTORS[:i]) for i, name in enumerate(VECTORS)
}
SUMS = (
    (COMP_MEAN, 16),
    (COMP_LOGVAR, 16),
    (EMB_GAIN, 1),
    (EMB_SHIFT, 1),
    (ATTN_GAIN, 1),
    (ATTN_SHIFT, 1),
    (B_QUERY, 1),
    (B_VALUE, 1),
    (B_OUT, 1),
    (FFN_GAIN, 1),
    (FFN_SHIFT, 1),
    (B_UP, 4),
    (B_DOWN, 1),
    (BOT_GAIN, 1),
    (BOT_SHIFT, 1),
    (B_ENC, 1),
    (B_LAT, 1),
    (DEC_GAIN, 1),
    (DEC_SHIFT, 1),
    (B_DEC, 2),
)
SUM_AT = {name: sum(n for _, n in SUMS[:i]) for i, (name, _) in enumerate(SUMS)}
SUM_ROWS = 64


def mm(left, right):
    return jnp.dot(left, right, preferred_element_type=jnp.float32)


def mm_last(left, right):
    return lax.dot_general(
        left, right, (((1,), (1,)), ((), ())), preferred_element_type=jnp.float32
    )


def mm_first(left, right):
    return lax.dot_general(
        left, right, (((0,), (0,)), ((), ())), preferred_element_type=jnp.float32
    )


def normed(values):
    center = jnp.mean(values, axis=-1, keepdims=True)
    centered = values - center
    spread = jnp.mean(centered * centered, axis=-1, keepdims=True)
    scale = lax.rsqrt(spread + norm_eps)
    return centered * scale, scale


def normed_back(grad, hat, scale, gain):
    pulled = grad * gain
    mean = jnp.mean(pulled, axis=-1, keepdims=True)
    along = jnp.mean(pulled * hat, axis=-1, keepdims=True)
    return scale * (pulled - mean - hat * along)


def column_sums(values):
    return jnp.sum(values.astype(jnp.float32), axis=0, keepdims=True)


def gelu(values):
    return values * (0.5 * (1.0 + lax.erf(values * (0.5**0.5))))


def gelu_slope(values):
    bell = 0.5 * (1.0 + lax.erf(values * (0.5**0.5)))
    return bell + values * jnp.exp(-0.5 * values * values) * (2.0 * math.pi) ** -0.5


LEFT_GROUPS = ((GENE,), (DEC,), (QKV, OUT, ENC, LAT))

BLOCKS = (
    (H2, 0, 1024, 512),
    (DEC, 0, 512, 128),
    (DEC, 512, 512, 256),
    (DEC, 1024, 1024, 512),
    (DOWN, 0, 1024, 512),
    (LAT, 0, 1024, 512),
    (ENC, 0, 1024, 512),
    (UP, 0, 1024, 512),
    (UP, 1024, 1024, 512),
    (UP, 2048, 1024, 512),
    (UP, 3072, 1024, 512),
    (OUT, 0, 1024, 512),
    (QKV, 0, 1024, 512),
    (QKV, 1024, 1024, 512),
    (QKV, 2048, 1024, 512),
    (GENE, 0, 1024, 256),
)


def grad_plan(layers):
    a_off, b_off, t_off, items, place = {}, {}, {}, [], {}
    a_at, b_at, t_at, row = 0, 0, 0, 0
    shares = {name: share for name, share, _ in layers}
    for name, share, columns in layers:
        b_off[name], t_off[name] = b_at, t_at
        for block in range(columns // WIDE):
            for start in range(0, share, PIECE):
                place[name, block, start] = row
                row += min(PIECE, share - start)
        t_at += -(-share // PIECE) * PIECE
        b_at += columns
    groups = []
    for names in LEFT_GROUPS:
        first = a_at
        for name in names:
            a_off[name] = a_at
            a_at += -(-shares[name] // PIECE) * PIECE
        groups.append((first, a_at - first))
    b_off[H2] = b_at
    shares[H2] = 0
    for block, (name, first, columns, step) in enumerate(BLOCKS):
        for start in range(0, shares[name], PIECE):
            rows = min(PIECE, shares[name] - start)
            for col in range(first, first + columns, step):
                items.append((block, start, rows, col, step, place[name, col // WIDE, start]))
    return a_off, b_off, t_off, items, row, groups, b_at + WIDE, t_at


ORDER = (
    0, 1, 2, 3, 100, 4, 5, 6, 7, 8, 9, 200, 101, 102, 10, 11, 12, 13,
    300, 201, 104, 400, 1000, 202, 301, 103, 401, 500, 501, 502, 503, 204, 106, 302, 600, 601,
    602, 603, 700, 402, 504, 505, 701, 702, 203, 703, 800, 902, 604, 801, 802, 304, 605, 803,
    704, 404, 508, 509, 14, 705, 510, 511, 206, 512, 15, 303, 513, 514, 608, 515, 107, 804,
    16, 108, 805, 609, 403, 506, 507, 17, 708, 610, 18, 306, 709, 611, 19, 710, 612, 207,
    109, 808, 406, 518, 519, 809, 711, 613, 810, 20, 712, 614, 208, 811, 110, 713, 615, 307,
    21, 714, 606, 209, 607, 812, 813, 715, 308, 111, 407, 520, 521, 814, 618, 815, 22, 706,
    707, 619, 210, 309, 718, 112, 408, 522, 523, 806, 620, 409, 211, 113, 524, 621, 525, 310,
    807, 719, 818, 23, 720, 622, 623, 819, 721, 212, 114, 624, 820, 311, 410, 526, 527, 416,
    722, 625, 411, 528, 544, 529, 821, 723, 213, 626, 822, 115, 312, 724, 627, 823, 725, 412,
    530, 531, 628, 214, 105, 824, 726, 629, 313, 825, 727, 630, 413, 532, 533, 826, 728, 215,
    631, 644, 827, 729, 314, 632, 828, 730, 414, 534, 535, 633, 829, 205, 731, 315, 830, 634,
    732, 744, 305, 415, 536, 537, 635, 538, 733, 539, 540, 405, 541, 542, 543, 734, 516, 636,
    517, 831, 832, 637, 833, 735, 638, 736, 639, 834, 844, 737, 640, 738, 641, 835, 739, 642,
    836, 740, 643, 837, 741, 616, 838, 742, 617, 839, 743, 840, 716, 841, 717, 842, 843, 816,
    817,
)


def everything(layers, n_vec, *refs):
    low, full = jnp.bfloat16, jnp.float32
    refs = list(refs)

    def pop(count):
        taken = refs[:count]
        del refs[:count]
        return taken

    expr_in, gene_masks_in, segments_in, mean_in, logvar_in = pop(5)
    vectors_in = pop(n_vec)
    table_ref, target_ref, noise_ref = pop(3)
    w_gene, w_qkv, w_out, w_up, w_down, w_enc, w_lat, w_dec = pop(8)
    (input_ref,) = pop(1)
    out_refs = dict(zip([name for name, _, _ in layers], pop(len(layers))))
    (tail_ref,) = pop(1)
    expr_ref, gene_masks_ref, segments_ref, tables, vec_all, in_sem = pop(6)
    ring, masks_own, masks_all, table, target_in, noise_in, x1_out, x1_in = pop(8)
    kv_all, query_own, probs, dkv_part, dkv_in, dx_out, dx_in = pop(7)
    hats, scales = pop(2)
    a_src, a_all, turned, up_part, b_all, v_src, v_all, near, far, v_near, v_far = pop(11)
    ring_sem, hand_send, hand_recv, hand_local, pair_send, pair_recv = pop(6)
    one_sem, a_send, a_recv, a_local, v_send, v_recv, b_send, b_recv, c_send, c_recv, o_sem = pop(11)

    expr_copy = pltpu.make_async_copy(expr_in, expr_ref, in_sem.at[0])
    mask_copies = (
        pltpu.make_async_copy(gene_masks_in, gene_masks_ref, in_sem.at[1]),
        pltpu.make_async_copy(segments_in, segments_ref, in_sem.at[2]),
    )
    mean_ref, logvar_ref = tables.at[0], tables.at[1]

    def start_inputs():
        for name, src in zip(VECTORS, vectors_in):
            at = pl.ds(VECTOR_AT[name] * WIDE, src.shape[1])
            pltpu.make_async_copy(src, vec_all.at[:, at], in_sem.at[3]).start()
        pltpu.make_async_copy(mean_in, mean_ref, in_sem.at[4]).start()
        pltpu.make_async_copy(logvar_in, logvar_ref, in_sem.at[4]).start()

    expr_copy.start()
    for copy in mask_copies:
        copy.start()

    d = lax.axis_index("dp")
    z = lax.axis_index("phase")
    base = (d // GROUP) * GROUP
    r = d % GROUP
    core, cx, cy = r % 2, (r // 2) % 2, r // 4
    partner = d + 1 - 2 * core
    owner = d - core + z // 2
    own = core == z // 2
    rc, rx, ry = r + 1 - 2 * core, r + 2 - 4 * cx, r + 4 - 8 * cy
    rxc, ryc = rx + 1 - 2 * core, ry + 1 - 2 * core
    rd = rx + 4 - 8 * cy
    rdc = rd + 1 - 2 * core
    middle = (z % 3) != 0
    inward = z + 1 - 2 * (z // 2)
    outward = z - 1 + 2 * (z // 2)
    a_off, b_off, t_off, items, _, left_groups, _, _ = grad_plan(layers)
    blocks = len(BLOCKS)
    shares = {name: share for name, share, _ in layers}
    seqs, rows, genes = expr_ref.shape
    tokens = seqs * rows
    width = table.shape[1]
    hidden = w_up.shape[1]
    length = segments_ref.shape[1]
    wide = WIDE

    barrier = pltpu.get_barrier_semaphore()

    def greet(to):
        pl.semaphore_signal(barrier, inc=1, device_id=to, device_id_type=MESH)

    for step in range(1, GROUP):
        greet((base + (r + step) % GROUP, z))
    greet((d, inward))

    @pl.when(middle)
    def _():
        greet((d, outward))

    for i in range(2):

        @pl.when(jnp.logical_not(own & (z % 2 == i)))
        def _():
            greet((owner, 2 * core + i))

    def barrier_wait():
        pl.semaphore_wait(barrier, GROUP + 1 + (z % 3 + 1) // 2 + (core + z // 2) % 2)

    def remote(src, dst, send, recv, to):
        return pltpu.make_async_remote_copy(
            src_ref=src,
            dst_ref=dst,
            send_sem=send,
            recv_sem=recv,
            device_id=to,
            device_id_type=MESH,
        )

    def columns_of(index):
        return pl.ds(*left_groups[index])

    def a_copy(index, step):
        at, to = columns_of(index), (r + step) % GROUP
        return remote(
            a_src.at[to, :, at],
            a_all.at[r, :, at],
            a_send.at[index],
            a_recv.at[index],
            (base + to, z),
        )

    def a_seven(index):
        part = a_all.at[pl.ds(0, GROUP - 1), :, columns_of(index)]
        return remote(part, part, a_send.at[index], a_recv.at[index], (base + rc, z))

    def a_own(index):
        at = columns_of(index)
        return pltpu.make_async_copy(a_src.at[r, :, at], a_all.at[r, :, at], a_local.at[index])

    def send_a(index):
        for step in range(1, GROUP):
            a_copy(index, step).start()
        a_own(index).start()

    def arrive_a(index):
        a_own(index).wait()
        a_seven(index).wait_recv()
        a_seven(index).wait_send()

    def v_copy(step):
        to = (r + step) % GROUP
        return remote(v_src.at[to], v_all.at[r], v_send.at[0], v_recv.at[0], (base + to, z))

    def v_seven():
        part = v_all.at[pl.ds(0, GROUP - 1)]
        return remote(part, part, v_send.at[0], v_recv.at[0], (base + rc, z))

    own_sums = pltpu.make_async_copy(v_src.at[r], v_all.at[r], one_sem.at[0])

    goes = (r, r, r, rx, ry, rx, ry, rd)
    counts = (0, 0, 2, 2, 2, 1, 1, 2)

    def b_start(kind, block):
        name, first, size, _ = BLOCKS[block]
        col = b_off[name] + first
        if kind in (5, 6):
            size //= 2
        if kind == 6:
            col += size
        to = (rx, ry, rc, rc, rc, ry, rx, rc)[kind]
        view = b_all.at[goes[kind], :, pl.ds(col, size)]
        recv = b_recv.at[block, counts[kind]]
        remote(view, view, b_send.at[block], recv, (base + to, z)).start()

    def b_bytes(block, way, many):
        name, first, size, _ = BLOCKS[block]
        part = b_all.at[pl.ds(0, many), :, pl.ds(b_off[name] + first, size)]
        return remote(part, part, b_send.at[block], b_recv.at[block, way], (base + rc, z))

    def neighbours_here(block):
        b_bytes(block, 0, 2).wait_recv()

    def halves_here(block):
        b_bytes(block, 1, 1).wait_recv()

    def beside_here(block):
        b_bytes(block, 2, 4).wait_recv()

    def block_sent(block):
        b_bytes(block, 0, GROUP - 1).wait_send()

    vectors = len(items)

    def place_of(ref, v_ref, index):
        if index == vectors:
            return v_ref
        _, _, count, col, size, row = items[index]
        return ref.at[pl.ds(row, count), pl.ds(col % WIDE, size)]

    def is_vec(index):
        return 1 if index == vectors else 0

    def to_middle(index, to):
        ref = place_of(near, v_near, index)
        return remote(ref, ref, c_send.at[0, is_vec(index)], c_recv.at[index, 0], (d, to))

    def across(index):
        src, dst = place_of(near, v_near, index), place_of(far, v_far, index)
        return remote(src, dst, c_send.at[1, is_vec(index)], c_recv.at[index, 1], (d, inward))

    def to_end(index, to):
        ref = place_of(far, v_far, index)
        return remote(ref, ref, c_send.at[0, is_vec(index)], c_recv.at[index, 0], (d, to))

    def result(index, ref, v_ref):
        src = place_of(ref, v_ref, index)
        if index == vectors:
            return pltpu.make_async_copy(src, tail_ref, o_sem.at[1])
        block, start, count, col, size, _ = items[index]
        to = out_refs[BLOCKS[block][0]].at[pl.ds(start, count), pl.ds(col, size)]
        return pltpu.make_async_copy(src, to, o_sem.at[0])

    def product(index):
        if index == vectors:
            return jnp.sum(v_all[...], axis=0)
        block, start, count, col, size, _ = items[index]
        name = BLOCKS[block][0]
        a_at = t_off[name] + start
        b_at = b_off[name] + col
        right = b_all[:, :, b_at : b_at + size].reshape(-1, size)
        value = mm(turned[a_at : a_at + PIECE, :], right)
        if count < PIECE:
            value = jnp.where(r % 2 == 1, value[count : 2 * count], value[:count])
        return value

    def end_push(index):
        @pl.when(jnp.logical_not(middle))
        def _():
            ref = place_of(near, v_near, index)
            ref[...] = product(index).astype(ref.dtype)
            to_middle(index, inward).start()

    def middle_join(index):
        @pl.when(middle)
        def _():
            value = product(index)
            to_middle(index, inward).wait_recv()
            ref = place_of(near, v_near, index)
            ref[...] = (value + ref[...].astype(full)).astype(ref.dtype)
            across(index).start()

    def middle_total(index):
        @pl.when(middle)
        def _():
            across(index).wait_recv()
            mine, theirs = place_of(near, v_near, index), place_of(far, v_far, index)
            both = mine[...].astype(full) + theirs[...].astype(full)
            theirs[...] = both.astype(theirs.dtype)
            to_end(index, outward).start()
            result(index, far, v_far).start()

    def end_land(index):
        @pl.when(jnp.logical_not(middle))
        def _():
            to_end(index, inward).wait_recv()
            result(index, far, v_far).start()


    up_columns = pl.ds(pl.multiple_of(r * shares[DOWN], PIECE), shares[DOWN])
    up_copy = pltpu.make_async_copy(w_up.at[:, up_columns], up_part, one_sem.at[4])
    up_copy.start()

    def make_lefts(_):
        own_columns = pl.ds(pl.multiple_of(b_off[H2] + r * PIECE, PIECE), PIECE)
        at = t_off[UP]
        turned[at : at + PIECE, :] = b_all[:, :, own_columns].reshape(-1, PIECE).T
        up_copy.wait()
        own_bias = pl.multiple_of(VECTOR_AT[B_UP] * WIDE + r * shares[DOWN], PIECE)
        bias = vec_all[:, pl.ds(own_bias, shares[DOWN])]
        count = GROUP // 2
        for slot in range(0, GROUP, count):
            h2 = b_all[slot : slot + count, :, b_off[H2] : b_off[H2] + width].reshape(-1, width)
            active = gelu(mm(h2, up_part[...]) + bias).astype(low)
            turned[
                t_off[DOWN] : t_off[DOWN] + shares[DOWN],
                slot * tokens : (slot + count) * tokens,
            ] = active.T

    group_of = {name: index for index, names in enumerate(LEFT_GROUPS) for name in names}
    gone, arrived, turned_already = [], set(), set()

    def get(block):
        if block == blocks:
            own_sums.wait()
            v_seven().wait_recv()
            return
        gone.append(block)
        beside_here(block)
        if len(gone) > 3:
            block_sent(gone[-4])
        name = BLOCKS[block][0]
        if name not in a_off or name in turned_already:
            return
        turned_already.add(name)
        if group_of[name] not in arrived:
            arrived.add(group_of[name])
            arrive_a(group_of[name])
        for start in range(0, shares[name], PIECE):
            at, to = a_off[name] + start, t_off[name] + start
            turned[to : to + PIECE, :] = a_all[:, :, at : at + PIECE].reshape(-1, PIECE).T

    table_copy = pltpu.make_async_copy(
        table_ref.at[pl.ds(z * rows, rows), :], table, one_sem.at[1]
    )
    input_copies = [
        pltpu.make_async_copy(
            hats.at[1 + j], input_ref.at[:, pl.ds(j * wide, wide)], one_sem.at[(2, 5)[j]]
        )
        for j in range(genes // wide)
    ]

    def held(j):
        each = 2 * width // wide
        return dkv_part.at[j // each, :, pl.ds(j % each * wide, wide)]

    pair_local = one_sem.at[3]
    table_copy.start()
    start_inputs()

    def rows_work():
        stream = []
        for j in range(genes // wide):
            stream.append(w_gene.at[pl.ds(j * wide, wide), :])
        for j in (1, 2, 0):
            stream.append(w_qkv.at[:, pl.ds(j * wide, wide)])
        stream.append(w_out)
        for j in range(hidden // wide):
            stream.append(w_up.at[:, pl.ds(j * wide, wide)])
            stream.append(w_down.at[pl.ds(j * wide, wide), :])
        stream.append(w_enc)
        stream.append(w_lat)
        for j in range(genes // wide):
            stream.append(w_dec.at[:, pl.ds(j * wide, wide)])
        stream.append(w_lat)
        stream.append(w_enc)
        for j in range(hidden // wide):
            stream.append(w_down.at[pl.ds(j * wide, wide), :])
            stream.append(w_up.at[:, pl.ds(j * wide, wide)])
        stream.append(w_out)
        for j in range(3):
            stream.append(w_qkv.at[:, pl.ds(j * wide, wide)])
        for j in range(genes // wide):
            stream.append(w_gene.at[pl.ds(j * wide, wide), :])

        def load(k):
            depth = stream[k].shape[0]
            return pltpu.make_async_copy(
                stream[k], ring.at[k % SLOTS, pl.ds(0, depth), :], ring_sem.at[k % SLOTS]
            )

        def fetch(k):
            if k < len(stream):
                load(k).start()

        place = [0]

        def take():
            k = place[0]
            place[0] += 1
            load(k).wait()
            return k

        def block(k):
            return ring[k % SLOTS, : stream[k].shape[0], :]

        for k in range(SLOTS):
            fetch(k)

        def hand(which, src, dst, i):
            return pltpu.make_async_remote_copy(
                src_ref=src.at[i],
                dst_ref=dst.at[z % 2],
                send_sem=hand_send.at[which, i],
                recv_sem=hand_recv.at[which, z % 2],
                device_id=(owner, 2 * core + i),
                device_id_type=MESH,
            )

        def hand_here(which, src, dst, i):
            return pltpu.make_async_copy(src.at[i], dst.at[i], hand_local.at[which])

        def hand_start(which, src, dst):
            for i in range(2):
                here = own & (z % 2 == i)

                @pl.when(here)
                def _():
                    hand_here(which, src, dst, i).start()

                @pl.when(jnp.logical_not(here))
                def _():
                    hand(which, src, dst, i).start()

        def hand_arrive(which, src, dst):
            for i in range(2):
                here = own & (z % 2 == i)

                @pl.when(here)
                def _():
                    hand_here(which, src, dst, i).wait()

                @pl.when(jnp.logical_not(here))
                def _():
                    pltpu.make_async_remote_copy(
                        src_ref=src.at[i],
                        dst_ref=dst.at[i],
                        send_sem=hand_send.at[which, i],
                        recv_sem=hand_recv.at[which, i],
                        device_id=(owner, 2 * core + i),
                        device_id_type=MESH,
                    ).wait_recv()

        def hand_sent(which, src, dst):
            for i in range(2):
                @pl.when(jnp.logical_not(own & (z % 2 == i)))
                def _():
                    hand(which, src, dst, i).wait_send()

        def pair(which, src, dst):
            return pltpu.make_async_remote_copy(
                src_ref=src,
                dst_ref=dst,
                send_sem=pair_send.at[which],
                recv_sem=pair_recv.at[which],
                device_id=(partner, z),
                device_id_type=MESH,
            )

        expr_copy.wait()
        for copy in mask_copies:
            copy.wait()
        masks_own[:seqs, :genes] = gene_masks_ref[...].astype(full)
        masks_own[:seqs, genes : genes + length] = segments_ref[...].astype(full)
        own_masks = pltpu.make_async_copy(masks_own, masks_all.at[core], pair_local)
        own_masks.start()

        def vec(name, j=0):
            at = (VECTOR_AT[name] + j) * wide
            return vec_all[:, at : at + wide]

        def put_a(name, values):
            off, share = a_off[name], shares[name]
            step = max(share, PIECE)
            for o in range(GROUP):
                start = o * share // step * step
                a_src[o, :, off : off + step] = values[:, start : start + step]

        def put_b(name, j, values):
            at = b_off[name] + j * wide
            b_all[r, :, at : at + wide] = values

        def put_sum(name, values, j=0):
            each = SUM_LANES[name]
            for o in range(values.shape[1] // 128):
                at = j * wide + o * 128
                to, row = at // (128 * each), SUM_AT[name] + at // 128 % each
                v_src[to, row : row + 1, :] = values[:, o * 128 : o * 128 + 128]

        def normalize(index, values, gain, shift):
            hat, scale = normed(values)
            hats[index] = hat
            scales[index] = jnp.broadcast_to(scale, scales.shape[1:])
            return hat * vec(gain) + vec(shift)

        def normalize_back(index, grad, gain, gain_name, shift_name):
            hat, scale = hats[index], scales[index, :, :1]
            put_sum(gain_name, jnp.sum(grad * hat, axis=0, keepdims=True))
            put_sum(shift_name, jnp.sum(grad, axis=0, keepdims=True))
            return normed_back(grad, hat, scale, vec(gain))

        keep = 1.0 - masks_own[:seqs, :genes]
        keep = jnp.concatenate(
            [jnp.broadcast_to(keep[s : s + 1], (rows, genes)) for s in range(seqs)], axis=0
        )
        masked = (expr_ref[...].reshape(tokens, genes).astype(full) * keep).astype(low)
        put_a(GENE, masked)
        table_copy.wait()
        embedded = jnp.concatenate([table[...]] * seqs, axis=0)
        for j in range(genes // wide):
            k = take()
            embedded += mm(masked[:, j * wide : (j + 1) * wide], block(k))
            fetch(k + SLOTS)
        pltpu.make_async_copy(vec_all, vec_all, in_sem.at[3]).wait()
        x1_out[...] = (
            normalize(0, embedded, EMB_GAIN, EMB_SHIFT).astype(low).reshape(seqs, rows, width)
        )
        barrier_wait()
        hand_start(0, x1_out, x1_in)
        pair(0, masks_own, masks_all.at[core]).start()
        send_a(0)
        yield
        own_masks.wait()
        pair(0, masks_own, masks_all.at[1 - core]).wait_recv()
        odd = z % 2 == 1
        both_masks = masks_all[pl.ds(z // 2, 1)][0]
        mask_row = jnp.where(odd, both_masks[1:2], both_masks[0:1])
        gene_row = mask_row[:, :genes]
        segments = mask_row[:, genes : genes + length]
        place_q = lax.broadcasted_iota(jnp.int32, (tokens, length), 0) + core * tokens
        place_k = lax.broadcasted_iota(jnp.int32, (tokens, length), 1)
        own_segments = jnp.sum(
            jnp.where(place_q == place_k, segments, 0.0), axis=-1, keepdims=True
        )
        same = own_segments == segments
        same = jnp.concatenate([same.astype(full)] * 2, axis=0) > 0.5

        hand_arrive(0, x1_out, x1_in)
        hand_start(1, noise_ref, noise_in)
        hand_start(2, target_ref, target_in)
        x1 = x1_in[...].reshape(tokens, width).astype(full)
        h1 = normalize(1, x1, ATTN_GAIN, ATTN_SHIFT).astype(low)
        put_a(QKV, h1)
        head = width // HEADS
        scale = head**-0.5
        for j in (1, 2):
            k = take()
            kv_all[core, :, (j - 1) * wide : j * wide] = (
                mm(h1, block(k)) + vec(B_QKV, j)
            ).astype(low)
            fetch(k + SLOTS)
        pair(1, kv_all.at[core], kv_all.at[core]).start()
        k = take()
        query_own[...] = (mm(h1, block(k)) + vec(B_QKV, 0)).astype(low)
        fetch(k + SLOTS)
        yield
        pair(1, kv_all.at[core], kv_all.at[1 - core]).wait_recv()

        lanes = lax.broadcasted_iota(jnp.int32, (tokens, 2 * head), 1)
        first = lanes < head
        pairs = HEADS // 2

        def two(values):
            none = jnp.zeros_like(values)
            return jnp.concatenate([jnp.where(first, values, none), jnp.where(first, none, values)], axis=0)

        def one(values):
            return jnp.where(first, values[:tokens], values[tokens:])

        def columns(p):
            return pl.ds(pl.multiple_of(p * 2 * head, 2 * head), 2 * head)

        def keys_of(p):
            return kv_all[:, :, columns(p)].reshape(length, 2 * head)

        def values_of(p):
            at = pl.ds(pl.multiple_of(width + p * 2 * head, 2 * head), 2 * head)
            return kv_all[:, :, at].reshape(length, 2 * head)

        def attend(p, carry):
            scores = mm_last(two(query_own[:, columns(p)]), keys_of(p)) * scale
            scores = jnp.where(same, scores, mask_fill)
            shifted = jnp.exp(scores - jnp.max(scores, axis=-1, keepdims=True))
            prob = shifted / jnp.sum(shifted, axis=-1, keepdims=True)
            probs[p] = prob
            att = one(mm(prob.astype(low), values_of(p))).astype(low)
            a_src[p, :, a_off[OUT] : a_off[OUT] + 2 * head] = att
            return carry

        lax.fori_loop(0, pairs, attend, 0)
        yield
        attended = jnp.concatenate(
            [a_src[o, :, a_off[OUT] : a_off[OUT] + 2 * head] for o in range(pairs)], axis=1
        )
        k = take()
        mixed = x1 + (mm(attended, block(k)) + vec(B_OUT))
        fetch(k + SLOTS)
        h2 = normalize(2, mixed, FFN_GAIN, FFN_SHIFT).astype(low)
        b_all[r, :, b_off[H2] : b_off[H2] + width] = h2
        yield
        x2 = mixed + vec(B_DOWN)
        for j in range(hidden // wide):
            k = take()
            before = mm(h2, block(k)) + vec(B_UP, j)
            fetch(k + SLOTS)
            held(j)[...] = before
            active = gelu(before).astype(low)
            k = take()
            x2 += mm(active, block(k))
            fetch(k + SLOTS)
            yield
        x2 = x2.astype(low).astype(full)
        h3 = normalize(3, x2, BOT_GAIN, BOT_SHIFT).astype(low)
        put_a(ENC, h3)
        k_enc = take()
        moments = mm(h3, block(k_enc)) + vec(B_ENC)
        latents = width // 2
        logvar = moments[:, latents:]
        hand_arrive(1, noise_ref, noise_in)
        swing = jnp.exp(0.5 * logvar) * noise_in[...].reshape(tokens, latents).astype(full)
        latent = moments[:, :latents] + swing
        latent_low = latent.astype(low)
        put_a(LAT, latent_low)
        fetch(k_enc + SLOTS)
        k_lat = take()
        lat_before = mm(latent_low, block(k_lat)) + vec(B_LAT)
        fetch(k_lat + SLOTS)
        x3 = gelu(lat_before).astype(low).astype(full)
        h4 = normalize(4, x3, DEC_GAIN, DEC_SHIFT).astype(low)
        put_a(DEC, h4)
        send_a(1)
        yield
        hand_arrive(2, target_ref, target_in)

        grad = jnp.zeros((tokens, width), full)
        for j in range(genes // wide):
            k = take()
            at = slice(j * wide, (j + 1) * wide)
            predicted = mm(h4, block(k)) + vec(B_DEC, j)
            wanted = target_in[:, :, at].reshape(tokens, wide).astype(full)
            d_pred = (gene_row[:, at] * (predicted - wanted)).astype(low)
            put_b(DEC, j, d_pred)
            put_sum(B_DEC, column_sums(d_pred), j)
            grad += mm_last(d_pred, block(k))
            fetch(k + SLOTS)
            yield
        d_x3 = normalize_back(4, grad, DEC_GAIN, DEC_GAIN, DEC_SHIFT).astype(low).astype(full)
        d_lat = (gelu_slope(lat_before) * d_x3).astype(low)
        put_b(LAT, 0, d_lat)
        put_sum(B_LAT, column_sums(d_lat))
        k = take()
        d_latent = mm_last(d_lat, block(k))
        fetch(k + SLOTS)
        yield

        pltpu.make_async_copy(tables, tables, in_sem.at[4]).wait()
        inverse = jnp.exp(-logvar_ref[...])
        volume = jnp.sum(logvar_ref[...], axis=-1, keepdims=True)
        count = mean_ref.shape[0]
        scaled = []
        for c in range(count):
            offset = latent - mean_ref[c : c + 1, :]
            quad = jnp.sum(offset * offset * inverse[c : c + 1], axis=-1, keepdims=True)
            scaled.append(-0.5 * (quad + volume[c : c + 1]))
        highest = functools.reduce(jnp.maximum, scaled)
        shares_c = [jnp.exp(s - highest) for s in scaled]
        whole = functools.reduce(jnp.add, shares_c)
        parts = [part / whole for part in shares_c]
        for c in range(count):
            pull = (latent - mean_ref[c : c + 1, :]) * inverse[c : c + 1]
            d_latent += parts[c] * pull
        d_moments = jnp.concatenate([d_latent, 0.5 * d_latent * swing - 0.5], axis=1).astype(low)
        put_b(ENC, 0, d_moments)
        put_sum(B_ENC, column_sums(d_moments))
        yield
        k = take()
        grad = mm_last(d_moments, block(k))
        fetch(k + SLOTS)
        g = normalize_back(3, grad, BOT_GAIN, BOT_GAIN, BOT_SHIFT).astype(low)
        put_b(DOWN, 0, g)
        put_sum(B_DOWN, column_sums(g))
        yield
        for c in range(count):
            offset = latent - mean_ref[c : c + 1, :]
            weighted = parts[c] * (offset * inverse[c : c + 1])
            mean_grad = -jnp.sum(weighted, axis=0, keepdims=True)
            logvar_grad = 0.5 * jnp.sum(parts[c] - weighted * offset, axis=0, keepdims=True)
            for o in range(GROUP):
                at = slice(o // 2 * 128, o // 2 * 128 + 128)
                row = SUM_AT[COMP_MEAN] + c
                v_src[o, row : row + 1, :] = mean_grad[:, at]
                row = SUM_AT[COMP_LOGVAR] + c
                v_src[o, row : row + 1, :] = logvar_grad[:, at]
        yield
        grad = jnp.zeros((tokens, width), full)
        for j in range(hidden // wide):
            k = take()
            d_active = mm_last(g, block(k))
            fetch(k + SLOTS)
            slope = gelu_slope(held(j)[...])
            d_before = (slope * d_active).astype(low)
            put_b(UP, j, d_before)
            put_sum(B_UP, column_sums(d_before), j)
            k = take()
            grad += mm_last(d_before, block(k))
            fetch(k + SLOTS)
            yield
        d_mixed = g.astype(full) + normalize_back(2, grad, FFN_GAIN, FFN_GAIN, FFN_SHIFT)
        hats[3] = d_mixed
        da = d_mixed.astype(low)
        put_b(OUT, 0, da)
        put_sum(B_OUT, column_sums(da))
        k = take()
        x1_in[...] = mm_last(da, block(k)).astype(low).reshape(seqs, rows, width)
        fetch(k + SLOTS)
        yield
        q_at = b_off[QKV]

        def attend_back(p, carry):
            query = two(query_own[:, columns(p)])
            d_att = two(x1_in[:, :, columns(p)].reshape(tokens, 2 * head))
            prob = probs[p]
            keys = keys_of(p)
            d_value = mm_first(prob.astype(low), d_att)
            d_prob = mm_last(d_att, values_of(p))
            d_score = prob * (d_prob - jnp.sum(prob * d_prob, axis=-1, keepdims=True))
            d_score = d_score.astype(low)
            d_query = one(mm(d_score, keys)) * scale
            d_key = mm_first(d_score, query) * scale
            to = pl.ds(pl.multiple_of(q_at + p * 2 * head, 2 * head), 2 * head)
            b_all[r, :, to] = d_query.astype(low)
            dkv_part[:, :, columns(p)] = d_key.reshape(2, tokens, 2 * head)
            at = pl.ds(pl.multiple_of(width + p * 2 * head, 2 * head), 2 * head)
            dkv_part[:, :, at] = d_value.reshape(2, tokens, 2 * head)
            return carry

        lax.fori_loop(0, pairs // 2, attend_back, 0)
        yield
        lax.fori_loop(pairs // 2, pairs, attend_back, 0)
        pair(2, dkv_part.at[1 - core], dkv_in).start()
        yield
        d_query = b_all[r, :, q_at : q_at + wide]
        put_sum(B_QUERY, column_sums(d_query))
        k = take()
        grad = mm_last(d_query, block(k))
        fetch(k + SLOTS)
        pair(2, dkv_part.at[1 - core], dkv_in).wait_recv()
        for j in (1, 2):
            at = slice((j - 1) * wide, j * wide)
            d_part = (dkv_part[core, :, at] + dkv_in[:, at]).astype(low)
            put_b(QKV, j, d_part)
            if j == 2:
                put_sum(B_VALUE, column_sums(d_part))
            k = take()
            grad += mm_last(d_part, block(k))
            fetch(k + SLOTS)
        d_x1 = hats[3] + normalize_back(1, grad, ATTN_GAIN, ATTN_GAIN, ATTN_SHIFT)
        dx_out[...] = d_x1.astype(low).reshape(seqs, rows, width)
        hand_start(3, dx_out, dx_in)
        yield
        hand_arrive(3, dx_out, dx_in)
        d_x1 = dx_in[...].reshape(tokens, width).astype(full)
        d_embedded = normalize_back(0, d_x1, EMB_GAIN, EMB_GAIN, EMB_SHIFT).astype(low)
        put_b(GENE, 0, d_embedded)
        for j in range(genes // wide):
            k = take()
            at = slice(j * wide, (j + 1) * wide)
            hats[1 + j] = mm_last(d_embedded, block(k)) * jnp.concatenate(
                [
                    jnp.broadcast_to(1.0 - masks_own[s : s + 1, at], (rows, wide))
                    for s in range(seqs)
                ],
                axis=0,
            )
        for copy in input_copies:
            copy.start()
        for step in range(1, GROUP):
            v_copy(step).start()
        own_sums.start()
        yield
        for copy in input_copies:
            copy.wait()
        hand_sent(0, x1_out, x1_in)
        hand_sent(1, noise_ref, noise_in)
        hand_sent(2, target_ref, target_in)
        hand_sent(3, dx_out, dx_in)
        pair(0, masks_own, masks_all.at[core]).wait_send()
        pair(1, kv_all.at[core], kv_all.at[core]).wait_send()
        pair(2, dkv_part.at[1 - core], dkv_in).wait_send()


    work = rows_work()
    for code in ORDER:
        kind, index = code // 100, code % 100
        if kind == 0:
            next(work)
        elif kind == 1:
            for way in (0, 1, 2):
                b_start(way, index)
        elif kind == 2:
            neighbours_here(index)
            for way in (5, 6, 3, 4):
                b_start(way, index)
        elif kind == 3:
            halves_here(index)
            b_start(7, index)
        else:
            (get, end_push, middle_join, middle_total, end_land, send_a, make_lefts)[kind - 4](index)
    next(work, None)
    for block in gone[-3:]:
        block_sent(block)
    v_seven().wait_send()

    def sums_sent(leg):
        for vec_too, ref in ((0, near), (1, v_near)):
            remote(ref, ref, c_send.at[leg, vec_too], c_recv.at[0, 0], (d, inward)).wait_send()

    sums_sent(0)

    @pl.when(middle)
    def _():
        sums_sent(1)

    pltpu.make_async_copy(near, far, o_sem.at[0]).wait()
    pltpu.make_async_copy(v_near, v_far, o_sem.at[1]).wait()


SUM_LANES = dict(SUMS)


def finish(layers, *refs):
    refs = list(refs)
    count = len(layers)
    low_refs, refs = refs[:count], refs[count:]
    input_ref, tail_ref = refs[:2]
    refs = refs[2:]
    full_refs, refs = refs[:count], refs[count:]
    input_out = refs[0]
    sum_refs = dict(zip([name for name, _ in SUMS], refs[1 : 1 + len(SUMS)]))
    refs = refs[1 + len(SUMS) :]
    low_bufs, full_bufs = refs[:count], refs[count : 2 * count]
    input_buf, tail_buf, mean_buf, logvar_buf, in_sem, out_sem, move_sem, sum_sem = refs[2 * count :]
    move_in = pltpu.make_async_copy(input_ref, input_buf, move_sem.at[0])
    move_out = pltpu.make_async_copy(input_buf, input_out, move_sem.at[1])
    tail_in = pltpu.make_async_copy(tail_ref, tail_buf, move_sem.at[2])
    ins = [
        pltpu.make_async_copy(src, dst, in_sem.at[i])
        for i, (src, dst) in enumerate(zip(low_refs, low_bufs))
    ]
    outs = [
        pltpu.make_async_copy(src, dst, out_sem.at[i])
        for i, (src, dst) in enumerate(zip(full_bufs, full_refs))
    ]
    for copy in ins:
        copy.start()
    tail_in.start()
    move_in.start()
    for i in range(count):
        ins[i].wait()
        full_bufs[i][...] = low_bufs[i][...].astype(jnp.float32)
        outs[i].start()
    move_in.wait()
    move_out.start()
    tail_in.wait()
    odd = lax.axis_index("dp") % 2 == 1
    rows_of = dict(SUMS)
    for name, buf in ((COMP_MEAN, mean_buf), (COMP_LOGVAR, logvar_buf)):
        both = tail_buf[SUM_AT[name] : SUM_AT[name] + rows_of[name], :]
        buf[...] = jnp.where(odd, both[:, 64:], both[:, :64])
    sums = [
        pltpu.make_async_copy(mean_buf, sum_refs[COMP_MEAN], sum_sem.at[0]),
        pltpu.make_async_copy(logvar_buf, sum_refs[COMP_LOGVAR], sum_sem.at[1]),
    ]
    for name, rows in SUMS[2:]:
        for row in range(rows):
            sums.append(
                pltpu.make_async_copy(
                    tail_buf.at[pl.ds(SUM_AT[name] + row, 1), :],
                    sum_refs[name].at[:, pl.ds(row * 128, 128)],
                    sum_sem.at[len(sums)],
                )
            )
    for copy in sums:
        copy.start()
    for copy in sums + outs:
        copy.wait()
    move_out.wait()


def positions(length, width):
    frequency = np.exp(np.arange(width // 2, dtype=np.float32) * np.float32(-2.0 * math.log(10000.0) / width))
    angles = np.arange(length, dtype=np.float32)[:, None] * frequency[None, :]
    return np.stack([np.sin(angles), np.cos(angles)], axis=-1).reshape(length, width)


def body(expression, targets, noise, gene_masks, segment_ids, w_gene, emb_gain, emb_shift, attn_gain, attn_shift, w_qkv, b_qkv, w_out, b_out, ffn_gain, ffn_shift, w_up, b_up, w_down, b_down, bot_gain, bot_shift, w_enc, b_enc, comp_mean, comp_logvar, w_lat, b_lat, dec_gain, dec_shift, w_dec, b_dec):
    low, full = jnp.bfloat16, jnp.float32
    seqs, rows, genes = expression.shape
    width = w_gene.shape[1]
    hidden = w_up.shape[1]
    latents = noise.shape[2]
    length = segment_ids.shape[1]
    tokens = seqs * rows
    given = {
        EMB_GAIN: emb_gain,
        EMB_SHIFT: emb_shift,
        ATTN_GAIN: attn_gain,
        ATTN_SHIFT: attn_shift,
        B_QKV: b_qkv,
        B_OUT: b_out,
        FFN_GAIN: ffn_gain,
        FFN_SHIFT: ffn_shift,
        B_UP: b_up,
        B_DOWN: b_down,
        BOT_GAIN: bot_gain,
        BOT_SHIFT: bot_shift,
        B_ENC: b_enc,
        B_LAT: b_lat,
        DEC_GAIN: dec_gain,
        DEC_SHIFT: dec_shift,
        B_DEC: b_dec,
    }
    weights = {
        GENE: w_gene,
        QKV: w_qkv,
        OUT: w_out,
        UP: w_up,
        DOWN: w_down,
        ENC: w_enc,
        LAT: w_lat,
        DEC: w_dec,
    }
    layers = [
        (name, weights[name].shape[0] // GROUP, weights[name].shape[1]) for name in LAYERS
    ]
    _, _, _, items, rows_all, left_groups, b_cols, t_rows = grad_plan(layers)
    a_cols = sum(size for _, size in left_groups)
    anywhere = pl.BlockSpec(memory_space=pl.ANY)
    dma = pltpu.SemaphoreType.DMA
    mask_lanes = genes + length + -length % 128
    share_shapes = [(share, columns) for _, share, columns in layers]
    chunks = len(items) + 1
    results = pl.pallas_call(
        functools.partial(everything, layers, len(VECTORS)),
        out_shape=(jax.ShapeDtypeStruct((tokens, genes), full),)
        + tuple(jax.ShapeDtypeStruct(shape, low) for shape in share_shapes)
        + (jax.ShapeDtypeStruct((SUM_ROWS, 128), full),),
        in_specs=[anywhere] * (16 + len(VECTORS)),
        out_specs=(anywhere,) * (2 + len(layers)),
        scratch_shapes=[
            pltpu.VMEM(expression.shape, low),
            pltpu.VMEM(gene_masks.shape, jnp.int32),
            pltpu.VMEM(segment_ids.shape, jnp.int32),
            pltpu.VMEM((2,) + comp_mean.shape, full),
            pltpu.VMEM((1, sum(given[name].shape[0] for name in VECTORS)), full),
            dma((5,)),
            pltpu.VMEM((SLOTS, WIDE, WIDE), low),
            pltpu.VMEM((8, mask_lanes), full),
            pltpu.VMEM((2, 8, mask_lanes), full),
            pltpu.VMEM((rows, width), full),
            pltpu.VMEM((2, rows, genes), low),
            pltpu.VMEM((2, rows, latents), low),
            pltpu.VMEM((2, rows, width), low),
            pltpu.VMEM((2, rows, width), low),
            pltpu.VMEM((2, tokens, 2 * width), low),
            pltpu.VMEM((tokens, width), low),
            pltpu.VMEM((HEADS // 2, 2 * tokens, 2 * tokens), full),
            pltpu.VMEM((2, tokens, 2 * width), full),
            pltpu.VMEM((tokens, 2 * width), full),
            pltpu.VMEM((2, rows, width), low),
            pltpu.VMEM((2, rows, width), low),
            pltpu.VMEM((5, tokens, width), full),
            pltpu.VMEM((5, tokens, 128), full),
            pltpu.VMEM((GROUP, tokens, a_cols), low),
            pltpu.VMEM((GROUP, tokens, a_cols), low),
            pltpu.VMEM((t_rows, GROUP * tokens), low),
            pltpu.VMEM((width, hidden // GROUP), low),
            pltpu.VMEM((GROUP, tokens, b_cols), low),
            pltpu.VMEM((GROUP, SUM_ROWS, 128), full),
            pltpu.VMEM((GROUP, SUM_ROWS, 128), full),
            pltpu.VMEM((rows_all, WIDE), low),
            pltpu.VMEM((rows_all, WIDE), low),
            pltpu.VMEM((SUM_ROWS, 128), full),
            pltpu.VMEM((SUM_ROWS, 128), full),
            dma((SLOTS,)),
            dma((4, 2)),
            dma((4, 2)),
            dma((4,)),
            dma((3,)),
            dma((3,)),
            dma((6,)),
            dma((len(LEFT_GROUPS),)),
            dma((len(LEFT_GROUPS),)),
            dma((len(LEFT_GROUPS),)),
            dma((1,)),
            dma((1,)),
            dma((len(BLOCKS),)),
            dma((len(BLOCKS), 3)),
            dma((2, 2)),
            dma((chunks, 2)),
            dma((2,)),
        ],
        compiler_params=pltpu.CompilerParams(
            collective_id=0, has_side_effects=True, vmem_limit_bytes=63 * 1024 * 1024
        ),
    )(
        expression,
        gene_masks,
        segment_ids,
        comp_mean,
        comp_logvar,
        *[given[name].reshape(1, -1) for name in VECTORS],
        positions(length, width),
        targets,
        noise,
        *weights.values(),
    )
    input_grad, sums, tail = results[0], results[1:-1], results[-1]

    def sum_shape(name, count):
        return (count, 64) if name in (COMP_MEAN, COMP_LOGVAR) else (1, count * 128)

    finished = pl.pallas_call(
        functools.partial(finish, layers),
        out_shape=tuple(jax.ShapeDtypeStruct(shape, full) for shape in share_shapes)
        + (jax.ShapeDtypeStruct((tokens, genes), full),)
        + tuple(jax.ShapeDtypeStruct(sum_shape(name, count), full) for name, count in SUMS),
        in_specs=[anywhere] * (len(layers) + 2),
        out_specs=(anywhere,) * (len(layers) + 1 + len(SUMS)),
        scratch_shapes=[pltpu.VMEM(shape, low) for shape in share_shapes]
        + [pltpu.VMEM(shape, full) for shape in share_shapes]
        + [
            pltpu.VMEM((tokens, genes), full),
            pltpu.VMEM((SUM_ROWS, 128), full),
            pltpu.VMEM((SUMS[0][1], 64), full),
            pltpu.VMEM((SUMS[1][1], 64), full),
            dma((len(layers),)),
            dma((len(layers),)),
            dma((3,)),
            dma((SUM_ROWS,)),
        ],
        compiler_params=pltpu.CompilerParams(vmem_limit_bytes=63 * 1024 * 1024),
    )(*sums, input_grad, tail)

    groups = lax.axis_size("dp") // GROUP
    d = lax.axis_index("dp")

    def shared_out(values, axis):
        if groups == 1:
            return values
        across = [[g * GROUP + r for g in range(groups)] for r in range(GROUP)]
        within = [[g * GROUP + r for r in range(GROUP)] for g in range(groups)]
        values = lax.psum(values, "dp", axis_index_groups=across)
        values = lax.all_gather(values, "dp", axis=axis, tiled=True, axis_index_groups=within)
        size = values.shape[axis] // (groups * GROUP)
        return lax.dynamic_slice_in_dim(values, d * size, size, axis=axis)

    grads = {}
    for name, values in zip(LAYERS, finished):
        grads[name] = shared_out(values, 0)
    for (name, _), values in zip(SUMS, finished[len(layers) + 1 :]):
        if name in (COMP_MEAN, COMP_LOGVAR):
            grads[name] = shared_out(values, 1)
        else:
            grads[name] = shared_out(values.reshape(-1), 0)
    return (
        finished[len(layers)].reshape(seqs, rows, genes),
        grads[GENE],
        grads[EMB_GAIN],
        grads[EMB_SHIFT],
        grads[ATTN_GAIN],
        grads[ATTN_SHIFT],
        grads[QKV],
        grads[B_QUERY],
        grads[B_VALUE],
        grads[OUT],
        grads[B_OUT],
        grads[FFN_GAIN],
        grads[FFN_SHIFT],
        grads[UP],
        grads[B_UP],
        grads[DOWN],
        grads[B_DOWN],
        grads[BOT_GAIN],
        grads[BOT_SHIFT],
        grads[ENC],
        grads[B_ENC],
        grads[COMP_MEAN],
        grads[COMP_LOGVAR],
        grads[LAT],
        grads[B_LAT],
        grads[DEC_GAIN],
        grads[DEC_SHIFT],
        grads[DEC],
        grads[B_DEC],
    )


def solution(mesh):
    rows = P("dp", "phase", None)
    return jax.shard_map(
        body,
        mesh=mesh,
        in_specs=(rows, rows, rows, P("dp", None), P("dp", None)) + (P(),) * 27,
        out_specs=(
            rows,
            P("dp", None),
            P("dp"),
            P("dp"),
            P("dp"),
            P("dp"),
            P("dp", None),
            P("dp"),
            P("dp"),
            P("dp", None),
            P("dp"),
            P("dp"),
            P("dp"),
            P("dp", None),
            P("dp"),
            P("dp", None),
            P("dp"),
            P("dp"),
            P("dp"),
            P("dp", None),
            P("dp"),
            P(None, "dp"),
            P(None, "dp"),
            P("dp", None),
            P("dp"),
            P("dp"),
            P("dp"),
            P("dp", None),
            P("dp"),
        ),
        check_vma=False,
    )
```
